32 devices in a mesh: replica: 2 (over y), group: 16 (over z, x, core).
Axes of the slice: x: 2, y: 2, z: 4, core: 2. Of those that a mesh axis runs over, the one named last changes fastest.
Arguments:
- hidden_in: bfloat16 [4, 1024, 1536], P('replica', 'group'), may hold values from -6 to 6
- lengths: int32 [4], P('replica'), may hold values from 256 to 1024, as said below
- gain_attn: bfloat16 [1536], P('group'), may hold values from 0.5 to 1.5
- w_query: bfloat16 [1536, 1536], P('group'), may hold values from -0.15625 to 0.15625
- b_query: bfloat16 [1536], P('group'), may hold values from -3 to 3
- w_key: bfloat16 [1536, 256], P('group'), may hold values from -0.3125 to 0.3125
- b_key: bfloat16 [256], P('group'), may hold values from -3 to 3
- w_value: bfloat16 [1536, 256], P('group'), may hold values from -0.15625 to 0.15625
- b_value: bfloat16 [256], P('group'), may hold values from -3 to 3
- w_out: bfloat16 [1536, 1536], P('group'), may hold values from -1.75 to 1.75
- gain_mlp: bfloat16 [1536], P('group'), may hold values from 0.25 to 2.5
- w_gate: bfloat16 [1536, 8960], P('group'), may hold values from -0.15625 to 0.15625
- w_up: bfloat16 [1536, 8960], P('group'), may hold values from -0.15625 to 0.15625
- w_down: bfloat16 [1536, 8960], P('group'), may hold values from -0.125 to 0.125
- cotangent: bfloat16 [4, 1024, 1536], P('replica', 'group'), may hold values from -6 to 6
Outputs:
- layer_out: bfloat16 [4, 1024, 1536], P('replica', 'group')
- grad_input: float32 [4, 1024, 1536], P('replica', 'group')
- grad_gain_attn: float32 [1536], P('group')
- grad_w_query: float32 [1536, 1536], P('group')
- grad_b_query: float32 [1536], P('group')
- grad_w_key: float32 [1536, 256], P('group')
- grad_b_key: float32 [256], P('group')
- grad_w_value: float32 [1536, 256], P('group')
- grad_b_value: float32 [256], P('group')
- grad_w_out: float32 [1536, 1536], P('group')
- grad_gain_mlp: float32 [1536], P('group')
- grad_w_gate: float32 [1536, 8960], P('group')
- grad_w_up: float32 [1536, 8960], P('group')
- grad_w_down: float32 [1536, 8960], P('group')
The draws below stay inside these ranges and needn't reach their ends.
Inputs may be any that keep to these rules, and one draw needn't show every extreme that they name: Slot s holds valid tokens at its first lengths[s] positions; in every draw one slot has 1024 and another 1024 // 4.
All inputs are finite; a program needn't handle non-finite values.
Results may differ from the reference program's by a relative error of at most 0.034.
Values may be sent and summed in bfloat16 or wider, within the bound.
A program may use at most 512 MiB of HBM per device.

```python
import math
import jax
import jax.numpy as jnp
from jax import lax

HEADS = 12
KV_HEADS = 2
HEAD_DIM = 128
FF = 8960
D = 1536
KVW = 256
SLOT = 1024
SLOTS = 4


def draw_lengths(key, part):
    key_base = jax.random.fold_in(key, 11)
    key_long = jax.random.fold_in(key, 12)
    key_short = jax.random.fold_in(key, 13)
    drawn = jax.random.randint(key_base, (SLOTS,), SLOT // 4, SLOT + 1)
    longest = jax.random.randint(key_long, (), 0, SLOTS)
    offset = jax.random.randint(key_short, (), 1, SLOTS)
    shortest = (longest + offset) % SLOTS
    places = jnp.arange(SLOTS)
    drawn = jnp.where(places == longest, SLOT, drawn)
    drawn = jnp.where(places == shortest, SLOT // 4, drawn)
    return drawn.astype(jnp.int32)


def with_spikes(result, stream_key, source, target, parts, factor):
    def block_of(dim):
        return (jnp.arange(result.shape[dim]) // (result.shape[dim] // parts)).reshape((-1,) + (1,) * (result.ndim - 1 - dim))

    one_side = jax.random.permutation(stream_key, parts)[block_of(target)]
    far = (block_of(target) + parts // 2) % parts
    return jnp.where((block_of(source) == one_side) | (block_of(source) == far), factor * result, result)


def steps_of(stream_key, shape, shards, smallest, top_value):
    gain = 1.0
    for axis_at, shards_of in shards:
        steps = jax.random.uniform(jax.random.fold_in(jax.random.fold_in(stream_key, 6), axis_at), (shards_of,), jnp.float32, smallest / len(shards), top_value / len(shards))
        gain = gain * jnp.repeat(jnp.exp(steps), shape[axis_at] // shards_of).reshape((-1,) + (1,) * (len(shape) - 1 - axis_at))
    return gain


def noise(stream_key, shape, scale, reach, shards=(), kind=jnp.bfloat16):
    entries = scale * jax.random.normal(stream_key, shape, jnp.float32)
    if shards:
        entries = entries * steps_of(stream_key, shape, shards, -0.22, 0.18)
    return jnp.clip(entries, -reach, reach).astype(kind)


def bell_draw_with(rng, shape, width, limit, split, heavy, held_as=jnp.bfloat16):
    entries = width * jax.random.normal(rng, shape, jnp.float32)
    if split:
        entries = entries * steps_of(rng, shape, split, -0.22, 0.18)
    return jnp.clip(with_spikes(entries, jax.random.fold_in(rng, 3), *heavy), -limit, limit).astype(held_as)


def setup_inputs(seed: int = 0) -> dict:
    keys = jax.random.split(jax.random.key(seed), 16)
    hidden_in = noise(keys[0], (SLOTS, SLOT, D), 1.0, 6.0, ((0, 2), (1, 16)))
    lengths = draw_lengths(jax.random.fold_in(keys[15], 71), 0)
    gain_attn = jnp.clip(1.0 + 0.1 * jax.random.normal(keys[2], (D,), jnp.float32), 0.5, 1.5).astype(jnp.bfloat16)
    w_query = noise(keys[3], (D, D), D ** -0.5, 0.15625, ((0, 16),))
    b_query = noise(keys[4], (D,), 0.5, 3.0, ((0, 16),))
    w_key = noise(keys[5], (D, KVW), (D // 4) ** -0.5, 0.3125, ((0, 16),))
    b_key = noise(keys[6], (KVW,), 0.5, 3.0, ((0, 16),))
    w_value = noise(keys[7], (D, KVW), D ** -0.5, 0.15625, ((0, 16),))
    b_value = noise(keys[8], (KVW,), 0.5, 3.0, ((0, 16),))
    w_out = noise(keys[9], (D, D), (D // 128) ** -0.5, 1.75, ((0, 16),))
    gain_mlp = jnp.clip(jnp.exp(math.log(2.5) - 2.3025851 * jax.random.uniform(keys[10], (D,), jnp.float32) ** steps_of(keys[10], (D,), ((0, 16),), -0.2, 0.2)), 0.25, 2.5).astype(jnp.bfloat16)
    w_gate = noise(keys[11], (D, FF), D ** -0.5, 0.15625, ((0, 16),))
    w_up = noise(keys[12], (D, FF), D ** -0.5, 0.15625, ((0, 16),))
    w_down = noise(keys[13], (D, FF), (FF // 4) ** -0.5, 0.125, ((0, 16),))
    cotangent = bell_draw_with(keys[14], (SLOTS, SLOT, D), 1.0, 6.0, ((0, 2), (1, 16)), (1, 2, 16, 2.0))
    return dict(hidden_in=hidden_in, lengths=lengths, gain_attn=gain_attn, w_query=w_query, b_query=b_query, w_key=w_key, b_key=b_key, w_value=w_value, b_value=b_value, w_out=w_out, gain_mlp=gain_mlp, w_gate=w_gate, w_up=w_up, w_down=w_down, cotangent=cotangent)


EPSILON = 1e-06
THETA = 1000000.0
HIGHEST = lax.Precision.HIGHEST

@jax.custom_vjp
def low(v):
    return lax.optimization_barrier(v.astype(jnp.bfloat16)).astype(jnp.float32)

@jax.custom_vjp
def low_back(v):
    return v

def low_keep(v):
    return (low(v), None)

def low_pass(kept, grad):
    return (grad,)

def back_keep(v):
    return (v, None)

def back_low(kept, grad):
    return (low(grad),)
low.defvjp(low_keep, low_pass)
low_back.defvjp(back_keep, back_low)

def rope_tables(positions, head_dim):
    freqs = THETA ** (-jnp.arange(0, head_dim, 2).astype(jnp.float32) / head_dim)
    angles = positions.astype(jnp.float32)[:, None] * freqs[None, :]
    angles = jnp.concatenate((angles, angles), axis=-1)
    return (jnp.cos(angles), jnp.sin(angles))

def rotate(tensor, cos_table, sin_table):
    halfway = tensor.shape[-1] // 2
    turned = jnp.concatenate((-tensor[..., halfway:], tensor[..., :halfway]), axis=-1)
    return tensor * cos_table + turned * sin_table

def normalize(row_values, gain_vec):
    return row_values * lax.rsqrt(lax.optimization_barrier(jnp.mean(row_values * row_values, axis=-1, keepdims=True)) + EPSILON) * gain_vec

def slot_layer(params, slot_rows, length):
    gain_one, query_w, query_b, key_w, key_b, value_w, value_b, out_w, gain_two, gate_w, up_w, down_w = params
    slot_span = slot_rows.shape[0]
    repeat = HEADS // KV_HEADS
    score_scale = HEAD_DIM ** (-0.5)
    positions = jnp.arange(slot_span, dtype=jnp.int32)
    cos_table, sin_table = rope_tables(positions, HEAD_DIM)
    cos_heads = cos_table[:, None, :]
    sin_heads = sin_table[:, None, :]
    normed = low(normalize(slot_rows, gain_one))
    query_pre = low_back(jnp.dot(normed, query_w, precision=HIGHEST) + query_b)
    key_pre = low_back(jnp.dot(normed, key_w, precision=HIGHEST) + key_b)
    value_pre = low_back(jnp.dot(normed, value_w, precision=HIGHEST) + value_b)
    queries = low(rotate(query_pre.reshape(slot_span, HEADS, HEAD_DIM), cos_heads, sin_heads))
    queries = queries.reshape(slot_span, KV_HEADS, repeat, HEAD_DIM)
    key_rows = low(rotate(key_pre.reshape(slot_span, KV_HEADS, HEAD_DIM), cos_heads, sin_heads))
    value_rows = low(value_pre).reshape(slot_span, KV_HEADS, HEAD_DIM)
    query_step = min(512, slot_span)

    def attend_block(first_row):
        block_queries = lax.dynamic_slice_in_dim(queries, first_row, query_step, 0)
        raw_scores = jnp.einsum('qgjd,kgd->gjqk', block_queries, key_rows, precision=HIGHEST)
        scores = low_back(raw_scores * score_scale)
        query_pos = first_row + jnp.arange(query_step, dtype=jnp.int32)
        allowed = (positions[None, :] <= query_pos[:, None]) & (positions[None, :] < length)
        weights = jnp.where(allowed[None, None], jnp.exp(scores), 0.0)
        totals = lax.optimization_barrier(jnp.sum(weights, axis=-1))
        numerator = low_back(jnp.einsum('gjqk,kgd->gjqd', low(weights), value_rows, precision=HIGHEST))
        attended = numerator / totals[..., None]
        return jnp.transpose(attended, (2, 0, 1, 3)).reshape(query_step, HEADS * HEAD_DIM)
    firsts = jnp.arange(0, slot_span, query_step, dtype=jnp.int32)
    attended = lax.map(jax.checkpoint(attend_block), firsts).reshape(slot_span, HEADS * HEAD_DIM)
    branch = low_back(jnp.dot(low(attended), out_w, precision=HIGHEST))
    residual_mid = slot_rows + branch
    normed_two = low(normalize(residual_mid, gain_two))
    gate_pre = low_back(jnp.dot(normed_two, gate_w, precision=HIGHEST))
    up_pre = low_back(jnp.dot(normed_two, up_w, precision=HIGHEST))
    hidden = low(jax.nn.silu(gate_pre) * up_pre)
    final_rows = residual_mid + low_back(jnp.dot(hidden, down_w.T, precision=HIGHEST))
    valid_rows = (positions < length).astype(final_rows.dtype)[:, None]
    return final_rows * valid_rows

def reference(hidden_in, lengths, gain_attn, w_query, b_query, w_key, b_key, w_value, b_value, w_out, gain_mlp, w_gate, w_up, w_down, cotangent):
    params = tuple((member.astype(jnp.float32) for member in (gain_attn, w_query, b_query, w_key, b_key, w_value, b_value, w_out, gain_mlp, w_gate, w_up, w_down)))
    inputs = hidden_in.astype(jnp.float32)

    def forward(row_values, weights):

        def one_slot(slot_pair):
            return slot_layer(weights, slot_pair[0], slot_pair[1])
        return lax.map(jax.checkpoint(one_slot), (row_values, lengths))
    final_rows, pullback = jax.vjp(forward, inputs, params)
    grad_rows, grads = pullback(cotangent.astype(jnp.float32))
    return (final_rows.astype(jnp.bfloat16), grad_rows, grads[0], grads[1], grads[2], grads[3], grads[4], grads[5], grads[6], grads[7], grads[8], grads[9], grads[10], grads[11])
```

```python
import jax
import jax.numpy as jnp
from jax import lax
from jax.sharding import PartitionSpec as P

HEADS = 12
KV_HEADS = 2
HEAD_DIM = 128
EPSILON = 1e-06
THETA = 1000000.0
BF = jnp.bfloat16
F32 = jnp.float32


def rope_tables(positions, head_dim):
    freqs = THETA ** (-jnp.arange(0, head_dim, 2).astype(F32) / head_dim)
    angles = positions.astype(F32)[:, None] * freqs[None, :]
    angles = jnp.concatenate((angles, angles), axis=-1)
    return (jnp.cos(angles), jnp.sin(angles))


def rotate(tensor, cos_table, sin_table):
    halfway = tensor.shape[-1] // 2
    turned = jnp.concatenate((-tensor[..., halfway:], tensor[..., :halfway]), axis=-1)
    return tensor * cos_table + turned * sin_table


def rotate_back(gradient, cos_table, sin_table):
    halfway = gradient.shape[-1] // 2
    scaled = gradient * sin_table
    turned = jnp.concatenate((scaled[..., halfway:], -scaled[..., :halfway]), axis=-1)
    return gradient * cos_table + turned


def normalize(row_values, gain_vec):
    factor = lax.rsqrt(jnp.mean(row_values * row_values, axis=-1, keepdims=True) + EPSILON)
    return (row_values * factor * gain_vec, factor)


def norm_back(row_values, factor, gain_vec, upstream):
    weighted = upstream * gain_vec
    inner_mean = jnp.mean(weighted * row_values, axis=-1, keepdims=True)
    grad_rows = factor * weighted - row_values * (factor * factor * factor) * inner_mean
    grad_gain = jnp.sum(upstream * row_values * factor, axis=0)
    return (grad_rows, grad_gain)


def matmul(a, b):
    return jnp.dot(a, b, preferred_element_type=F32)


def matmul_nt(a, b):
    return lax.dot_general(a, b, (((1,), (1,)), ((), ())), preferred_element_type=F32)


def matmul_tn(a, b):
    return lax.dot_general(a, b, (((0,), (0,)), ((), ())), preferred_element_type=F32)


def arrange(per_token, kv_heads):
    block_len, head_count, head_dim = per_token.shape
    repeat = head_count // kv_heads
    grouped = per_token.reshape(block_len, kv_heads, repeat, head_dim)
    return jnp.transpose(grouped, (1, 2, 0, 3)).reshape(kv_heads, repeat * block_len, head_dim)


def restore(per_group, block_len):
    kv_heads, row_count, head_dim = per_group.shape
    repeat = row_count // block_len
    grouped = per_group.reshape(kv_heads, repeat, block_len, head_dim)
    return jnp.transpose(grouped, (2, 0, 1, 3)).reshape(block_len, kv_heads * repeat * head_dim)


def masked_exp(query_rows, key_block, row_pos, first_key, length, score_scale):
    key_step = key_block.shape[0]
    raw_scores = jnp.einsum("grd,kgd->grk", query_rows, key_block, preferred_element_type=F32)
    key_pos = first_key + jnp.arange(key_step, dtype=jnp.int32)
    allowed = (key_pos[None, :] <= row_pos[:, None]) & (key_pos[None, :] < length)
    return jnp.where(allowed[None], jnp.exp(raw_scores * score_scale), 0.0)


def block_total(length, rank_end, key_step):
    key_limit = jnp.minimum(length, rank_end)
    return (key_limit + key_step - 1) // key_step


def attend_forward(query_rows, key_all, value_all, row_pos, length, rank_end, key_step, scale):
    kv_heads, row_count, head_dim = query_rows.shape

    def visit(block_index, state_tuple):
        totals, numerator = state_tuple
        first_key = block_index * key_step
        key_block = lax.dynamic_slice_in_dim(key_all, first_key, key_step, 0)
        value_block = lax.dynamic_slice_in_dim(value_all, first_key, key_step, 0)
        weights = masked_exp(query_rows, key_block, row_pos, first_key, length, scale)
        totals = totals + jnp.sum(weights, axis=-1)
        numerator = numerator + jnp.einsum(
            "grk,kgd->grd", weights.astype(BF), value_block, preferred_element_type=F32
        )
        return (totals, numerator)

    initial = (
        jnp.zeros((kv_heads, row_count), F32),
        jnp.zeros((kv_heads, row_count, head_dim), F32),
    )
    return lax.fori_loop(0, block_total(length, rank_end, key_step), visit, initial)


def attend_backward(
    query_rows, key_all, value_all, row_pos, length, rank_end, key_step, scale, grad_numer, grad_total
):
    kv_heads, row_count, head_dim = query_rows.shape

    def visit(block_index, state_tuple):
        grad_query, grad_key, grad_value = state_tuple
        first_key = block_index * key_step
        key_block = lax.dynamic_slice_in_dim(key_all, first_key, key_step, 0)
        value_block = lax.dynamic_slice_in_dim(value_all, first_key, key_step, 0)
        weights = masked_exp(query_rows, key_block, row_pos, first_key, length, scale)
        grad_prob = jnp.einsum("grd,kgd->grk", grad_numer, value_block, preferred_element_type=F32)
        grad_score = (weights * (grad_prob + grad_total[..., None])).astype(BF)
        grad_query = grad_query + jnp.einsum(
            "grk,kgd->grd", grad_score, key_block, preferred_element_type=F32
        )
        key_part = jnp.einsum("grk,grd->kgd", grad_score, query_rows, preferred_element_type=F32)
        value_part = jnp.einsum(
            "grk,grd->kgd", weights.astype(BF), grad_numer, preferred_element_type=F32
        )
        key_old = lax.dynamic_slice_in_dim(grad_key, first_key, key_step, 0)
        value_old = lax.dynamic_slice_in_dim(grad_value, first_key, key_step, 0)
        grad_key = lax.dynamic_update_slice_in_dim(grad_key, key_old + key_part, first_key, 0)
        grad_value = lax.dynamic_update_slice_in_dim(
            grad_value, value_old + value_part, first_key, 0
        )
        return (grad_query, grad_key, grad_value)

    initial = (
        jnp.zeros((kv_heads, row_count, head_dim), F32),
        jnp.zeros(key_all.shape, F32),
        jnp.zeros(value_all.shape, F32),
    )
    return lax.fori_loop(0, block_total(length, rank_end, key_step), visit, initial)


def gather(x):
    return lax.all_gather(x, "group", axis=0, tiled=True)


def scatter_sum(x):
    return lax.psum_scatter(x, "group", scatter_dimension=0, tiled=True)


def shards(
    hidden_in,
    lengths,
    gain_attn,
    w_query,
    b_query,
    w_key,
    b_key,
    w_value,
    b_value,
    w_out,
    gain_mlp,
    w_gate,
    w_up,
    w_down,
    cotangent,
):
    group_count = lax.axis_size("group")
    group_rank = lax.axis_index("group")
    slot_count, block_len, model_width = hidden_in.shape
    kv_heads = KV_HEADS
    head_dim = HEAD_DIM
    kv_width = kv_heads * head_dim
    repeat = HEADS // kv_heads
    slot_span = block_len * group_count
    key_step = min(512, slot_span)
    score_scale = head_dim ** (-0.5)
    tokens = slot_count * block_len
    hidden_units = w_gate.shape[1]
    own_rows = w_gate.shape[0]
    share = hidden_units // group_count
    positions = group_rank * block_len + jnp.arange(block_len, dtype=jnp.int32)
    valid_rows = (positions[None, :] < lengths[:, None]).astype(F32).reshape(tokens, 1)
    cos_table, sin_table = rope_tables(positions, head_dim)
    cos_heads = cos_table[:, None, :]
    sin_heads = sin_table[:, None, :]
    rank_end = (group_rank + 1) * block_len
    row_pos = jnp.tile(positions, repeat)

    pieces = (gain_attn, b_query, b_key, b_value, gain_mlp)
    sizes = [p.shape[0] for p in pieces]
    small = gather(jnp.concatenate(pieces)[None])
    offsets = [sum(sizes[:i]) for i in range(len(sizes) + 1)]
    gain_one, query_b, key_b, value_b, gain_two = [
        small[:, offsets[i] : offsets[i + 1]].reshape(-1).astype(F32) for i in range(len(sizes))
    ]
    qkv_w = gather(jnp.concatenate((w_query, w_key, w_value), axis=1))
    out_w = gather(w_out)
    qkv_b = jnp.concatenate((query_b, key_b, value_b))

    stacked = jnp.stack((w_gate, w_up, w_down)).reshape(3, own_rows, group_count, share)
    stacked = jnp.transpose(stacked, (2, 1, 0, 3)).reshape(group_count, own_rows, 3 * share)
    columns = lax.all_to_all(stacked, "group", 0, 0, tiled=True).reshape(model_width, 3 * share)
    gate_up_w = columns[:, : 2 * share]
    down_w = columns[:, 2 * share :]

    grad_final = cotangent.reshape(tokens, model_width).astype(F32) * valid_rows
    grad_all = gather(grad_final.astype(BF))

    inputs = hidden_in.reshape(tokens, model_width).astype(F32)
    normed_full, factor_one = normalize(inputs, gain_one)
    normed = normed_full.astype(BF)
    qkv = matmul(normed, qkv_w) + qkv_b
    query_rot = rotate(
        qkv[:, :model_width].reshape(slot_count, block_len, HEADS, head_dim), cos_heads, sin_heads
    ).astype(BF)
    key_rot = rotate(
        qkv[:, model_width : model_width + kv_width].reshape(
            slot_count, block_len, kv_heads, head_dim
        ),
        cos_heads,
        sin_heads,
    ).astype(BF)
    value_low = qkv[:, model_width + kv_width :].astype(BF)
    pair = jnp.concatenate(
        (key_rot.reshape(tokens, kv_width), value_low), axis=1
    ).reshape(1, slot_count, block_len, 2 * kv_width)
    pair_all = jnp.transpose(gather(pair), (1, 0, 2, 3)).reshape(
        slot_count, slot_span, 2, kv_heads, head_dim
    )
    key_all = pair_all[:, :, 0]
    value_all = pair_all[:, :, 1]
    query_groups = []
    slot_totals = []
    slot_attended = []
    attended_rows = []
    for s in range(slot_count):
        query_rows = arrange(query_rot[s], kv_heads)
        totals, numerator = attend_forward(
            query_rows, key_all[s], value_all[s], row_pos, lengths[s], rank_end, key_step, score_scale
        )
        attended = numerator / totals[..., None]
        query_groups.append(query_rows)
        slot_totals.append(totals)
        slot_attended.append(attended)
        attended_rows.append(restore(attended, block_len))
    attended_low = jnp.concatenate(attended_rows, axis=0).astype(BF)
    residual_mid = inputs + matmul(attended_low, out_w)
    normed_two_full, factor_two = normalize(residual_mid, gain_two)
    normed_all = gather(normed_two_full.astype(BF))

    pre = matmul(normed_all, gate_up_w)
    gate_pre = pre[:, :share]
    up_pre = pre[:, share:]
    sigmoid_gate = jax.nn.sigmoid(gate_pre)
    silu_gate = gate_pre * sigmoid_gate
    hidden = (silu_gate * up_pre).astype(BF)
    grad_hidden = matmul(grad_all, down_w)
    grad_gate = (
        grad_hidden * up_pre * (sigmoid_gate * (1.0 + gate_pre * (1.0 - sigmoid_gate)))
    ).astype(BF)
    grad_up = (grad_hidden * silu_gate).astype(BF)
    gate_up_grad = jnp.concatenate((grad_gate, grad_up), axis=1)
    grad_normed_two = scatter_sum(matmul_nt(gate_up_grad, gate_up_w).astype(BF)).astype(F32)
    mlp_out = scatter_sum(matmul_nt(hidden, down_w).astype(BF)).astype(F32)
    down_term = matmul_tn(grad_all, hidden)
    gate_up_term = matmul_tn(normed_all, gate_up_grad)
    terms = jnp.concatenate((gate_up_term, down_term), axis=1).astype(BF)
    back = lax.all_to_all(
        terms.reshape(group_count, own_rows, 3 * share), "group", 0, 0, tiled=True
    )
    summed = back.astype(F32) + lax.ppermute(back, "replica", [(0, 1), (1, 0)]).astype(F32)
    summed = jnp.transpose(summed.reshape(group_count, own_rows, 3, share), (2, 1, 0, 3))
    gate_sum, up_sum, down_sum = summed.reshape(3, own_rows, hidden_units)

    final_rows = residual_mid + mlp_out
    layer_out = (final_rows * valid_rows).reshape(slot_count, block_len, model_width).astype(BF)
    grad_mid_norm, grad_gain_two = norm_back(residual_mid, factor_two, gain_two, grad_normed_two)
    grad_mid = grad_final + grad_mid_norm
    grad_branch = grad_mid.astype(BF)
    out_term = matmul_tn(attended_low, grad_branch)
    grad_attended = matmul_nt(grad_branch, out_w)
    grad_query_rows = []
    grad_pairs = []
    for s in range(slot_count):
        slot_grad = grad_attended[s * block_len : (s + 1) * block_len].reshape(
            block_len, HEADS, head_dim
        )
        grad_out = arrange(slot_grad, kv_heads)
        totals = slot_totals[s]
        grad_total = -jnp.sum(grad_out * slot_attended[s], axis=-1) / totals
        grad_numer = (grad_out / totals[..., None]).astype(BF)
        grad_query, grad_key, grad_value = attend_backward(
            query_groups[s],
            key_all[s],
            value_all[s],
            row_pos,
            lengths[s],
            rank_end,
            key_step,
            score_scale,
            grad_numer,
            grad_total,
        )
        query_back_rows = restore(grad_query * score_scale, block_len).reshape(
            block_len, HEADS, head_dim
        )
        grad_query_rows.append(
            rotate_back(query_back_rows, cos_heads, sin_heads).reshape(block_len, HEADS * head_dim)
        )
        grad_pairs.append(
            jnp.concatenate(
                (grad_key.reshape(slot_span, kv_width), grad_value.reshape(slot_span, kv_width)),
                axis=1,
            )
        )
    pair_grads = jnp.stack(grad_pairs).reshape(slot_count, group_count, block_len, 2 * kv_width)
    pair_grads = jnp.transpose(pair_grads, (1, 0, 2, 3)).astype(BF)
    pair_sum = scatter_sum(pair_grads).reshape(slot_count, block_len, 2 * kv_width).astype(F32)
    grad_query_pre = jnp.concatenate(grad_query_rows, axis=0).astype(BF)
    key_sum = pair_sum[..., :kv_width].reshape(slot_count, block_len, kv_heads, head_dim)
    grad_key_pre = (
        rotate_back(key_sum * score_scale, cos_heads, sin_heads).astype(BF).reshape(tokens, kv_width)
    )
    grad_value_pre = pair_sum[..., kv_width:].astype(BF).reshape(tokens, kv_width)
    grad_qkv = jnp.concatenate((grad_query_pre, grad_key_pre, grad_value_pre), axis=1)
    grad_normed = matmul_nt(grad_qkv, qkv_w)
    grad_in_norm, grad_gain_one = norm_back(inputs, factor_one, gain_one, grad_normed)
    grad_input = (grad_mid + grad_in_norm).reshape(slot_count, block_len, model_width)
    qkv_term = matmul_tn(normed, grad_qkv)
    qkv_bias = jnp.sum(grad_qkv.astype(F32), axis=0)

    weight_share = scatter_sum(
        jnp.concatenate((qkv_term, out_term), axis=1).astype(BF)
    )
    weight_sum = weight_share.astype(F32) + lax.ppermute(
        weight_share, "replica", [(0, 1), (1, 0)]
    ).astype(F32)
    vectors = jnp.concatenate(
        [
            grad_gain_one.reshape(group_count, -1),
            qkv_bias[:model_width].reshape(group_count, -1),
            qkv_bias[model_width : model_width + kv_width].reshape(group_count, -1),
            qkv_bias[model_width + kv_width :].reshape(group_count, -1),
            grad_gain_two.reshape(group_count, -1),
        ],
        axis=1,
    )
    vector_sum = lax.psum(scatter_sum(vectors), "replica").reshape(-1)
    gain_one_sum, query_bias_sum, key_bias_sum, value_bias_sum, gain_two_sum = [
        vector_sum[offsets[i] : offsets[i + 1]] for i in range(len(sizes))
    ]
    ends = (0, model_width, model_width + kv_width, model_width + 2 * kv_width)
    query_sum, key_sum_w, value_sum_w = [weight_sum[:, ends[i] : ends[i + 1]] for i in range(3)]
    out_sum = weight_sum[:, ends[3] :]
    return (
        layer_out,
        grad_input,
        gain_one_sum,
        query_sum,
        query_bias_sum,
        key_sum_w,
        key_bias_sum,
        value_sum_w,
        value_bias_sum,
        out_sum,
        gain_two_sum,
        gate_sum,
        up_sum,
        down_sum,
    )


def solution(mesh):
    act = P("replica", "group", None)
    vec = P("group")
    mat = P("group", None)
    return jax.shard_map(
        shards,
        mesh=mesh,
        in_specs=(act, P("replica"), vec, mat, vec, mat, vec, mat, vec, mat, vec, mat, mat, mat, act),
        out_specs=(act, act, vec, mat, vec, mat, vec, mat, vec, mat, vec, mat, mat, mat),
        check_vma=False,
    )
```

```python
import functools

import jax
import jax.numpy as jnp
from jax import lax
from jax.experimental import pallas as pl
from jax.experimental.pallas import tpu as pltpu
from jax.sharding import PartitionSpec as P

MESH = pl.DeviceIdType.MESH
NZ = 4
MAIN = 512
HEADS = 12
KV_HEADS = 2
HEAD_DIM = 128
EPSILON = 1e-06
THETA = 1000000.0
BF = jnp.bfloat16
F32 = jnp.float32


def rope_tables(positions, head_dim):
    freqs = THETA ** (-jnp.arange(0, head_dim, 2).astype(F32) / head_dim)
    angles = positions.astype(F32)[:, None] * freqs[None, :]
    angles = jnp.concatenate((angles, angles), axis=-1)
    return (jnp.cos(angles), jnp.sin(angles))


def rotate(tensor, cos_table, sin_table):
    halfway = tensor.shape[-1] // 2
    turned = jnp.concatenate((-tensor[..., halfway:], tensor[..., :halfway]), axis=-1)
    return tensor * cos_table + turned * sin_table


def rotate_back(gradient, cos_table, sin_table):
    halfway = gradient.shape[-1] // 2
    scaled = gradient * sin_table
    turned = jnp.concatenate((scaled[..., halfway:], -scaled[..., :halfway]), axis=-1)
    return gradient * cos_table + turned


def normalize(row_values, gain_vec):
    factor = lax.rsqrt(jnp.mean(row_values * row_values, axis=-1, keepdims=True) + EPSILON)
    return (row_values * factor * gain_vec, factor)


def norm_back(row_values, factor, gain_vec, upstream):
    weighted = upstream * gain_vec
    inner_mean = jnp.mean(weighted * row_values, axis=-1, keepdims=True)
    grad_rows = factor * weighted - row_values * (factor * factor * factor) * inner_mean
    grad_gain = jnp.sum(upstream * row_values * factor, axis=0)
    return (grad_rows, grad_gain)


def matmul(a, b):
    return jnp.dot(a, b, preferred_element_type=F32)


def matmul_nt(a, b):
    return lax.dot_general(a, b, (((1,), (1,)), ((), ())), preferred_element_type=F32)


def matmul_tn(a, b):
    return lax.dot_general(a, b, (((0,), (0,)), ((), ())), preferred_element_type=F32)


def arrange(per_token, kv_heads):
    block_len, head_count, head_dim = per_token.shape
    repeat = head_count // kv_heads
    grouped = per_token.reshape(block_len, kv_heads, repeat, head_dim)
    return jnp.transpose(grouped, (1, 2, 0, 3)).reshape(kv_heads, repeat * block_len, head_dim)


def restore(per_group, block_len):
    kv_heads, row_count, head_dim = per_group.shape
    repeat = row_count // block_len
    grouped = per_group.reshape(kv_heads, repeat, block_len, head_dim)
    return jnp.transpose(grouped, (2, 0, 1, 3)).reshape(block_len, kv_heads * repeat * head_dim)


def masked_exp(query_rows, key_block, row_pos, first_key, length, score_scale):
    key_step = key_block.shape[0]
    raw_scores = jnp.einsum("grd,kgd->grk", query_rows, key_block, preferred_element_type=F32)
    key_pos = first_key + jnp.arange(key_step, dtype=jnp.int32)
    allowed = (key_pos[None, :] <= row_pos[:, None]) & (key_pos[None, :] < length)
    return jnp.where(allowed[None], jnp.exp(raw_scores * score_scale), 0.0)


def block_total(length, rank_end, key_step):
    key_limit = jnp.minimum(length, rank_end)
    return (key_limit + key_step - 1) // key_step


def attend_forward(query_rows, key_all, value_all, row_pos, length, rank_end, key_step, scale):
    kv_heads, row_count, head_dim = query_rows.shape

    def visit(block_index, state_tuple):
        totals, numerator = state_tuple
        first_key = block_index * key_step
        key_block = lax.dynamic_slice_in_dim(key_all, first_key, key_step, 0)
        value_block = lax.dynamic_slice_in_dim(value_all, first_key, key_step, 0)
        weights = masked_exp(query_rows, key_block, row_pos, first_key, length, scale)
        totals = totals + jnp.sum(weights, axis=-1)
        numerator = numerator + jnp.einsum(
            "grk,kgd->grd", weights.astype(BF), value_block, preferred_element_type=F32
        )
        return (totals, numerator)

    initial = (
        jnp.zeros((kv_heads, row_count), F32),
        jnp.zeros((kv_heads, row_count, head_dim), F32),
    )
    return lax.fori_loop(0, block_total(length, rank_end, key_step), visit, initial)


def attend_backward(
    query_rows, key_all, value_all, row_pos, length, rank_end, key_step, scale, grad_numer, grad_total
):
    kv_heads, row_count, head_dim = query_rows.shape

    def visit(block_index, state_tuple):
        grad_query, grad_key, grad_value = state_tuple
        first_key = block_index * key_step
        key_block = lax.dynamic_slice_in_dim(key_all, first_key, key_step, 0)
        value_block = lax.dynamic_slice_in_dim(value_all, first_key, key_step, 0)
        weights = masked_exp(query_rows, key_block, row_pos, first_key, length, scale)
        grad_prob = jnp.einsum("grd,kgd->grk", grad_numer, value_block, preferred_element_type=F32)
        grad_score = (weights * (grad_prob + grad_total[..., None])).astype(BF)
        grad_query = grad_query + jnp.einsum(
            "grk,kgd->grd", grad_score, key_block, preferred_element_type=F32
        )
        key_part = jnp.einsum("grk,grd->kgd", grad_score, query_rows, preferred_element_type=F32)
        value_part = jnp.einsum(
            "grk,grd->kgd", weights.astype(BF), grad_numer, preferred_element_type=F32
        )
        key_old = lax.dynamic_slice_in_dim(grad_key, first_key, key_step, 0)
        value_old = lax.dynamic_slice_in_dim(grad_value, first_key, key_step, 0)
        grad_key = lax.dynamic_update_slice_in_dim(grad_key, key_old + key_part, first_key, 0)
        grad_value = lax.dynamic_update_slice_in_dim(
            grad_value, value_old + value_part, first_key, 0
        )
        return (grad_query, grad_key, grad_value)

    initial = (
        jnp.zeros((kv_heads, row_count, head_dim), F32),
        jnp.zeros(key_all.shape, F32),
        jnp.zeros(value_all.shape, F32),
    )
    return lax.fori_loop(0, block_total(length, rank_end, key_step), visit, initial)


def place():
    g = lax.axis_index("group")
    r = lax.axis_index("replica")
    return r, g // 4, lax.rem(g // 2, 2), lax.rem(g, 2)

def idx(z, x, c):
    return (z * 2 + x) * 2 + c

def greet(r, z, x, c, with_y=False):
    bar = pltpu.get_barrier_semaphore()
    def hail(dev):
        pl.semaphore_signal(bar, inc=1, device_id=dev, device_id_type=MESH)
    hail((r, idx(z, 1 - x, c)))
    hail((r, idx(z, x, 1 - c)))
    if with_y:
        hail((1 - r, idx(z, x, c)))
    @pl.when(z > 0)
    def _():
        hail((r, idx(z - 1, x, c)))
    @pl.when(z < NZ - 1)
    def _():
        hail((r, idx(z + 1, x, c)))
    ends = jnp.where((z > 0) & (z < NZ - 1), 1, 0)
    pl.semaphore_wait(bar, (4 if with_y else 3) + ends)

def when(cond, fn):
    pl.when(cond)(fn)

class Gather:
    def __init__(self, at, src, out, send, recv, local):
        self.r, self.z, self.x, self.c = at
        self.src, self.out, self.send, self.recv, self.local = src, out, send, recv, local
    def put(self, src, b, k, dev):
        pltpu.make_async_remote_copy(src, self.out.at[b], self.send.at[k], self.recv.at[b], device_id=dev, device_id_type=MESH).start()
    def sent(self, k):
        b = 0
        pltpu.make_async_remote_copy(self.out.at[b], self.out.at[b], self.send.at[k], self.recv.at[b], device_id=(self.r, 0), device_id_type=MESH).wait_send()
    def got(self, b):
        pltpu.make_async_remote_copy(self.out.at[b], self.out.at[b], self.send.at[0], self.recv.at[b], device_id=(self.r, 0), device_id_type=MESH).wait_recv()
    def zdev(self, s): return (self.r, idx(self.z + s, self.x, self.c))
    def xdev(self): return (self.r, idx(self.z, 1 - self.x, self.c))
    def cdev(self): return (self.r, idx(self.z, self.x, 1 - self.c))
    def begin(self):
        z, x, c = self.z, self.x, self.c
        me = idx(z, x, c)
        for s in (1, -1):
            when(self.inside(z + s), lambda s=s: self.put(self.src, me, 0 if s == 1 else 3, self.zdev(s)))
        self.put(self.src, me, 6 + z, self.xdev())
        self.put(self.src, me, 10 + 2 * z + x, self.cdev())
        pltpu.make_async_copy(self.src, self.out.at[me], self.local).start()
    def inside(self, z): return (z >= 0) & (z < NZ)
    def step_z(self, d):
        z, x, c = self.z, self.x, self.c
        for s in (-1, 1):
            zz = z + s * d
            def arrive(s=s, zz=zz):
                b = idx(zz, x, c)
                self.got(b)
                if d < NZ - 1:
                    when(self.inside(z - s), lambda: self.put(self.out.at[b], b, (0 if s == -1 else 3) + d, self.zdev(-s)))
                self.put(self.out.at[b], b, 6 + zz, self.xdev())
                self.put(self.out.at[b], b, 10 + 2 * zz + x, self.cdev())
            when(self.inside(zz), arrive)
    def step_x(self, d):
        z, x, c = self.z, self.x, self.c
        for s in ((-1, 1) if d else (1,)):
            zz = z + s * d
            def arrive(zz=zz):
                b = idx(zz, 1 - x, c)
                self.got(b)
                self.put(self.out.at[b], b, 10 + 2 * zz + 1 - x, self.cdev())
            when(self.inside(zz), arrive)
    def step_c(self, d):
        z, x, c = self.z, self.x, self.c
        for s in ((-1, 1) if d else (1,)):
            zz = z + s * d
            def arrive(zz=zz):
                self.got(idx(zz, x, 1 - c))
                self.got(idx(zz, 1 - x, 1 - c))
            when(self.inside(zz), arrive)
    def end(self):
        z = self.z
        for d in range(NZ - 1):
            when((z - d >= 0) & (z < NZ - 1), lambda d=d: self.sent(d))
            when((z + d < NZ) & (z > 0), lambda d=d: self.sent(3 + d))
        for k in range(6, 18):
            self.sent(k)
        pltpu.make_async_copy(self.src, self.out.at[0], self.local).wait()

def gather_kernel(n, with_side, *refs):
    srcs, outs = refs[:n], refs[n:2*n]
    send, recv, local = refs[2*n:]
    at = place()
    greet(*at)
    eng = [Gather(at, srcs[i], outs[i], send.at[i], recv.at[i], local.at[i]) for i in range(n)]
    for e in eng: e.begin()
    for d in range(1, NZ):
        for e in eng: e.step_z(d)
        for e in eng: e.step_x(d - 1)
    for e in eng: e.step_x(NZ - 1)
    for d in range(NZ):
        for e in eng: e.step_c(d)
    for e in eng: e.end()

def gather(arrays, cid, chunks=None):
    n = len(arrays)
    return pl.pallas_call(
        functools.partial(gather_kernel, n, False),
        out_shape=[jax.ShapeDtypeStruct((16,) + a.shape, a.dtype) for a in arrays],
        in_specs=[pl.BlockSpec(memory_space=pl.ANY)] * n,
        out_specs=[pl.BlockSpec(memory_space=pl.ANY)] * n,
        scratch_shapes=[pltpu.SemaphoreType.DMA((n, 18)), pltpu.SemaphoreType.DMA((n, 16)), pltpu.SemaphoreType.DMA((n,))],
        compiler_params=pltpu.CompilerParams(collective_id=cid, has_side_effects=True),
    )(*arrays)

class Scatter:
    def __init__(self, at, part, rc, rx, rz, send, rcs, rxs, rzs):
        self.r, self.z, self.x, self.c = at
        self.part, self.rc, self.rx, self.rz = part, rc, rx, rz
        self.send, self.rcs, self.rxs, self.rzs = send, rcs, rxs, rzs
    def inside(self, z): return (z >= 0) & (z < NZ)
    def copy(self, src, dst, k, rs, dev):
        return pltpu.make_async_remote_copy(src, dst, self.send.at[k], rs, device_id=dev, device_id_type=MESH)
    def over(self, d):
        return [(s, self.z + s * d) for s in ((-1, 1) if d else (1,))]
    def begin(self, far_first=True):
        z, x, c = self.z, self.x, self.c
        dev = (self.r, idx(z, x, 1 - c))
        for xx in (1 - x, x):
            for d in range(NZ - 1, -1, -1):
                for s, zz in self.over(d):
                    k = 2 * zz + xx
                    when(self.inside(zz), lambda zz=zz, k=k, xx=xx: self.copy(self.part.at[idx(zz, xx, 1 - c)], self.rc.at[k], k, self.rcs.at[k], dev).start())
    def step_x(self, d):
        z, x, c = self.z, self.x, self.c
        dev = (self.r, idx(z, 1 - x, c))
        for s, zz in self.over(d):
            def go(zz=zz):
                k = 2 * zz + 1 - x
                b = idx(zz, 1 - x, c)
                self.copy(self.rc.at[k], self.rc.at[k], 0, self.rcs.at[k], dev).wait_recv()
                self.part[b] = (self.part[b].astype(F32) + self.rc[k].astype(F32)).astype(BF)
                self.copy(self.part.at[b], self.rx.at[zz], 8 + zz, self.rxs.at[zz], dev).start()
            when(self.inside(zz), go)
    def step_z(self, d):
        z, x, c = self.z, self.x, self.c
        for s, zz in self.over(d):
            def go(zz=zz, s=s):
                k = 2 * zz + x
                b = idx(zz, x, c)
                self.copy(self.rc.at[k], self.rc.at[k], 0, self.rcs.at[k], (self.r, 0)).wait_recv()
                self.copy(self.rx.at[zz], self.rx.at[zz], 0, self.rxs.at[zz], (self.r, 0)).wait_recv()
                both = self.part[b].astype(F32) + self.rc[k].astype(F32) + self.rx[zz].astype(F32)
                dev = (self.r, idx(z + s, x, c))
                slot = jnp.where(zz == z + s, NZ, zz) if s == -1 else zz
                self.part[b] = both.astype(BF)
                def more():
                    self.copy(self.rz.at[zz], self.rz.at[zz], 0, self.rzs.at[zz], dev).wait_recv()
                    self.part[b] = (self.part[b].astype(F32) + self.rz[zz].astype(F32)).astype(BF)
                when(self.inside(z - s), more)
                self.copy(self.part.at[b], self.rz.at[slot], 12 + zz, self.rzs.at[slot], dev).start()
            when(self.inside(zz), go)
    def finish(self, out):
        z, x, c = self.z, self.x, self.c
        k = 2 * z + x
        b = idx(z, x, c)
        self.copy(self.rc.at[k], self.rc.at[k], 0, self.rcs.at[k], (self.r, 0)).wait_recv()
        self.copy(self.rx.at[z], self.rx.at[z], 0, self.rxs.at[z], (self.r, 0)).wait_recv()
        out[...] = self.part[b].astype(F32) + self.rc[k].astype(F32) + self.rx[z].astype(F32)
        def lo():
            self.copy(self.rz.at[z], self.rz.at[z], 0, self.rzs.at[z], (self.r, 0)).wait_recv()
            out[...] += self.rz[z].astype(F32)
        when(z > 0, lo)
        def hi():
            self.copy(self.rz.at[NZ], self.rz.at[NZ], 0, self.rzs.at[NZ], (self.r, 0)).wait_recv()
            out[...] += self.rz[NZ].astype(F32)
        when(z < NZ - 1, hi)
        for k in range(8):
            self.copy(self.part.at[0], self.part.at[0], k, self.rcs.at[0], (self.r, 0)).wait_send()
        for k in range(8, 12):
            self.copy(self.part.at[0], self.part.at[0], k, self.rcs.at[0], (self.r, 0)).wait_send()
        for zz in range(NZ):
            when(z != zz, lambda zz=zz: self.copy(self.part.at[0], self.part.at[0], 12 + zz, self.rcs.at[0], (self.r, 0)).wait_send())

def scatter_steps(engines):
    for e in engines: e.begin()
    order = [("x", 3), ("x", 2), ("z", 3), ("x", 1), ("z", 2), ("x", 0), ("z", 1)]
    for kind, d in order:
        for e in engines:
            (e.step_x if kind == "x" else e.step_z)(d)

def scatter_kernel(n, pair, *refs):
    ps, os = refs[:n], refs[n:2*n]
    s = refs[2*n:]
    vm = [s[4*i:4*i+4] for i in range(n)]
    ysb = s[4*n:4*n+2*n] if pair else None
    send, rcs, rxs, rzs, lsem, ysem = s[4*n+(2*n if pair else 0):]
    at = place()
    for i in range(n):
        pltpu.make_async_copy(ps[i], vm[i][0], lsem.at[i]).start()
    greet(*at, with_y=pair)
    for i in range(n):
        pltpu.make_async_copy(ps[i], vm[i][0], lsem.at[i]).wait()
    engines = [Scatter(at, *vm[i], send.at[i], rcs.at[i], rxs.at[i], rzs.at[i]) for i in range(n)]
    scatter_steps(engines)
    r, z, x, c = at
    for i, e in enumerate(engines):
        e.finish(os[i])
        if pair:
            ysb[2*i][...] = os[i][...].astype(BF)
            pltpu.make_async_remote_copy(ysb[2*i], ysb[2*i+1], ysem.at[2*i], ysem.at[2*i+1], device_id=(1 - r, idx(z, x, c)), device_id_type=MESH).start()
    if pair:
        for i, e in enumerate(engines):
            pltpu.make_async_remote_copy(ysb[2*i], ysb[2*i+1], ysem.at[2*i], ysem.at[2*i+1], device_id=(1 - r, idx(z, x, c)), device_id_type=MESH).wait()
            os[i][...] = ysb[2*i][...].astype(F32) + ysb[2*i+1][...].astype(F32)

def scatter(parts, cid, pair=False):
    n = len(parts)
    scratch = []
    for p in parts:
        blk = p.shape[1:]
        scratch += [pltpu.VMEM((k,) + blk, BF) for k in (16, 8, 4, 5)]
    if pair:
        for p in parts:
            scratch += [pltpu.VMEM(p.shape[1:], BF)] * 2
    dma = pltpu.SemaphoreType.DMA
    return pl.pallas_call(
        functools.partial(scatter_kernel, n, pair),
        out_shape=[jax.ShapeDtypeStruct(p.shape[1:], F32) for p in parts],
        in_specs=[pl.BlockSpec(memory_space=pl.ANY)] * n,
        out_specs=[pl.BlockSpec(memory_space=pltpu.VMEM)] * n,
        scratch_shapes=scratch + [dma((n, 16)), dma((n, 8)), dma((n, 4)), dma((n, 5)), dma((n,)), dma((2 * n,))],
        compiler_params=pltpu.CompilerParams(collective_id=cid, has_side_effects=True, vmem_limit_bytes=60 * 2**20),
    )(*parts)


def gather_all(arrays, cid, fast):
    if fast:
        return gather(arrays, cid)
    return [lax.all_gather(a, "group", axis=0) for a in arrays]


def swap(x):
    return lax.ppermute(x, "replica", [(0, 1), (1, 0)])


def scatter_all(parts, cid, fast, pair=False):
    if fast:
        return scatter(parts, cid, pair)
    sums = [
        lax.psum_scatter(p, "group", scatter_dimension=0, tiled=True)[0].astype(F32) for p in parts
    ]
    if pair:
        low = [p.astype(BF) for p in sums]
        sums = [p.astype(F32) + swap(p).astype(F32) for p in low]
    return sums


def other_half(x, dim, rank):
    half = x.shape[dim] // 2
    return lax.dynamic_slice_in_dim(x, (1 - rank) * half, half, dim)


def own_half(x, dim, rank):
    half = x.shape[dim] // 2
    return lax.dynamic_slice_in_dim(x, rank * half, half, dim)


def shards(
    hidden_in,
    lengths,
    gain_attn,
    w_query,
    b_query,
    w_key,
    b_key,
    w_value,
    b_value,
    w_out,
    gain_mlp,
    w_gate,
    w_up,
    w_down,
    cotangent,
):
    group_count = lax.axis_size("group")
    group_rank = lax.axis_index("group")
    slot_count, block_len, model_width = hidden_in.shape
    kv_heads = KV_HEADS
    head_dim = HEAD_DIM
    kv_width = kv_heads * head_dim
    repeat = HEADS // kv_heads
    slot_span = block_len * group_count
    key_step = min(512, slot_span)
    score_scale = head_dim ** (-0.5)
    tokens = slot_count * block_len
    hidden_units = w_gate.shape[1]
    own_rows = w_gate.shape[0]
    share = hidden_units // group_count
    positions = group_rank * block_len + jnp.arange(block_len, dtype=jnp.int32)
    valid_rows = (positions[None, :] < lengths[:, None]).astype(F32).reshape(tokens, 1)
    cos_table, sin_table = rope_tables(positions, head_dim)
    cos_heads = cos_table[:, None, :]
    sin_heads = sin_table[:, None, :]
    rank_end = (group_rank + 1) * block_len
    row_pos = jnp.tile(positions, repeat)

    fast = group_count == 16
    replica_rank = lax.axis_index("replica")
    pieces = (gain_attn, b_query, b_key, b_value, gain_mlp)
    sizes = [p.shape[0] for p in pieces]
    offsets = [sum(sizes[:i]) for i in range(len(sizes) + 1)]
    small = jnp.zeros((16 * 128,), BF).at[: offsets[-1]].set(jnp.concatenate(pieces))
    qkv_w, small = gather_all(
        [jnp.concatenate((w_query, w_key, w_value), axis=1), small.reshape(16, 128)], 1, fast
    )
    qkv_w = qkv_w.reshape(model_width, model_width + 2 * kv_width)
    small = small.reshape(group_count, 16 * 128)
    gain_one, query_b, key_b, value_b, gain_two = [
        small[:, offsets[i] : offsets[i + 1]].reshape(-1).astype(F32) for i in range(len(sizes))
    ]
    qkv_b = jnp.concatenate((query_b, key_b, value_b))

    main = (hidden_units // 128 // group_count) * 128
    spare = hidden_units // group_count - main
    mains = [
        w[:, : main * group_count].reshape(own_rows, group_count, main) for w in (w_gate, w_up, w_down)
    ]
    spares = [
        w[:, main * group_count :].reshape(own_rows, group_count, spare)
        for w in (w_gate, w_up, w_down)
    ]
    gap = jnp.zeros((own_rows, group_count, 128 - 2 * spare), BF)
    gap_down = jnp.zeros((own_rows, group_count, 128 - spare), BF)
    blocks = jnp.concatenate(mains + [spares[0], spares[1], gap, spares[2], gap_down], axis=2)
    blocks = jnp.transpose(own_half(blocks, 0, replica_rank), (1, 0, 2))
    own_part = lax.all_to_all(blocks, "group", 0, 0, tiled=True)
    other_part = swap(own_part)
    first = jnp.where(replica_rank == 0, own_part, other_part)
    second = jnp.where(replica_rank == 0, other_part, own_part)
    columns = jnp.concatenate((first, second), axis=1).reshape(model_width, 3 * main + 256)
    rest = 3 * main
    gate_up_w = jnp.concatenate(
        (
            columns[:, :main],
            columns[:, rest : rest + spare],
            columns[:, main : 2 * main],
            columns[:, rest + spare : rest + 2 * spare],
        ),
        axis=1,
    )
    down_w = jnp.concatenate(
        (columns[:, 2 * main : rest], columns[:, rest + 128 : rest + 128 + spare]), axis=1
    )

    grad_final = cotangent.reshape(tokens, model_width).astype(F32) * valid_rows

    inputs = hidden_in.reshape(tokens, model_width).astype(F32)
    normed_full, factor_one = normalize(inputs, gain_one)
    normed = normed_full.astype(BF)
    qkv = matmul(normed, qkv_w) + qkv_b
    query_rot = rotate(
        qkv[:, :model_width].reshape(slot_count, block_len, HEADS, head_dim), cos_heads, sin_heads
    ).astype(BF)
    key_rot = rotate(
        qkv[:, model_width : model_width + kv_width].reshape(
            slot_count, block_len, kv_heads, head_dim
        ),
        cos_heads,
        sin_heads,
    ).astype(BF)
    value_low = qkv[:, model_width + kv_width :].astype(BF)
    pair = jnp.concatenate(
        (key_rot.reshape(tokens, kv_width), value_low), axis=1
    )
    pair_all, grad_all, out_w = gather_all([pair, grad_final.astype(BF), w_out], 2, fast)
    out_w = out_w.reshape(model_width, model_width)
    grad_all = grad_all.reshape(group_count * tokens, model_width)
    pair_all = jnp.transpose(
        pair_all.reshape(group_count, slot_count, block_len, 2 * kv_width), (1, 0, 2, 3)
    ).reshape(slot_count, slot_span, 2, kv_heads, head_dim)
    key_all = pair_all[:, :, 0]
    value_all = pair_all[:, :, 1]
    query_groups = []
    slot_totals = []
    slot_attended = []
    attended_rows = []
    for s in range(slot_count):
        query_rows = arrange(query_rot[s], kv_heads)
        totals, numerator = attend_forward(
            query_rows, key_all[s], value_all[s], row_pos, lengths[s], rank_end, key_step, score_scale
        )
        attended = numerator / totals[..., None]
        query_groups.append(query_rows)
        slot_totals.append(totals)
        slot_attended.append(attended)
        attended_rows.append(restore(attended, block_len))
    attended_low = jnp.concatenate(attended_rows, axis=0).astype(BF)
    residual_mid = inputs + matmul(attended_low, out_w)
    normed_two_full, factor_two = normalize(residual_mid, gain_two)
    (normed_all,) = gather_all([normed_two_full.astype(BF)], 3, fast)
    normed_all = normed_all.reshape(group_count * tokens, model_width)

    pre = matmul(normed_all, gate_up_w)
    gate_pre = pre[:, :share]
    up_pre = pre[:, share:]
    sigmoid_gate = jax.nn.sigmoid(gate_pre)
    silu_gate = gate_pre * sigmoid_gate
    hidden = (silu_gate * up_pre).astype(BF)
    grad_hidden = matmul(grad_all, down_w)
    grad_gate = (
        grad_hidden * up_pre * (sigmoid_gate * (1.0 + gate_pre * (1.0 - sigmoid_gate)))
    ).astype(BF)
    grad_up = (grad_hidden * silu_gate).astype(BF)
    gate_up_grad = jnp.concatenate((grad_gate, grad_up), axis=1)
    sums = [
        p.astype(BF).reshape(group_count, tokens, model_width)
        for p in (matmul_nt(gate_up_grad, gate_up_w), matmul_nt(hidden, down_w))
    ]
    grad_normed_two, mlp_out = scatter_all(sums, 4, fast)
    down_term = matmul_tn(grad_all, hidden).astype(BF)
    gate_up_term = matmul_tn(normed_all, gate_up_grad).astype(BF)
    zeros = jnp.zeros((model_width, 128), BF)
    terms = jnp.concatenate(
        (
            gate_up_term[:, :main],
            gate_up_term[:, share : share + main],
            down_term[:, :main],
            gate_up_term[:, main:share],
            gate_up_term[:, share + main :],
            zeros[:, : 128 - 2 * spare],
            down_term[:, main:],
            zeros[:, : 128 - spare],
        ),
        axis=1,
    ).reshape(group_count, own_rows, 3 * main + 256)
    half_sum = own_half(terms, 1, replica_rank).astype(F32) + swap(
        other_half(terms, 1, replica_rank)
    ).astype(F32)
    half_back = lax.all_to_all(half_sum.astype(BF), "group", 0, 0, tiled=True)
    half_other = swap(half_back)
    first = jnp.where(replica_rank == 0, half_back, half_other)
    second = jnp.where(replica_rank == 0, half_other, half_back)
    back = jnp.transpose(jnp.concatenate((first, second), axis=1), (1, 0, 2))
    gate_sum, up_sum, down_sum = [
        jnp.concatenate(
            (
                back[:, :, i * main : (i + 1) * main].reshape(own_rows, group_count * main),
                back[:, :, at : at + spare].reshape(own_rows, group_count * spare),
            ),
            axis=1,
        ).astype(F32)
        for i, at in ((0, rest), (1, rest + spare), (2, rest + 128))
    ]

    final_rows = residual_mid + mlp_out
    layer_out = (final_rows * valid_rows).reshape(slot_count, block_len, model_width).astype(BF)
    grad_mid_norm, grad_gain_two = norm_back(residual_mid, factor_two, gain_two, grad_normed_two)
    grad_mid = grad_final + grad_mid_norm
    grad_branch = grad_mid.astype(BF)
    out_term = matmul_tn(attended_low, grad_branch)
    grad_attended = matmul_nt(grad_branch, out_w)
    grad_query_rows = []
    grad_pairs = []
    for s in range(slot_count):
        slot_grad = grad_attended[s * block_len : (s + 1) * block_len].reshape(
            block_len, HEADS, head_dim
        )
        grad_out = arrange(slot_grad, kv_heads)
        totals = slot_totals[s]
        grad_total = -jnp.sum(grad_out * slot_attended[s], axis=-1) / totals
        grad_numer = (grad_out / totals[..., None]).astype(BF)
        grad_query, grad_key, grad_value = attend_backward(
            query_groups[s],
            key_all[s],
            value_all[s],
            row_pos,
            lengths[s],
            rank_end,
            key_step,
            score_scale,
            grad_numer,
            grad_total,
        )
        query_back_rows = restore(grad_query * score_scale, block_len).reshape(
            block_len, HEADS, head_dim
        )
        grad_query_rows.append(
            rotate_back(query_back_rows, cos_heads, sin_heads).reshape(block_len, HEADS * head_dim)
        )
        grad_pairs.append(
            jnp.concatenate(
                (grad_key.reshape(slot_span, kv_width), grad_value.reshape(slot_span, kv_width)),
                axis=1,
            )
        )
    pair_grads = jnp.stack(grad_pairs).reshape(slot_count, group_count, block_len, 2 * kv_width)
    pair_grads = jnp.transpose(pair_grads, (1, 0, 2, 3)).astype(BF)
    (pair_sum,) = scatter_all(
        [pair_grads.reshape(group_count, tokens, 2 * kv_width)], 5, fast
    )
    pair_sum = pair_sum.reshape(slot_count, block_len, 2 * kv_width)
    grad_query_pre = jnp.concatenate(grad_query_rows, axis=0).astype(BF)
    key_sum = pair_sum[..., :kv_width].reshape(slot_count, block_len, kv_heads, head_dim)
    grad_key_pre = (
        rotate_back(key_sum * score_scale, cos_heads, sin_heads).astype(BF).reshape(tokens, kv_width)
    )
    grad_value_pre = pair_sum[..., kv_width:].astype(BF).reshape(tokens, kv_width)
    grad_qkv = jnp.concatenate((grad_query_pre, grad_key_pre, grad_value_pre), axis=1)
    grad_normed = matmul_nt(grad_qkv, qkv_w)
    grad_in_norm, grad_gain_one = norm_back(inputs, factor_one, gain_one, grad_normed)
    grad_input = (grad_mid + grad_in_norm).reshape(slot_count, block_len, model_width)
    qkv_term = matmul_tn(normed, grad_qkv)
    qkv_bias = jnp.sum(grad_qkv.astype(F32), axis=0)

    vectors = jnp.concatenate(
        [
            grad_gain_one.reshape(group_count, -1),
            qkv_bias[:model_width].reshape(group_count, -1),
            qkv_bias[model_width : model_width + kv_width].reshape(group_count, -1),
            qkv_bias[model_width + kv_width :].reshape(group_count, -1),
            grad_gain_two.reshape(group_count, -1),
        ],
        axis=1,
    )
    vectors = jnp.concatenate(
        (vectors, jnp.zeros((group_count, 16 * 128 - offsets[-1]), F32)), axis=1
    ).reshape(group_count, 16, 128)
    weight_sum, out_sum, vector_sum = scatter_all(
        [
            p.astype(BF).reshape(group_count, p.shape[0] // group_count, -1)
            for p in (qkv_term, out_term)
        ]
        + [vectors.astype(BF)],
        6,
        fast,
        pair=True,
    )
    vector_sum = vector_sum.reshape(-1)
    gain_one_sum, query_bias_sum, key_bias_sum, value_bias_sum, gain_two_sum = [
        vector_sum[offsets[i] : offsets[i + 1]] for i in range(len(sizes))
    ]
    ends = (0, model_width, model_width + kv_width, model_width + 2 * kv_width)
    query_sum, key_sum_w, value_sum_w = [weight_sum[:, ends[i] : ends[i + 1]] for i in range(3)]
    return (
        layer_out,
        grad_input,
        gain_one_sum,
        query_sum,
        query_bias_sum,
        key_sum_w,
        key_bias_sum,
        value_sum_w,
        value_bias_sum,
        out_sum,
        gain_two_sum,
        gate_sum,
        up_sum,
        down_sum,
    )


def solution(mesh):
    act = P("replica", "group", None)
    vec = P("group")
    mat = P("group", None)
    return jax.shard_map(
        shards,
        mesh=mesh,
        in_specs=(act, P("replica"), vec, mat, vec, mat, vec, mat, vec, mat, vec, mat, mat, mat, act),
        out_specs=(act, act, vec, mat, vec, mat, vec, mat, vec, mat, vec, mat, mat, mat),
        check_vma=False,
    )
```

```python
import functools

import jax
import jax.numpy as jnp
from jax import lax
from jax.experimental import pallas as pl
from jax.experimental.pallas import tpu as pltpu
from jax.sharding import PartitionSpec as P

MESH = pl.DeviceIdType.MESH
NZ = 4
MAIN = 512
HEADS = 12
KV_HEADS = 2
HEAD_DIM = 128
EPSILON = 1e-06
THETA = 1000000.0
BF = jnp.bfloat16
F32 = jnp.float32


def rope_tables(positions, head_dim):
    freqs = THETA ** (-jnp.arange(0, head_dim, 2).astype(F32) / head_dim)
    angles = positions.astype(F32)[:, None] * freqs[None, :]
    angles = jnp.concatenate((angles, angles), axis=-1)
    return (jnp.cos(angles), jnp.sin(angles))


def rotate(tensor, cos_table, sin_table):
    halfway = tensor.shape[-1] // 2
    turned = jnp.concatenate((-tensor[..., halfway:], tensor[..., :halfway]), axis=-1)
    return tensor * cos_table + turned * sin_table


def rotate_back(gradient, cos_table, sin_table):
    halfway = gradient.shape[-1] // 2
    scaled = gradient * sin_table
    turned = jnp.concatenate((scaled[..., halfway:], -scaled[..., :halfway]), axis=-1)
    return gradient * cos_table + turned


def normalize(row_values, gain_vec):
    factor = lax.rsqrt(jnp.mean(row_values * row_values, axis=-1, keepdims=True) + EPSILON)
    return (row_values * factor * gain_vec, factor)


def norm_back(row_values, factor, gain_vec, upstream):
    weighted = upstream * gain_vec
    inner_mean = jnp.mean(weighted * row_values, axis=-1, keepdims=True)
    grad_rows = factor * weighted - row_values * (factor * factor * factor) * inner_mean
    grad_gain = jnp.sum(upstream * row_values * factor, axis=0)
    return (grad_rows, grad_gain)


def matmul(a, b):
    return jnp.dot(a, b, preferred_element_type=F32)


def matmul_nt(a, b):
    return lax.dot_general(a, b, (((1,), (1,)), ((), ())), preferred_element_type=F32)


def matmul_tn(a, b):
    return lax.dot_general(a, b, (((0,), (0,)), ((), ())), preferred_element_type=F32)


def arrange(per_token, kv_heads):
    block_len, head_count, head_dim = per_token.shape
    repeat = head_count // kv_heads
    grouped = per_token.reshape(block_len, kv_heads, repeat, head_dim)
    return jnp.transpose(grouped, (1, 2, 0, 3)).reshape(kv_heads, repeat * block_len, head_dim)


def restore(per_group, block_len):
    kv_heads, row_count, head_dim = per_group.shape
    repeat = row_count // block_len
    grouped = per_group.reshape(kv_heads, repeat, block_len, head_dim)
    return jnp.transpose(grouped, (2, 0, 1, 3)).reshape(block_len, kv_heads * repeat * head_dim)


def masked_exp(query_rows, key_block, row_pos, first_key, length, score_scale):
    key_step = key_block.shape[0]
    raw_scores = jnp.einsum("grd,kgd->grk", query_rows, key_block, preferred_element_type=F32)
    key_pos = first_key + jnp.arange(key_step, dtype=jnp.int32)
    allowed = (key_pos[None, :] <= row_pos[:, None]) & (key_pos[None, :] < length)
    return jnp.where(allowed[None], jnp.exp(raw_scores * score_scale), 0.0)


def block_total(length, rank_end, key_step):
    key_limit = jnp.minimum(length, rank_end)
    return (key_limit + key_step - 1) // key_step


def attend_forward(query_rows, key_all, value_all, row_pos, length, rank_end, key_step, scale):
    kv_heads, row_count, head_dim = query_rows.shape

    def visit(block_index, state_tuple):
        totals, numerator = state_tuple
        first_key = block_index * key_step
        key_block = lax.dynamic_slice_in_dim(key_all, first_key, key_step, 0)
        value_block = lax.dynamic_slice_in_dim(value_all, first_key, key_step, 0)
        weights = masked_exp(query_rows, key_block, row_pos, first_key, length, scale)
        totals = totals + jnp.sum(weights, axis=-1)
        numerator = numerator + jnp.einsum(
            "grk,kgd->grd", weights.astype(BF), value_block, preferred_element_type=F32
        )
        return (totals, numerator)

    initial = (
        jnp.zeros((kv_heads, row_count), F32),
        jnp.zeros((kv_heads, row_count, head_dim), F32),
    )
    return lax.fori_loop(0, block_total(length, rank_end, key_step), visit, initial)


def attend_backward(
    query_rows, key_all, value_all, row_pos, length, rank_end, key_step, scale, grad_numer, grad_total
):
    kv_heads, row_count, head_dim = query_rows.shape

    def visit(block_index, state_tuple):
        grad_query, grad_key, grad_value = state_tuple
        first_key = block_index * key_step
        key_block = lax.dynamic_slice_in_dim(key_all, first_key, key_step, 0)
        value_block = lax.dynamic_slice_in_dim(value_all, first_key, key_step, 0)
        weights = masked_exp(query_rows, key_block, row_pos, first_key, length, scale)
        grad_prob = jnp.einsum("grd,kgd->grk", grad_numer, value_block, preferred_element_type=F32)
        grad_score = (weights * (grad_prob + grad_total[..., None])).astype(BF)
        grad_query = grad_query + jnp.einsum(
            "grk,kgd->grd", grad_score, key_block, preferred_element_type=F32
        )
        key_part = jnp.einsum("grk,grd->kgd", grad_score, query_rows, preferred_element_type=F32)
        value_part = jnp.einsum(
            "grk,grd->kgd", weights.astype(BF), grad_numer, preferred_element_type=F32
        )
        key_old = lax.dynamic_slice_in_dim(grad_key, first_key, key_step, 0)
        value_old = lax.dynamic_slice_in_dim(grad_value, first_key, key_step, 0)
        grad_key = lax.dynamic_update_slice_in_dim(grad_key, key_old + key_part, first_key, 0)
        grad_value = lax.dynamic_update_slice_in_dim(
            grad_value, value_old + value_part, first_key, 0
        )
        return (grad_query, grad_key, grad_value)

    initial = (
        jnp.zeros((kv_heads, row_count, head_dim), F32),
        jnp.zeros(key_all.shape, F32),
        jnp.zeros(value_all.shape, F32),
    )
    return lax.fori_loop(0, block_total(length, rank_end, key_step), visit, initial)


D = 1536
COLS = 3 * MAIN + 256


def place():
    g = lax.axis_index("group")
    r = lax.axis_index("replica")
    return r, g // 4, lax.rem(g // 2, 2), lax.rem(g, 2)

def idx(z, x, c):
    return (z * 2 + x) * 2 + c

def greet(r, z, x, c, with_y=False):
    bar = pltpu.get_barrier_semaphore()
    def hail(dev):
        pl.semaphore_signal(bar, inc=1, device_id=dev, device_id_type=MESH)
    hail((r, idx(z, 1 - x, c)))
    hail((r, idx(z, x, 1 - c)))
    if with_y:
        hail((1 - r, idx(z, x, c)))
    @pl.when(z > 0)
    def _():
        hail((r, idx(z - 1, x, c)))
    @pl.when(z < NZ - 1)
    def _():
        hail((r, idx(z + 1, x, c)))
    ends = jnp.where((z > 0) & (z < NZ - 1), 1, 0)
    pl.semaphore_wait(bar, (4 if with_y else 3) + ends)

def when(cond, fn):
    pl.when(cond)(fn)

class Gather:
    def __init__(self, at, src, out, send, recv, local):
        self.r, self.z, self.x, self.c = at
        self.src, self.out, self.send, self.recv, self.local = src, out, send, recv, local
    def put(self, src, b, k, dev):
        pltpu.make_async_remote_copy(src, self.out.at[b], self.send.at[k], self.recv.at[b], device_id=dev, device_id_type=MESH).start()
    def sent(self, k):
        b = 0
        pltpu.make_async_remote_copy(self.out.at[b], self.out.at[b], self.send.at[k], self.recv.at[b], device_id=(self.r, 0), device_id_type=MESH).wait_send()
    def got(self, b):
        pltpu.make_async_remote_copy(self.out.at[b], self.out.at[b], self.send.at[0], self.recv.at[b], device_id=(self.r, 0), device_id_type=MESH).wait_recv()
    def zdev(self, s): return (self.r, idx(self.z + s, self.x, self.c))
    def xdev(self): return (self.r, idx(self.z, 1 - self.x, self.c))
    def cdev(self): return (self.r, idx(self.z, self.x, 1 - self.c))
    def begin(self):
        z, x, c = self.z, self.x, self.c
        me = idx(z, x, c)
        for s in (1, -1):
            when(self.inside(z + s), lambda s=s: self.put(self.src, me, 0 if s == 1 else 3, self.zdev(s)))
        self.put(self.src, me, 6 + z, self.xdev())
        self.put(self.src, me, 10 + 2 * z + x, self.cdev())
        pltpu.make_async_copy(self.src, self.out.at[me], self.local).start()
    def inside(self, z): return (z >= 0) & (z < NZ)
    def step_z(self, d):
        z, x, c = self.z, self.x, self.c
        for s in (-1, 1):
            zz = z + s * d
            def arrive(s=s, zz=zz):
                b = idx(zz, x, c)
                self.got(b)
                if d < NZ - 1:
                    when(self.inside(z - s), lambda: self.put(self.out.at[b], b, (0 if s == -1 else 3) + d, self.zdev(-s)))
                self.put(self.out.at[b], b, 6 + zz, self.xdev())
                self.put(self.out.at[b], b, 10 + 2 * zz + x, self.cdev())
            when(self.inside(zz), arrive)
    def step_x(self, d):
        z, x, c = self.z, self.x, self.c
        for s in ((-1, 1) if d else (1,)):
            zz = z + s * d
            def arrive(zz=zz):
                b = idx(zz, 1 - x, c)
                self.got(b)
                self.put(self.out.at[b], b, 10 + 2 * zz + 1 - x, self.cdev())
            when(self.inside(zz), arrive)
    def step_c(self, d):
        z, x, c = self.z, self.x, self.c
        for s in ((-1, 1) if d else (1,)):
            zz = z + s * d
            def arrive(zz=zz):
                self.got(idx(zz, x, 1 - c))
                self.got(idx(zz, 1 - x, 1 - c))
            when(self.inside(zz), arrive)
    def from_z(self, zz):
        z, x, c = self.z, self.x, self.c
        b = idx(zz, x, c)
        self.got(b)
        s = jnp.where(zz < z, 1, -1)
        d = jnp.abs(zz - z)
        slot = jnp.where(zz < z, 0, 3) + d
        when(self.inside(z + s), lambda: self.put(self.out.at[b], b, slot, (self.r, idx(z + s, x, c))))
        self.put(self.out.at[b], b, 6 + zz, self.xdev())
        self.put(self.out.at[b], b, 10 + 2 * zz + x, self.cdev())
    def from_x(self, zz):
        b = idx(zz, 1 - self.x, self.c)
        self.got(b)
        self.put(self.out.at[b], b, 10 + 2 * zz + 1 - self.x, self.cdev())
    def from_c(self, zz):
        self.got(idx(zz, self.x, 1 - self.c))
        self.got(idx(zz, 1 - self.x, 1 - self.c))
    def end(self, local=True):
        z = self.z
        for d in range(NZ - 1):
            when((z - d >= 0) & (z < NZ - 1), lambda d=d: self.sent(d))
            when((z + d < NZ) & (z > 0), lambda d=d: self.sent(3 + d))
        for k in range(6, 18):
            self.sent(k)
        if local:
            pltpu.make_async_copy(self.src, self.out.at[0], self.local).wait()

def gather_kernel(n, with_side, *refs):
    srcs, outs = refs[:n], refs[n:2*n]
    send, recv, local = refs[2*n:]
    at = place()
    greet(*at)
    eng = [Gather(at, srcs[i], outs[i], send.at[i], recv.at[i], local.at[i]) for i in range(n)]
    for e in eng: e.begin()
    for d in range(1, NZ):
        for e in eng: e.step_z(d)
        for e in eng: e.step_x(d - 1)
    for e in eng: e.step_x(NZ - 1)
    for d in range(NZ):
        for e in eng: e.step_c(d)
    for e in eng: e.end()

def gather(arrays, cid, chunks=None):
    n = len(arrays)
    return pl.pallas_call(
        functools.partial(gather_kernel, n, False),
        out_shape=[jax.ShapeDtypeStruct((16,) + a.shape, a.dtype) for a in arrays],
        in_specs=[pl.BlockSpec(memory_space=pl.ANY)] * n,
        out_specs=[pl.BlockSpec(memory_space=pl.ANY)] * n,
        scratch_shapes=[pltpu.SemaphoreType.DMA((n, 18)), pltpu.SemaphoreType.DMA((n, 16)), pltpu.SemaphoreType.DMA((n,))],
        compiler_params=pltpu.CompilerParams(collective_id=cid, has_side_effects=True),
    )(*arrays)

class Scatter:
    def __init__(self, at, part, rc, rx, rz, send, rcs, rxs, rzs):
        self.r, self.z, self.x, self.c = at
        self.part, self.rc, self.rx, self.rz = part, rc, rx, rz
        self.send, self.rcs, self.rxs, self.rzs = send, rcs, rxs, rzs
    def inside(self, z): return (z >= 0) & (z < NZ)
    def copy(self, src, dst, k, rs, dev):
        return pltpu.make_async_remote_copy(src, dst, self.send.at[k], rs, device_id=dev, device_id_type=MESH)
    def over(self, d):
        return [(s, self.z + s * d) for s in ((-1, 1) if d else (1,))]
    def begin(self, far_first=True):
        z, x, c = self.z, self.x, self.c
        dev = (self.r, idx(z, x, 1 - c))
        for xx in (1 - x, x):
            for d in range(NZ - 1, -1, -1):
                for s, zz in self.over(d):
                    k = 2 * zz + xx
                    when(self.inside(zz), lambda zz=zz, k=k, xx=xx: self.copy(self.part.at[idx(zz, xx, 1 - c)], self.rc.at[k], k, self.rcs.at[k], dev).start())
    def send_c(self, zz):
        z, x, c = self.z, self.x, self.c
        dev = (self.r, idx(z, x, 1 - c))
        for xx in (1 - x, x):
            k = 2 * zz + xx
            self.copy(self.part.at[idx(zz, xx, 1 - c)], self.rc.at[k], k, self.rcs.at[k], dev).start()
    def step_x(self, d):
        z, x, c = self.z, self.x, self.c
        dev = (self.r, idx(z, 1 - x, c))
        for s, zz in self.over(d):
            def go(zz=zz):
                k = 2 * zz + 1 - x
                b = idx(zz, 1 - x, c)
                self.copy(self.rc.at[k], self.rc.at[k], 0, self.rcs.at[k], dev).wait_recv()
                self.part[b] = (self.part[b].astype(F32) + self.rc[k].astype(F32)).astype(BF)
                self.copy(self.part.at[b], self.rx.at[zz], 8 + zz, self.rxs.at[zz], dev).start()
            when(self.inside(zz), go)
    def step_z(self, d):
        z, x, c = self.z, self.x, self.c
        for s, zz in self.over(d):
            def go(zz=zz, s=s):
                k = 2 * zz + x
                b = idx(zz, x, c)
                self.copy(self.rc.at[k], self.rc.at[k], 0, self.rcs.at[k], (self.r, 0)).wait_recv()
                self.copy(self.rx.at[zz], self.rx.at[zz], 0, self.rxs.at[zz], (self.r, 0)).wait_recv()
                both = self.part[b].astype(F32) + self.rc[k].astype(F32) + self.rx[zz].astype(F32)
                dev = (self.r, idx(z + s, x, c))
                slot = jnp.where(zz == z + s, NZ, zz) if s == -1 else zz
                self.part[b] = both.astype(BF)
                def more():
                    self.copy(self.rz.at[zz], self.rz.at[zz], 0, self.rzs.at[zz], dev).wait_recv()
                    self.part[b] = (self.part[b].astype(F32) + self.rz[zz].astype(F32)).astype(BF)
                when(self.inside(z - s), more)
                self.copy(self.part.at[b], self.rz.at[slot], 12 + zz, self.rzs.at[slot], dev).start()
            when(self.inside(zz), go)
    def finish(self, out):
        z, x, c = self.z, self.x, self.c
        k = 2 * z + x
        b = idx(z, x, c)
        self.copy(self.rc.at[k], self.rc.at[k], 0, self.rcs.at[k], (self.r, 0)).wait_recv()
        self.copy(self.rx.at[z], self.rx.at[z], 0, self.rxs.at[z], (self.r, 0)).wait_recv()
        out[...] = self.part[b].astype(F32) + self.rc[k].astype(F32) + self.rx[z].astype(F32)
        def lo():
            self.copy(self.rz.at[z], self.rz.at[z], 0, self.rzs.at[z], (self.r, 0)).wait_recv()
            out[...] += self.rz[z].astype(F32)
        when(z > 0, lo)
        def hi():
            self.copy(self.rz.at[NZ], self.rz.at[NZ], 0, self.rzs.at[NZ], (self.r, 0)).wait_recv()
            out[...] += self.rz[NZ].astype(F32)
        when(z < NZ - 1, hi)
        for k in range(8):
            self.copy(self.part.at[0], self.part.at[0], k, self.rcs.at[0], (self.r, 0)).wait_send()
        for k in range(8, 12):
            self.copy(self.part.at[0], self.part.at[0], k, self.rcs.at[0], (self.r, 0)).wait_send()
        for zz in range(NZ):
            when(z != zz, lambda zz=zz: self.copy(self.part.at[0], self.part.at[0], 12 + zz, self.rcs.at[0], (self.r, 0)).wait_send())

def scatter_steps(engines):
    for e in engines: e.begin()
    order = [("x", 3), ("x", 2), ("z", 3), ("x", 1), ("z", 2), ("x", 0), ("z", 1)]
    for kind, d in order:
        for e in engines:
            (e.step_x if kind == "x" else e.step_z)(d)

def scatter_kernel(n, pair, *refs):
    ps, os = refs[:n], refs[n:2*n]
    s = refs[2*n:]
    vm = [s[4*i:4*i+4] for i in range(n)]
    ysb = s[4*n:4*n+2*n] if pair else None
    send, rcs, rxs, rzs, lsem, ysem = s[4*n+(2*n if pair else 0):]
    at = place()
    for i in range(n):
        pltpu.make_async_copy(ps[i], vm[i][0], lsem.at[i]).start()
    greet(*at, with_y=pair)
    for i in range(n):
        pltpu.make_async_copy(ps[i], vm[i][0], lsem.at[i]).wait()
    engines = [Scatter(at, *vm[i], send.at[i], rcs.at[i], rxs.at[i], rzs.at[i]) for i in range(n)]
    scatter_steps(engines)
    r, z, x, c = at
    for i, e in enumerate(engines):
        e.finish(os[i])
        if pair:
            ysb[2*i][...] = os[i][...].astype(BF)
            pltpu.make_async_remote_copy(ysb[2*i], ysb[2*i+1], ysem.at[2*i], ysem.at[2*i+1], device_id=(1 - r, idx(z, x, c)), device_id_type=MESH).start()
    if pair:
        for i, e in enumerate(engines):
            pltpu.make_async_remote_copy(ysb[2*i], ysb[2*i+1], ysem.at[2*i], ysem.at[2*i+1], device_id=(1 - r, idx(z, x, c)), device_id_type=MESH).wait()
            os[i][...] = ysb[2*i][...].astype(F32) + ysb[2*i+1][...].astype(F32)

def scatter(parts, cid, pair=False):
    n = len(parts)
    scratch = []
    for p in parts:
        blk = p.shape[1:]
        scratch += [pltpu.VMEM((k,) + blk, BF) for k in (16, 8, 4, 5)]
    if pair:
        for p in parts:
            scratch += [pltpu.VMEM(p.shape[1:], BF)] * 2
    dma = pltpu.SemaphoreType.DMA
    return pl.pallas_call(
        functools.partial(scatter_kernel, n, pair),
        out_shape=[jax.ShapeDtypeStruct(p.shape[1:], F32) for p in parts],
        in_specs=[pl.BlockSpec(memory_space=pl.ANY)] * n,
        out_specs=[pl.BlockSpec(memory_space=pltpu.VMEM)] * n,
        scratch_shapes=scratch + [dma((n, 16)), dma((n, 8)), dma((n, 4)), dma((n, 5)), dma((n,)), dma((2 * n,))],
        compiler_params=pltpu.CompilerParams(collective_id=cid, has_side_effects=True, vmem_limit_bytes=60 * 2**20),
    )(*parts)


def dot(a, b):
    return lax.dot_general(a, b, (((1,), (0,)), ((), ())), preferred_element_type=F32)
def dot_nt(a, b):
    return lax.dot_general(a, b, (((1,), (1,)), ((), ())), preferred_element_type=F32)
def dot_tn(a, b):
    return lax.dot_general(a, b, (((0,), (0,)), ((), ())), preferred_element_type=F32)

def gated(g, u, gh):
    sig = jax.nn.sigmoid(g)
    silu = g * sig
    return (gh * u * (sig * (1.0 + g * (1.0 - sig)))).astype(BF), (gh * silu).astype(BF), (silu * u).astype(BF)

def mlp_kernel(spare, n2_ref, cot_ref, w_ref, gsum, osum, half_ref,
               n2, cot, w, act, pg, po, rcg, rxg, rzg, rco, rxo, rzo, yb,
               gsend, grecv, glocal, lsem, ssend, srcs, srxs, srzs, ysend, yrecv):
    at = place()
    r, z, x, c = at
    loads = [pltpu.make_async_copy(w_ref, w, lsem.at[0]), pltpu.make_async_copy(cot_ref, cot, lsem.at[1])]
    for l in loads: l.start()
    greet(*at, with_y=True)
    g = Gather(at, n2_ref, n2, gsend, grecv, glocal)
    rg = Scatter(at, pg, rcg, rxg, rzg, ssend.at[0], srcs.at[0], srxs.at[0], srzs.at[0])
    ro = Scatter(at, po, rco, rxo, rzo, ssend.at[1], srcs.at[1], srxs.at[1], srzs.at[1])
    g.begin()
    for l in loads: l.wait()
    mid = (z > 0) & (z < NZ - 1)
    p = [z,
         jnp.where(z == 0, 1, jnp.where(z == 1, 0, jnp.where(z == 2, 3, 2))),
         jnp.where(z == 0, 2, jnp.where(z == 1, 2, 1)),
         jnp.where(z < 2, 3, 0)]

    def tiles(zz):
        rows = pl.ds(pl.multiple_of(4 * zz, 4), 4)
        tok = pl.ds(pl.multiple_of(512 * zz, 512), 512)
        @pl.loop(0, 2)
        def _(t):
            a = n2[rows].reshape(512, D)
            k = cot[rows].reshape(512, D)
            def col(base):
                return pl.ds(pl.multiple_of(base + 256 * t, 256), 256)
            dg, du, h = gated(dot(a, w[:, col(0)]), dot(a, w[:, col(MAIN)]), dot(k, w[:, col(2 * MAIN)]))
            act[tok, col(0)] = dg
            act[tok, col(MAIN)] = du
            act[tok, col(2 * MAIN)] = h
        a = n2[rows].reshape(512, D)
        k = cot[rows].reshape(512, D)
        pre = dot(a, w[:, 3 * MAIN : 3 * MAIN + 128])
        gh = dot(k, w[:, 3 * MAIN + 128 :])
        lane = lax.broadcasted_iota(jnp.int32, (512, 128), 1)
        sig = jax.nn.sigmoid(pre)
        silu = pre * sig
        up = pltpu.roll(pre, 128 - spare, 1)
        dg = gh * up * (sig * (1.0 + pre * (1.0 - sig)))
        du = pltpu.roll(gh * silu, spare, 1)
        act[tok, 3 * MAIN : 3 * MAIN + 128] = jnp.where(lane < spare, dg, jnp.where(lane < 2 * spare, du, 0.0)).astype(BF)
        act[tok, 3 * MAIN + 128 :] = jnp.where(lane < spare, silu * up, 0.0).astype(BF)
        @pl.loop(0, D // 256)
        def _(t):
            dr = pl.ds(pl.multiple_of(256 * t, 256), 256)
            v = dot_nt(act[tok, : 2 * MAIN], w[dr, : 2 * MAIN]) + dot_nt(act[tok, 3 * MAIN : 3 * MAIN + 128], w[dr, 3 * MAIN : 3 * MAIN + 128])
            pg[rows, :, dr] = v.astype(BF).reshape(4, 128, 256)
            v = dot_nt(act[tok, 2 * MAIN : 3 * MAIN], w[dr, 2 * MAIN : 3 * MAIN]) + dot_nt(act[tok, 3 * MAIN + 128 :], w[dr, 3 * MAIN + 128 :])
            po[rows, :, dr] = v.astype(BF).reshape(4, 128, 256)
        rg.send_c(zz)
        ro.send_c(zz)

    g.from_z(p[1])
    when(mid, lambda: g.from_z(p[2]))
    g.from_x(p[0])
    g.from_c(p[0])
    pltpu.make_async_copy(n2_ref, n2.at[0], glocal).wait()
    tiles(p[0])
    g.from_z(jnp.where(mid, p[3], p[2]))
    g.from_x(p[1])
    g.from_c(p[1])
    tiles(p[1])
    when(~mid, lambda: g.from_z(p[3]))
    g.from_x(p[2])
    g.from_c(p[2])
    tiles(p[2])
    g.from_x(p[3])
    g.from_c(p[3])
    tiles(p[3])

    ydev = (1 - r, idx(z, x, c))
    own = D // 16
    half = own // 2
    def ycopy(j):
        src = w.at[pl.ds(pl.multiple_of(own * j + half * (1 - r), half), half)]
        return pltpu.make_async_remote_copy(src, yb.at[j], ysend.at[j], yrecv.at[j], device_id=ydev, device_id_type=MESH)
    def grads(q):
        dr = slice(384 * q, 384 * (q + 1))
        row = slice(384 * q, 384 * (q + 1))
        @pl.loop(0, 4)
        def _(t):
            col = pl.ds(pl.multiple_of(256 * t, 256), 256)
            w[row, col] = dot_tn(n2[:, :, dr].reshape(2048, 384), act[:, col]).astype(BF)
        @pl.loop(0, 2)
        def _(t):
            col = pl.ds(pl.multiple_of(2 * MAIN + 256 * t, 256), 256)
            w[row, col] = dot_tn(cot[:, :, dr].reshape(2048, 384), act[:, col]).astype(BF)
        w[row, 3 * MAIN : 3 * MAIN + 128] = dot_tn(n2[:, :, dr].reshape(2048, 384), act[:, 3 * MAIN : 3 * MAIN + 128]).astype(BF)
        w[row, 3 * MAIN + 128 :] = dot_tn(cot[:, :, dr].reshape(2048, 384), act[:, 3 * MAIN + 128 :]).astype(BF)
        for j in range(4 * q, 4 * q + 4):
            ycopy(j).start()
    def yadd(j):
        ycopy(j).wait()
        mine = w[pl.ds(pl.multiple_of(own * j + half * r, half), half)]
        yb[j] = (mine.astype(F32) + yb[j].astype(F32)).astype(BF)
        pltpu.make_async_copy(yb.at[j], half_ref.at[j], lsem.at[2]).start()

    rg.step_x(3)
    rg.step_x(2)
    grads(0)
    rg.step_z(3)
    rg.step_x(1)
    grads(1)
    rg.step_z(2)
    rg.step_x(0)
    grads(2)
    rg.step_z(1)
    ro.step_x(3)
    ro.step_x(2)
    grads(3)
    rg.finish(gsum)
    ro.step_z(3)
    ro.step_x(1)
    for j in range(0, 4): yadd(j)
    ro.step_z(2)
    ro.step_x(0)
    for j in range(4, 8): yadd(j)
    ro.step_z(1)
    for j in range(8, 12): yadd(j)
    ro.finish(osum)
    for j in range(12, 16): yadd(j)
    pltpu.make_async_copy(yb, half_ref, lsem.at[2]).wait()
    g.end(local=False)

def mlp(n2, cot, w, spare, cid):
    blk = n2.shape
    dma = pltpu.SemaphoreType.DMA
    full = (16,) + blk
    return pl.pallas_call(
        functools.partial(mlp_kernel, spare),
        out_shape=[jax.ShapeDtypeStruct(blk, F32)] * 2 + [jax.ShapeDtypeStruct((16, D // 32, COLS), BF)],
        in_specs=[pl.BlockSpec(memory_space=pl.ANY)] * 3,
        out_specs=[pl.BlockSpec(memory_space=pltpu.VMEM)] * 2 + [pl.BlockSpec(memory_space=pl.ANY)],
        scratch_shapes=[pltpu.VMEM(full, BF), pltpu.VMEM(full, BF), pltpu.VMEM((D, COLS), BF), pltpu.VMEM((16 * blk[0], COLS), BF),
                        pltpu.VMEM(full, BF), pltpu.VMEM(full, BF)]
        + [pltpu.VMEM((k,) + blk, BF) for k in (8, 4, 5, 8, 4, 5)]
        + [pltpu.VMEM((16, D // 32, COLS), BF)]
        + [dma((18,)), dma((16,)), dma(()), dma((3,)), dma((2, 16)), dma((2, 8)), dma((2, 4)), dma((2, 5)), dma((16,)), dma((16,))],
        compiler_params=pltpu.CompilerParams(collective_id=cid, has_side_effects=True, vmem_limit_bytes=60 * 2**20),
    )(n2, cot, w)


def gather_all(arrays, cid, fast):
    if fast:
        return gather(arrays, cid)
    return [lax.all_gather(a, "group", axis=0) for a in arrays]


def swap(x):
    return lax.ppermute(x, "replica", [(0, 1), (1, 0)])


def scatter_all(parts, cid, fast, pair=False):
    if fast:
        return scatter(parts, cid, pair)
    sums = [
        lax.psum_scatter(p, "group", scatter_dimension=0, tiled=True)[0].astype(F32) for p in parts
    ]
    if pair:
        low = [p.astype(BF) for p in sums]
        sums = [p.astype(F32) + swap(p).astype(F32) for p in low]
    return sums


def other_half(x, dim, rank):
    half = x.shape[dim] // 2
    return lax.dynamic_slice_in_dim(x, (1 - rank) * half, half, dim)


def own_half(x, dim, rank):
    half = x.shape[dim] // 2
    return lax.dynamic_slice_in_dim(x, rank * half, half, dim)


def mlp_plain(normed_two, grad_all, columns, main, spare, own_rows):
    group_count = lax.axis_size("group")
    replica_rank = lax.axis_index("replica")
    tokens, model_width = normed_two.shape
    share = main + spare
    rest = 3 * main
    gate_up_w = jnp.concatenate(
        (
            columns[:, :main],
            columns[:, rest : rest + spare],
            columns[:, main : 2 * main],
            columns[:, rest + spare : rest + 2 * spare],
        ),
        axis=1,
    )
    down_w = jnp.concatenate(
        (columns[:, 2 * main : rest], columns[:, rest + 128 : rest + 128 + spare]), axis=1
    )

    normed_all = lax.all_gather(normed_two, "group", axis=0)
    normed_all = normed_all.reshape(group_count * tokens, model_width)

    pre = matmul(normed_all, gate_up_w)
    gate_pre = pre[:, :share]
    up_pre = pre[:, share:]
    sigmoid_gate = jax.nn.sigmoid(gate_pre)
    silu_gate = gate_pre * sigmoid_gate
    hidden = (silu_gate * up_pre).astype(BF)
    grad_hidden = matmul(grad_all, down_w)
    grad_gate = (
        grad_hidden * up_pre * (sigmoid_gate * (1.0 + gate_pre * (1.0 - sigmoid_gate)))
    ).astype(BF)
    grad_up = (grad_hidden * silu_gate).astype(BF)
    gate_up_grad = jnp.concatenate((grad_gate, grad_up), axis=1)
    sums = [
        p.astype(BF).reshape(group_count, tokens, model_width)
        for p in (matmul_nt(gate_up_grad, gate_up_w), matmul_nt(hidden, down_w))
    ]
    grad_normed_two, mlp_out = scatter_all(sums, 4, False)
    down_term = matmul_tn(grad_all, hidden).astype(BF)
    gate_up_term = matmul_tn(normed_all, gate_up_grad).astype(BF)
    zeros = jnp.zeros((model_width, 128), BF)
    terms = jnp.concatenate(
        (
            gate_up_term[:, :main],
            gate_up_term[:, share : share + main],
            down_term[:, :main],
            gate_up_term[:, main:share],
            gate_up_term[:, share + main :],
            zeros[:, : 128 - 2 * spare],
            down_term[:, main:],
            zeros[:, : 128 - spare],
        ),
        axis=1,
    ).reshape(group_count, own_rows, 3 * main + 256)
    half_sum = own_half(terms, 1, replica_rank).astype(F32) + swap(
        other_half(terms, 1, replica_rank)
    ).astype(F32)
    return (grad_normed_two, mlp_out, half_sum.astype(BF))


def shards(
    hidden_in,
    lengths,
    gain_attn,
    w_query,
    b_query,
    w_key,
    b_key,
    w_value,
    b_value,
    w_out,
    gain_mlp,
    w_gate,
    w_up,
    w_down,
    cotangent,
):
    group_count = lax.axis_size("group")
    group_rank = lax.axis_index("group")
    slot_count, block_len, model_width = hidden_in.shape
    kv_heads = KV_HEADS
    head_dim = HEAD_DIM
    kv_width = kv_heads * head_dim
    repeat = HEADS // kv_heads
    slot_span = block_len * group_count
    key_step = min(512, slot_span)
    score_scale = head_dim ** (-0.5)
    tokens = slot_count * block_len
    hidden_units = w_gate.shape[1]
    own_rows = w_gate.shape[0]
    share = hidden_units // group_count
    positions = group_rank * block_len + jnp.arange(block_len, dtype=jnp.int32)
    valid_rows = (positions[None, :] < lengths[:, None]).astype(F32).reshape(tokens, 1)
    cos_table, sin_table = rope_tables(positions, head_dim)
    cos_heads = cos_table[:, None, :]
    sin_heads = sin_table[:, None, :]
    rank_end = (group_rank + 1) * block_len
    row_pos = jnp.tile(positions, repeat)

    fast = group_count == 16
    replica_rank = lax.axis_index("replica")
    pieces = (gain_attn, b_query, b_key, b_value, gain_mlp)
    sizes = [p.shape[0] for p in pieces]
    offsets = [sum(sizes[:i]) for i in range(len(sizes) + 1)]
    small = jnp.zeros((16 * 128,), BF).at[: offsets[-1]].set(jnp.concatenate(pieces))
    qkv_w, small = gather_all(
        [jnp.concatenate((w_query, w_key, w_value), axis=1), small.reshape(16, 128)], 1, fast
    )
    qkv_w = qkv_w.reshape(model_width, model_width + 2 * kv_width)
    small = small.reshape(group_count, 16 * 128)
    gain_one, query_b, key_b, value_b, gain_two = [
        small[:, offsets[i] : offsets[i + 1]].reshape(-1).astype(F32) for i in range(len(sizes))
    ]
    qkv_b = jnp.concatenate((query_b, key_b, value_b))

    main = (hidden_units // 128 // group_count) * 128
    spare = hidden_units // group_count - main
    mains = [
        w[:, : main * group_count].reshape(own_rows, group_count, main) for w in (w_gate, w_up, w_down)
    ]
    spares = [
        w[:, main * group_count :].reshape(own_rows, group_count, spare)
        for w in (w_gate, w_up, w_down)
    ]
    gap = jnp.zeros((own_rows, group_count, 128 - 2 * spare), BF)
    gap_down = jnp.zeros((own_rows, group_count, 128 - spare), BF)
    blocks = jnp.concatenate(mains + [spares[0], spares[1], gap, spares[2], gap_down], axis=2)
    blocks = jnp.transpose(own_half(blocks, 0, replica_rank), (1, 0, 2))
    own_part = lax.all_to_all(blocks, "group", 0, 0, tiled=True)
    other_part = swap(own_part)
    first = jnp.where(replica_rank == 0, own_part, other_part)
    second = jnp.where(replica_rank == 0, other_part, own_part)
    columns = jnp.concatenate((first, second), axis=1).reshape(model_width, 3 * main + 256)
    rest = 3 * main
    grad_final = cotangent.reshape(tokens, model_width).astype(F32) * valid_rows

    inputs = hidden_in.reshape(tokens, model_width).astype(F32)
    normed_full, factor_one = normalize(inputs, gain_one)
    normed = normed_full.astype(BF)
    qkv = matmul(normed, qkv_w) + qkv_b
    query_rot = rotate(
        qkv[:, :model_width].reshape(slot_count, block_len, HEADS, head_dim), cos_heads, sin_heads
    ).astype(BF)
    key_rot = rotate(
        qkv[:, model_width : model_width + kv_width].reshape(
            slot_count, block_len, kv_heads, head_dim
        ),
        cos_heads,
        sin_heads,
    ).astype(BF)
    value_low = qkv[:, model_width + kv_width :].astype(BF)
    pair = jnp.concatenate(
        (key_rot.reshape(tokens, kv_width), value_low), axis=1
    )
    pair_all, grad_all, out_w = gather_all([pair, grad_final.astype(BF), w_out], 2, fast)
    out_w = out_w.reshape(model_width, model_width)
    grad_all = grad_all.reshape(group_count * tokens, model_width)
    pair_all = jnp.transpose(
        pair_all.reshape(group_count, slot_count, block_len, 2 * kv_width), (1, 0, 2, 3)
    ).reshape(slot_count, slot_span, 2, kv_heads, head_dim)
    key_all = pair_all[:, :, 0]
    value_all = pair_all[:, :, 1]
    query_groups = []
    slot_totals = []
    slot_attended = []
    attended_rows = []
    for s in range(slot_count):
        query_rows = arrange(query_rot[s], kv_heads)
        totals, numerator = attend_forward(
            query_rows, key_all[s], value_all[s], row_pos, lengths[s], rank_end, key_step, score_scale
        )
        attended = numerator / totals[..., None]
        query_groups.append(query_rows)
        slot_totals.append(totals)
        slot_attended.append(attended)
        attended_rows.append(restore(attended, block_len))
    attended_low = jnp.concatenate(attended_rows, axis=0).astype(BF)
    residual_mid = inputs + matmul(attended_low, out_w)
    normed_two_full, factor_two = normalize(residual_mid, gain_two)
    normed_two = normed_two_full.astype(BF)
    if fast:
        grad_normed_two, mlp_out, half_sum = mlp(
            normed_two, grad_all.reshape(group_count, tokens, model_width), columns, spare, 3
        )
    else:
        grad_normed_two, mlp_out, half_sum = mlp_plain(
            normed_two, grad_all, columns, main, spare, own_rows
        )
    half_back = lax.all_to_all(half_sum, "group", 0, 0, tiled=True)
    half_other = swap(half_back)
    first = jnp.where(replica_rank == 0, half_back, half_other)
    second = jnp.where(replica_rank == 0, half_other, half_back)
    back = jnp.transpose(jnp.concatenate((first, second), axis=1), (1, 0, 2))
    gate_sum, up_sum, down_sum = [
        jnp.concatenate(
            (
                back[:, :, i * main : (i + 1) * main].reshape(own_rows, group_count * main),
                back[:, :, at : at + spare].reshape(own_rows, group_count * spare),
            ),
            axis=1,
        ).astype(F32)
        for i, at in ((0, rest), (1, rest + spare), (2, rest + 128))
    ]

    final_rows = residual_mid + mlp_out
    layer_out = (final_rows * valid_rows).reshape(slot_count, block_len, model_width).astype(BF)
    grad_mid_norm, grad_gain_two = norm_back(residual_mid, factor_two, gain_two, grad_normed_two)
    grad_mid = grad_final + grad_mid_norm
    grad_branch = grad_mid.astype(BF)
    out_term = matmul_tn(attended_low, grad_branch)
    grad_attended = matmul_nt(grad_branch, out_w)
    grad_query_rows = []
    grad_pairs = []
    for s in range(slot_count):
        slot_grad = grad_attended[s * block_len : (s + 1) * block_len].reshape(
            block_len, HEADS, head_dim
        )
        grad_out = arrange(slot_grad, kv_heads)
        totals = slot_totals[s]
        grad_total = -jnp.sum(grad_out * slot_attended[s], axis=-1) / totals
        grad_numer = (grad_out / totals[..., None]).astype(BF)
        grad_query, grad_key, grad_value = attend_backward(
            query_groups[s],
            key_all[s],
            value_all[s],
            row_pos,
            lengths[s],
            rank_end,
            key_step,
            score_scale,
            grad_numer,
            grad_total,
        )
        query_back_rows = restore(grad_query * score_scale, block_len).reshape(
            block_len, HEADS, head_dim
        )
        grad_query_rows.append(
            rotate_back(query_back_rows, cos_heads, sin_heads).reshape(block_len, HEADS * head_dim)
        )
        grad_pairs.append(
            jnp.concatenate(
                (grad_key.reshape(slot_span, kv_width), grad_value.reshape(slot_span, kv_width)),
                axis=1,
            )
        )
    pair_grads = jnp.stack(grad_pairs).reshape(slot_count, group_count, block_len, 2 * kv_width)
    pair_grads = jnp.transpose(pair_grads, (1, 0, 2, 3)).astype(BF)
    (pair_sum,) = scatter_all(
        [pair_grads.reshape(group_count, tokens, 2 * kv_width)], 5, fast
    )
    pair_sum = pair_sum.reshape(slot_count, block_len, 2 * kv_width)
    grad_query_pre = jnp.concatenate(grad_query_rows, axis=0).astype(BF)
    key_sum = pair_sum[..., :kv_width].reshape(slot_count, block_len, kv_heads, head_dim)
    grad_key_pre = (
        rotate_back(key_sum * score_scale, cos_heads, sin_heads).astype(BF).reshape(tokens, kv_width)
    )
    grad_value_pre = pair_sum[..., kv_width:].astype(BF).reshape(tokens, kv_width)
    grad_qkv = jnp.concatenate((grad_query_pre, grad_key_pre, grad_value_pre), axis=1)
    grad_normed = matmul_nt(grad_qkv, qkv_w)
    grad_in_norm, grad_gain_one = norm_back(inputs, factor_one, gain_one, grad_normed)
    grad_input = (grad_mid + grad_in_norm).reshape(slot_count, block_len, model_width)
    qkv_term = matmul_tn(normed, grad_qkv)
    qkv_bias = jnp.sum(grad_qkv.astype(F32), axis=0)

    vectors = jnp.concatenate(
        [
            grad_gain_one.reshape(group_count, -1),
            qkv_bias[:model_width].reshape(group_count, -1),
            qkv_bias[model_width : model_width + kv_width].reshape(group_count, -1),
            qkv_bias[model_width + kv_width :].reshape(group_count, -1),
            grad_gain_two.reshape(group_count, -1),
        ],
        axis=1,
    )
    vectors = jnp.concatenate(
        (vectors, jnp.zeros((group_count, 16 * 128 - offsets[-1]), F32)), axis=1
    ).reshape(group_count, 16, 128)
    weight_sum, out_sum, vector_sum = scatter_all(
        [
            p.astype(BF).reshape(group_count, p.shape[0] // group_count, -1)
            for p in (qkv_term, out_term)
        ]
        + [vectors.astype(BF)],
        6,
        fast,
        pair=True,
    )
    vector_sum = vector_sum.reshape(-1)
    gain_one_sum, query_bias_sum, key_bias_sum, value_bias_sum, gain_two_sum = [
        vector_sum[offsets[i] : offsets[i + 1]] for i in range(len(sizes))
    ]
    ends = (0, model_width, model_width + kv_width, model_width + 2 * kv_width)
    query_sum, key_sum_w, value_sum_w = [weight_sum[:, ends[i] : ends[i + 1]] for i in range(3)]
    return (
        layer_out,
        grad_input,
        gain_one_sum,
        query_sum,
        query_bias_sum,
        key_sum_w,
        key_bias_sum,
        value_sum_w,
        value_bias_sum,
        out_sum,
        gain_two_sum,
        gate_sum,
        up_sum,
        down_sum,
    )


def solution(mesh):
    act = P("replica", "group", None)
    vec = P("group")
    mat = P("group", None)
    return jax.shard_map(
        shards,
        mesh=mesh,
        in_specs=(act, P("replica"), vec, mat, vec, mat, vec, mat, vec, mat, vec, mat, mat, mat, act),
        out_specs=(act, act, vec, mat, vec, mat, vec, mat, vec, mat, vec, mat, mat, mat),
        check_vma=False,
    )
```

```python
import functools

import jax
import jax.numpy as jnp
from jax import lax
from jax.experimental import pallas as pl
from jax.experimental.pallas import tpu as pltpu
from jax.sharding import PartitionSpec as P

MESH = pl.DeviceIdType.MESH
NZ = 4
MAIN = 512
HEADS = 12
KV_HEADS = 2
HEAD_DIM = 128
EPSILON = 1e-06
THETA = 1000000.0
BF = jnp.bfloat16
F32 = jnp.float32


def rope_tables(positions, head_dim):
    freqs = THETA ** (-jnp.arange(0, head_dim, 2).astype(F32) / head_dim)
    angles = positions.astype(F32)[:, None] * freqs[None, :]
    angles = jnp.concatenate((angles, angles), axis=-1)
    return (jnp.cos(angles), jnp.sin(angles))


def rotate(tensor, cos_table, sin_table):
    halfway = tensor.shape[-1] // 2
    turned = jnp.concatenate((-tensor[..., halfway:], tensor[..., :halfway]), axis=-1)
    return tensor * cos_table + turned * sin_table


def rotate_back(gradient, cos_table, sin_table):
    halfway = gradient.shape[-1] // 2
    scaled = gradient * sin_table
    turned = jnp.concatenate((scaled[..., halfway:], -scaled[..., :halfway]), axis=-1)
    return gradient * cos_table + turned


def normalize(row_values, gain_vec):
    factor = lax.rsqrt(jnp.mean(row_values * row_values, axis=-1, keepdims=True) + EPSILON)
    return (row_values * factor * gain_vec, factor)


def norm_back(row_values, factor, gain_vec, upstream):
    weighted = upstream * gain_vec
    inner_mean = jnp.mean(weighted * row_values, axis=-1, keepdims=True)
    grad_rows = factor * weighted - row_values * (factor * factor * factor) * inner_mean
    grad_gain = jnp.sum(upstream * row_values * factor, axis=0)
    return (grad_rows, grad_gain)


def matmul(a, b):
    return jnp.dot(a, b, preferred_element_type=F32)


def matmul_nt(a, b):
    return lax.dot_general(a, b, (((1,), (1,)), ((), ())), preferred_element_type=F32)


def matmul_tn(a, b):
    return lax.dot_general(a, b, (((0,), (0,)), ((), ())), preferred_element_type=F32)


def arrange(per_token, kv_heads):
    block_len, head_count, head_dim = per_token.shape
    repeat = head_count // kv_heads
    grouped = per_token.reshape(block_len, kv_heads, repeat, head_dim)
    return jnp.transpose(grouped, (1, 2, 0, 3)).reshape(kv_heads, repeat * block_len, head_dim)


def restore(per_group, block_len):
    kv_heads, row_count, head_dim = per_group.shape
    repeat = row_count // block_len
    grouped = per_group.reshape(kv_heads, repeat, block_len, head_dim)
    return jnp.transpose(grouped, (2, 0, 1, 3)).reshape(block_len, kv_heads * repeat * head_dim)


def masked_exp(query_rows, key_block, row_pos, first_key, length, score_scale):
    key_step = key_block.shape[0]
    raw_scores = jnp.einsum("grd,kgd->grk", query_rows, key_block, preferred_element_type=F32)
    key_pos = first_key + jnp.arange(key_step, dtype=jnp.int32)
    allowed = (key_pos[None, :] <= row_pos[:, None]) & (key_pos[None, :] < length)
    return jnp.where(allowed[None], jnp.exp(raw_scores * score_scale), 0.0)


def block_total(length, rank_end, key_step):
    key_limit = jnp.minimum(length, rank_end)
    return (key_limit + key_step - 1) // key_step


def attend_forward(query_rows, key_all, value_all, row_pos, length, rank_end, key_step, scale):
    kv_heads, row_count, head_dim = query_rows.shape

    def visit(block_index, state_tuple):
        totals, numerator = state_tuple
        first_key = block_index * key_step
        key_block = lax.dynamic_slice_in_dim(key_all, first_key, key_step, 0)
        value_block = lax.dynamic_slice_in_dim(value_all, first_key, key_step, 0)
        weights = masked_exp(query_rows, key_block, row_pos, first_key, length, scale)
        totals = totals + jnp.sum(weights, axis=-1)
        numerator = numerator + jnp.einsum(
            "grk,kgd->grd", weights.astype(BF), value_block, preferred_element_type=F32
        )
        return (totals, numerator)

    initial = (
        jnp.zeros((kv_heads, row_count), F32),
        jnp.zeros((kv_heads, row_count, head_dim), F32),
    )
    return lax.fori_loop(0, block_total(length, rank_end, key_step), visit, initial)


def attend_backward(
    query_rows, key_all, value_all, row_pos, length, rank_end, key_step, scale, grad_numer, grad_total
):
    kv_heads, row_count, head_dim = query_rows.shape

    def visit(block_index, state_tuple):
        grad_query, grad_key, grad_value = state_tuple
        first_key = block_index * key_step
        key_block = lax.dynamic_slice_in_dim(key_all, first_key, key_step, 0)
        value_block = lax.dynamic_slice_in_dim(value_all, first_key, key_step, 0)
        weights = masked_exp(query_rows, key_block, row_pos, first_key, length, scale)
        grad_prob = jnp.einsum("grd,kgd->grk", grad_numer, value_block, preferred_element_type=F32)
        grad_score = (weights * (grad_prob + grad_total[..., None])).astype(BF)
        grad_query = grad_query + jnp.einsum(
            "grk,kgd->grd", grad_score, key_block, preferred_element_type=F32
        )
        key_part = jnp.einsum("grk,grd->kgd", grad_score, query_rows, preferred_element_type=F32)
        value_part = jnp.einsum(
            "grk,grd->kgd", weights.astype(BF), grad_numer, preferred_element_type=F32
        )
        key_old = lax.dynamic_slice_in_dim(grad_key, first_key, key_step, 0)
        value_old = lax.dynamic_slice_in_dim(grad_value, first_key, key_step, 0)
        grad_key = lax.dynamic_update_slice_in_dim(grad_key, key_old + key_part, first_key, 0)
        grad_value = lax.dynamic_update_slice_in_dim(
            grad_value, value_old + value_part, first_key, 0
        )
        return (grad_query, grad_key, grad_value)

    initial = (
        jnp.zeros((kv_heads, row_count, head_dim), F32),
        jnp.zeros(key_all.shape, F32),
        jnp.zeros(value_all.shape, F32),
    )
    return lax.fori_loop(0, block_total(length, rank_end, key_step), visit, initial)


D = 1536
COLS = 3 * MAIN + 256


def place():
    g = lax.axis_index("group")
    r = lax.axis_index("replica")
    return r, g // 4, lax.rem(g // 2, 2), lax.rem(g, 2)

def idx(z, x, c):
    return (z * 2 + x) * 2 + c

def greet(r, z, x, c, with_y=False):
    bar = pltpu.get_barrier_semaphore()
    def hail(dev):
        pl.semaphore_signal(bar, inc=1, device_id=dev, device_id_type=MESH)
    hail((r, idx(z, 1 - x, c)))
    hail((r, idx(z, x, 1 - c)))
    if with_y:
        hail((1 - r, idx(z, x, c)))
    @pl.when(z > 0)
    def _():
        hail((r, idx(z - 1, x, c)))
    @pl.when(z < NZ - 1)
    def _():
        hail((r, idx(z + 1, x, c)))
    ends = jnp.where((z > 0) & (z < NZ - 1), 1, 0)
    pl.semaphore_wait(bar, (4 if with_y else 3) + ends)

def planes(z):
    return (
        z,
        jnp.where(z == 0, 1, jnp.where(z == 1, 0, jnp.where(z == 2, 3, 2))),
        jnp.where(z == 0, 2, jnp.where(z == 1, 2, 1)),
        jnp.where(z < 2, 3, 0),
    )

def when(cond, fn):
    pl.when(cond)(fn)

class Gather:
    def __init__(self, at, src, out, send, recv, local):
        self.r, self.z, self.x, self.c = at
        self.src, self.out, self.send, self.recv, self.local = src, out, send, recv, local
        self.mid = (self.z > 0) & (self.z < NZ - 1)
        self.p = planes(self.z)
    def put(self, src, b, k, dev):
        pltpu.make_async_remote_copy(src, self.out.at[b], self.send.at[k], self.recv.at[b], device_id=dev, device_id_type=MESH).start()
    def sent(self, k):
        b = 0
        pltpu.make_async_remote_copy(self.out.at[b], self.out.at[b], self.send.at[k], self.recv.at[b], device_id=(self.r, 0), device_id_type=MESH).wait_send()
    def got(self, b):
        pltpu.make_async_remote_copy(self.out.at[b], self.out.at[b], self.send.at[0], self.recv.at[b], device_id=(self.r, 0), device_id_type=MESH).wait_recv()
    def zdev(self, s): return (self.r, idx(self.z + s, self.x, self.c))
    def xdev(self): return (self.r, idx(self.z, 1 - self.x, self.c))
    def cdev(self): return (self.r, idx(self.z, self.x, 1 - self.c))
    def begin(self):
        z, x, c = self.z, self.x, self.c
        me = idx(z, x, c)
        for s in (1, -1):
            when(self.inside(z + s), lambda s=s: self.put(self.src, me, 0 if s == 1 else 3, self.zdev(s)))
        self.put(self.src, me, 6 + z, self.xdev())
        self.put(self.src, me, 10 + 2 * z + x, self.cdev())
        pltpu.make_async_copy(self.src, self.out.at[me], self.local).start()
    def inside(self, z): return (z >= 0) & (z < NZ)
    def from_z(self, zz):
        z, x, c = self.z, self.x, self.c
        b = idx(zz, x, c)
        self.got(b)
        s = jnp.where(zz < z, 1, -1)
        d = jnp.abs(zz - z)
        slot = jnp.where(zz < z, 0, 3) + d
        when(self.inside(z + s), lambda: self.put(self.out.at[b], b, slot, (self.r, idx(z + s, x, c))))
        self.put(self.out.at[b], b, 6 + zz, self.xdev())
        self.put(self.out.at[b], b, 10 + 2 * zz + x, self.cdev())
    def first(self):
        self.from_z(self.p[1])
        when(self.mid, lambda: self.from_z(self.p[2]))
        self.from_x(self.p[0])
    def second(self):
        self.from_z(jnp.where(self.mid, self.p[3], self.p[2]))
        self.from_x(self.p[1])
    def third(self):
        when(~self.mid, lambda: self.from_z(self.p[3]))
        self.from_x(self.p[2])
    def fourth(self):
        self.from_x(self.p[3])
    def from_x(self, zz):
        b = idx(zz, 1 - self.x, self.c)
        self.got(b)
        self.put(self.out.at[b], b, 10 + 2 * zz + 1 - self.x, self.cdev())
    def from_c(self, zz):
        self.got(idx(zz, self.x, 1 - self.c))
        self.got(idx(zz, 1 - self.x, 1 - self.c))
    def end(self, local=True):
        z = self.z
        for d in range(NZ - 1):
            when((z - d >= 0) & (z < NZ - 1), lambda d=d: self.sent(d))
            when((z + d < NZ) & (z > 0), lambda d=d: self.sent(3 + d))
        for k in range(6, 18):
            self.sent(k)
        if local:
            pltpu.make_async_copy(self.src, self.out.at[0], self.local).wait()

def gather_kernel(n, *refs):
    srcs, outs = refs[:n], refs[n:2*n]
    send, recv, local = refs[2*n:]
    at = place()
    greet(*at)
    eng = [Gather(at, srcs[i], outs[i], send.at[i], recv.at[i], local.at[i]) for i in range(n)]
    for e in eng: e.begin()
    for e in eng: e.first()
    for e in eng: e.second()
    for e in eng: e.third()
    for e in eng: e.fourth()
    for d in range(NZ):
        for e in eng: e.from_c(d)
    for e in eng: e.end()

def gather(arrays, cid):
    n = len(arrays)
    return pl.pallas_call(
        functools.partial(gather_kernel, n),
        out_shape=[jax.ShapeDtypeStruct((16,) + a.shape, a.dtype) for a in arrays],
        in_specs=[pl.BlockSpec(memory_space=pl.ANY)] * n,
        out_specs=[pl.BlockSpec(memory_space=pl.ANY)] * n,
        scratch_shapes=[pltpu.SemaphoreType.DMA((n, 18)), pltpu.SemaphoreType.DMA((n, 16)), pltpu.SemaphoreType.DMA((n,))],
        compiler_params=pltpu.CompilerParams(collective_id=cid, has_side_effects=True),
    )(*arrays)

class Scatter:
    def __init__(self, at, part, rc, rx, rz, send, rcs, rxs, rzs):
        self.r, self.z, self.x, self.c = at
        self.part, self.rc, self.rx, self.rz = part, rc, rx, rz
        self.send, self.rcs, self.rxs, self.rzs = send, rcs, rxs, rzs
    def inside(self, z): return (z >= 0) & (z < NZ)
    def copy(self, src, dst, k, rs, dev):
        return pltpu.make_async_remote_copy(src, dst, self.send.at[k], rs, device_id=dev, device_id_type=MESH)
    def over(self, d):
        return [(s, self.z + s * d) for s in ((-1, 1) if d else (1,))]
    def begin(self, far_first=True):
        z, x, c = self.z, self.x, self.c
        dev = (self.r, idx(z, x, 1 - c))
        for xx in (1 - x, x):
            for d in range(NZ - 1, -1, -1):
                for s, zz in self.over(d):
                    k = 2 * zz + xx
                    when(self.inside(zz), lambda zz=zz, k=k, xx=xx: self.copy(self.part.at[idx(zz, xx, 1 - c)], self.rc.at[k], k, self.rcs.at[k], dev).start())
    def send_c(self, zz):
        z, x, c = self.z, self.x, self.c
        dev = (self.r, idx(z, x, 1 - c))
        for xx in (1 - x, x):
            k = 2 * zz + xx
            self.copy(self.part.at[idx(zz, xx, 1 - c)], self.rc.at[k], k, self.rcs.at[k], dev).start()
    def step_x(self, d):
        z, x, c = self.z, self.x, self.c
        dev = (self.r, idx(z, 1 - x, c))
        for s, zz in self.over(d):
            def go(zz=zz):
                k = 2 * zz + 1 - x
                b = idx(zz, 1 - x, c)
                self.copy(self.rc.at[k], self.rc.at[k], 0, self.rcs.at[k], dev).wait_recv()
                self.part[b] = (self.part[b].astype(F32) + self.rc[k].astype(F32)).astype(BF)
                self.copy(self.part.at[b], self.rx.at[zz], 8 + zz, self.rxs.at[zz], dev).start()
            when(self.inside(zz), go)
    def step_z(self, d):
        z, x, c = self.z, self.x, self.c
        for s, zz in self.over(d):
            def go(zz=zz, s=s):
                k = 2 * zz + x
                b = idx(zz, x, c)
                self.copy(self.rc.at[k], self.rc.at[k], 0, self.rcs.at[k], (self.r, 0)).wait_recv()
                self.copy(self.rx.at[zz], self.rx.at[zz], 0, self.rxs.at[zz], (self.r, 0)).wait_recv()
                both = self.part[b].astype(F32) + self.rc[k].astype(F32) + self.rx[zz].astype(F32)
                dev = (self.r, idx(z + s, x, c))
                slot = jnp.where(zz == z + s, NZ, zz) if s == -1 else zz
                self.part[b] = both.astype(BF)
                def more():
                    self.copy(self.rz.at[zz], self.rz.at[zz], 0, self.rzs.at[zz], dev).wait_recv()
                    self.part[b] = (self.part[b].astype(F32) + self.rz[zz].astype(F32)).astype(BF)
                when(self.inside(z - s), more)
                self.copy(self.part.at[b], self.rz.at[slot], 12 + zz, self.rzs.at[slot], dev).start()
            when(self.inside(zz), go)
    def finish(self, out):
        z, x, c = self.z, self.x, self.c
        k = 2 * z + x
        b = idx(z, x, c)
        self.copy(self.rc.at[k], self.rc.at[k], 0, self.rcs.at[k], (self.r, 0)).wait_recv()
        self.copy(self.rx.at[z], self.rx.at[z], 0, self.rxs.at[z], (self.r, 0)).wait_recv()
        out[...] = self.part[b].astype(F32) + self.rc[k].astype(F32) + self.rx[z].astype(F32)
        def lo():
            self.copy(self.rz.at[z], self.rz.at[z], 0, self.rzs.at[z], (self.r, 0)).wait_recv()
            out[...] += self.rz[z].astype(F32)
        when(z > 0, lo)
        def hi():
            self.copy(self.rz.at[NZ], self.rz.at[NZ], 0, self.rzs.at[NZ], (self.r, 0)).wait_recv()
            out[...] += self.rz[NZ].astype(F32)
        when(z < NZ - 1, hi)
        for k in range(8):
            self.copy(self.part.at[0], self.part.at[0], k, self.rcs.at[0], (self.r, 0)).wait_send()
        for k in range(8, 12):
            self.copy(self.part.at[0], self.part.at[0], k, self.rcs.at[0], (self.r, 0)).wait_send()
        for zz in range(NZ):
            when(z != zz, lambda zz=zz: self.copy(self.part.at[0], self.part.at[0], 12 + zz, self.rcs.at[0], (self.r, 0)).wait_send())

def scatter_steps(engines):
    for e in engines: e.begin()
    order = [("x", 3), ("x", 2), ("z", 3), ("x", 1), ("z", 2), ("x", 0), ("z", 1)]
    for kind, d in order:
        for e in engines:
            (e.step_x if kind == "x" else e.step_z)(d)

def scatter_kernel(n, pair, *refs):
    ps, os = refs[:n], refs[n:2*n]
    s = refs[2*n:]
    vm = [s[4*i:4*i+4] for i in range(n)]
    ysb = s[4*n:4*n+2*n] if pair else None
    send, rcs, rxs, rzs, lsem, ysem = s[4*n+(2*n if pair else 0):]
    at = place()
    for i in range(n):
        pltpu.make_async_copy(ps[i], vm[i][0], lsem.at[i]).start()
    greet(*at, with_y=pair)
    for i in range(n):
        pltpu.make_async_copy(ps[i], vm[i][0], lsem.at[i]).wait()
    engines = [Scatter(at, *vm[i], send.at[i], rcs.at[i], rxs.at[i], rzs.at[i]) for i in range(n)]
    scatter_steps(engines)
    r, z, x, c = at
    for i, e in enumerate(engines):
        e.finish(os[i])
        if pair:
            ysb[2*i][...] = os[i][...].astype(BF)
            pltpu.make_async_remote_copy(ysb[2*i], ysb[2*i+1], ysem.at[2*i], ysem.at[2*i+1], device_id=(1 - r, idx(z, x, c)), device_id_type=MESH).start()
    if pair:
        for i, e in enumerate(engines):
            pltpu.make_async_remote_copy(ysb[2*i], ysb[2*i+1], ysem.at[2*i], ysem.at[2*i+1], device_id=(1 - r, idx(z, x, c)), device_id_type=MESH).wait()
            os[i][...] = ysb[2*i][...].astype(F32) + ysb[2*i+1][...].astype(F32)

def scatter(parts, cid, pair=False):
    n = len(parts)
    scratch = []
    for p in parts:
        blk = p.shape[1:]
        scratch += [pltpu.VMEM((k,) + blk, BF) for k in (16, 8, 4, 5)]
    if pair:
        for p in parts:
            scratch += [pltpu.VMEM(p.shape[1:], BF)] * 2
    dma = pltpu.SemaphoreType.DMA
    return pl.pallas_call(
        functools.partial(scatter_kernel, n, pair),
        out_shape=[jax.ShapeDtypeStruct(p.shape[1:], F32) for p in parts],
        in_specs=[pl.BlockSpec(memory_space=pl.ANY)] * n,
        out_specs=[pl.BlockSpec(memory_space=pltpu.VMEM)] * n,
        scratch_shapes=scratch + [dma((n, 16)), dma((n, 8)), dma((n, 4)), dma((n, 5)), dma((n,)), dma((2 * n,))],
        compiler_params=pltpu.CompilerParams(collective_id=cid, has_side_effects=True, vmem_limit_bytes=60 * 2**20),
    )(*parts)


KS = (8, 1, 9, 2, 10, 3, 11, 4, 12, 5, 13, 6, 14, 7, 15)
WINDOW = 4

class Deal:
    def __init__(self, at, ws, rem, buf, send, recv, ysend, yrecv, local):
        self.r, self.z, self.x, self.c = at
        self.me = idx(self.z, self.x, self.c)
        self.ws, self.rem, self.buf = ws, rem, buf
        self.send, self.recv, self.ysend, self.yrecv, self.local = send, recv, ysend, yrecv, local
        self.half = ws[0].shape[0] // 2
    def rows(self, j, h):
        n = self.half
        return self.buf.at[pl.ds(pl.multiple_of((2 * j + h) * n, n), n)]
    def launch(self, k):
        r, me, n = self.r, self.me, self.half
        row = pl.ds(pl.multiple_of(r * n, n), n)
        j = jnp.bitwise_xor(me, k)
        dev = (r, j)
        dst = self.rows(me, r)
        col = pl.ds(pl.multiple_of(j * MAIN, MAIN), MAIN)
        for i in range(3):
            pltpu.make_async_remote_copy(self.ws[i].at[row, col], dst.at[:, pl.ds(i * MAIN, MAIN)], self.send.at[k], self.recv.at[k], device_id=dev, device_id_type=MESH).start()
        pltpu.make_async_remote_copy(self.rem.at[j, row], dst.at[:, pl.ds(3 * MAIN, 256)], self.send.at[k], self.recv.at[k], device_id=dev, device_id_type=MESH).start()
    def begin(self):
        me, n = self.me, self.half
        for k in KS[:WINDOW]:
            self.launch(k)
        col = pl.ds(pl.multiple_of(me * MAIN, MAIN), MAIN)
        own = self.buf.at[pl.ds(pl.multiple_of(2 * me * n, 2 * n), 2 * n)]
        for i in range(3):
            pltpu.make_async_copy(self.ws[i].at[:, col], own.at[:, pl.ds(i * MAIN, MAIN)], self.local).start()
        pltpu.make_async_copy(self.rem.at[me], own.at[:, pl.ds(3 * MAIN, 256)], self.local).start()
    def step(self, i):
        k = KS[i]
        r, me = self.r, self.me
        j = jnp.bitwise_xor(me, k)
        blk = self.rows(j, r)
        dev = (1 - r, me)
        pltpu.make_async_remote_copy(blk, blk, self.send.at[k], self.recv.at[k], device_id=dev, device_id_type=MESH).wait_recv()
        pltpu.make_async_remote_copy(blk, blk, self.ysend.at[k], self.yrecv.at[k], device_id=dev, device_id_type=MESH).start()
        if i + WINDOW < 15:
            self.launch(KS[i + WINDOW])
    def end(self):
        r, me = self.r, self.me
        dev = (1 - r, me)
        for k in range(1, 16):
            j = jnp.bitwise_xor(me, k)
            blk = self.rows(j, 1 - r)
            pltpu.make_async_remote_copy(blk, blk, self.ysend.at[k], self.yrecv.at[k], device_id=dev, device_id_type=MESH).wait()
            pltpu.make_async_remote_copy(blk, blk, self.send.at[k], self.recv.at[k], device_id=dev, device_id_type=MESH).wait_send()
        own = self.buf.at[pl.ds(pl.multiple_of(2 * me * self.half, 2 * self.half), 2 * self.half)]
        pltpu.make_async_copy(own, own, self.local).wait()

def hail_all(r, z, x, c):
    bar = pltpu.get_barrier_semaphore()
    me = idx(z, x, c)
    for k in range(1, 16):
        pl.semaphore_signal(bar, inc=1, device_id=(r, lax.rem(me + k, 16)), device_id_type=MESH)
    pl.semaphore_signal(bar, inc=1, device_id=(1 - r, me), device_id_type=MESH)
    pl.semaphore_wait(bar, 16)

def weights_kernel(wq, wk, wv, wg, wu, wd, rem, small, qkv_out, small_out, buf, qkv_own, gs, gr, gl, ss, sr, sl, ds, dr, ys, yr, dl, lsem):
    at = place()
    width = wq.shape[1]
    kw = wk.shape[1]
    loads = [pltpu.make_async_copy(w, qkv_own.at[:, pl.ds(o, n)], lsem.at[i]) for i, (w, o, n) in enumerate(((wq, 0, width), (wk, width, kw), (wv, width + kw, kw)))]
    for l in loads: l.start()
    hail_all(*at)
    for l in loads: l.wait()
    g = Gather(at, qkv_own, qkv_out, gs, gr, gl)
    v = Gather(at, small, small_out, ss, sr, sl)
    d = Deal(at, (wg, wu, wd), rem, buf, ds, dr, ys, yr, dl)
    g.begin()
    v.begin()
    d.begin()
    steps = iter(range(15))
    def some(n):
        for _ in range(n):
            i = next(steps, None)
            if i is not None:
                d.step(i)
    for phase, n in ((lambda e: e.first(), PACE[0]), (lambda e: e.second(), PACE[1]), (lambda e: e.third(), PACE[2]), (lambda e: e.fourth(), 15)):
        phase(g)
        phase(v)
        some(n)
    for e in (g, v):
        for zz in range(NZ):
            e.from_c(zz)
        e.end()
    d.end()

PACE = (2, 2, 3)

def weights(wq, wk, wv, wg, wu, wd, rem, small, cid):
    any_ = pl.BlockSpec(memory_space=pl.ANY)
    dma = pltpu.SemaphoreType.DMA
    rows = wq.shape[0]
    width = wq.shape[1] + 2 * wk.shape[1]
    return pl.pallas_call(
        weights_kernel,
        out_shape=[jax.ShapeDtypeStruct((16, rows, width), BF), jax.ShapeDtypeStruct((16,) + small.shape, BF), jax.ShapeDtypeStruct((16 * rows, 3 * MAIN + 256), BF)],
        in_specs=[any_] * 8,
        out_specs=[any_] * 3,
        scratch_shapes=[pltpu.VMEM((rows, width), BF), dma((18,)), dma((16,)), dma(()), dma((18,)), dma((16,)), dma(())] + [dma((16,))] * 4 + [dma(()), dma((3,))],
        compiler_params=pltpu.CompilerParams(collective_id=cid, has_side_effects=True),
    )(wq, wk, wv, wg, wu, wd, rem, small)


def dot(a, b):
    return lax.dot_general(a, b, (((1,), (0,)), ((), ())), preferred_element_type=F32)
def dot_nt(a, b):
    return lax.dot_general(a, b, (((1,), (1,)), ((), ())), preferred_element_type=F32)
def dot_tn(a, b):
    return lax.dot_general(a, b, (((0,), (0,)), ((), ())), preferred_element_type=F32)

def gated(g, u, gh):
    sig = jax.nn.sigmoid(g)
    silu = g * sig
    return (gh * u * (sig * (1.0 + g * (1.0 - sig)))).astype(BF), (gh * silu).astype(BF), (silu * u).astype(BF)

def mlp_kernel(spare, n2_ref, cot_ref, w_ref, gsum, osum, half_ref,
               n2, cot, w, act, pg, po, rcg, rxg, rzg, rco, rxo, rzo, yb,
               gsend, grecv, glocal, lsem, ssend, srcs, srxs, srzs, ysend, yrecv):
    at = place()
    r, z, x, c = at
    loads = [pltpu.make_async_copy(w_ref, w, lsem.at[0]), pltpu.make_async_copy(cot_ref, cot, lsem.at[1])]
    for l in loads: l.start()
    greet(*at, with_y=True)
    g = Gather(at, n2_ref, n2, gsend, grecv, glocal)
    rg = Scatter(at, pg, rcg, rxg, rzg, ssend.at[0], srcs.at[0], srxs.at[0], srzs.at[0])
    ro = Scatter(at, po, rco, rxo, rzo, ssend.at[1], srcs.at[1], srxs.at[1], srzs.at[1])
    g.begin()
    for l in loads: l.wait()
    mid = (z > 0) & (z < NZ - 1)
    p = [z,
         jnp.where(z == 0, 1, jnp.where(z == 1, 0, jnp.where(z == 2, 3, 2))),
         jnp.where(z == 0, 2, jnp.where(z == 1, 2, 1)),
         jnp.where(z < 2, 3, 0)]

    def tiles(zz):
        rows = pl.ds(pl.multiple_of(4 * zz, 4), 4)
        tok = pl.ds(pl.multiple_of(512 * zz, 512), 512)
        @pl.loop(0, 2)
        def _(t):
            a = n2[rows].reshape(512, D)
            k = cot[rows].reshape(512, D)
            def col(base):
                return pl.ds(pl.multiple_of(base + 256 * t, 256), 256)
            dg, du, h = gated(dot(a, w[:, col(0)]), dot(a, w[:, col(MAIN)]), dot(k, w[:, col(2 * MAIN)]))
            act[tok, col(0)] = dg
            act[tok, col(MAIN)] = du
            act[tok, col(2 * MAIN)] = h
        a = n2[rows].reshape(512, D)
        k = cot[rows].reshape(512, D)
        pre = dot(a, w[:, 3 * MAIN : 3 * MAIN + 128])
        gh = dot(k, w[:, 3 * MAIN + 128 :])
        lane = lax.broadcasted_iota(jnp.int32, (512, 128), 1)
        sig = jax.nn.sigmoid(pre)
        silu = pre * sig
        up = pltpu.roll(pre, 128 - spare, 1)
        dg = gh * up * (sig * (1.0 + pre * (1.0 - sig)))
        du = pltpu.roll(gh * silu, spare, 1)
        act[tok, 3 * MAIN : 3 * MAIN + 128] = jnp.where(lane < spare, dg, jnp.where(lane < 2 * spare, du, 0.0)).astype(BF)
        act[tok, 3 * MAIN + 128 :] = jnp.where(lane < spare, silu * up, 0.0).astype(BF)
        @pl.loop(0, D // 256)
        def _(t):
            dr = pl.ds(pl.multiple_of(256 * t, 256), 256)
            v = dot_nt(act[tok, : 2 * MAIN], w[dr, : 2 * MAIN]) + dot_nt(act[tok, 3 * MAIN : 3 * MAIN + 128], w[dr, 3 * MAIN : 3 * MAIN + 128])
            pg[rows, :, dr] = v.astype(BF).reshape(4, 128, 256)
            v = dot_nt(act[tok, 2 * MAIN : 3 * MAIN], w[dr, 2 * MAIN : 3 * MAIN]) + dot_nt(act[tok, 3 * MAIN + 128 :], w[dr, 3 * MAIN + 128 :])
            po[rows, :, dr] = v.astype(BF).reshape(4, 128, 256)
        rg.send_c(zz)
        ro.send_c(zz)

    g.from_z(p[1])
    when(mid, lambda: g.from_z(p[2]))
    g.from_x(p[0])
    g.from_c(p[0])
    pltpu.make_async_copy(n2_ref, n2.at[0], glocal).wait()
    tiles(p[0])
    g.from_z(jnp.where(mid, p[3], p[2]))
    g.from_x(p[1])
    g.from_c(p[1])
    tiles(p[1])
    when(~mid, lambda: g.from_z(p[3]))
    g.from_x(p[2])
    g.from_c(p[2])
    tiles(p[2])
    g.from_x(p[3])
    g.from_c(p[3])
    tiles(p[3])

    ydev = (1 - r, idx(z, x, c))
    own = D // 16
    half = own // 2
    def ycopy(j):
        src = w.at[pl.ds(pl.multiple_of(own * j + half * (1 - r), half), half)]
        return pltpu.make_async_remote_copy(src, yb.at[j], ysend.at[j], yrecv.at[j], device_id=ydev, device_id_type=MESH)
    def grads(q):
        dr = slice(384 * q, 384 * (q + 1))
        row = slice(384 * q, 384 * (q + 1))
        @pl.loop(0, 4)
        def _(t):
            col = pl.ds(pl.multiple_of(256 * t, 256), 256)
            w[row, col] = dot_tn(n2[:, :, dr].reshape(2048, 384), act[:, col]).astype(BF)
        @pl.loop(0, 2)
        def _(t):
            col = pl.ds(pl.multiple_of(2 * MAIN + 256 * t, 256), 256)
            w[row, col] = dot_tn(cot[:, :, dr].reshape(2048, 384), act[:, col]).astype(BF)
        w[row, 3 * MAIN : 3 * MAIN + 128] = dot_tn(n2[:, :, dr].reshape(2048, 384), act[:, 3 * MAIN : 3 * MAIN + 128]).astype(BF)
        w[row, 3 * MAIN + 128 :] = dot_tn(cot[:, :, dr].reshape(2048, 384), act[:, 3 * MAIN + 128 :]).astype(BF)
        for j in range(4 * q, 4 * q + 4):
            ycopy(j).start()
    def yadd(j):
        ycopy(j).wait()
        mine = w[pl.ds(pl.multiple_of(own * j + half * r, half), half)]
        yb[j] = (mine.astype(F32) + yb[j].astype(F32)).astype(BF)
        pltpu.make_async_copy(yb.at[j], half_ref.at[j], lsem.at[2]).start()

    rg.step_x(3)
    rg.step_x(2)
    grads(0)
    rg.step_z(3)
    rg.step_x(1)
    grads(1)
    rg.step_z(2)
    rg.step_x(0)
    grads(2)
    rg.step_z(1)
    ro.step_x(3)
    ro.step_x(2)
    grads(3)
    rg.finish(gsum)
    ro.step_z(3)
    ro.step_x(1)
    for j in range(0, 4): yadd(j)
    ro.step_z(2)
    ro.step_x(0)
    for j in range(4, 8): yadd(j)
    ro.step_z(1)
    for j in range(8, 12): yadd(j)
    ro.finish(osum)
    for j in range(12, 16): yadd(j)
    pltpu.make_async_copy(yb, half_ref, lsem.at[2]).wait()
    g.end(local=False)

def mlp(n2, cot, w, spare, cid):
    blk = n2.shape
    dma = pltpu.SemaphoreType.DMA
    full = (16,) + blk
    return pl.pallas_call(
        functools.partial(mlp_kernel, spare),
        out_shape=[jax.ShapeDtypeStruct(blk, F32)] * 2 + [jax.ShapeDtypeStruct((16, D // 32, COLS), BF)],
        in_specs=[pl.BlockSpec(memory_space=pl.ANY)] * 3,
        out_specs=[pl.BlockSpec(memory_space=pltpu.VMEM)] * 2 + [pl.BlockSpec(memory_space=pl.ANY)],
        scratch_shapes=[pltpu.VMEM(full, BF), pltpu.VMEM(full, BF), pltpu.VMEM((D, COLS), BF), pltpu.VMEM((16 * blk[0], COLS), BF),
                        pltpu.VMEM(full, BF), pltpu.VMEM(full, BF)]
        + [pltpu.VMEM((k,) + blk, BF) for k in (8, 4, 5, 8, 4, 5)]
        + [pltpu.VMEM((16, D // 32, COLS), BF)]
        + [dma((18,)), dma((16,)), dma(()), dma((3,)), dma((2, 16)), dma((2, 8)), dma((2, 4)), dma((2, 5)), dma((16,)), dma((16,))],
        compiler_params=pltpu.CompilerParams(collective_id=cid, has_side_effects=True, vmem_limit_bytes=60 * 2**20),
    )(n2, cot, w)


def gather_all(arrays, cid, fast):
    if fast:
        return gather(arrays, cid)
    return [lax.all_gather(a, "group", axis=0) for a in arrays]


def swap(x):
    return lax.ppermute(x, "replica", [(0, 1), (1, 0)])


def scatter_all(parts, cid, fast, pair=False):
    if fast:
        return scatter(parts, cid, pair)
    sums = [
        lax.psum_scatter(p, "group", scatter_dimension=0, tiled=True)[0].astype(F32) for p in parts
    ]
    if pair:
        low = [p.astype(BF) for p in sums]
        sums = [p.astype(F32) + swap(p).astype(F32) for p in low]
    return sums


def other_half(x, dim, rank):
    half = x.shape[dim] // 2
    return lax.dynamic_slice_in_dim(x, (1 - rank) * half, half, dim)


def own_half(x, dim, rank):
    half = x.shape[dim] // 2
    return lax.dynamic_slice_in_dim(x, rank * half, half, dim)


def spare_blocks(ff, main, spare):
    group_count = lax.axis_size("group")
    rows = ff[0].shape[0]
    ends = [w[:, main * group_count :].reshape(rows, group_count, spare) for w in ff]
    gap = jnp.zeros((rows, group_count, 128 - 2 * spare), BF)
    gap_down = jnp.zeros((rows, group_count, 128 - spare), BF)
    return jnp.transpose(
        jnp.concatenate([ends[0], ends[1], gap, ends[2], gap_down], axis=2), (1, 0, 2)
    )


def columns_plain(ff, main, spare):
    group_count = lax.axis_size("group")
    replica_rank = lax.axis_index("replica")
    rows = ff[0].shape[0]
    mains = [w[:, : main * group_count].reshape(rows, group_count, main) for w in ff]
    blocks = jnp.concatenate(
        [jnp.transpose(m, (1, 0, 2)) for m in mains] + [spare_blocks(ff, main, spare)], axis=2
    )
    own_part = lax.all_to_all(own_half(blocks, 1, replica_rank), "group", 0, 0, tiled=True)
    other_part = swap(own_part)
    first = jnp.where(replica_rank == 0, own_part, other_part)
    second = jnp.where(replica_rank == 0, other_part, own_part)
    return jnp.concatenate((first, second), axis=1).reshape(rows * group_count, 3 * main + 256)


def mlp_plain(normed_two, grad_all, columns, main, spare, own_rows):
    group_count = lax.axis_size("group")
    replica_rank = lax.axis_index("replica")
    tokens, model_width = normed_two.shape
    share = main + spare
    rest = 3 * main
    gate_up_w = jnp.concatenate(
        (
            columns[:, :main],
            columns[:, rest : rest + spare],
            columns[:, main : 2 * main],
            columns[:, rest + spare : rest + 2 * spare],
        ),
        axis=1,
    )
    down_w = jnp.concatenate(
        (columns[:, 2 * main : rest], columns[:, rest + 128 : rest + 128 + spare]), axis=1
    )

    normed_all = lax.all_gather(normed_two, "group", axis=0)
    normed_all = normed_all.reshape(group_count * tokens, model_width)

    pre = matmul(normed_all, gate_up_w)
    gate_pre = pre[:, :share]
    up_pre = pre[:, share:]
    sigmoid_gate = jax.nn.sigmoid(gate_pre)
    silu_gate = gate_pre * sigmoid_gate
    hidden = (silu_gate * up_pre).astype(BF)
    grad_hidden = matmul(grad_all, down_w)
    grad_gate = (
        grad_hidden * up_pre * (sigmoid_gate * (1.0 + gate_pre * (1.0 - sigmoid_gate)))
    ).astype(BF)
    grad_up = (grad_hidden * silu_gate).astype(BF)
    gate_up_grad = jnp.concatenate((grad_gate, grad_up), axis=1)
    sums = [
        p.astype(BF).reshape(group_count, tokens, model_width)
        for p in (matmul_nt(gate_up_grad, gate_up_w), matmul_nt(hidden, down_w))
    ]
    grad_normed_two, mlp_out = scatter_all(sums, 4, False)
    down_term = matmul_tn(grad_all, hidden).astype(BF)
    gate_up_term = matmul_tn(normed_all, gate_up_grad).astype(BF)
    zeros = jnp.zeros((model_width, 128), BF)
    terms = jnp.concatenate(
        (
            gate_up_term[:, :main],
            gate_up_term[:, share : share + main],
            down_term[:, :main],
            gate_up_term[:, main:share],
            gate_up_term[:, share + main :],
            zeros[:, : 128 - 2 * spare],
            down_term[:, main:],
            zeros[:, : 128 - spare],
        ),
        axis=1,
    ).reshape(group_count, own_rows, 3 * main + 256)
    half_sum = own_half(terms, 1, replica_rank).astype(F32) + swap(
        other_half(terms, 1, replica_rank)
    ).astype(F32)
    return (grad_normed_two, mlp_out, half_sum.astype(BF))


def shards(
    hidden_in,
    lengths,
    gain_attn,
    w_query,
    b_query,
    w_key,
    b_key,
    w_value,
    b_value,
    w_out,
    gain_mlp,
    w_gate,
    w_up,
    w_down,
    cotangent,
):
    group_count = lax.axis_size("group")
    group_rank = lax.axis_index("group")
    slot_count, block_len, model_width = hidden_in.shape
    kv_heads = KV_HEADS
    head_dim = HEAD_DIM
    kv_width = kv_heads * head_dim
    repeat = HEADS // kv_heads
    slot_span = block_len * group_count
    key_step = min(512, slot_span)
    score_scale = head_dim ** (-0.5)
    tokens = slot_count * block_len
    hidden_units = w_gate.shape[1]
    own_rows = w_gate.shape[0]
    share = hidden_units // group_count
    positions = group_rank * block_len + jnp.arange(block_len, dtype=jnp.int32)
    valid_rows = (positions[None, :] < lengths[:, None]).astype(F32).reshape(tokens, 1)
    cos_table, sin_table = rope_tables(positions, head_dim)
    cos_heads = cos_table[:, None, :]
    sin_heads = sin_table[:, None, :]
    rank_end = (group_rank + 1) * block_len
    row_pos = jnp.tile(positions, repeat)

    fast = group_count == 16
    replica_rank = lax.axis_index("replica")
    pieces = (gain_attn, b_query, b_key, b_value, gain_mlp)
    sizes = [p.shape[0] for p in pieces]
    offsets = [sum(sizes[:i]) for i in range(len(sizes) + 1)]
    small = jnp.zeros((16 * 128,), BF).at[: offsets[-1]].set(jnp.concatenate(pieces))
    main = (hidden_units // 128 // group_count) * 128
    spare = hidden_units // group_count - main
    ff = (w_gate, w_up, w_down)
    if fast:
        qkv_w, small, columns = weights(
            w_query, w_key, w_value, *ff, spare_blocks(ff, main, spare), small.reshape(16, 128), 1
        )
    else:
        qkv_w, small = gather_all(
            [jnp.concatenate((w_query, w_key, w_value), axis=1), small.reshape(16, 128)], 1, fast
        )
        columns = columns_plain(ff, main, spare)
    qkv_w = qkv_w.reshape(model_width, model_width + 2 * kv_width)
    small = small.reshape(group_count, 16 * 128)
    gain_one, query_b, key_b, value_b, gain_two = [
        small[:, offsets[i] : offsets[i + 1]].reshape(-1).astype(F32) for i in range(len(sizes))
    ]
    qkv_b = jnp.concatenate((query_b, key_b, value_b))

    grad_final = cotangent.reshape(tokens, model_width).astype(F32) * valid_rows

    inputs = hidden_in.reshape(tokens, model_width).astype(F32)
    normed_full, factor_one = normalize(inputs, gain_one)
    normed = normed_full.astype(BF)
    qkv = matmul(normed, qkv_w) + qkv_b
    query_rot = rotate(
        qkv[:, :model_width].reshape(slot_count, block_len, HEADS, head_dim), cos_heads, sin_heads
    ).astype(BF)
    key_rot = rotate(
        qkv[:, model_width : model_width + kv_width].reshape(
            slot_count, block_len, kv_heads, head_dim
        ),
        cos_heads,
        sin_heads,
    ).astype(BF)
    value_low = qkv[:, model_width + kv_width :].astype(BF)
    pair = jnp.concatenate(
        (key_rot.reshape(tokens, kv_width), value_low), axis=1
    )
    pair_all, grad_all, out_w = gather_all([pair, grad_final.astype(BF), w_out], 2, fast)
    out_w = out_w.reshape(model_width, model_width)
    grad_all = grad_all.reshape(group_count * tokens, model_width)
    pair_all = jnp.transpose(
        pair_all.reshape(group_count, slot_count, block_len, 2 * kv_width), (1, 0, 2, 3)
    ).reshape(slot_count, slot_span, 2, kv_heads, head_dim)
    key_all = pair_all[:, :, 0]
    value_all = pair_all[:, :, 1]
    query_groups = []
    slot_totals = []
    slot_attended = []
    attended_rows = []
    for s in range(slot_count):
        query_rows = arrange(query_rot[s], kv_heads)
        totals, numerator = attend_forward(
            query_rows, key_all[s], value_all[s], row_pos, lengths[s], rank_end, key_step, score_scale
        )
        attended = numerator / totals[..., None]
        query_groups.append(query_rows)
        slot_totals.append(totals)
        slot_attended.append(attended)
        attended_rows.append(restore(attended, block_len))
    attended_low = jnp.concatenate(attended_rows, axis=0).astype(BF)
    residual_mid = inputs + matmul(attended_low, out_w)
    normed_two_full, factor_two = normalize(residual_mid, gain_two)
    normed_two = normed_two_full.astype(BF)
    if fast:
        grad_normed_two, mlp_out, half_sum = mlp(
            normed_two, grad_all.reshape(group_count, tokens, model_width), columns, spare, 3
        )
    else:
        grad_normed_two, mlp_out, half_sum = mlp_plain(
            normed_two, grad_all, columns, main, spare, own_rows
        )
    rest = 3 * main
    half_back = lax.all_to_all(half_sum, "group", 0, 0, tiled=True)
    half_other = swap(half_back)
    first = jnp.where(replica_rank == 0, half_back, half_other)
    second = jnp.where(replica_rank == 0, half_other, half_back)
    back = jnp.transpose(jnp.concatenate((first, second), axis=1), (1, 0, 2))
    gate_sum, up_sum, down_sum = [
        jnp.concatenate(
            (
                back[:, :, i * main : (i + 1) * main].reshape(own_rows, group_count * main),
                back[:, :, at : at + spare].reshape(own_rows, group_count * spare),
            ),
            axis=1,
        ).astype(F32)
        for i, at in ((0, rest), (1, rest + spare), (2, rest + 128))
    ]

    final_rows = residual_mid + mlp_out
    layer_out = (final_rows * valid_rows).reshape(slot_count, block_len, model_width).astype(BF)
    grad_mid_norm, grad_gain_two = norm_back(residual_mid, factor_two, gain_two, grad_normed_two)
    grad_mid = grad_final + grad_mid_norm
    grad_branch = grad_mid.astype(BF)
    out_term = matmul_tn(attended_low, grad_branch)
    grad_attended = matmul_nt(grad_branch, out_w)
    grad_query_rows = []
    grad_pairs = []
    for s in range(slot_count):
        slot_grad = grad_attended[s * block_len : (s + 1) * block_len].reshape(
            block_len, HEADS, head_dim
        )
        grad_out = arrange(slot_grad, kv_heads)
        totals = slot_totals[s]
        grad_total = -jnp.sum(grad_out * slot_attended[s], axis=-1) / totals
        grad_numer = (grad_out / totals[..., None]).astype(BF)
        grad_query, grad_key, grad_value = attend_backward(
            query_groups[s],
            key_all[s],
            value_all[s],
            row_pos,
            lengths[s],
            rank_end,
            key_step,
            score_scale,
            grad_numer,
            grad_total,
        )
        query_back_rows = restore(grad_query * score_scale, block_len).reshape(
            block_len, HEADS, head_dim
        )
        grad_query_rows.append(
            rotate_back(query_back_rows, cos_heads, sin_heads).reshape(block_len, HEADS * head_dim)
        )
        grad_pairs.append(
            jnp.concatenate(
                (grad_key.reshape(slot_span, kv_width), grad_value.reshape(slot_span, kv_width)),
                axis=1,
            )
        )
    pair_grads = jnp.stack(grad_pairs).reshape(slot_count, group_count, block_len, 2 * kv_width)
    pair_grads = jnp.transpose(pair_grads, (1, 0, 2, 3)).astype(BF)
    (pair_sum,) = scatter_all(
        [pair_grads.reshape(group_count, tokens, 2 * kv_width)], 5, fast
    )
    pair_sum = pair_sum.reshape(slot_count, block_len, 2 * kv_width)
    grad_query_pre = jnp.concatenate(grad_query_rows, axis=0).astype(BF)
    key_sum = pair_sum[..., :kv_width].reshape(slot_count, block_len, kv_heads, head_dim)
    grad_key_pre = (
        rotate_back(key_sum * score_scale, cos_heads, sin_heads).astype(BF).reshape(tokens, kv_width)
    )
    grad_value_pre = pair_sum[..., kv_width:].astype(BF).reshape(tokens, kv_width)
    grad_qkv = jnp.concatenate((grad_query_pre, grad_key_pre, grad_value_pre), axis=1)
    grad_normed = matmul_nt(grad_qkv, qkv_w)
    grad_in_norm, grad_gain_one = norm_back(inputs, factor_one, gain_one, grad_normed)
    grad_input = (grad_mid + grad_in_norm).reshape(slot_count, block_len, model_width)
    qkv_term = matmul_tn(normed, grad_qkv)
    qkv_bias = jnp.sum(grad_qkv.astype(F32), axis=0)

    vectors = jnp.concatenate(
        [
            grad_gain_one.reshape(group_count, -1),
            qkv_bias[:model_width].reshape(group_count, -1),
            qkv_bias[model_width : model_width + kv_width].reshape(group_count, -1),
            qkv_bias[model_width + kv_width :].reshape(group_count, -1),
            grad_gain_two.reshape(group_count, -1),
        ],
        axis=1,
    )
    vectors = jnp.concatenate(
        (vectors, jnp.zeros((group_count, 16 * 128 - offsets[-1]), F32)), axis=1
    ).reshape(group_count, 16, 128)
    weight_sum, out_sum, vector_sum = scatter_all(
        [
            p.astype(BF).reshape(group_count, p.shape[0] // group_count, -1)
            for p in (qkv_term, out_term)
        ]
        + [vectors.astype(BF)],
        6,
        fast,
        pair=True,
    )
    vector_sum = vector_sum.reshape(-1)
    gain_one_sum, query_bias_sum, key_bias_sum, value_bias_sum, gain_two_sum = [
        vector_sum[offsets[i] : offsets[i + 1]] for i in range(len(sizes))
    ]
    ends = (0, model_width, model_width + kv_width, model_width + 2 * kv_width)
    query_sum, key_sum_w, value_sum_w = [weight_sum[:, ends[i] : ends[i + 1]] for i in range(3)]
    return (
        layer_out,
        grad_input,
        gain_one_sum,
        query_sum,
        query_bias_sum,
        key_sum_w,
        key_bias_sum,
        value_sum_w,
        value_bias_sum,
        out_sum,
        gain_two_sum,
        gate_sum,
        up_sum,
        down_sum,
    )


def solution(mesh):
    act = P("replica", "group", None)
    vec = P("group")
    mat = P("group", None)
    return jax.shard_map(
        shards,
        mesh=mesh,
        in_specs=(act, P("replica"), vec, mat, vec, mat, vec, mat, vec, mat, vec, mat, mat, mat, act),
        out_specs=(act, act, vec, mat, vec, mat, vec, mat, vec, mat, vec, mat, mat, mat),
        check_vma=False,
    )
```

```python
import functools

import jax
import jax.numpy as jnp
from jax import lax
from jax.experimental import pallas as pl
from jax.experimental.pallas import tpu as pltpu
from jax.sharding import PartitionSpec as P

MESH = pl.DeviceIdType.MESH
NZ = 4
MAIN = 512
D = 1536
COLS = 3 * MAIN + 256
HEADS = 12
KV_HEADS = 2
HEAD_DIM = 128
EPSILON = 1e-06
THETA = 1000000.0
BF = jnp.bfloat16
F32 = jnp.float32


def rope_tables(positions, head_dim):
    freqs = THETA ** (-jnp.arange(0, head_dim, 2).astype(F32) / head_dim)
    angles = positions.astype(F32)[:, None] * freqs[None, :]
    angles = jnp.concatenate((angles, angles), axis=-1)
    return (jnp.cos(angles), jnp.sin(angles))


def rotate(tensor, cos_table, sin_table):
    halfway = tensor.shape[-1] // 2
    turned = jnp.concatenate((-tensor[..., halfway:], tensor[..., :halfway]), axis=-1)
    return tensor * cos_table + turned * sin_table


def rotate_back(gradient, cos_table, sin_table):
    halfway = gradient.shape[-1] // 2
    scaled = gradient * sin_table
    turned = jnp.concatenate((scaled[..., halfway:], -scaled[..., :halfway]), axis=-1)
    return gradient * cos_table + turned


def normalize(row_values, gain_vec):
    factor = lax.rsqrt(jnp.mean(row_values * row_values, axis=-1, keepdims=True) + EPSILON)
    return (row_values * factor * gain_vec, factor)


def norm_back(row_values, factor, gain_vec, upstream):
    weighted = upstream * gain_vec
    inner_mean = jnp.mean(weighted * row_values, axis=-1, keepdims=True)
    grad_rows = factor * weighted - row_values * (factor * factor * factor) * inner_mean
    grad_gain = jnp.sum(upstream * row_values * factor, axis=0)
    return (grad_rows, grad_gain)


def matmul(a, b):
    return jnp.dot(a, b, preferred_element_type=F32)


def matmul_nt(a, b):
    return lax.dot_general(a, b, (((1,), (1,)), ((), ())), preferred_element_type=F32)


def matmul_tn(a, b):
    return lax.dot_general(a, b, (((0,), (0,)), ((), ())), preferred_element_type=F32)


def arrange(per_token, kv_heads):
    block_len, head_count, head_dim = per_token.shape
    repeat = head_count // kv_heads
    grouped = per_token.reshape(block_len, kv_heads, repeat, head_dim)
    return jnp.transpose(grouped, (1, 2, 0, 3)).reshape(kv_heads, repeat * block_len, head_dim)


def restore(per_group, block_len):
    kv_heads, row_count, head_dim = per_group.shape
    repeat = row_count // block_len
    grouped = per_group.reshape(kv_heads, repeat, block_len, head_dim)
    return jnp.transpose(grouped, (2, 0, 1, 3)).reshape(block_len, kv_heads * repeat * head_dim)


def masked_exp(query_rows, key_block, row_pos, first_key, length, score_scale):
    key_step = key_block.shape[0]
    raw_scores = jnp.einsum("grd,kgd->grk", query_rows, key_block, preferred_element_type=F32)
    key_pos = first_key + jnp.arange(key_step, dtype=jnp.int32)
    allowed = (key_pos[None, :] <= row_pos[:, None]) & (key_pos[None, :] < length)
    return jnp.where(allowed[None], jnp.exp(raw_scores * score_scale), 0.0)


def block_total(length, rank_end, key_step):
    key_limit = jnp.minimum(length, rank_end)
    return (key_limit + key_step - 1) // key_step


def attend_forward(query_rows, key_all, value_all, row_pos, length, rank_end, key_step, scale):
    kv_heads, row_count, head_dim = query_rows.shape

    def visit(block_index, state_tuple):
        totals, numerator = state_tuple
        first_key = block_index * key_step
        key_block = lax.dynamic_slice_in_dim(key_all, first_key, key_step, 0)
        value_block = lax.dynamic_slice_in_dim(value_all, first_key, key_step, 0)
        weights = masked_exp(query_rows, key_block, row_pos, first_key, length, scale)
        totals = totals + jnp.sum(weights, axis=-1)
        numerator = numerator + jnp.einsum(
            "grk,kgd->grd", weights.astype(BF), value_block, preferred_element_type=F32
        )
        return (totals, numerator)

    initial = (
        jnp.zeros((kv_heads, row_count), F32),
        jnp.zeros((kv_heads, row_count, head_dim), F32),
    )
    return lax.fori_loop(0, block_total(length, rank_end, key_step), visit, initial)


def attend_backward(
    query_rows, key_all, value_all, row_pos, length, rank_end, key_step, scale, grad_numer, grad_total
):
    kv_heads, row_count, head_dim = query_rows.shape

    def visit(block_index, state_tuple):
        grad_query, grad_key, grad_value = state_tuple
        first_key = block_index * key_step
        key_block = lax.dynamic_slice_in_dim(key_all, first_key, key_step, 0)
        value_block = lax.dynamic_slice_in_dim(value_all, first_key, key_step, 0)
        weights = masked_exp(query_rows, key_block, row_pos, first_key, length, scale)
        grad_prob = jnp.einsum("grd,kgd->grk", grad_numer, value_block, preferred_element_type=F32)
        grad_score = (weights * (grad_prob + grad_total[..., None])).astype(BF)
        grad_query = grad_query + jnp.einsum(
            "grk,kgd->grd", grad_score, key_block, preferred_element_type=F32
        )
        key_part = jnp.einsum("grk,grd->kgd", grad_score, query_rows, preferred_element_type=F32)
        value_part = jnp.einsum(
            "grk,grd->kgd", weights.astype(BF), grad_numer, preferred_element_type=F32
        )
        key_old = lax.dynamic_slice_in_dim(grad_key, first_key, key_step, 0)
        value_old = lax.dynamic_slice_in_dim(grad_value, first_key, key_step, 0)
        grad_key = lax.dynamic_update_slice_in_dim(grad_key, key_old + key_part, first_key, 0)
        grad_value = lax.dynamic_update_slice_in_dim(
            grad_value, value_old + value_part, first_key, 0
        )
        return (grad_query, grad_key, grad_value)

    initial = (
        jnp.zeros((kv_heads, row_count, head_dim), F32),
        jnp.zeros(key_all.shape, F32),
        jnp.zeros(value_all.shape, F32),
    )
    return lax.fori_loop(0, block_total(length, rank_end, key_step), visit, initial)


def gather_plain(x):
    return lax.all_gather(x, "group", axis=0, tiled=True)


def scatter_sum(x):
    return lax.psum_scatter(x, "group", scatter_dimension=0, tiled=True)


def shards_plain(
    hidden_in,
    lengths,
    gain_attn,
    w_query,
    b_query,
    w_key,
    b_key,
    w_value,
    b_value,
    w_out,
    gain_mlp,
    w_gate,
    w_up,
    w_down,
    cotangent,
):
    group_count = lax.axis_size("group")
    group_rank = lax.axis_index("group")
    slot_count, block_len, model_width = hidden_in.shape
    kv_heads = KV_HEADS
    head_dim = HEAD_DIM
    kv_width = kv_heads * head_dim
    repeat = HEADS // kv_heads
    slot_span = block_len * group_count
    key_step = min(512, slot_span)
    score_scale = head_dim ** (-0.5)
    tokens = slot_count * block_len
    hidden_units = w_gate.shape[1]
    own_rows = w_gate.shape[0]
    share = hidden_units // group_count
    positions = group_rank * block_len + jnp.arange(block_len, dtype=jnp.int32)
    valid_rows = (positions[None, :] < lengths[:, None]).astype(F32).reshape(tokens, 1)
    cos_table, sin_table = rope_tables(positions, head_dim)
    cos_heads = cos_table[:, None, :]
    sin_heads = sin_table[:, None, :]
    rank_end = (group_rank + 1) * block_len
    row_pos = jnp.tile(positions, repeat)

    pieces = (gain_attn, b_query, b_key, b_value, gain_mlp)
    sizes = [p.shape[0] for p in pieces]
    small = gather_plain(jnp.concatenate(pieces)[None])
    offsets = [sum(sizes[:i]) for i in range(len(sizes) + 1)]
    gain_one, query_b, key_b, value_b, gain_two = [
        small[:, offsets[i] : offsets[i + 1]].reshape(-1).astype(F32) for i in range(len(sizes))
    ]
    qkv_w = gather_plain(jnp.concatenate((w_query, w_key, w_value), axis=1))
    out_w = gather_plain(w_out)
    qkv_b = jnp.concatenate((query_b, key_b, value_b))

    stacked = jnp.stack((w_gate, w_up, w_down)).reshape(3, own_rows, group_count, share)
    stacked = jnp.transpose(stacked, (2, 1, 0, 3)).reshape(group_count, own_rows, 3 * share)
    columns = lax.all_to_all(stacked, "group", 0, 0, tiled=True).reshape(model_width, 3 * share)
    gate_up_w = columns[:, : 2 * share]
    down_w = columns[:, 2 * share :]

    grad_final = cotangent.reshape(tokens, model_width).astype(F32) * valid_rows
    grad_all = gather_plain(grad_final.astype(BF))

    inputs = hidden_in.reshape(tokens, model_width).astype(F32)
    normed_full, factor_one = normalize(inputs, gain_one)
    normed = normed_full.astype(BF)
    qkv = matmul(normed, qkv_w) + qkv_b
    query_rot = rotate(
        qkv[:, :model_width].reshape(slot_count, block_len, HEADS, head_dim), cos_heads, sin_heads
    ).astype(BF)
    key_rot = rotate(
        qkv[:, model_width : model_width + kv_width].reshape(
            slot_count, block_len, kv_heads, head_dim
        ),
        cos_heads,
        sin_heads,
    ).astype(BF)
    value_low = qkv[:, model_width + kv_width :].astype(BF)
    pair = jnp.concatenate(
        (key_rot.reshape(tokens, kv_width), value_low), axis=1
    ).reshape(1, slot_count, block_len, 2 * kv_width)
    pair_all = jnp.transpose(gather_plain(pair), (1, 0, 2, 3)).reshape(
        slot_count, slot_span, 2, kv_heads, head_dim
    )
    key_all = pair_all[:, :, 0]
    value_all = pair_all[:, :, 1]
    query_groups = []
    slot_totals = []
    slot_attended = []
    attended_rows = []
    for s in range(slot_count):
        query_rows = arrange(query_rot[s], kv_heads)
        totals, numerator = attend_forward(
            query_rows, key_all[s], value_all[s], row_pos, lengths[s], rank_end, key_step, score_scale
        )
        attended = numerator / totals[..., None]
        query_groups.append(query_rows)
        slot_totals.append(totals)
        slot_attended.append(attended)
        attended_rows.append(restore(attended, block_len))
    attended_low = jnp.concatenate(attended_rows, axis=0).astype(BF)
    residual_mid = inputs + matmul(attended_low, out_w)
    normed_two_full, factor_two = normalize(residual_mid, gain_two)
    normed_all = gather_plain(normed_two_full.astype(BF))

    pre = matmul(normed_all, gate_up_w)
    gate_pre = pre[:, :share]
    up_pre = pre[:, share:]
    sigmoid_gate = jax.nn.sigmoid(gate_pre)
    silu_gate = gate_pre * sigmoid_gate
    hidden = (silu_gate * up_pre).astype(BF)
    grad_hidden = matmul(grad_all, down_w)
    grad_gate = (
        grad_hidden * up_pre * (sigmoid_gate * (1.0 + gate_pre * (1.0 - sigmoid_gate)))
    ).astype(BF)
    grad_up = (grad_hidden * silu_gate).astype(BF)
    gate_up_grad = jnp.concatenate((grad_gate, grad_up), axis=1)
    grad_normed_two = scatter_sum(matmul_nt(gate_up_grad, gate_up_w).astype(BF)).astype(F32)
    mlp_out = scatter_sum(matmul_nt(hidden, down_w).astype(BF)).astype(F32)
    down_term = matmul_tn(grad_all, hidden)
    gate_up_term = matmul_tn(normed_all, gate_up_grad)
    terms = jnp.concatenate((gate_up_term, down_term), axis=1).astype(BF)
    back = lax.all_to_all(
        terms.reshape(group_count, own_rows, 3 * share), "group", 0, 0, tiled=True
    )
    summed = back.astype(F32) + lax.ppermute(back, "replica", [(0, 1), (1, 0)]).astype(F32)
    summed = jnp.transpose(summed.reshape(group_count, own_rows, 3, share), (2, 1, 0, 3))
    gate_sum, up_sum, down_sum = summed.reshape(3, own_rows, hidden_units)

    final_rows = residual_mid + mlp_out
    layer_out = (final_rows * valid_rows).reshape(slot_count, block_len, model_width).astype(BF)
    grad_mid_norm, grad_gain_two = norm_back(residual_mid, factor_two, gain_two, grad_normed_two)
    grad_mid = grad_final + grad_mid_norm
    grad_branch = grad_mid.astype(BF)
    out_term = matmul_tn(attended_low, grad_branch)
    grad_attended = matmul_nt(grad_branch, out_w)
    grad_query_rows = []
    grad_pairs = []
    for s in range(slot_count):
        slot_grad = grad_attended[s * block_len : (s + 1) * block_len].reshape(
            block_len, HEADS, head_dim
        )
        grad_out = arrange(slot_grad, kv_heads)
        totals = slot_totals[s]
        grad_total = -jnp.sum(grad_out * slot_attended[s], axis=-1) / totals
        grad_numer = (grad_out / totals[..., None]).astype(BF)
        grad_query, grad_key, grad_value = attend_backward(
            query_groups[s],
            key_all[s],
            value_all[s],
            row_pos,
            lengths[s],
            rank_end,
            key_step,
            score_scale,
            grad_numer,
            grad_total,
        )
        query_back_rows = restore(grad_query * score_scale, block_len).reshape(
            block_len, HEADS, head_dim
        )
        grad_query_rows.append(
            rotate_back(query_back_rows, cos_heads, sin_heads).reshape(block_len, HEADS * head_dim)
        )
        grad_pairs.append(
            jnp.concatenate(
                (grad_key.reshape(slot_span, kv_width), grad_value.reshape(slot_span, kv_width)),
                axis=1,
            )
        )
    pair_grads = jnp.stack(grad_pairs).reshape(slot_count, group_count, block_len, 2 * kv_width)
    pair_grads = jnp.transpose(pair_grads, (1, 0, 2, 3)).astype(BF)
    pair_sum = scatter_sum(pair_grads).reshape(slot_count, block_len, 2 * kv_width).astype(F32)
    grad_query_pre = jnp.concatenate(grad_query_rows, axis=0).astype(BF)
    key_sum = pair_sum[..., :kv_width].reshape(slot_count, block_len, kv_heads, head_dim)
    grad_key_pre = (
        rotate_back(key_sum * score_scale, cos_heads, sin_heads).astype(BF).reshape(tokens, kv_width)
    )
    grad_value_pre = pair_sum[..., kv_width:].astype(BF).reshape(tokens, kv_width)
    grad_qkv = jnp.concatenate((grad_query_pre, grad_key_pre, grad_value_pre), axis=1)
    grad_normed = matmul_nt(grad_qkv, qkv_w)
    grad_in_norm, grad_gain_one = norm_back(inputs, factor_one, gain_one, grad_normed)
    grad_input = (grad_mid + grad_in_norm).reshape(slot_count, block_len, model_width)
    qkv_term = matmul_tn(normed, grad_qkv)
    qkv_bias = jnp.sum(grad_qkv.astype(F32), axis=0)

    weight_share = scatter_sum(
        jnp.concatenate((qkv_term, out_term), axis=1).astype(BF)
    )
    weight_sum = weight_share.astype(F32) + lax.ppermute(
        weight_share, "replica", [(0, 1), (1, 0)]
    ).astype(F32)
    vectors = jnp.concatenate(
        [
            grad_gain_one.reshape(group_count, -1),
            qkv_bias[:model_width].reshape(group_count, -1),
            qkv_bias[model_width : model_width + kv_width].reshape(group_count, -1),
            qkv_bias[model_width + kv_width :].reshape(group_count, -1),
            grad_gain_two.reshape(group_count, -1),
        ],
        axis=1,
    )
    vector_sum = lax.psum(scatter_sum(vectors), "replica").reshape(-1)
    gain_one_sum, query_bias_sum, key_bias_sum, value_bias_sum, gain_two_sum = [
        vector_sum[offsets[i] : offsets[i + 1]] for i in range(len(sizes))
    ]
    ends = (0, model_width, model_width + kv_width, model_width + 2 * kv_width)
    query_sum, key_sum_w, value_sum_w = [weight_sum[:, ends[i] : ends[i + 1]] for i in range(3)]
    out_sum = weight_sum[:, ends[3] :]
    return (
        layer_out,
        grad_input,
        gain_one_sum,
        query_sum,
        query_bias_sum,
        key_sum_w,
        key_bias_sum,
        value_sum_w,
        value_bias_sum,
        out_sum,
        gain_two_sum,
        gate_sum,
        up_sum,
        down_sum,
    )


def place():
    g = lax.axis_index("group")
    r = lax.axis_index("replica")
    return r, g // 4, lax.rem(g // 2, 2), lax.rem(g, 2)

def idx(z, x, c):
    return (z * 2 + x) * 2 + c

def greet(r, z, x, c, with_y=False):
    bar = pltpu.get_barrier_semaphore()
    def hail(dev):
        pl.semaphore_signal(bar, inc=1, device_id=dev, device_id_type=MESH)
    hail((r, idx(z, 1 - x, c)))
    hail((r, idx(z, x, 1 - c)))
    if with_y:
        hail((1 - r, idx(z, x, c)))
    @pl.when(z > 0)
    def _():
        hail((r, idx(z - 1, x, c)))
    @pl.when(z < NZ - 1)
    def _():
        hail((r, idx(z + 1, x, c)))
    ends = jnp.where((z > 0) & (z < NZ - 1), 1, 0)
    pl.semaphore_wait(bar, (4 if with_y else 3) + ends)

def planes(z):
    return (
        z,
        jnp.where(z == 0, 1, jnp.where(z == 1, 0, jnp.where(z == 2, 3, 2))),
        jnp.where(z == 0, 2, jnp.where(z == 1, 2, 1)),
        jnp.where(z < 2, 3, 0),
    )

def when(cond, fn):
    pl.when(cond)(fn)

class Gather:
    def __init__(self, at, src, out, send, recv, local):
        self.r, self.z, self.x, self.c = at
        self.src, self.out, self.send, self.recv, self.local = src, out, send, recv, local
        self.mid = (self.z > 0) & (self.z < NZ - 1)
        self.p = planes(self.z)
    def put(self, src, b, k, dev):
        pltpu.make_async_remote_copy(src, self.out.at[b], self.send.at[k], self.recv.at[b], device_id=dev, device_id_type=MESH).start()
    def sent(self, k):
        b = 0
        pltpu.make_async_remote_copy(self.out.at[b], self.out.at[b], self.send.at[k], self.recv.at[b], device_id=(self.r, 0), device_id_type=MESH).wait_send()
    def got(self, b):
        pltpu.make_async_remote_copy(self.out.at[b], self.out.at[b], self.send.at[0], self.recv.at[b], device_id=(self.r, 0), device_id_type=MESH).wait_recv()
    def zdev(self, s): return (self.r, idx(self.z + s, self.x, self.c))
    def xdev(self): return (self.r, idx(self.z, 1 - self.x, self.c))
    def cdev(self): return (self.r, idx(self.z, self.x, 1 - self.c))
    def begin(self):
        z, x, c = self.z, self.x, self.c
        me = idx(z, x, c)
        for s in (1, -1):
            when(self.inside(z + s), lambda s=s: self.put(self.src, me, 0 if s == 1 else 3, self.zdev(s)))
        self.put(self.src, me, 6 + z, self.xdev())
        self.put(self.src, me, 10 + 2 * z + x, self.cdev())
        pltpu.make_async_copy(self.src, self.out.at[me], self.local).start()
    def inside(self, z): return (z >= 0) & (z < NZ)
    def from_z(self, zz):
        z, x, c = self.z, self.x, self.c
        b = idx(zz, x, c)
        self.got(b)
        s = jnp.where(zz < z, 1, -1)
        d = jnp.abs(zz - z)
        slot = jnp.where(zz < z, 0, 3) + d
        when(self.inside(z + s), lambda: self.put(self.out.at[b], b, slot, (self.r, idx(z + s, x, c))))
        self.put(self.out.at[b], b, 6 + zz, self.xdev())
        self.put(self.out.at[b], b, 10 + 2 * zz + x, self.cdev())
    def first(self):
        self.from_z(self.p[1])
        when(self.mid, lambda: self.from_z(self.p[2]))
        self.from_x(self.p[0])
    def second(self):
        self.from_z(jnp.where(self.mid, self.p[3], self.p[2]))
        self.from_x(self.p[1])
    def third(self):
        when(~self.mid, lambda: self.from_z(self.p[3]))
        self.from_x(self.p[2])
    def fourth(self):
        self.from_x(self.p[3])
    def from_x(self, zz):
        b = idx(zz, 1 - self.x, self.c)
        self.got(b)
        self.put(self.out.at[b], b, 10 + 2 * zz + 1 - self.x, self.cdev())
    def from_c(self, zz):
        self.got(idx(zz, self.x, 1 - self.c))
        self.got(idx(zz, 1 - self.x, 1 - self.c))
    def end(self, local=True):
        z = self.z
        for d in range(NZ - 1):
            when((z - d >= 0) & (z < NZ - 1), lambda d=d: self.sent(d))
            when((z + d < NZ) & (z > 0), lambda d=d: self.sent(3 + d))
        for k in range(6, 18):
            self.sent(k)
        if local:
            pltpu.make_async_copy(self.src, self.out.at[0], self.local).wait()

def gather_kernel(n, *refs):
    srcs, outs = refs[:n], refs[n:2*n]
    send, recv, local = refs[2*n:]
    at = place()
    greet(*at)
    eng = [Gather(at, srcs[i], outs[i], send.at[i], recv.at[i], local.at[i]) for i in range(n)]
    for e in eng: e.begin()
    for e in eng: e.first()
    for e in eng: e.second()
    for e in eng: e.third()
    for e in eng: e.fourth()
    for d in range(NZ):
        for e in eng: e.from_c(d)
    for e in eng: e.end()

def gather(arrays, cid):
    n = len(arrays)
    return pl.pallas_call(
        functools.partial(gather_kernel, n),
        out_shape=[jax.ShapeDtypeStruct((16,) + a.shape, a.dtype) for a in arrays],
        in_specs=[pl.BlockSpec(memory_space=pl.ANY)] * n,
        out_specs=[pl.BlockSpec(memory_space=pl.ANY)] * n,
        scratch_shapes=[pltpu.SemaphoreType.DMA((n, 18)), pltpu.SemaphoreType.DMA((n, 16)), pltpu.SemaphoreType.DMA((n,))],
        compiler_params=pltpu.CompilerParams(collective_id=cid, has_side_effects=True),
    )(*arrays)

class Scatter:
    def __init__(self, at, part, rc, rx, rz, send, rcs, rxs, rzs):
        self.r, self.z, self.x, self.c = at
        self.part, self.rc, self.rx, self.rz = part, rc, rx, rz
        self.send, self.rcs, self.rxs, self.rzs = send, rcs, rxs, rzs
    def inside(self, z): return (z >= 0) & (z < NZ)
    def copy(self, src, dst, k, rs, dev):
        return pltpu.make_async_remote_copy(src, dst, self.send.at[k], rs, device_id=dev, device_id_type=MESH)
    def over(self, d):
        return [(s, self.z + s * d) for s in ((-1, 1) if d else (1,))]
    def begin(self, far_first=True):
        z, x, c = self.z, self.x, self.c
        dev = (self.r, idx(z, x, 1 - c))
        for xx in (1 - x, x):
            for d in range(NZ - 1, -1, -1):
                for s, zz in self.over(d):
                    k = 2 * zz + xx
                    when(self.inside(zz), lambda zz=zz, k=k, xx=xx: self.copy(self.part.at[idx(zz, xx, 1 - c)], self.rc.at[k], k, self.rcs.at[k], dev).start())
    def send_c(self, zz):
        z, x, c = self.z, self.x, self.c
        dev = (self.r, idx(z, x, 1 - c))
        for xx in (1 - x, x):
            k = 2 * zz + xx
            self.copy(self.part.at[idx(zz, xx, 1 - c)], self.rc.at[k], k, self.rcs.at[k], dev).start()
    def step_x(self, d):
        z, x, c = self.z, self.x, self.c
        dev = (self.r, idx(z, 1 - x, c))
        for s, zz in self.over(d):
            def go(zz=zz):
                k = 2 * zz + 1 - x
                b = idx(zz, 1 - x, c)
                self.copy(self.rc.at[k], self.rc.at[k], 0, self.rcs.at[k], dev).wait_recv()
                self.part[b] = (self.part[b].astype(F32) + self.rc[k].astype(F32)).astype(BF)
                self.copy(self.part.at[b], self.rx.at[zz], 8 + zz, self.rxs.at[zz], dev).start()
            when(self.inside(zz), go)
    def step_z(self, d):
        z, x, c = self.z, self.x, self.c
        for s, zz in self.over(d):
            def go(zz=zz, s=s):
                k = 2 * zz + x
                b = idx(zz, x, c)
                self.copy(self.rc.at[k], self.rc.at[k], 0, self.rcs.at[k], (self.r, 0)).wait_recv()
                self.copy(self.rx.at[zz], self.rx.at[zz], 0, self.rxs.at[zz], (self.r, 0)).wait_recv()
                both = self.part[b].astype(F32) + self.rc[k].astype(F32) + self.rx[zz].astype(F32)
                dev = (self.r, idx(z + s, x, c))
                slot = jnp.where(zz == z + s, NZ, zz) if s == -1 else zz
                self.part[b] = both.astype(BF)
                def more():
                    self.copy(self.rz.at[zz], self.rz.at[zz], 0, self.rzs.at[zz], dev).wait_recv()
                    self.part[b] = (self.part[b].astype(F32) + self.rz[zz].astype(F32)).astype(BF)
                when(self.inside(z - s), more)
                self.copy(self.part.at[b], self.rz.at[slot], 12 + zz, self.rzs.at[slot], dev).start()
            when(self.inside(zz), go)
    def finish(self, out):
        z, x, c = self.z, self.x, self.c
        k = 2 * z + x
        b = idx(z, x, c)
        self.copy(self.rc.at[k], self.rc.at[k], 0, self.rcs.at[k], (self.r, 0)).wait_recv()
        self.copy(self.rx.at[z], self.rx.at[z], 0, self.rxs.at[z], (self.r, 0)).wait_recv()
        out[...] = self.part[b].astype(F32) + self.rc[k].astype(F32) + self.rx[z].astype(F32)
        def lo():
            self.copy(self.rz.at[z], self.rz.at[z], 0, self.rzs.at[z], (self.r, 0)).wait_recv()
            out[...] += self.rz[z].astype(F32)
        when(z > 0, lo)
        def hi():
            self.copy(self.rz.at[NZ], self.rz.at[NZ], 0, self.rzs.at[NZ], (self.r, 0)).wait_recv()
            out[...] += self.rz[NZ].astype(F32)
        when(z < NZ - 1, hi)
        for k in range(8):
            self.copy(self.part.at[0], self.part.at[0], k, self.rcs.at[0], (self.r, 0)).wait_send()
        for k in range(8, 12):
            self.copy(self.part.at[0], self.part.at[0], k, self.rcs.at[0], (self.r, 0)).wait_send()
        for zz in range(NZ):
            when(z != zz, lambda zz=zz: self.copy(self.part.at[0], self.part.at[0], 12 + zz, self.rcs.at[0], (self.r, 0)).wait_send())

def scatter_steps(engines):
    for e in engines: e.begin()
    order = [("x", 3), ("x", 2), ("z", 3), ("x", 1), ("z", 2), ("x", 0), ("z", 1)]
    for kind, d in order:
        for e in engines:
            (e.step_x if kind == "x" else e.step_z)(d)

def scatter_kernel(n, pair, *refs):
    ps, os = refs[:n], refs[n:2*n]
    s = refs[2*n:]
    vm = [s[4*i:4*i+4] for i in range(n)]
    ysb = s[4*n:4*n+2*n] if pair else None
    send, rcs, rxs, rzs, lsem, ysem = s[4*n+(2*n if pair else 0):]
    at = place()
    for i in range(n):
        pltpu.make_async_copy(ps[i], vm[i][0], lsem.at[i]).start()
    greet(*at, with_y=pair)
    for i in range(n):
        pltpu.make_async_copy(ps[i], vm[i][0], lsem.at[i]).wait()
    engines = [Scatter(at, *vm[i], send.at[i], rcs.at[i], rxs.at[i], rzs.at[i]) for i in range(n)]
    scatter_steps(engines)
    r, z, x, c = at
    for i, e in enumerate(engines):
        e.finish(os[i])
        if pair:
            ysb[2*i][...] = os[i][...].astype(BF)
            pltpu.make_async_remote_copy(ysb[2*i], ysb[2*i+1], ysem.at[2*i], ysem.at[2*i+1], device_id=(1 - r, idx(z, x, c)), device_id_type=MESH).start()
    if pair:
        for i, e in enumerate(engines):
            pltpu.make_async_remote_copy(ysb[2*i], ysb[2*i+1], ysem.at[2*i], ysem.at[2*i+1], device_id=(1 - r, idx(z, x, c)), device_id_type=MESH).wait()
            os[i][...] = ysb[2*i][...].astype(F32) + ysb[2*i+1][...].astype(F32)

def scatter(parts, cid, pair=False):
    n = len(parts)
    scratch = []
    for p in parts:
        blk = p.shape[1:]
        scratch += [pltpu.VMEM((k,) + blk, BF) for k in (16, 8, 4, 5)]
    if pair:
        for p in parts:
            scratch += [pltpu.VMEM(p.shape[1:], BF)] * 2
    dma = pltpu.SemaphoreType.DMA
    return pl.pallas_call(
        functools.partial(scatter_kernel, n, pair),
        out_shape=[jax.ShapeDtypeStruct(p.shape[1:], F32) for p in parts],
        in_specs=[pl.BlockSpec(memory_space=pl.ANY)] * n,
        out_specs=[pl.BlockSpec(memory_space=pltpu.VMEM)] * n,
        scratch_shapes=scratch + [dma((n, 16)), dma((n, 8)), dma((n, 4)), dma((n, 5)), dma((n,)), dma((2 * n,))],
        compiler_params=pltpu.CompilerParams(collective_id=cid, has_side_effects=True, vmem_limit_bytes=60 * 2**20),
    )(*parts)


KS = (8, 1, 9, 2, 10, 3, 11, 4, 12, 5, 13, 6, 14, 7, 15)
WINDOW = 4

class Deal:
    def __init__(self, at, ws, rem, buf, send, recv, ysend, yrecv, local):
        self.r, self.z, self.x, self.c = at
        self.me = idx(self.z, self.x, self.c)
        self.ws, self.rem, self.buf = ws, rem, buf
        self.send, self.recv, self.ysend, self.yrecv, self.local = send, recv, ysend, yrecv, local
        self.half = ws[0].shape[0] // 2
    def rows(self, j, h):
        n = self.half
        return self.buf.at[pl.ds(pl.multiple_of((2 * j + h) * n, n), n)]
    def launch(self, k):
        r, me, n = self.r, self.me, self.half
        row = pl.ds(pl.multiple_of(r * n, n), n)
        j = jnp.bitwise_xor(me, k)
        dev = (r, j)
        dst = self.rows(me, r)
        col = pl.ds(pl.multiple_of(j * MAIN, MAIN), MAIN)
        for i in range(3):
            pltpu.make_async_remote_copy(self.ws[i].at[row, col], dst.at[:, pl.ds(i * MAIN, MAIN)], self.send.at[k], self.recv.at[k], device_id=dev, device_id_type=MESH).start()
        pltpu.make_async_remote_copy(self.rem.at[j, row], dst.at[:, pl.ds(3 * MAIN, 256)], self.send.at[k], self.recv.at[k], device_id=dev, device_id_type=MESH).start()
    def begin(self):
        me, n = self.me, self.half
        for k in KS[:WINDOW]:
            self.launch(k)
        col = pl.ds(pl.multiple_of(me * MAIN, MAIN), MAIN)
        own = self.buf.at[pl.ds(pl.multiple_of(2 * me * n, 2 * n), 2 * n)]
        for i in range(3):
            pltpu.make_async_copy(self.ws[i].at[:, col], own.at[:, pl.ds(i * MAIN, MAIN)], self.local).start()
        pltpu.make_async_copy(self.rem.at[me], own.at[:, pl.ds(3 * MAIN, 256)], self.local).start()
    def step(self, i):
        k = KS[i]
        r, me = self.r, self.me
        j = jnp.bitwise_xor(me, k)
        blk = self.rows(j, r)
        dev = (1 - r, me)
        pltpu.make_async_remote_copy(blk, blk, self.send.at[k], self.recv.at[k], device_id=dev, device_id_type=MESH).wait_recv()
        pltpu.make_async_remote_copy(blk, blk, self.ysend.at[k], self.yrecv.at[k], device_id=dev, device_id_type=MESH).start()
        if i + WINDOW < 15:
            self.launch(KS[i + WINDOW])
    def end(self):
        r, me = self.r, self.me
        dev = (1 - r, me)
        for k in range(1, 16):
            j = jnp.bitwise_xor(me, k)
            blk = self.rows(j, 1 - r)
            pltpu.make_async_remote_copy(blk, blk, self.ysend.at[k], self.yrecv.at[k], device_id=dev, device_id_type=MESH).wait()
            pltpu.make_async_remote_copy(blk, blk, self.send.at[k], self.recv.at[k], device_id=dev, device_id_type=MESH).wait_send()
        own = self.buf.at[pl.ds(pl.multiple_of(2 * me * self.half, 2 * self.half), 2 * self.half)]
        pltpu.make_async_copy(own, own, self.local).wait()

def hail_all(r, z, x, c):
    bar = pltpu.get_barrier_semaphore()
    me = idx(z, x, c)
    for k in range(1, 16):
        pl.semaphore_signal(bar, inc=1, device_id=(r, lax.rem(me + k, 16)), device_id_type=MESH)
    pl.semaphore_signal(bar, inc=1, device_id=(1 - r, me), device_id_type=MESH)
    pl.semaphore_wait(bar, 16)

def weights_kernel(wq, wk, wv, wg, wu, wd, rem, small, qkv_out, small_out, buf, qkv_own, gs, gr, gl, ss, sr, sl, ds, dr, ys, yr, dl, lsem):
    at = place()
    width = wq.shape[1]
    kw = wk.shape[1]
    loads = [pltpu.make_async_copy(w, qkv_own.at[:, pl.ds(o, n)], lsem.at[i]) for i, (w, o, n) in enumerate(((wq, 0, width), (wk, width, kw), (wv, width + kw, kw)))]
    for l in loads: l.start()
    hail_all(*at)
    for l in loads: l.wait()
    g = Gather(at, qkv_own, qkv_out, gs, gr, gl)
    v = Gather(at, small, small_out, ss, sr, sl)
    d = Deal(at, (wg, wu, wd), rem, buf, ds, dr, ys, yr, dl)
    g.begin()
    v.begin()
    d.begin()
    steps = iter(range(15))
    def some(n):
        for _ in range(n):
            i = next(steps, None)
            if i is not None:
                d.step(i)
    for phase, n in ((lambda e: e.first(), PACE[0]), (lambda e: e.second(), PACE[1]), (lambda e: e.third(), PACE[2]), (lambda e: e.fourth(), 15)):
        phase(g)
        phase(v)
        some(n)
    for e in (g, v):
        for zz in range(NZ):
            e.from_c(zz)
        e.end()
    d.end()

PACE = (2, 2, 3)

def weights(wq, wk, wv, wg, wu, wd, rem, small, cid):
    any_ = pl.BlockSpec(memory_space=pl.ANY)
    dma = pltpu.SemaphoreType.DMA
    rows = wq.shape[0]
    width = wq.shape[1] + 2 * wk.shape[1]
    return pl.pallas_call(
        weights_kernel,
        out_shape=[jax.ShapeDtypeStruct((16, rows, width), BF), jax.ShapeDtypeStruct((16,) + small.shape, BF), jax.ShapeDtypeStruct((16 * rows, 3 * MAIN + 256), BF)],
        in_specs=[any_] * 8,
        out_specs=[any_] * 3,
        scratch_shapes=[pltpu.VMEM((rows, width), BF), dma((18,)), dma((16,)), dma(()), dma((18,)), dma((16,)), dma(())] + [dma((16,))] * 4 + [dma(()), dma((3,))],
        compiler_params=pltpu.CompilerParams(collective_id=cid, has_side_effects=True),
    )(wq, wk, wv, wg, wu, wd, rem, small)


def dot(a, b):
    return lax.dot_general(a, b, (((1,), (0,)), ((), ())), preferred_element_type=F32)
def dot_nt(a, b):
    return lax.dot_general(a, b, (((1,), (1,)), ((), ())), preferred_element_type=F32)
def dot_tn(a, b):
    return lax.dot_general(a, b, (((0,), (0,)), ((), ())), preferred_element_type=F32)

def gated(g, u, gh):
    sig = jax.nn.sigmoid(g)
    silu = g * sig
    return (gh * u * (sig * (1.0 + g * (1.0 - sig)))).astype(BF), (gh * silu).astype(BF), (silu * u).astype(BF)

def mlp_kernel(spare, n2_ref, cot_ref, w_ref, gsum, osum, half_ref,
               n2, cot, w, act, pg, po, rcg, rxg, rzg, rco, rxo, rzo, yb,
               gsend, grecv, glocal, lsem, ssend, srcs, srxs, srzs, ysend, yrecv):
    at = place()
    r, z, x, c = at
    loads = [pltpu.make_async_copy(w_ref, w, lsem.at[0]), pltpu.make_async_copy(cot_ref, cot, lsem.at[1])]
    for l in loads: l.start()
    greet(*at, with_y=True)
    g = Gather(at, n2_ref, n2, gsend, grecv, glocal)
    rg = Scatter(at, pg, rcg, rxg, rzg, ssend.at[0], srcs.at[0], srxs.at[0], srzs.at[0])
    ro = Scatter(at, po, rco, rxo, rzo, ssend.at[1], srcs.at[1], srxs.at[1], srzs.at[1])
    g.begin()
    for l in loads: l.wait()
    mid = (z > 0) & (z < NZ - 1)
    p = [z,
         jnp.where(z == 0, 1, jnp.where(z == 1, 0, jnp.where(z == 2, 3, 2))),
         jnp.where(z == 0, 2, jnp.where(z == 1, 2, 1)),
         jnp.where(z < 2, 3, 0)]

    def tiles(zz):
        rows = pl.ds(pl.multiple_of(4 * zz, 4), 4)
        tok = pl.ds(pl.multiple_of(512 * zz, 512), 512)
        @pl.loop(0, 2)
        def _(t):
            a = n2[rows].reshape(512, D)
            k = cot[rows].reshape(512, D)
            def col(base):
                return pl.ds(pl.multiple_of(base + 256 * t, 256), 256)
            dg, du, h = gated(dot(a, w[:, col(0)]), dot(a, w[:, col(MAIN)]), dot(k, w[:, col(2 * MAIN)]))
            act[tok, col(0)] = dg
            act[tok, col(MAIN)] = du
            act[tok, col(2 * MAIN)] = h
        a = n2[rows].reshape(512, D)
        k = cot[rows].reshape(512, D)
        pre = dot(a, w[:, 3 * MAIN : 3 * MAIN + 128])
        gh = dot(k, w[:, 3 * MAIN + 128 :])
        lane = lax.broadcasted_iota(jnp.int32, (512, 128), 1)
        sig = jax.nn.sigmoid(pre)
        silu = pre * sig
        up = pltpu.roll(pre, 128 - spare, 1)
        dg = gh * up * (sig * (1.0 + pre * (1.0 - sig)))
        du = pltpu.roll(gh * silu, spare, 1)
        act[tok, 3 * MAIN : 3 * MAIN + 128] = jnp.where(lane < spare, dg, jnp.where(lane < 2 * spare, du, 0.0)).astype(BF)
        act[tok, 3 * MAIN + 128 :] = jnp.where(lane < spare, silu * up, 0.0).astype(BF)
        @pl.loop(0, D // 256)
        def _(t):
            dr = pl.ds(pl.multiple_of(256 * t, 256), 256)
            v = dot_nt(act[tok, : 2 * MAIN], w[dr, : 2 * MAIN]) + dot_nt(act[tok, 3 * MAIN : 3 * MAIN + 128], w[dr, 3 * MAIN : 3 * MAIN + 128])
            pg[rows, :, dr] = v.astype(BF).reshape(4, 128, 256)
            v = dot_nt(act[tok, 2 * MAIN : 3 * MAIN], w[dr, 2 * MAIN : 3 * MAIN]) + dot_nt(act[tok, 3 * MAIN + 128 :], w[dr, 3 * MAIN + 128 :])
            po[rows, :, dr] = v.astype(BF).reshape(4, 128, 256)
        rg.send_c(zz)
        ro.send_c(zz)

    g.from_z(p[1])
    when(mid, lambda: g.from_z(p[2]))
    g.from_x(p[0])
    g.from_c(p[0])
    pltpu.make_async_copy(n2_ref, n2.at[0], glocal).wait()
    tiles(p[0])
    g.from_z(jnp.where(mid, p[3], p[2]))
    g.from_x(p[1])
    g.from_c(p[1])
    tiles(p[1])
    when(~mid, lambda: g.from_z(p[3]))
    g.from_x(p[2])
    g.from_c(p[2])
    tiles(p[2])
    g.from_x(p[3])
    g.from_c(p[3])
    tiles(p[3])

    ydev = (1 - r, idx(z, x, c))
    own = D // 16
    half = own // 2
    def ycopy(j):
        src = w.at[pl.ds(pl.multiple_of(own * j + half * (1 - r), half), half)]
        return pltpu.make_async_remote_copy(src, yb.at[j], ysend.at[j], yrecv.at[j], device_id=ydev, device_id_type=MESH)
    def grads(q):
        dr = slice(384 * q, 384 * (q + 1))
        row = slice(384 * q, 384 * (q + 1))
        @pl.loop(0, 4)
        def _(t):
            col = pl.ds(pl.multiple_of(256 * t, 256), 256)
            w[row, col] = dot_tn(n2[:, :, dr].reshape(2048, 384), act[:, col]).astype(BF)
        @pl.loop(0, 2)
        def _(t):
            col = pl.ds(pl.multiple_of(2 * MAIN + 256 * t, 256), 256)
            w[row, col] = dot_tn(cot[:, :, dr].reshape(2048, 384), act[:, col]).astype(BF)
        w[row, 3 * MAIN : 3 * MAIN + 128] = dot_tn(n2[:, :, dr].reshape(2048, 384), act[:, 3 * MAIN : 3 * MAIN + 128]).astype(BF)
        w[row, 3 * MAIN + 128 :] = dot_tn(cot[:, :, dr].reshape(2048, 384), act[:, 3 * MAIN + 128 :]).astype(BF)
        for j in range(4 * q, 4 * q + 4):
            ycopy(j).start()
    def yadd(j):
        ycopy(j).wait()
        mine = w[pl.ds(pl.multiple_of(own * j + half * r, half), half)]
        yb[j] = (mine.astype(F32) + yb[j].astype(F32)).astype(BF)
        pltpu.make_async_copy(yb.at[j], half_ref.at[j], lsem.at[2]).start()

    rg.step_x(3)
    rg.step_x(2)
    grads(0)
    rg.step_z(3)
    rg.step_x(1)
    grads(1)
    rg.step_z(2)
    rg.step_x(0)
    grads(2)
    rg.step_z(1)
    ro.step_x(3)
    ro.step_x(2)
    grads(3)
    rg.finish(gsum)
    ro.step_z(3)
    ro.step_x(1)
    for j in range(0, 4): yadd(j)
    ro.step_z(2)
    ro.step_x(0)
    for j in range(4, 8): yadd(j)
    ro.step_z(1)
    for j in range(8, 12): yadd(j)
    ro.finish(osum)
    for j in range(12, 16): yadd(j)
    pltpu.make_async_copy(yb, half_ref, lsem.at[2]).wait()
    g.end(local=False)

def mlp(n2, cot, w, spare, cid):
    blk = n2.shape
    dma = pltpu.SemaphoreType.DMA
    full = (16,) + blk
    return pl.pallas_call(
        functools.partial(mlp_kernel, spare),
        out_shape=[jax.ShapeDtypeStruct(blk, F32)] * 2 + [jax.ShapeDtypeStruct((16, D // 32, COLS), BF)],
        in_specs=[pl.BlockSpec(memory_space=pl.ANY)] * 3,
        out_specs=[pl.BlockSpec(memory_space=pltpu.VMEM)] * 2 + [pl.BlockSpec(memory_space=pl.ANY)],
        scratch_shapes=[pltpu.VMEM(full, BF), pltpu.VMEM(full, BF), pltpu.VMEM((D, COLS), BF), pltpu.VMEM((16 * blk[0], COLS), BF),
                        pltpu.VMEM(full, BF), pltpu.VMEM(full, BF)]
        + [pltpu.VMEM((k,) + blk, BF) for k in (8, 4, 5, 8, 4, 5)]
        + [pltpu.VMEM((16, D // 32, COLS), BF)]
        + [dma((18,)), dma((16,)), dma(()), dma((3,)), dma((2, 16)), dma((2, 8)), dma((2, 4)), dma((2, 5)), dma((16,)), dma((16,))],
        compiler_params=pltpu.CompilerParams(collective_id=cid, has_side_effects=True, vmem_limit_bytes=60 * 2**20),
    )(n2, cot, w)


def spin(u, cos, sin):
    return u * cos + pltpu.roll(u, HEAD_DIM // 2, 1) * sin

def stack_heads(v):
    n = v.shape[1] // HEAD_DIM
    return jnp.concatenate([v[:, HEAD_DIM * i : HEAD_DIM * (i + 1)] for i in range(n)], axis=0)

def spread_heads(v, rows):
    n = v.shape[0] // rows
    return jnp.concatenate([v[rows * i : rows * (i + 1)] for i in range(n)], axis=1)

def exp_scores(q, k, first_row, block, length):
    sc = dot_nt(q, k) * (HEAD_DIM ** -0.5)
    key = lax.broadcasted_iota(jnp.int32, sc.shape, 1)
    row = jnp.bitwise_and(lax.broadcasted_iota(jnp.int32, sc.shape, 0), block - 1) + first_row
    return jnp.where((key <= row) & (key < length), jnp.exp(sc), 0.0)

def rms(v, gain):
    factor = lax.rsqrt(jnp.mean(v * v, axis=-1, keepdims=True) + EPSILON)
    return v * factor * gain

def attend_kernel(block, lens, x_ref, cot_ref, wqkv_ref, wo_ref, vec, cos_ref, sin_ref,
                  q_out, normed_out, att_out, mid_out, n2_out, kv_out, cot_out, wo_out,
                  wqkv, own, kv, wo, cs, cr, cl, ws, wr, wl, ks, kr, kl, lsem):
    at = place()
    width = HEADS * HEAD_DIM
    kw = KV_HEADS * HEAD_DIM
    load = pltpu.make_async_copy(wqkv_ref, wqkv, lsem.at[0])
    load.start()
    greet(*at)
    gc = Gather(at, cot_ref, cot_out, cs, cr, cl)
    gw = Gather(at, wo_ref, wo, ws, wr, wl)
    gk = Gather(at, own, kv, ks, kr, kl)
    gw.begin()
    gc.begin()
    x = x_ref[...].astype(F32)
    normed_out[...] = rms(x, vec[0:1, :width]).astype(BF)
    load.wait()
    cos, sin = cos_ref[...], sin_ref[...]
    def product(base):
        return dot(normed_out[...], wqkv[:, pl.ds(pl.multiple_of(base, 256), 256)]) + vec[1:2, pl.ds(pl.multiple_of(base, 256), 256)]
    pre = product(width)
    own[:, :HEAD_DIM] = spin(pre[:, :HEAD_DIM], cos, sin).astype(BF)
    own[:, HEAD_DIM : 2 * HEAD_DIM] = spin(pre[:, HEAD_DIM:], cos, sin).astype(BF)
    own[:, kw:] = product(width + kw).astype(BF)
    gk.begin()
    @pl.loop(0, width // 256)
    def _(t):
        pre = product(t * 256)
        for i in range(2):
            col = pl.ds(pl.multiple_of(256 * t + HEAD_DIM * i, HEAD_DIM), HEAD_DIM)
            q_out[:, col] = spin(pre[:, HEAD_DIM * i : HEAD_DIM * (i + 1)], cos, sin).astype(BF)
    gk.first()
    gw.first()
    gc.first()
    gk.second()
    gw.second()
    gc.second()
    gk.third()
    gk.fourth()
    gw.third()
    gc.third()
    for zz in range(NZ):
        gk.from_c(zz)
    gk.end()
    pltpu.make_async_copy(kv, kv_out, lsem.at[1]).start()
    first_row = lax.axis_index("group") * block
    span = 16 * block
    @pl.loop(0, 4)
    def _(u):
        s, h = u // 2, lax.rem(u, 2)
        rows = pl.ds(pl.multiple_of(block * s, block), block)
        cols = pl.ds(pl.multiple_of(width // 2 * h, width // 2), width // 2)
        q = stack_heads(q_out[rows, cols])
        k = kv[:, rows, pl.ds(pl.multiple_of(HEAD_DIM * h, HEAD_DIM), HEAD_DIM)].reshape(span, HEAD_DIM)
        v = kv[:, rows, pl.ds(pl.multiple_of(kw + HEAD_DIM * h, HEAD_DIM), HEAD_DIM)].reshape(span, HEAD_DIM)
        e = exp_scores(q, k, first_row, block, lens[s])
        total = jnp.sum(e, axis=-1, keepdims=True)
        att_out[rows, cols] = spread_heads(dot(e.astype(BF), v) / total, block)
    gw.fourth()
    gc.fourth()
    for zz in range(NZ):
        gw.from_c(zz)
    gw.end()
    out_copy = pltpu.make_async_copy(wo, wo_out, lsem.at[2])
    out_copy.start()
    @pl.loop(0, width // 256)
    def _(t):
        col = pl.ds(pl.multiple_of(256 * t, 256), 256)
        mid_out[:, col] = x_ref[:, col].astype(F32) + dot(att_out[...].astype(BF), wo[:, :, col].reshape(width, 256))
    n2_out[...] = rms(mid_out[...], vec[2:3, :width]).astype(BF)
    for zz in range(NZ):
        gc.from_c(zz)
    gc.end()
    pltpu.make_async_copy(kv, kv_out, lsem.at[1]).wait()
    out_copy.wait()

def attend(lens, x, cot, wqkv, wo, vec, cos, sin, block, cid):
    rows, width = x.shape
    any_ = pl.BlockSpec(memory_space=pl.ANY)
    vm = pl.BlockSpec(memory_space=pltpu.VMEM)
    dma = pltpu.SemaphoreType.DMA
    act = (rows, width)
    kvw = 2 * KV_HEADS * HEAD_DIM
    sds = jax.ShapeDtypeStruct
    return pl.pallas_call(
        functools.partial(attend_kernel, block),
        out_shape=[sds(act, BF), sds(act, BF), sds(act, F32), sds(act, F32), sds(act, BF), sds((16, rows, kvw), BF), sds((16,) + act, BF), sds((16,) + wo.shape, BF)],
        in_specs=[pl.BlockSpec(memory_space=pltpu.SMEM), vm, any_, any_, any_, vm, vm, vm],
        out_specs=[vm] * 5 + [any_] * 3,
        scratch_shapes=[pltpu.VMEM(wqkv.shape, BF), pltpu.VMEM((rows, kvw), BF), pltpu.VMEM((16, rows, kvw), BF), pltpu.VMEM((16,) + wo.shape, BF)]
        + [dma((18,)), dma((16,)), dma(())] * 3 + [dma((3,))],
        compiler_params=pltpu.CompilerParams(collective_id=cid, has_side_effects=True, vmem_limit_bytes=60 * 2**20),
    )(lens, x, cot, wqkv, wo, vec, cos, sin)


class Return:
    def __init__(self, at, half_ref, main, spare, send, recv, ysend, yrecv, local):
        self.r, self.z, self.x, self.c = at
        self.me = idx(self.z, self.x, self.c)
        self.src, self.main, self.spare = half_ref, main, spare
        self.send, self.recv, self.ysend, self.yrecv, self.local = send, recv, ysend, yrecv, local
        self.n = half_ref.shape[1]
    def places(self, j, h):
        row = pl.ds(pl.multiple_of(h * self.n, self.n), self.n)
        col = pl.ds(pl.multiple_of(j * MAIN, MAIN), MAIN)
        return [self.main.at[i, row, col] for i in range(3)] + [self.spare.at[j, row]]
    def parts(self, j):
        return [self.src.at[j, :, pl.ds(i * MAIN, MAIN)] for i in range(3)] + [self.src.at[j, :, pl.ds(3 * MAIN, 256)]]
    def launch(self, k):
        j = jnp.bitwise_xor(self.me, k)
        for a, b in zip(self.parts(j), self.places(self.me, self.r)):
            pltpu.make_async_remote_copy(a, b, self.send.at[k], self.recv.at[k], device_id=(self.r, j), device_id_type=MESH).start()
    def forward(self, j, k):
        for a in self.places(j, self.r):
            pltpu.make_async_remote_copy(a, a, self.ysend.at[k], self.yrecv.at[k], device_id=(1 - self.r, self.me), device_id_type=MESH).start()
    def begin(self, window):
        self.window = window
        for a, b in zip(self.parts(self.me), self.places(self.me, self.r)):
            pltpu.make_async_copy(a, b, self.local).start()
        for k in KS[:window]:
            self.launch(k)
    def whole(self, send, recv):
        blk = self.src.at[0]
        return pltpu.make_async_remote_copy(blk, blk, send, recv, device_id=(1 - self.r, self.me), device_id_type=MESH)
    def own(self):
        pltpu.make_async_copy(self.src.at[0], self.src.at[0], self.local).wait()
        self.forward(self.me, 0)
    def step(self, i):
        k = KS[i]
        self.whole(self.send.at[k], self.recv.at[k]).wait_recv()
        self.forward(jnp.bitwise_xor(self.me, k), k)
        if i + self.window < 15:
            self.launch(KS[i + self.window])
    def end(self):
        for k in (0,) + KS:
            self.whole(self.ysend.at[k], self.yrecv.at[k]).wait()
            if k:
                self.whole(self.send.at[k], self.recv.at[k]).wait_send()

def norm_gradient(v, gain, upstream):
    factor = lax.rsqrt(jnp.mean(v * v, axis=-1, keepdims=True) + EPSILON)
    weighted = upstream * gain
    inner = jnp.mean(weighted * v, axis=-1, keepdims=True)
    return factor * weighted - v * (factor * factor * factor) * inner, jnp.sum(upstream * v * factor, axis=0, keepdims=True)

def backward_kernel(block, window, lens, gn2, mlp_out, mid, cot, x_ref, att, q_ref, normed, vec, cos_ref, sin_ref, valid, sel, fold, selk, foldk, kv_ref, wo_ref, wqkv_ref, half_ref,
                    layer_out, grad_input, qkv_out, wo_out, vec_out, g_main, g_spare,
                    kv, wo, wqkv, gmid, branch, gatt, gqkv, pv,
                    p_kv, c_kv, x_kv, z_kv, p_wo, c_wo, x_wo, z_wo, p_qk, c_qk, x_qk, z_qk, p_ve, c_ve, x_ve, z_ve,
                    kvsum, y0, y1, y2, y3, y4, y5,
                    ss, sc, sx, sz, rs, rr, rys, ryr, rl, ysem, lsem):
    at = place()
    r, z, x, c = at
    width = HEADS * HEAD_DIM
    kw = KV_HEADS * HEAD_DIM
    loads = [pltpu.make_async_copy(a, b, lsem.at[i]) for i, (a, b) in enumerate(((wo_ref, wo), (kv_ref, kv), (wqkv_ref, wqkv)))]
    for l in loads: l.start()
    hail_all(*at)
    back = Return(at, half_ref, g_main, g_spare, rs, rr, rys, ryr, rl)
    back.begin(window)
    sets = ((p_kv, c_kv, x_kv, z_kv), (p_wo, c_wo, x_wo, z_wo), (p_qk, c_qk, x_qk, z_qk), (p_ve, c_ve, x_ve, z_ve))
    ek, eo, eq, ev = [Scatter(at, *b, ss.at[i], sc.at[i], sx.at[i], sz.at[i]) for i, b in enumerate(sets)]
    steps = iter(range(15))
    def some(n):
        for _ in range(n):
            i = next(steps, None)
            if i is not None:
                back.step(i)
    ydev = (1 - r, idx(z, x, c))
    def trade(i, out, a, b):
        a[...] = out[...].astype(BF)
        pltpu.make_async_remote_copy(a, b, ysem.at[2 * i], ysem.at[2 * i + 1], device_id=ydev, device_id_type=MESH).start()
    def traded(i, out, a, b):
        pltpu.make_async_remote_copy(a, b, ysem.at[2 * i], ysem.at[2 * i + 1], device_id=ydev, device_id_type=MESH).wait()
        out[...] = a[...].astype(F32) + b[...].astype(F32)

    grad_norm, gain_two = norm_gradient(mid[...], vec[2:3, :width], gn2[...])
    gmid[...] = cot[...].astype(F32) + grad_norm
    branch[...] = gmid[...].astype(BF)
    loads[0].wait()
    @pl.loop(0, 4)
    def _(t):
        blocks = pl.ds(pl.multiple_of(4 * t, 4), 4)
        col = pl.ds(pl.multiple_of(384 * t, 384), 384)
        low = att[:, col].astype(BF)
        p_wo[blocks] = dot_tn(low, branch[...]).astype(BF).reshape(4, 96, width)
        gatt[:, col] = dot_nt(branch[...], wo[blocks].reshape(384, width))
    eo.begin()
    eo.step_x(3)
    eo.step_x(2)
    back.own()
    layer_out[...] = ((mid[...] + mlp_out[...]) * valid[...]).astype(BF)
    loads[1].wait()
    first_row = lax.axis_index("group") * block
    span = 16 * block
    def unit(u):
        s, h = u // 2, lax.rem(u, 2)
        rows = pl.ds(pl.multiple_of(block * s, block), block)
        cols = pl.ds(pl.multiple_of(width // 2 * h, width // 2), width // 2)
        kcol = pl.ds(pl.multiple_of(HEAD_DIM * h, HEAD_DIM), HEAD_DIM)
        vcol = pl.ds(pl.multiple_of(kw + HEAD_DIM * h, HEAD_DIM), HEAD_DIM)
        q = stack_heads(q_ref[rows, cols])
        k = kv[:, rows, kcol].reshape(span, HEAD_DIM)
        v = kv[:, rows, vcol].reshape(span, HEAD_DIM)
        e = exp_scores(q, k, first_row, block, lens[s])
        total = jnp.sum(e, axis=-1, keepdims=True)
        ga = stack_heads(gatt[rows, cols])
        gt = -jnp.sum(ga * stack_heads(att[rows, cols]), axis=-1, keepdims=True) / total
        gn = (ga / total).astype(BF)
        gs = (e * (dot_nt(gn, v) + gt)).astype(BF)
        p_kv[:, rows, kcol] = dot_tn(gs, q).astype(BF).reshape(16, block, HEAD_DIM)
        p_kv[:, rows, vcol] = dot_tn(e.astype(BF), gn).astype(BF).reshape(16, block, HEAD_DIM)
        gq = dot(gs, k) * (HEAD_DIM ** -0.5)
        cos, sin = cos_ref[:block], sin_ref[:block]
        gqkv[rows, cols] = jnp.concatenate([spin(gq[block * i : block * (i + 1)], cos, -sin) for i in range(HEADS // KV_HEADS)], axis=1).astype(BF)
    unit(0)
    some(1)
    eo.step_z(3)
    eo.step_x(1)
    unit(1)
    some(1)
    eo.step_z(2)
    eo.step_x(0)
    unit(2)
    some(1)
    eo.step_z(1)
    unit(3)
    ek.begin()
    some(1)
    ek.step_x(3)
    ek.step_x(2)
    eo.finish(wo_out)
    trade(0, wo_out, y0, y1)
    some(1)
    ek.step_z(3)
    ek.step_x(1)
    some(1)
    ek.step_z(2)
    ek.step_x(0)
    some(1)
    ek.step_z(1)
    some(1)
    ek.finish(kvsum)
    cos, sin = cos_ref[...], sin_ref[...]
    for h in range(KV_HEADS):
        kcol = slice(HEAD_DIM * h, HEAD_DIM * (h + 1))
        gqkv[:, width + HEAD_DIM * h : width + HEAD_DIM * (h + 1)] = spin(kvsum[:, kcol] * (HEAD_DIM ** -0.5), cos, -sin).astype(BF)
    gqkv[:, width + kw :] = kvsum[:, kw:].astype(BF)
    loads[2].wait()
    @pl.loop(0, 4)
    def _(t):
        blocks = pl.ds(pl.multiple_of(4 * t, 4), 4)
        col = pl.ds(pl.multiple_of(384 * t, 384), 384)
        p_qk[blocks] = dot_tn(normed[:, col], gqkv[...]).astype(BF).reshape(4, 96, width + 2 * kw)
        gatt[:, col] = dot_nt(gqkv[...], wqkv[blocks].reshape(384, width + 2 * kw))
    eq.begin()
    eq.step_x(3)
    eq.step_x(2)
    grad_norm, gain_one = norm_gradient(x_ref[...].astype(F32), vec[0:1, :width], gatt[...])
    grad_input[...] = gmid[...] + grad_norm
    bias = jnp.sum(gqkv[...].astype(F32), axis=0, keepdims=True)
    pv[...] = jnp.zeros_like(pv)
    for i, (v, a, b) in enumerate(((gain_one, sel, fold), (bias[:, :width], sel, fold), (bias[:, width : width + kw], selk, foldk), (bias[:, width + kw :], selk, foldk), (gain_two, sel, fold))):
        pv[:, i, :] = dot((a[...] * v).astype(BF), b[...])
    p_ve[...] = pv[...].astype(BF)
    ev.begin()
    ev.step_x(3)
    ev.step_x(2)
    some(2)
    for kind, d in (("z", 3), ("x", 1), ("z", 2), ("x", 0), ("z", 1)):
        for e in (eq, ev):
            (e.step_x if kind == "x" else e.step_z)(d)
        some(1)
    some(15)
    eq.finish(qkv_out)
    trade(1, qkv_out, y2, y3)
    ev.finish(vec_out)
    trade(2, vec_out, y4, y5)
    traded(0, wo_out, y0, y1)
    traded(1, qkv_out, y2, y3)
    traded(2, vec_out, y4, y5)
    back.end()

def backward(lens, gn2, mlp_out, mid, cot, x, att, q, normed, vec, cos, sin, valid, sel, fold, selk, foldk, kv, wo, wqkv, half, block, cid, window=4):
    any_ = pl.BlockSpec(memory_space=pl.ANY)
    vm = pl.BlockSpec(memory_space=pltpu.VMEM)
    dma = pltpu.SemaphoreType.DMA
    sds = jax.ShapeDtypeStruct
    rows, width = x.shape
    wide = wqkv.shape[-1]
    own = wo.shape[1]
    kvw = kv.shape[-1]
    VM = pltpu.VMEM
    def four(blk):
        return [VM((k,) + blk, BF) for k in (16, 8, 4, 5)]
    return pl.pallas_call(
        functools.partial(backward_kernel, block, window),
        out_shape=[sds((rows, width), BF), sds((rows, width), F32), sds((own, wide), F32), sds((own, width), F32), sds((16, 128), F32), sds((3, own, 16 * MAIN), BF), sds((16, own, 256), BF)],
        in_specs=[pl.BlockSpec(memory_space=pltpu.SMEM)] + [vm] * 16 + [any_] * 4,
        out_specs=[vm] * 5 + [any_] * 2,
        scratch_shapes=[VM(kv.shape, BF), VM(wo.shape, BF), VM(wqkv.shape, BF), VM((rows, width), F32), VM((rows, width), BF), VM((rows, width), F32), VM((rows, wide), BF), VM((16, 16, 128), F32)]
        + four((rows, kvw)) + four((own, width)) + four((own, wide)) + four((16, 128))
        + [VM((rows, kvw), F32)] + [VM((own, width), BF)] * 2 + [VM((own, wide), BF)] * 2 + [VM((16, 128), BF)] * 2
        + [dma((4, 16)), dma((4, 8)), dma((4, 4)), dma((4, 5))] + [dma((16,))] * 4 + [dma(()), dma((6,)), dma((3,))],
        compiler_params=pltpu.CompilerParams(collective_id=cid, has_side_effects=True, vmem_limit_bytes=60 * 2**20),
    )(lens, gn2, mlp_out, mid, cot, x, att, q, normed, vec, cos, sin, valid, sel, fold, selk, foldk, kv, wo, wqkv, half)


def spare_blocks(ff, main, spare):
    group_count = lax.axis_size("group")
    rows = ff[0].shape[0]
    ends = [w[:, main * group_count :].reshape(rows, group_count, spare) for w in ff]
    gap = jnp.zeros((rows, group_count, 128 - 2 * spare), BF)
    gap_down = jnp.zeros((rows, group_count, 128 - spare), BF)
    return jnp.transpose(
        jnp.concatenate([ends[0], ends[1], gap, ends[2], gap_down], axis=2), (1, 0, 2)
    )


def folding(group_count, width):
    share = width // group_count
    at = jnp.arange(width)
    sel = (at[None, :] // share == jnp.arange(group_count)[:, None]).astype(F32)
    fold = (at[:, None] % share == jnp.arange(128)[None, :]).astype(BF)
    return sel, fold


def shards_fast(
    hidden_in,
    lengths,
    gain_attn,
    w_query,
    b_query,
    w_key,
    b_key,
    w_value,
    b_value,
    w_out,
    gain_mlp,
    w_gate,
    w_up,
    w_down,
    cotangent,
):
    group_count = lax.axis_size("group")
    group_rank = lax.axis_index("group")
    slot_count, block_len, model_width = hidden_in.shape
    kv_width = KV_HEADS * HEAD_DIM
    tokens = slot_count * block_len
    hidden_units = w_gate.shape[1]
    own_rows = w_gate.shape[0]
    positions = group_rank * block_len + jnp.arange(block_len, dtype=jnp.int32)
    valid_rows = (positions[None, :] < lengths[:, None]).astype(F32).reshape(tokens, 1)
    cos_table, sin_table = rope_tables(positions, HEAD_DIM)
    turn = jnp.where(jnp.arange(HEAD_DIM) < HEAD_DIM // 2, -1.0, 1.0)
    cos_rows = jnp.tile(cos_table, (slot_count, 1))
    sin_rows = jnp.tile(sin_table * turn, (slot_count, 1))

    pieces = (gain_attn, b_query, b_key, b_value, gain_mlp)
    sizes = [p.shape[0] for p in pieces]
    offsets = [sum(sizes[:i]) for i in range(len(sizes) + 1)]
    small = jnp.pad(jnp.concatenate(pieces), (0, 16 * 128 - offsets[-1])).reshape(16, 128)
    main = (hidden_units // 128 // group_count) * 128
    spare = hidden_units // group_count - main
    ff = (w_gate, w_up, w_down)
    qkv_w, small, columns = weights(
        w_query, w_key, w_value, *ff, spare_blocks(ff, main, spare), small, 1
    )
    small = small.reshape(group_count, 16 * 128)
    gain_one, query_b, key_b, value_b, gain_two = [
        small[:, offsets[i] : offsets[i + 1]].reshape(-1).astype(F32) for i in range(len(sizes))
    ]
    gap = (0, 2 * kv_width)
    vec = jnp.stack(
        [jnp.pad(gain_one, gap), jnp.concatenate((query_b, key_b, value_b)), jnp.pad(gain_two, gap)]
    )
    vec = jnp.pad(vec, ((0, 5), (0, 0)))

    rows_in = hidden_in.reshape(tokens, model_width)
    grad_final = (cotangent.reshape(tokens, model_width).astype(F32) * valid_rows).astype(BF)
    q_rows, normed, attended, mid, normed_two, pair_all, grad_all, out_w = attend(
        lengths,
        rows_in,
        grad_final,
        qkv_w.reshape(model_width, model_width + 2 * kv_width),
        w_out,
        vec,
        cos_rows,
        sin_rows,
        block_len,
        2,
    )
    grad_normed_two, mlp_out, half_sum = mlp(normed_two, grad_all, columns, spare, 3)
    sel, fold = folding(group_count, model_width)
    selk, foldk = folding(group_count, kv_width)
    layer_out, grad_input, qkv_sum, out_sum, vector_sum, main_sum, spare_sum = backward(
        lengths,
        grad_normed_two,
        mlp_out,
        mid,
        grad_final,
        rows_in,
        attended,
        q_rows,
        normed,
        vec,
        cos_rows,
        sin_rows,
        jnp.broadcast_to(valid_rows, (tokens, model_width)),
        sel,
        fold,
        selk,
        foldk,
        pair_all,
        out_w,
        qkv_w,
        half_sum,
        block_len,
        4,
    )
    ff_sums = [
        jnp.concatenate(
            (
                main_sum[i],
                jnp.transpose(spare_sum[:, :, at : at + spare], (1, 0, 2)).reshape(own_rows, -1),
            ),
            axis=1,
        ).astype(F32)
        for i, at in ((0, 0), (1, spare), (2, 128))
    ]
    gain_one_sum, query_bias_sum, key_bias_sum, value_bias_sum, gain_two_sum = [
        vector_sum[i, : sizes[i]] for i in range(len(sizes))
    ]
    return (
        layer_out.reshape(hidden_in.shape),
        grad_input.reshape(hidden_in.shape),
        gain_one_sum,
        qkv_sum[:, :model_width],
        query_bias_sum,
        qkv_sum[:, model_width : model_width + kv_width],
        key_bias_sum,
        qkv_sum[:, model_width + kv_width :],
        value_bias_sum,
        out_sum,
        gain_two_sum,
        *ff_sums,
    )


def solution(mesh):
    act = P("replica", "group", None)
    vec = P("group")
    mat = P("group", None)
    return jax.shard_map(
        shards_fast if mesh.shape["group"] == 16 else shards_plain,
        mesh=mesh,
        in_specs=(act, P("replica"), vec, mat, vec, mat, vec, mat, vec, mat, vec, mat, mat, mat, act),
        out_specs=(act, act, vec, mat, vec, mat, vec, mat, vec, mat, vec, mat, mat, mat),
        check_vma=False,
    )
```

```python
import functools

import jax
import jax.numpy as jnp
from jax import lax
from jax.experimental import pallas as pl
from jax.experimental.pallas import tpu as pltpu
from jax.sharding import PartitionSpec as P

MESH = pl.DeviceIdType.MESH
NZ = 4
MAIN = 512
D = 1536
COLS = 3 * MAIN + 256
HEADS = 12
KV_HEADS = 2
HEAD_DIM = 128
EPSILON = 1e-06
THETA = 1000000.0
BF = jnp.bfloat16
F32 = jnp.float32


def rope_tables(positions, head_dim):
    freqs = THETA ** (-jnp.arange(0, head_dim, 2).astype(F32) / head_dim)
    angles = positions.astype(F32)[:, None] * freqs[None, :]
    angles = jnp.concatenate((angles, angles), axis=-1)
    return (jnp.cos(angles), jnp.sin(angles))


def rotate(tensor, cos_table, sin_table):
    halfway = tensor.shape[-1] // 2
    turned = jnp.concatenate((-tensor[..., halfway:], tensor[..., :halfway]), axis=-1)
    return tensor * cos_table + turned * sin_table


def rotate_back(gradient, cos_table, sin_table):
    halfway = gradient.shape[-1] // 2
    scaled = gradient * sin_table
    turned = jnp.concatenate((scaled[..., halfway:], -scaled[..., :halfway]), axis=-1)
    return gradient * cos_table + turned


def normalize(row_values, gain_vec):
    factor = lax.rsqrt(jnp.mean(row_values * row_values, axis=-1, keepdims=True) + EPSILON)
    return (row_values * factor * gain_vec, factor)


def norm_back(row_values, factor, gain_vec, upstream):
    weighted = upstream * gain_vec
    inner_mean = jnp.mean(weighted * row_values, axis=-1, keepdims=True)
    grad_rows = factor * weighted - row_values * (factor * factor * factor) * inner_mean
    grad_gain = jnp.sum(upstream * row_values * factor, axis=0)
    return (grad_rows, grad_gain)


def matmul(a, b):
    return jnp.dot(a, b, preferred_element_type=F32)


def matmul_nt(a, b):
    return lax.dot_general(a, b, (((1,), (1,)), ((), ())), preferred_element_type=F32)


def matmul_tn(a, b):
    return lax.dot_general(a, b, (((0,), (0,)), ((), ())), preferred_element_type=F32)


def arrange(per_token, kv_heads):
    block_len, head_count, head_dim = per_token.shape
    repeat = head_count // kv_heads
    grouped = per_token.reshape(block_len, kv_heads, repeat, head_dim)
    return jnp.transpose(grouped, (1, 2, 0, 3)).reshape(kv_heads, repeat * block_len, head_dim)


def restore(per_group, block_len):
    kv_heads, row_count, head_dim = per_group.shape
    repeat = row_count // block_len
    grouped = per_group.reshape(kv_heads, repeat, block_len, head_dim)
    return jnp.transpose(grouped, (2, 0, 1, 3)).reshape(block_len, kv_heads * repeat * head_dim)


def masked_exp(query_rows, key_block, row_pos, first_key, length, score_scale):
    key_step = key_block.shape[0]
    raw_scores = jnp.einsum("grd,kgd->grk", query_rows, key_block, preferred_element_type=F32)
    key_pos = first_key + jnp.arange(key_step, dtype=jnp.int32)
    allowed = (key_pos[None, :] <= row_pos[:, None]) & (key_pos[None, :] < length)
    return jnp.where(allowed[None], jnp.exp(raw_scores * score_scale), 0.0)


def block_total(length, rank_end, key_step):
    key_limit = jnp.minimum(length, rank_end)
    return (key_limit + key_step - 1) // key_step


def attend_forward(query_rows, key_all, value_all, row_pos, length, rank_end, key_step, scale):
    kv_heads, row_count, head_dim = query_rows.shape

    def visit(block_index, state_tuple):
        totals, numerator = state_tuple
        first_key = block_index * key_step
        key_block = lax.dynamic_slice_in_dim(key_all, first_key, key_step, 0)
        value_block = lax.dynamic_slice_in_dim(value_all, first_key, key_step, 0)
        weights = masked_exp(query_rows, key_block, row_pos, first_key, length, scale)
        totals = totals + jnp.sum(weights, axis=-1)
        numerator = numerator + jnp.einsum(
            "grk,kgd->grd", weights.astype(BF), value_block, preferred_element_type=F32
        )
        return (totals, numerator)

    initial = (
        jnp.zeros((kv_heads, row_count), F32),
        jnp.zeros((kv_heads, row_count, head_dim), F32),
    )
    return lax.fori_loop(0, block_total(length, rank_end, key_step), visit, initial)


def attend_backward(
    query_rows, key_all, value_all, row_pos, length, rank_end, key_step, scale, grad_numer, grad_total
):
    kv_heads, row_count, head_dim = query_rows.shape

    def visit(block_index, state_tuple):
        grad_query, grad_key, grad_value = state_tuple
        first_key = block_index * key_step
        key_block = lax.dynamic_slice_in_dim(key_all, first_key, key_step, 0)
        value_block = lax.dynamic_slice_in_dim(value_all, first_key, key_step, 0)
        weights = masked_exp(query_rows, key_block, row_pos, first_key, length, scale)
        grad_prob = jnp.einsum("grd,kgd->grk", grad_numer, value_block, preferred_element_type=F32)
        grad_score = (weights * (grad_prob + grad_total[..., None])).astype(BF)
        grad_query = grad_query + jnp.einsum(
            "grk,kgd->grd", grad_score, key_block, preferred_element_type=F32
        )
        key_part = jnp.einsum("grk,grd->kgd", grad_score, query_rows, preferred_element_type=F32)
        value_part = jnp.einsum(
            "grk,grd->kgd", weights.astype(BF), grad_numer, preferred_element_type=F32
        )
        key_old = lax.dynamic_slice_in_dim(grad_key, first_key, key_step, 0)
        value_old = lax.dynamic_slice_in_dim(grad_value, first_key, key_step, 0)
        grad_key = lax.dynamic_update_slice_in_dim(grad_key, key_old + key_part, first_key, 0)
        grad_value = lax.dynamic_update_slice_in_dim(
            grad_value, value_old + value_part, first_key, 0
        )
        return (grad_query, grad_key, grad_value)

    initial = (
        jnp.zeros((kv_heads, row_count, head_dim), F32),
        jnp.zeros(key_all.shape, F32),
        jnp.zeros(value_all.shape, F32),
    )
    return lax.fori_loop(0, block_total(length, rank_end, key_step), visit, initial)


def gather_plain(x):
    return lax.all_gather(x, "group", axis=0, tiled=True)


def scatter_sum(x):
    return lax.psum_scatter(x, "group", scatter_dimension=0, tiled=True)


def shards_plain(
    hidden_in,
    lengths,
    gain_attn,
    w_query,
    b_query,
    w_key,
    b_key,
    w_value,
    b_value,
    w_out,
    gain_mlp,
    w_gate,
    w_up,
    w_down,
    cotangent,
):
    group_count = lax.axis_size("group")
    group_rank = lax.axis_index("group")
    slot_count, block_len, model_width = hidden_in.shape
    kv_heads = KV_HEADS
    head_dim = HEAD_DIM
    kv_width = kv_heads * head_dim
    repeat = HEADS // kv_heads
    slot_span = block_len * group_count
    key_step = min(512, slot_span)
    score_scale = head_dim ** (-0.5)
    tokens = slot_count * block_len
    hidden_units = w_gate.shape[1]
    own_rows = w_gate.shape[0]
    share = hidden_units // group_count
    positions = group_rank * block_len + jnp.arange(block_len, dtype=jnp.int32)
    valid_rows = (positions[None, :] < lengths[:, None]).astype(F32).reshape(tokens, 1)
    cos_table, sin_table = rope_tables(positions, head_dim)
    cos_heads = cos_table[:, None, :]
    sin_heads = sin_table[:, None, :]
    rank_end = (group_rank + 1) * block_len
    row_pos = jnp.tile(positions, repeat)

    pieces = (gain_attn, b_query, b_key, b_value, gain_mlp)
    sizes = [p.shape[0] for p in pieces]
    small = gather_plain(jnp.concatenate(pieces)[None])
    offsets = [sum(sizes[:i]) for i in range(len(sizes) + 1)]
    gain_one, query_b, key_b, value_b, gain_two = [
        small[:, offsets[i] : offsets[i + 1]].reshape(-1).astype(F32) for i in range(len(sizes))
    ]
    qkv_w = gather_plain(jnp.concatenate((w_query, w_key, w_value), axis=1))
    out_w = gather_plain(w_out)
    qkv_b = jnp.concatenate((query_b, key_b, value_b))

    stacked = jnp.stack((w_gate, w_up, w_down)).reshape(3, own_rows, group_count, share)
    stacked = jnp.transpose(stacked, (2, 1, 0, 3)).reshape(group_count, own_rows, 3 * share)
    columns = lax.all_to_all(stacked, "group", 0, 0, tiled=True).reshape(model_width, 3 * share)
    gate_up_w = columns[:, : 2 * share]
    down_w = columns[:, 2 * share :]

    grad_final = cotangent.reshape(tokens, model_width).astype(F32) * valid_rows
    grad_all = gather_plain(grad_final.astype(BF))

    inputs = hidden_in.reshape(tokens, model_width).astype(F32)
    normed_full, factor_one = normalize(inputs, gain_one)
    normed = normed_full.astype(BF)
    qkv = matmul(normed, qkv_w) + qkv_b
    query_rot = rotate(
        qkv[:, :model_width].reshape(slot_count, block_len, HEADS, head_dim), cos_heads, sin_heads
    ).astype(BF)
    key_rot = rotate(
        qkv[:, model_width : model_width + kv_width].reshape(
            slot_count, block_len, kv_heads, head_dim
        ),
        cos_heads,
        sin_heads,
    ).astype(BF)
    value_low = qkv[:, model_width + kv_width :].astype(BF)
    pair = jnp.concatenate(
        (key_rot.reshape(tokens, kv_width), value_low), axis=1
    ).reshape(1, slot_count, block_len, 2 * kv_width)
    pair_all = jnp.transpose(gather_plain(pair), (1, 0, 2, 3)).reshape(
        slot_count, slot_span, 2, kv_heads, head_dim
    )
    key_all = pair_all[:, :, 0]
    value_all = pair_all[:, :, 1]
    query_groups = []
    slot_totals = []
    slot_attended = []
    attended_rows = []
    for s in range(slot_count):
        query_rows = arrange(query_rot[s], kv_heads)
        totals, numerator = attend_forward(
            query_rows, key_all[s], value_all[s], row_pos, lengths[s], rank_end, key_step, score_scale
        )
        attended = numerator / totals[..., None]
        query_groups.append(query_rows)
        slot_totals.append(totals)
        slot_attended.append(attended)
        attended_rows.append(restore(attended, block_len))
    attended_low = jnp.concatenate(attended_rows, axis=0).astype(BF)
    residual_mid = inputs + matmul(attended_low, out_w)
    normed_two_full, factor_two = normalize(residual_mid, gain_two)
    normed_all = gather_plain(normed_two_full.astype(BF))

    pre = matmul(normed_all, gate_up_w)
    gate_pre = pre[:, :share]
    up_pre = pre[:, share:]
    sigmoid_gate = jax.nn.sigmoid(gate_pre)
    silu_gate = gate_pre * sigmoid_gate
    hidden = (silu_gate * up_pre).astype(BF)
    grad_hidden = matmul(grad_all, down_w)
    grad_gate = (
        grad_hidden * up_pre * (sigmoid_gate * (1.0 + gate_pre * (1.0 - sigmoid_gate)))
    ).astype(BF)
    grad_up = (grad_hidden * silu_gate).astype(BF)
    gate_up_grad = jnp.concatenate((grad_gate, grad_up), axis=1)
    grad_normed_two = scatter_sum(matmul_nt(gate_up_grad, gate_up_w).astype(BF)).astype(F32)
    mlp_out = scatter_sum(matmul_nt(hidden, down_w).astype(BF)).astype(F32)
    down_term = matmul_tn(grad_all, hidden)
    gate_up_term = matmul_tn(normed_all, gate_up_grad)
    terms = jnp.concatenate((gate_up_term, down_term), axis=1).astype(BF)
    back = lax.all_to_all(
        terms.reshape(group_count, own_rows, 3 * share), "group", 0, 0, tiled=True
    )
    summed = back.astype(F32) + lax.ppermute(back, "replica", [(0, 1), (1, 0)]).astype(F32)
    summed = jnp.transpose(summed.reshape(group_count, own_rows, 3, share), (2, 1, 0, 3))
    gate_sum, up_sum, down_sum = summed.reshape(3, own_rows, hidden_units)

    final_rows = residual_mid + mlp_out
    layer_out = (final_rows * valid_rows).reshape(slot_count, block_len, model_width).astype(BF)
    grad_mid_norm, grad_gain_two = norm_back(residual_mid, factor_two, gain_two, grad_normed_two)
    grad_mid = grad_final + grad_mid_norm
    grad_branch = grad_mid.astype(BF)
    out_term = matmul_tn(attended_low, grad_branch)
    grad_attended = matmul_nt(grad_branch, out_w)
    grad_query_rows = []
    grad_pairs = []
    for s in range(slot_count):
        slot_grad = grad_attended[s * block_len : (s + 1) * block_len].reshape(
            block_len, HEADS, head_dim
        )
        grad_out = arrange(slot_grad, kv_heads)
        totals = slot_totals[s]
        grad_total = -jnp.sum(grad_out * slot_attended[s], axis=-1) / totals
        grad_numer = (grad_out / totals[..., None]).astype(BF)
        grad_query, grad_key, grad_value = attend_backward(
            query_groups[s],
            key_all[s],
            value_all[s],
            row_pos,
            lengths[s],
            rank_end,
            key_step,
            score_scale,
            grad_numer,
            grad_total,
        )
        query_back_rows = restore(grad_query * score_scale, block_len).reshape(
            block_len, HEADS, head_dim
        )
        grad_query_rows.append(
            rotate_back(query_back_rows, cos_heads, sin_heads).reshape(block_len, HEADS * head_dim)
        )
        grad_pairs.append(
            jnp.concatenate(
                (grad_key.reshape(slot_span, kv_width), grad_value.reshape(slot_span, kv_width)),
                axis=1,
            )
        )
    pair_grads = jnp.stack(grad_pairs).reshape(slot_count, group_count, block_len, 2 * kv_width)
    pair_grads = jnp.transpose(pair_grads, (1, 0, 2, 3)).astype(BF)
    pair_sum = scatter_sum(pair_grads).reshape(slot_count, block_len, 2 * kv_width).astype(F32)
    grad_query_pre = jnp.concatenate(grad_query_rows, axis=0).astype(BF)
    key_sum = pair_sum[..., :kv_width].reshape(slot_count, block_len, kv_heads, head_dim)
    grad_key_pre = (
        rotate_back(key_sum * score_scale, cos_heads, sin_heads).astype(BF).reshape(tokens, kv_width)
    )
    grad_value_pre = pair_sum[..., kv_width:].astype(BF).reshape(tokens, kv_width)
    grad_qkv = jnp.concatenate((grad_query_pre, grad_key_pre, grad_value_pre), axis=1)
    grad_normed = matmul_nt(grad_qkv, qkv_w)
    grad_in_norm, grad_gain_one = norm_back(inputs, factor_one, gain_one, grad_normed)
    grad_input = (grad_mid + grad_in_norm).reshape(slot_count, block_len, model_width)
    qkv_term = matmul_tn(normed, grad_qkv)
    qkv_bias = jnp.sum(grad_qkv.astype(F32), axis=0)

    weight_share = scatter_sum(
        jnp.concatenate((qkv_term, out_term), axis=1).astype(BF)
    )
    weight_sum = weight_share.astype(F32) + lax.ppermute(
        weight_share, "replica", [(0, 1), (1, 0)]
    ).astype(F32)
    vectors = jnp.concatenate(
        [
            grad_gain_one.reshape(group_count, -1),
            qkv_bias[:model_width].reshape(group_count, -1),
            qkv_bias[model_width : model_width + kv_width].reshape(group_count, -1),
            qkv_bias[model_width + kv_width :].reshape(group_count, -1),
            grad_gain_two.reshape(group_count, -1),
        ],
        axis=1,
    )
    vector_sum = lax.psum(scatter_sum(vectors), "replica").reshape(-1)
    gain_one_sum, query_bias_sum, key_bias_sum, value_bias_sum, gain_two_sum = [
        vector_sum[offsets[i] : offsets[i + 1]] for i in range(len(sizes))
    ]
    ends = (0, model_width, model_width + kv_width, model_width + 2 * kv_width)
    query_sum, key_sum_w, value_sum_w = [weight_sum[:, ends[i] : ends[i + 1]] for i in range(3)]
    out_sum = weight_sum[:, ends[3] :]
    return (
        layer_out,
        grad_input,
        gain_one_sum,
        query_sum,
        query_bias_sum,
        key_sum_w,
        key_bias_sum,
        value_sum_w,
        value_bias_sum,
        out_sum,
        gain_two_sum,
        gate_sum,
        up_sum,
        down_sum,
    )


def place():
    g = lax.axis_index("group")
    r = lax.axis_index("replica")
    return r, g // 4, lax.rem(g // 2, 2), lax.rem(g, 2)

def idx(z, x, c):
    return (z * 2 + x) * 2 + c

def greet(r, z, x, c, with_y=False):
    bar = pltpu.get_barrier_semaphore()
    def hail(dev):
        pl.semaphore_signal(bar, inc=1, device_id=dev, device_id_type=MESH)
    hail((r, idx(z, 1 - x, c)))
    hail((r, idx(z, x, 1 - c)))
    if with_y:
        hail((1 - r, idx(z, x, c)))
    @pl.when(z > 0)
    def _():
        hail((r, idx(z - 1, x, c)))
    @pl.when(z < NZ - 1)
    def _():
        hail((r, idx(z + 1, x, c)))
    ends = jnp.where((z > 0) & (z < NZ - 1), 1, 0)
    pl.semaphore_wait(bar, (4 if with_y else 3) + ends)

def planes(z):
    return (
        z,
        jnp.where(z == 0, 1, jnp.where(z == 1, 0, jnp.where(z == 2, 3, 2))),
        jnp.where(z == 0, 2, jnp.where(z == 1, 2, 1)),
        jnp.where(z < 2, 3, 0),
    )

def when(cond, fn):
    pl.when(cond)(fn)

class Gather:
    def __init__(self, at, src, out, send, recv, local):
        self.r, self.z, self.x, self.c = at
        self.src, self.out, self.send, self.recv, self.local = src, out, send, recv, local
        self.mid = (self.z > 0) & (self.z < NZ - 1)
        self.p = planes(self.z)
    def put(self, src, b, k, dev):
        pltpu.make_async_remote_copy(src, self.out.at[b], self.send.at[k], self.recv.at[b], device_id=dev, device_id_type=MESH).start()
    def sent(self, k):
        b = 0
        pltpu.make_async_remote_copy(self.out.at[b], self.out.at[b], self.send.at[k], self.recv.at[b], device_id=(self.r, 0), device_id_type=MESH).wait_send()
    def got(self, b):
        pltpu.make_async_remote_copy(self.out.at[b], self.out.at[b], self.send.at[0], self.recv.at[b], device_id=(self.r, 0), device_id_type=MESH).wait_recv()
    def zdev(self, s): return (self.r, idx(self.z + s, self.x, self.c))
    def xdev(self): return (self.r, idx(self.z, 1 - self.x, self.c))
    def cdev(self): return (self.r, idx(self.z, self.x, 1 - self.c))
    def begin(self):
        z, x, c = self.z, self.x, self.c
        me = idx(z, x, c)
        for s in (1, -1):
            when(self.inside(z + s), lambda s=s: self.put(self.src, me, 0 if s == 1 else 3, self.zdev(s)))
        self.put(self.src, me, 6 + z, self.xdev())
        self.put(self.src, me, 10 + 2 * z + x, self.cdev())
        pltpu.make_async_copy(self.src, self.out.at[me], self.local).start()
    def inside(self, z): return (z >= 0) & (z < NZ)
    def from_z(self, zz):
        z, x, c = self.z, self.x, self.c
        b = idx(zz, x, c)
        self.got(b)
        s = jnp.where(zz < z, 1, -1)
        d = jnp.abs(zz - z)
        slot = jnp.where(zz < z, 0, 3) + d
        when(self.inside(z + s), lambda: self.put(self.out.at[b], b, slot, (self.r, idx(z + s, x, c))))
        self.put(self.out.at[b], b, 6 + zz, self.xdev())
        self.put(self.out.at[b], b, 10 + 2 * zz + x, self.cdev())
    def first(self):
        self.from_z(self.p[1])
        when(self.mid, lambda: self.from_z(self.p[2]))
        self.from_x(self.p[0])
    def second(self):
        self.from_z(jnp.where(self.mid, self.p[3], self.p[2]))
        self.from_x(self.p[1])
    def third(self):
        when(~self.mid, lambda: self.from_z(self.p[3]))
        self.from_x(self.p[2])
    def fourth(self):
        self.from_x(self.p[3])
    def from_x(self, zz):
        b = idx(zz, 1 - self.x, self.c)
        self.got(b)
        self.put(self.out.at[b], b, 10 + 2 * zz + 1 - self.x, self.cdev())
    def from_c(self, zz):
        self.got(idx(zz, self.x, 1 - self.c))
        self.got(idx(zz, 1 - self.x, 1 - self.c))
    def end(self, local=True):
        z = self.z
        for d in range(NZ - 1):
            when((z - d >= 0) & (z < NZ - 1), lambda d=d: self.sent(d))
            when((z + d < NZ) & (z > 0), lambda d=d: self.sent(3 + d))
        for k in range(6, 18):
            self.sent(k)
        if local:
            pltpu.make_async_copy(self.src, self.out.at[0], self.local).wait()

class Scatter:
    def __init__(self, at, part, rc, rx, rz, send, rcs, rxs, rzs):
        self.r, self.z, self.x, self.c = at
        self.part, self.rc, self.rx, self.rz = part, rc, rx, rz
        self.send, self.rcs, self.rxs, self.rzs = send, rcs, rxs, rzs
    def inside(self, z): return (z >= 0) & (z < NZ)
    def copy(self, src, dst, k, rs, dev):
        return pltpu.make_async_remote_copy(src, dst, self.send.at[k], rs, device_id=dev, device_id_type=MESH)
    def over(self, d):
        return [(s, self.z + s * d) for s in ((-1, 1) if d else (1,))]
    def begin(self, far_first=True):
        z, x, c = self.z, self.x, self.c
        dev = (self.r, idx(z, x, 1 - c))
        for xx in (1 - x, x):
            for d in range(NZ - 1, -1, -1):
                for s, zz in self.over(d):
                    k = 2 * zz + xx
                    when(self.inside(zz), lambda zz=zz, k=k, xx=xx: self.copy(self.part.at[idx(zz, xx, 1 - c)], self.rc.at[k], k, self.rcs.at[k], dev).start())
    def send_c(self, zz):
        z, x, c = self.z, self.x, self.c
        dev = (self.r, idx(z, x, 1 - c))
        for xx in (1 - x, x):
            k = 2 * zz + xx
            self.copy(self.part.at[idx(zz, xx, 1 - c)], self.rc.at[k], k, self.rcs.at[k], dev).start()
    def step_x(self, d):
        z, x, c = self.z, self.x, self.c
        dev = (self.r, idx(z, 1 - x, c))
        for s, zz in self.over(d):
            def go(zz=zz):
                k = 2 * zz + 1 - x
                b = idx(zz, 1 - x, c)
                self.copy(self.rc.at[k], self.rc.at[k], 0, self.rcs.at[k], dev).wait_recv()
                self.part[b] = (self.part[b].astype(F32) + self.rc[k].astype(F32)).astype(BF)
                self.copy(self.part.at[b], self.rx.at[zz], 8 + zz, self.rxs.at[zz], dev).start()
            when(self.inside(zz), go)
    def step_z(self, d):
        z, x, c = self.z, self.x, self.c
        for s, zz in self.over(d):
            def go(zz=zz, s=s):
                k = 2 * zz + x
                b = idx(zz, x, c)
                self.copy(self.rc.at[k], self.rc.at[k], 0, self.rcs.at[k], (self.r, 0)).wait_recv()
                self.copy(self.rx.at[zz], self.rx.at[zz], 0, self.rxs.at[zz], (self.r, 0)).wait_recv()
                both = self.part[b].astype(F32) + self.rc[k].astype(F32) + self.rx[zz].astype(F32)
                dev = (self.r, idx(z + s, x, c))
                slot = jnp.where(zz == z + s, NZ, zz) if s == -1 else zz
                self.part[b] = both.astype(BF)
                def more():
                    self.copy(self.rz.at[zz], self.rz.at[zz], 0, self.rzs.at[zz], dev).wait_recv()
                    self.part[b] = (self.part[b].astype(F32) + self.rz[zz].astype(F32)).astype(BF)
                when(self.inside(z - s), more)
                self.copy(self.part.at[b], self.rz.at[slot], 12 + zz, self.rzs.at[slot], dev).start()
            when(self.inside(zz), go)
    def finish(self, out):
        z, x, c = self.z, self.x, self.c
        k = 2 * z + x
        b = idx(z, x, c)
        self.copy(self.rc.at[k], self.rc.at[k], 0, self.rcs.at[k], (self.r, 0)).wait_recv()
        self.copy(self.rx.at[z], self.rx.at[z], 0, self.rxs.at[z], (self.r, 0)).wait_recv()
        out[...] = self.part[b].astype(F32) + self.rc[k].astype(F32) + self.rx[z].astype(F32)
        def lo():
            self.copy(self.rz.at[z], self.rz.at[z], 0, self.rzs.at[z], (self.r, 0)).wait_recv()
            out[...] += self.rz[z].astype(F32)
        when(z > 0, lo)
        def hi():
            self.copy(self.rz.at[NZ], self.rz.at[NZ], 0, self.rzs.at[NZ], (self.r, 0)).wait_recv()
            out[...] += self.rz[NZ].astype(F32)
        when(z < NZ - 1, hi)
        for k in range(8):
            self.copy(self.part.at[0], self.part.at[0], k, self.rcs.at[0], (self.r, 0)).wait_send()
        for k in range(8, 12):
            self.copy(self.part.at[0], self.part.at[0], k, self.rcs.at[0], (self.r, 0)).wait_send()
        for zz in range(NZ):
            when(z != zz, lambda zz=zz: self.copy(self.part.at[0], self.part.at[0], 12 + zz, self.rcs.at[0], (self.r, 0)).wait_send())


KS = (8, 1, 9, 2, 10, 3, 11, 4, 12, 5, 13, 6, 14, 7, 15)
WINDOW = 4

class Deal:
    def __init__(self, at, ws, rem, buf, send, recv, ysend, yrecv, local):
        self.r, self.z, self.x, self.c = at
        self.me = idx(self.z, self.x, self.c)
        self.ws, self.rem, self.buf = ws, rem, buf
        self.send, self.recv, self.ysend, self.yrecv, self.local = send, recv, ysend, yrecv, local
        self.half = ws[0].shape[0] // 2
    def rows(self, j, h):
        n = self.half
        return self.buf.at[pl.ds(pl.multiple_of((2 * j + h) * n, n), n)]
    def launch(self, k):
        r, me, n = self.r, self.me, self.half
        row = pl.ds(pl.multiple_of(r * n, n), n)
        j = jnp.bitwise_xor(me, k)
        dev = (r, j)
        dst = self.rows(me, r)
        col = pl.ds(pl.multiple_of(j * MAIN, MAIN), MAIN)
        for i in range(3):
            pltpu.make_async_remote_copy(self.ws[i].at[row, col], dst.at[:, pl.ds(i * MAIN, MAIN)], self.send.at[k], self.recv.at[k], device_id=dev, device_id_type=MESH).start()
        pltpu.make_async_remote_copy(self.rem.at[j, row], dst.at[:, pl.ds(3 * MAIN, 256)], self.send.at[k], self.recv.at[k], device_id=dev, device_id_type=MESH).start()
    def begin(self):
        me, n = self.me, self.half
        for k in KS[:WINDOW]:
            self.launch(k)
        col = pl.ds(pl.multiple_of(me * MAIN, MAIN), MAIN)
        own = self.buf.at[pl.ds(pl.multiple_of(2 * me * n, 2 * n), 2 * n)]
        for i in range(3):
            pltpu.make_async_copy(self.ws[i].at[:, col], own.at[:, pl.ds(i * MAIN, MAIN)], self.local).start()
        pltpu.make_async_copy(self.rem.at[me], own.at[:, pl.ds(3 * MAIN, 256)], self.local).start()
    def step(self, i):
        k = KS[i]
        r, me = self.r, self.me
        j = jnp.bitwise_xor(me, k)
        blk = self.rows(j, r)
        dev = (1 - r, me)
        pltpu.make_async_remote_copy(blk, blk, self.send.at[k], self.recv.at[k], device_id=dev, device_id_type=MESH).wait_recv()
        pltpu.make_async_remote_copy(blk, blk, self.ysend.at[k], self.yrecv.at[k], device_id=dev, device_id_type=MESH).start()
        if i + WINDOW < 15:
            self.launch(KS[i + WINDOW])
    def end(self):
        r, me = self.r, self.me
        dev = (1 - r, me)
        for k in range(1, 16):
            j = jnp.bitwise_xor(me, k)
            blk = self.rows(j, 1 - r)
            pltpu.make_async_remote_copy(blk, blk, self.ysend.at[k], self.yrecv.at[k], device_id=dev, device_id_type=MESH).wait()
            pltpu.make_async_remote_copy(blk, blk, self.send.at[k], self.recv.at[k], device_id=dev, device_id_type=MESH).wait_send()
        own = self.buf.at[pl.ds(pl.multiple_of(2 * me * self.half, 2 * self.half), 2 * self.half)]
        pltpu.make_async_copy(own, own, self.local).wait()

def hail_all(r, z, x, c):
    bar = pltpu.get_barrier_semaphore()
    me = idx(z, x, c)
    for k in range(1, 16):
        pl.semaphore_signal(bar, inc=1, device_id=(r, lax.rem(me + k, 16)), device_id_type=MESH)
    pl.semaphore_signal(bar, inc=1, device_id=(1 - r, me), device_id_type=MESH)
    pl.semaphore_wait(bar, 16)


def dot(a, b):
    return lax.dot_general(a, b, (((1,), (0,)), ((), ())), preferred_element_type=F32)
def dot_nt(a, b):
    return lax.dot_general(a, b, (((1,), (1,)), ((), ())), preferred_element_type=F32)
def dot_tn(a, b):
    return lax.dot_general(a, b, (((0,), (0,)), ((), ())), preferred_element_type=F32)

def gated(g, u, gh):
    sig = jax.nn.sigmoid(g)
    silu = g * sig
    return (gh * u * (sig * (1.0 + g * (1.0 - sig)))).astype(BF), (gh * silu).astype(BF), (silu * u).astype(BF)

def mlp_kernel(spare, n2_ref, cot_ref, w_ref, gsum, osum, half_ref,
               n2, cot, w, act, pg, po, rcg, rxg, rzg, rco, rxo, rzo, yb,
               gsend, grecv, glocal, lsem, ssend, srcs, srxs, srzs, ysend, yrecv):
    at = place()
    r, z, x, c = at
    loads = [pltpu.make_async_copy(w_ref, w, lsem.at[0]), pltpu.make_async_copy(cot_ref, cot, lsem.at[1])]
    for l in loads: l.start()
    greet(*at, with_y=True)
    g = Gather(at, n2_ref, n2, gsend, grecv, glocal)
    rg = Scatter(at, pg, rcg, rxg, rzg, ssend.at[0], srcs.at[0], srxs.at[0], srzs.at[0])
    ro = Scatter(at, po, rco, rxo, rzo, ssend.at[1], srcs.at[1], srxs.at[1], srzs.at[1])
    g.begin()
    for l in loads: l.wait()
    mid = (z > 0) & (z < NZ - 1)
    p = [z,
         jnp.where(z == 0, 1, jnp.where(z == 1, 0, jnp.where(z == 2, 3, 2))),
         jnp.where(z == 0, 2, jnp.where(z == 1, 2, 1)),
         jnp.where(z < 2, 3, 0)]

    def tiles(zz):
        rows = pl.ds(pl.multiple_of(4 * zz, 4), 4)
        tok = pl.ds(pl.multiple_of(512 * zz, 512), 512)
        @pl.loop(0, 2)
        def _(t):
            a = n2[rows].reshape(512, D)
            k = cot[rows].reshape(512, D)
            def col(base):
                return pl.ds(pl.multiple_of(base + 256 * t, 256), 256)
            dg, du, h = gated(dot(a, w[:, col(0)]), dot(a, w[:, col(MAIN)]), dot(k, w[:, col(2 * MAIN)]))
            act[tok, col(0)] = dg
            act[tok, col(MAIN)] = du
            act[tok, col(2 * MAIN)] = h
        a = n2[rows].reshape(512, D)
        k = cot[rows].reshape(512, D)
        pre = dot(a, w[:, 3 * MAIN : 3 * MAIN + 128])
        gh = dot(k, w[:, 3 * MAIN + 128 :])
        lane = lax.broadcasted_iota(jnp.int32, (512, 128), 1)
        sig = jax.nn.sigmoid(pre)
        silu = pre * sig
        up = pltpu.roll(pre, 128 - spare, 1)
        dg = gh * up * (sig * (1.0 + pre * (1.0 - sig)))
        du = pltpu.roll(gh * silu, spare, 1)
        act[tok, 3 * MAIN : 3 * MAIN + 128] = jnp.where(lane < spare, dg, jnp.where(lane < 2 * spare, du, 0.0)).astype(BF)
        act[tok, 3 * MAIN + 128 :] = jnp.where(lane < spare, silu * up, 0.0).astype(BF)
        @pl.loop(0, D // 256)
        def _(t):
            dr = pl.ds(pl.multiple_of(256 * t, 256), 256)
            v = dot_nt(act[tok, : 2 * MAIN], w[dr, : 2 * MAIN]) + dot_nt(act[tok, 3 * MAIN : 3 * MAIN + 128], w[dr, 3 * MAIN : 3 * MAIN + 128])
            pg[rows, :, dr] = v.astype(BF).reshape(4, 128, 256)
            v = dot_nt(act[tok, 2 * MAIN : 3 * MAIN], w[dr, 2 * MAIN : 3 * MAIN]) + dot_nt(act[tok, 3 * MAIN + 128 :], w[dr, 3 * MAIN + 128 :])
            po[rows, :, dr] = v.astype(BF).reshape(4, 128, 256)
        rg.send_c(zz)
        ro.send_c(zz)

    g.from_z(p[1])
    when(mid, lambda: g.from_z(p[2]))
    g.from_x(p[0])
    g.from_c(p[0])
    pltpu.make_async_copy(n2_ref, n2.at[0], glocal).wait()
    tiles(p[0])
    g.from_z(jnp.where(mid, p[3], p[2]))
    g.from_x(p[1])
    g.from_c(p[1])
    tiles(p[1])
    when(~mid, lambda: g.from_z(p[3]))
    g.from_x(p[2])
    g.from_c(p[2])
    tiles(p[2])
    g.from_x(p[3])
    g.from_c(p[3])
    tiles(p[3])

    ydev = (1 - r, idx(z, x, c))
    own = D // 16
    half = own // 2
    def ycopy(j):
        src = w.at[pl.ds(pl.multiple_of(own * j + half * (1 - r), half), half)]
        return pltpu.make_async_remote_copy(src, yb.at[j], ysend.at[j], yrecv.at[j], device_id=ydev, device_id_type=MESH)
    def grads(q):
        dr = slice(384 * q, 384 * (q + 1))
        row = slice(384 * q, 384 * (q + 1))
        @pl.loop(0, 4)
        def _(t):
            col = pl.ds(pl.multiple_of(256 * t, 256), 256)
            w[row, col] = dot_tn(n2[:, :, dr].reshape(2048, 384), act[:, col]).astype(BF)
        @pl.loop(0, 2)
        def _(t):
            col = pl.ds(pl.multiple_of(2 * MAIN + 256 * t, 256), 256)
            w[row, col] = dot_tn(cot[:, :, dr].reshape(2048, 384), act[:, col]).astype(BF)
        w[row, 3 * MAIN : 3 * MAIN + 128] = dot_tn(n2[:, :, dr].reshape(2048, 384), act[:, 3 * MAIN : 3 * MAIN + 128]).astype(BF)
        w[row, 3 * MAIN + 128 :] = dot_tn(cot[:, :, dr].reshape(2048, 384), act[:, 3 * MAIN + 128 :]).astype(BF)
        for j in range(4 * q, 4 * q + 4):
            ycopy(j).start()
    def yadd(j):
        ycopy(j).wait()
        mine = w[pl.ds(pl.multiple_of(own * j + half * r, half), half)]
        yb[j] = (mine.astype(F32) + yb[j].astype(F32)).astype(BF)
        pltpu.make_async_copy(yb.at[j], half_ref.at[j], lsem.at[2]).start()

    rg.step_x(3)
    rg.step_x(2)
    grads(0)
    rg.step_z(3)
    rg.step_x(1)
    grads(1)
    rg.step_z(2)
    rg.step_x(0)
    grads(2)
    rg.step_z(1)
    ro.step_x(3)
    ro.step_x(2)
    grads(3)
    rg.finish(gsum)
    ro.step_z(3)
    ro.step_x(1)
    for j in range(0, 4): yadd(j)
    ro.step_z(2)
    ro.step_x(0)
    for j in range(4, 8): yadd(j)
    ro.step_z(1)
    for j in range(8, 12): yadd(j)
    ro.finish(osum)
    for j in range(12, 16): yadd(j)
    pltpu.make_async_copy(yb, half_ref, lsem.at[2]).wait()
    g.end(local=False)

def mlp(n2, cot, w, spare, cid):
    blk = n2.shape
    dma = pltpu.SemaphoreType.DMA
    full = (16,) + blk
    return pl.pallas_call(
        functools.partial(mlp_kernel, spare),
        out_shape=[jax.ShapeDtypeStruct(blk, F32)] * 2 + [jax.ShapeDtypeStruct((16, D // 32, COLS), BF)],
        in_specs=[pl.BlockSpec(memory_space=pl.ANY)] * 3,
        out_specs=[pl.BlockSpec(memory_space=pltpu.VMEM)] * 2 + [pl.BlockSpec(memory_space=pl.ANY)],
        scratch_shapes=[pltpu.VMEM(full, BF), pltpu.VMEM(full, BF), pltpu.VMEM((D, COLS), BF), pltpu.VMEM((16 * blk[0], COLS), BF),
                        pltpu.VMEM(full, BF), pltpu.VMEM(full, BF)]
        + [pltpu.VMEM((k,) + blk, BF) for k in (8, 4, 5, 8, 4, 5)]
        + [pltpu.VMEM((16, D // 32, COLS), BF)]
        + [dma((18,)), dma((16,)), dma(()), dma((3,)), dma((2, 16)), dma((2, 8)), dma((2, 4)), dma((2, 5)), dma((16,)), dma((16,))],
        compiler_params=pltpu.CompilerParams(collective_id=cid, has_side_effects=True, vmem_limit_bytes=60 * 2**20),
    )(n2, cot, w)


def spin(u, cos, sin):
    return u * cos + pltpu.roll(u, HEAD_DIM // 2, 1) * sin

def stack_heads(v):
    n = v.shape[1] // HEAD_DIM
    return jnp.concatenate([v[:, HEAD_DIM * i : HEAD_DIM * (i + 1)] for i in range(n)], axis=0)

def spread_heads(v, rows):
    n = v.shape[0] // rows
    return jnp.concatenate([v[rows * i : rows * (i + 1)] for i in range(n)], axis=1)

def exp_scores(q, k, first_row, block, length):
    sc = dot_nt(q, k) * (HEAD_DIM ** -0.5)
    key = lax.broadcasted_iota(jnp.int32, sc.shape, 1)
    row = jnp.bitwise_and(lax.broadcasted_iota(jnp.int32, sc.shape, 0), block - 1) + first_row
    return jnp.where((key <= row) & (key < length), jnp.exp(sc), 0.0)

def rms(v, gain):
    factor = lax.rsqrt(jnp.mean(v * v, axis=-1, keepdims=True) + EPSILON)
    return v * factor * gain


class GatherY(Gather):
    def __init__(self, at, src, out, send, recv, local):
        Gather.__init__(self, at, src, out, send, recv, local)
        self.n = src.shape[0] // 2
        self.ydev = (1 - self.r, idx(self.z, self.x, self.c))
    def rows(self, h):
        return pl.ds(pl.multiple_of(h * self.n, self.n), self.n)
    def half(self, b, h):
        return self.out.at[b, self.rows(h)]
    def move(self, src, dst, k, q, dev):
        return pltpu.make_async_remote_copy(src, dst, self.send.at[k], self.recv.at[q], device_id=dev, device_id_type=MESH)
    def arrived(self, b, h):
        self.move(self.half(b, h), self.half(b, h), 0, 2 * b + h, self.ydev).wait_recv()
    def begin(self):
        z, x, c, r = self.z, self.x, self.c, self.r
        me = idx(z, x, c)
        mine, dst = self.src.at[self.rows(r)], self.half(me, r)
        for s in (1, -1):
            when(self.inside(z + s), lambda s=s: self.move(mine, dst, 0 if s == 1 else 3, 2 * me + r, self.zdev(s)).start())
        self.move(mine, dst, 6 + z, 2 * me + r, self.xdev()).start()
        self.move(self.src, self.out.at[me], 18 + 2 * z + x, 2 * me, self.cdev()).start()
        pltpu.make_async_copy(self.src, self.out.at[me], self.local).start()
    def from_z(self, zz):
        z, x, c, r = self.z, self.x, self.c, self.r
        b = idx(zz, x, c)
        q = 2 * b + r
        self.arrived(b, r)
        s = jnp.where(zz < z, 1, -1)
        slot = jnp.where(zz < z, 0, 3) + jnp.abs(zz - z)
        a = self.half(b, r)
        when(self.inside(z + s), lambda: self.move(a, a, slot, q, (r, idx(z + s, x, c))).start())
        self.move(a, a, 6 + zz, q, self.xdev()).start()
        self.move(a, a, 18 + 2 * zz + x, q, self.cdev()).start()
        self.move(a, a, 10 + 2 * zz + x, q, self.ydev).start()
    def from_x(self, zz):
        x, c, r = self.x, self.c, self.r
        b = idx(zz, 1 - x, c)
        q = 2 * b + r
        self.arrived(b, r)
        a = self.half(b, r)
        self.move(a, a, 18 + 2 * zz + 1 - x, q, self.cdev()).start()
        self.move(a, a, 10 + 2 * zz + 1 - x, q, self.ydev).start()
    def from_y(self, zz):
        x, c, r = self.x, self.c, self.r
        def take(xx):
            b = idx(zz, xx, c)
            self.arrived(b, 1 - r)
            a = self.half(b, 1 - r)
            self.move(a, a, 26 + 2 * zz + xx, 2 * b + 1 - r, self.cdev()).start()
        when(zz != self.z, lambda: take(x))
        take(1 - x)
    def from_c(self, zz):
        x, c, r = self.x, self.c, self.r
        b = idx(zz, x, 1 - c)
        whole = self.out.at[b]
        when(zz == self.z, lambda: self.move(whole, whole, 0, 2 * b, self.ydev).wait_recv())
        def both(b):
            self.arrived(b, r)
            self.arrived(b, 1 - r)
        when(zz != self.z, lambda: both(b))
        both(idx(zz, 1 - x, 1 - c))
    def end(self):
        z, x = self.z, self.x
        own = 2 * z + x
        a = self.half(0, 0)
        def sent(k, a=a):
            self.move(a, a, k, 0, self.ydev).wait_send()
        for d in range(NZ - 1):
            when((z - d >= 0) & (z < NZ - 1), lambda d=d: sent(d))
            when((z + d < NZ) & (z > 0), lambda d=d: sent(3 + d))
        for k in range(6, 10):
            sent(k)
        for k in range(8):
            def other(k=k):
                sent(10 + k)
                sent(18 + k)
                sent(26 + k)
            when(own != k, other)
        sent(18 + own, self.out.at[0])
        pltpu.make_async_copy(self.src, self.out.at[0], self.local).wait()

def front_kernel(block, lens, x_ref, cos_ref, sin_ref, sel, fold, selk, foldk, small, wq, wk, wv, wg, wu, wd, rem, cot_ref, wo_ref,
                 q_out, normed_out, att_out, mid_out, n2_out, vec, buf, qkv_out, kv_out, cot_out, wo_out,
                 qkv_own, wqkv, small_all, own, kv, wo,
                 qs, qr, ql, vs, vr, vl, ks, kr, kl, cs, cr, cl, ws, wr, wl, ds, dr, ys, yr, dl, lsem):
    at = place()
    width = HEADS * HEAD_DIM
    kw = KV_HEADS * HEAD_DIM
    loads = [pltpu.make_async_copy(w, qkv_own.at[:, pl.ds(o, n)], lsem.at[i]) for i, (w, o, n) in enumerate(((wq, 0, width), (wk, width, kw), (wv, width + kw, kw)))]
    for l in loads: l.start()
    hail_all(*at)
    for l in loads: l.wait()
    gq = GatherY(at, qkv_own, wqkv, qs, qr, ql)
    gv = Gather(at, small, small_all, vs, vr, vl)
    gk = Gather(at, own, kv, ks, kr, kl)
    gc = Gather(at, cot_ref, cot_out, cs, cr, cl)
    gw = GatherY(at, wo_ref, wo, ws, wr, wl)
    d = Deal(at, (wg, wu, wd), rem, buf, ds, dr, ys, yr, dl)
    steps = iter(range(15))
    def some(n):
        for _ in range(n):
            i = next(steps, None)
            if i is not None:
                d.step(i)
    gq.begin()
    gv.begin()
    d.begin()
    x = x_ref[...].astype(F32)
    gq.first()
    gv.first()
    gq.second()
    gv.second()
    gq.from_y(gq.p[0])
    some(EARLY[0])
    gq.third()
    gv.third()
    gq.from_y(gq.p[1])
    gq.fourth()
    gv.fourth()
    gc.begin()
    gq.from_y(gq.p[2])
    gq.from_y(gq.p[3])
    for zz in range(NZ):
        gv.from_c(zz)
        gq.from_c(zz)
    gv.end()
    gq.end()
    keep = [pltpu.make_async_copy(wqkv, qkv_out, lsem.at[3]), pltpu.make_async_copy(kv, kv_out, lsem.at[4]), pltpu.make_async_copy(wo, wo_out, lsem.at[5])]
    keep[0].start()
    vec[...] = jnp.zeros_like(vec)
    for i, row, first, a, b in ((0, 0, 0, sel, fold), (1, 1, 0, sel, fold), (2, 1, width, selk, foldk), (3, 1, width + kw, selk, foldk), (4, 2, 0, sel, fold)):
        t = dot_nt(small_all[:, i, :].astype(BF), b[...])
        vec[row : row + 1, first : first + a.shape[1]] = jnp.sum(t * a[...], axis=0, keepdims=True)
    normed_out[...] = rms(x, vec[0:1, :width]).astype(BF)
    cos, sin = cos_ref[...], sin_ref[...]
    def product(base):
        return dot(normed_out[...], wqkv[:, :, pl.ds(pl.multiple_of(base, 256), 256)].reshape(width, 256)) + vec[1:2, pl.ds(pl.multiple_of(base, 256), 256)]
    pre = product(width)
    own[:, :HEAD_DIM] = spin(pre[:, :HEAD_DIM], cos, sin).astype(BF)
    own[:, HEAD_DIM : 2 * HEAD_DIM] = spin(pre[:, HEAD_DIM:], cos, sin).astype(BF)
    own[:, kw:] = product(width + kw).astype(BF)
    gk.begin()
    gw.begin()
    @pl.loop(0, width // 256)
    def _(t):
        pre = product(t * 256)
        for i in range(2):
            col = pl.ds(pl.multiple_of(256 * t + HEAD_DIM * i, HEAD_DIM), HEAD_DIM)
            q_out[:, col] = spin(pre[:, HEAD_DIM * i : HEAD_DIM * (i + 1)], cos, sin).astype(BF)
    some(EARLY[1])
    gc.first()
    gk.first()
    gw.first()
    some(EARLY[2])
    gk.second()
    gc.second()
    gw.second()
    gw.from_y(gw.p[0])
    gk.third()
    some(EARLY[3])
    gk.fourth()
    gc.third()
    gw.third()
    gw.from_y(gw.p[1])
    for zz in range(NZ):
        gk.from_c(zz)
    gk.end()
    keep[1].start()
    first_row = lax.axis_index("group") * block
    span = 16 * block
    @pl.loop(0, 4)
    def _(u):
        s, h = u // 2, lax.rem(u, 2)
        rows = pl.ds(pl.multiple_of(block * s, block), block)
        cols = pl.ds(pl.multiple_of(width // 2 * h, width // 2), width // 2)
        q = stack_heads(q_out[rows, cols])
        k = kv[:, rows, pl.ds(pl.multiple_of(HEAD_DIM * h, HEAD_DIM), HEAD_DIM)].reshape(span, HEAD_DIM)
        v = kv[:, rows, pl.ds(pl.multiple_of(kw + HEAD_DIM * h, HEAD_DIM), HEAD_DIM)].reshape(span, HEAD_DIM)
        e = exp_scores(q, k, first_row, block, lens[s])
        total = jnp.sum(e, axis=-1, keepdims=True)
        att_out[rows, cols] = spread_heads(dot(e.astype(BF), v) / total, block)
    some(EARLY[4])
    gw.fourth()
    gc.fourth()
    gw.from_y(gw.p[2])
    gw.from_y(gw.p[3])
    for zz in range(NZ):
        gw.from_c(zz)
    gw.end()
    keep[2].start()
    @pl.loop(0, width // 256)
    def _(t):
        col = pl.ds(pl.multiple_of(256 * t, 256), 256)
        mid_out[:, col] = x_ref[:, col].astype(F32) + dot(att_out[...].astype(BF), wo[:, :, col].reshape(width, 256))
    n2_out[...] = rms(mid_out[...], vec[2:3, :width]).astype(BF)
    some(15)
    for zz in range(NZ):
        gc.from_c(zz)
    gc.end()
    for k in keep:
        k.wait()
    d.end()

EARLY = (2, 1, 1, 2, 3)

def front(lens, x, cos, sin, sel, fold, selk, foldk, small, wq, wk, wv, wg, wu, wd, rem, cot, wo, block, cid):
    rows, width = x.shape
    any_ = pl.BlockSpec(memory_space=pl.ANY)
    vm = pl.BlockSpec(memory_space=pltpu.VMEM)
    dma = pltpu.SemaphoreType.DMA
    act = (rows, width)
    own = wq.shape[0]
    kvw = 2 * KV_HEADS * HEAD_DIM
    wide = width + kvw
    sds = jax.ShapeDtypeStruct
    VM = pltpu.VMEM
    return pl.pallas_call(
        functools.partial(front_kernel, block),
        out_shape=[sds(act, BF), sds(act, BF), sds(act, F32), sds(act, F32), sds(act, BF), sds((8, wide), F32),
                   sds((16 * own, 3 * MAIN + 256), BF), sds((16, own, wide), BF), sds((16, rows, kvw), BF), sds((16,) + act, BF), sds((16,) + wo.shape, BF)],
        in_specs=[pl.BlockSpec(memory_space=pltpu.SMEM)] + [vm] * 7 + [any_] * 10,
        out_specs=[vm] * 6 + [any_] * 5,
        scratch_shapes=[VM((own, wide), BF), VM((16, own, wide), BF), VM((16,) + small.shape, F32), VM((rows, kvw), BF), VM((16, rows, kvw), BF), VM((16,) + wo.shape, BF)]
        + [dma((34,)), dma((32,)), dma(())] + [dma((18,)), dma((16,)), dma(())] * 3 + [dma((34,)), dma((32,)), dma(())]
        + [dma((16,))] * 4 + [dma(()), dma((6,))],
        compiler_params=pltpu.CompilerParams(collective_id=cid, has_side_effects=True, vmem_limit_bytes=60 * 2**20),
    )(lens, x, cos, sin, sel, fold, selk, foldk, small, wq, wk, wv, wg, wu, wd, rem, cot, wo)


class Return:
    def __init__(self, at, half_ref, main, spare, send, recv, ysend, yrecv, local):
        self.r, self.z, self.x, self.c = at
        self.me = idx(self.z, self.x, self.c)
        self.src, self.main, self.spare = half_ref, main, spare
        self.send, self.recv, self.ysend, self.yrecv, self.local = send, recv, ysend, yrecv, local
        self.n = half_ref.shape[1]
    def places(self, j, h):
        row = pl.ds(pl.multiple_of(h * self.n, self.n), self.n)
        col = pl.ds(pl.multiple_of(j * MAIN, MAIN), MAIN)
        return [self.main.at[i, row, col] for i in range(3)] + [self.spare.at[j, row]]
    def parts(self, j):
        return [self.src.at[j, :, pl.ds(i * MAIN, MAIN)] for i in range(3)] + [self.src.at[j, :, pl.ds(3 * MAIN, 256)]]
    def launch(self, k):
        j = jnp.bitwise_xor(self.me, k)
        for a, b in zip(self.parts(j), self.places(self.me, self.r)):
            pltpu.make_async_remote_copy(a, b, self.send.at[k], self.recv.at[k], device_id=(self.r, j), device_id_type=MESH).start()
    def forward(self, j, k):
        for a in self.places(j, self.r):
            pltpu.make_async_remote_copy(a, a, self.ysend.at[k], self.yrecv.at[k], device_id=(1 - self.r, self.me), device_id_type=MESH).start()
    def begin(self, window):
        self.window = window
        for a, b in zip(self.parts(self.me), self.places(self.me, self.r)):
            pltpu.make_async_copy(a, b, self.local).start()
        for k in KS[:window]:
            self.launch(k)
    def whole(self, send, recv):
        blk = self.src.at[0]
        return pltpu.make_async_remote_copy(blk, blk, send, recv, device_id=(1 - self.r, self.me), device_id_type=MESH)
    def own(self):
        pltpu.make_async_copy(self.src.at[0], self.src.at[0], self.local).wait()
        self.forward(self.me, 0)
    def step(self, i):
        k = KS[i]
        self.whole(self.send.at[k], self.recv.at[k]).wait_recv()
        self.forward(jnp.bitwise_xor(self.me, k), k)
        if i + self.window < 15:
            self.launch(KS[i + self.window])
    def end(self):
        for k in (0,) + KS:
            self.whole(self.ysend.at[k], self.yrecv.at[k]).wait()
            if k:
                self.whole(self.send.at[k], self.recv.at[k]).wait_send()

def norm_gradient(v, gain, upstream):
    factor = lax.rsqrt(jnp.mean(v * v, axis=-1, keepdims=True) + EPSILON)
    weighted = upstream * gain
    inner = jnp.mean(weighted * v, axis=-1, keepdims=True)
    return factor * weighted - v * (factor * factor * factor) * inner, jnp.sum(upstream * v * factor, axis=0, keepdims=True)

def backward_kernel(block, window, lens, gn2, mlp_out, mid, cot, x_ref, att, q_ref, normed, vec, cos_ref, sin_ref, valid, sel, fold, selk, foldk, kv_ref, wo_ref, wqkv_ref, half_ref,
                    layer_out, grad_input, q_out, pair_out, wo_out, vec_out, g_main, g_spare,
                    kv, wo, wqkv, gmid, branch, gatt, gqkv, pv,
                    p_kv, c_kv, x_kv, z_kv, p_wo, c_wo, x_wo, z_wo, p_qk, c_qk, x_qk, z_qk, p_pw, c_pw, x_pw, z_pw, p_ve, c_ve, x_ve, z_ve,
                    kvsum, y0, y1, y2, y3, y4, y5, y6, y7,
                    ss, sc, sx, sz, rs, rr, rys, ryr, rl, ysem, lsem):
    at = place()
    r, z, x, c = at
    width = HEADS * HEAD_DIM
    kw = KV_HEADS * HEAD_DIM
    loads = [pltpu.make_async_copy(a, b, lsem.at[i]) for i, (a, b) in enumerate(((wo_ref, wo), (kv_ref, kv), (wqkv_ref, wqkv)))]
    for l in loads: l.start()
    hail_all(*at)
    back = Return(at, half_ref, g_main, g_spare, rs, rr, rys, ryr, rl)
    back.begin(window)
    sets = ((p_kv, c_kv, x_kv, z_kv), (p_wo, c_wo, x_wo, z_wo), (p_qk, c_qk, x_qk, z_qk), (p_pw, c_pw, x_pw, z_pw), (p_ve, c_ve, x_ve, z_ve))
    ek, eo, eq, ep, ev = [Scatter(at, *b, ss.at[i], sc.at[i], sx.at[i], sz.at[i]) for i, b in enumerate(sets)]
    steps = iter(range(15))
    def some(n):
        for _ in range(n):
            i = next(steps, None)
            if i is not None:
                back.step(i)
    ydev = (1 - r, idx(z, x, c))
    def trade(i, out, a, b):
        a[...] = out[...].astype(BF)
        pltpu.make_async_remote_copy(a, b, ysem.at[2 * i], ysem.at[2 * i + 1], device_id=ydev, device_id_type=MESH).start()
    def traded(i, out, a, b):
        pltpu.make_async_remote_copy(a, b, ysem.at[2 * i], ysem.at[2 * i + 1], device_id=ydev, device_id_type=MESH).wait()
        out[...] = a[...].astype(F32) + b[...].astype(F32)

    grad_norm, gain_two = norm_gradient(mid[...], vec[2:3, :width], gn2[...])
    gmid[...] = cot[...].astype(F32) + grad_norm
    branch[...] = gmid[...].astype(BF)
    loads[0].wait()
    @pl.loop(0, 4)
    def _(t):
        blocks = pl.ds(pl.multiple_of(4 * t, 4), 4)
        col = pl.ds(pl.multiple_of(384 * t, 384), 384)
        low = att[:, col].astype(BF)
        p_wo[blocks] = dot_tn(low, branch[...]).astype(BF).reshape(4, 96, width)
        gatt[:, col] = dot_nt(branch[...], wo[blocks].reshape(384, width))
    eo.begin()
    eo.step_x(3)
    eo.step_x(2)
    back.own()
    layer_out[...] = ((mid[...] + mlp_out[...]) * valid[...]).astype(BF)
    loads[1].wait()
    first_row = lax.axis_index("group") * block
    span = 16 * block
    def unit(u):
        s, h = u // 2, lax.rem(u, 2)
        rows = pl.ds(pl.multiple_of(block * s, block), block)
        cols = pl.ds(pl.multiple_of(width // 2 * h, width // 2), width // 2)
        kcol = pl.ds(pl.multiple_of(HEAD_DIM * h, HEAD_DIM), HEAD_DIM)
        vcol = pl.ds(pl.multiple_of(kw + HEAD_DIM * h, HEAD_DIM), HEAD_DIM)
        q = stack_heads(q_ref[rows, cols])
        k = kv[:, rows, kcol].reshape(span, HEAD_DIM)
        v = kv[:, rows, vcol].reshape(span, HEAD_DIM)
        e = exp_scores(q, k, first_row, block, lens[s])
        total = jnp.sum(e, axis=-1, keepdims=True)
        ga = stack_heads(gatt[rows, cols])
        gt = -jnp.sum(ga * stack_heads(att[rows, cols]), axis=-1, keepdims=True) / total
        gn = (ga / total).astype(BF)
        gs = (e * (dot_nt(gn, v) + gt)).astype(BF)
        p_kv[:, rows, kcol] = dot_tn(gs, q).astype(BF).reshape(16, block, HEAD_DIM)
        p_kv[:, rows, vcol] = dot_tn(e.astype(BF), gn).astype(BF).reshape(16, block, HEAD_DIM)
        gq = dot(gs, k) * (HEAD_DIM ** -0.5)
        cos, sin = cos_ref[:block], sin_ref[:block]
        gqkv[rows, cols] = jnp.concatenate([spin(gq[block * i : block * (i + 1)], cos, -sin) for i in range(HEADS // KV_HEADS)], axis=1).astype(BF)
    unit(0)
    some(1)
    eo.step_z(3)
    eo.step_x(1)
    unit(1)
    some(1)
    eo.step_z(2)
    eo.step_x(0)
    unit(2)
    some(1)
    eo.step_z(1)
    unit(3)
    ek.begin()
    ek.step_x(3)
    ek.step_x(2)
    some(1)
    loads[2].wait()
    @pl.loop(0, 4)
    def _(t):
        blocks = pl.ds(pl.multiple_of(4 * t, 4), 4)
        col = pl.ds(pl.multiple_of(384 * t, 384), 384)
        p_qk[blocks] = dot_tn(normed[:, col], gqkv[:, :width]).astype(BF).reshape(4, 96, width)
    ek.step_z(3)
    ek.step_x(1)
    eq.begin()
    eo.finish(wo_out)
    trade(0, wo_out, y0, y1)
    ek.step_z(2)
    ek.step_x(0)
    eq.step_x(3)
    eq.step_x(2)
    some(1)
    @pl.loop(0, 4)
    def _(t):
        blocks = pl.ds(pl.multiple_of(4 * t, 4), 4)
        col = pl.ds(pl.multiple_of(384 * t, 384), 384)
        gatt[:, col] = dot_nt(gqkv[:, :width], wqkv[blocks, :, :width].reshape(384, width))
    ek.step_z(1)
    some(1)
    ek.finish(kvsum)
    cos, sin = cos_ref[...], sin_ref[...]
    for h in range(KV_HEADS):
        kcol = slice(HEAD_DIM * h, HEAD_DIM * (h + 1))
        gqkv[:, width + HEAD_DIM * h : width + HEAD_DIM * (h + 1)] = spin(kvsum[:, kcol] * (HEAD_DIM ** -0.5), cos, -sin).astype(BF)
    gqkv[:, width + kw :] = kvsum[:, kw:].astype(BF)
    @pl.loop(0, 4)
    def _(t):
        blocks = pl.ds(pl.multiple_of(4 * t, 4), 4)
        col = pl.ds(pl.multiple_of(384 * t, 384), 384)
        p_pw[blocks] = dot_tn(normed[:, col], gqkv[:, width:]).astype(BF).reshape(4, 96, 2 * kw)
        gatt[:, col] += dot_nt(gqkv[:, width:], wqkv[blocks, :, width:].reshape(384, 2 * kw))
    ep.begin()
    ep.step_x(3)
    ep.step_x(2)
    eq.step_z(3)
    eq.step_x(1)
    some(1)
    grad_norm, gain_one = norm_gradient(x_ref[...].astype(F32), vec[0:1, :width], gatt[...])
    grad_input[...] = gmid[...] + grad_norm
    bias = jnp.sum(gqkv[...].astype(F32), axis=0, keepdims=True)
    pv[...] = jnp.zeros_like(pv)
    for i, (v, a, b) in enumerate(((gain_one, sel, fold), (bias[:, :width], sel, fold), (bias[:, width : width + kw], selk, foldk), (bias[:, width + kw :], selk, foldk), (gain_two, sel, fold))):
        pv[:, i, :] = dot((a[...] * v).astype(BF), b[...])
    p_ve[...] = pv[...].astype(BF)
    ev.begin()
    ev.step_x(3)
    ev.step_x(2)
    some(1)
    late = (ep, ev)
    for kind, d in (("z", 3), ("x", 1), ("z", 2), ("x", 0), ("z", 1)):
        for e in late:
            (e.step_x if kind == "x" else e.step_z)(d)
        if (kind, d) not in (("z", 3), ("x", 1)):
            (eq.step_x if kind == "x" else eq.step_z)(d)
        some(1)
    some(15)
    eq.finish(q_out)
    trade(1, q_out, y2, y3)
    ep.finish(pair_out)
    trade(2, pair_out, y4, y5)
    ev.finish(vec_out)
    trade(3, vec_out, y6, y7)
    traded(0, wo_out, y0, y1)
    traded(1, q_out, y2, y3)
    traded(2, pair_out, y4, y5)
    traded(3, vec_out, y6, y7)
    back.end()

def backward(lens, gn2, mlp_out, mid, cot, x, att, q, normed, vec, cos, sin, valid, sel, fold, selk, foldk, kv, wo, wqkv, half, block, cid, window=4):
    any_ = pl.BlockSpec(memory_space=pl.ANY)
    vm = pl.BlockSpec(memory_space=pltpu.VMEM)
    dma = pltpu.SemaphoreType.DMA
    sds = jax.ShapeDtypeStruct
    rows, width = x.shape
    wide = wqkv.shape[-1]
    own = wo.shape[1]
    kvw = kv.shape[-1]
    VM = pltpu.VMEM
    def four(blk):
        return [VM((k,) + blk, BF) for k in (16, 8, 4, 5)]
    return pl.pallas_call(
        functools.partial(backward_kernel, block, window),
        out_shape=[sds((rows, width), BF), sds((rows, width), F32), sds((own, width), F32), sds((own, wide - width), F32), sds((own, width), F32), sds((16, 128), F32), sds((3, own, 16 * MAIN), BF), sds((16, own, 256), BF)],
        in_specs=[pl.BlockSpec(memory_space=pltpu.SMEM)] + [vm] * 16 + [any_] * 4,
        out_specs=[vm] * 6 + [any_] * 2,
        scratch_shapes=[VM(kv.shape, BF), VM(wo.shape, BF), VM(wqkv.shape, BF), VM((rows, width), F32), VM((rows, width), BF), VM((rows, width), F32), VM((rows, wide), BF), VM((16, 16, 128), F32)]
        + four((rows, kvw)) + four((own, width)) + four((own, width)) + four((own, wide - width)) + four((16, 128))
        + [VM((rows, kvw), F32)] + [VM((own, width), BF)] * 4 + [VM((own, wide - width), BF)] * 2 + [VM((16, 128), BF)] * 2
        + [dma((5, 16)), dma((5, 8)), dma((5, 4)), dma((5, 5))] + [dma((16,))] * 4 + [dma(()), dma((8,)), dma((3,))],
        compiler_params=pltpu.CompilerParams(collective_id=cid, has_side_effects=True, vmem_limit_bytes=60 * 2**20),
    )(lens, gn2, mlp_out, mid, cot, x, att, q, normed, vec, cos, sin, valid, sel, fold, selk, foldk, kv, wo, wqkv, half)


def spare_blocks(ff, main, spare):
    group_count = lax.axis_size("group")
    rows = ff[0].shape[0]
    ends = [w[:, main * group_count :].reshape(rows, group_count, spare) for w in ff]
    gap = jnp.zeros((rows, group_count, 128 - 2 * spare), BF)
    gap_down = jnp.zeros((rows, group_count, 128 - spare), BF)
    return jnp.transpose(
        jnp.concatenate([ends[0], ends[1], gap, ends[2], gap_down], axis=2), (1, 0, 2)
    )


def folding(group_count, width):
    share = width // group_count
    at = jnp.arange(width)
    sel = (at[None, :] // share == jnp.arange(group_count)[:, None]).astype(F32)
    fold = (at[:, None] % share == jnp.arange(128)[None, :]).astype(BF)
    return sel, fold


def shards_fast(
    hidden_in,
    lengths,
    gain_attn,
    w_query,
    b_query,
    w_key,
    b_key,
    w_value,
    b_value,
    w_out,
    gain_mlp,
    w_gate,
    w_up,
    w_down,
    cotangent,
):
    group_count = lax.axis_size("group")
    group_rank = lax.axis_index("group")
    slot_count, block_len, model_width = hidden_in.shape
    kv_width = KV_HEADS * HEAD_DIM
    tokens = slot_count * block_len
    hidden_units = w_gate.shape[1]
    own_rows = w_gate.shape[0]
    positions = group_rank * block_len + jnp.arange(block_len, dtype=jnp.int32)
    valid_rows = (positions[None, :] < lengths[:, None]).astype(F32).reshape(tokens, 1)
    cos_table, sin_table = rope_tables(positions, HEAD_DIM)
    turn = jnp.where(jnp.arange(HEAD_DIM) < HEAD_DIM // 2, -1.0, 1.0)
    cos_rows = jnp.tile(cos_table, (slot_count, 1))
    sin_rows = jnp.tile(sin_table * turn, (slot_count, 1))

    pieces = (gain_attn, b_query, b_key, b_value, gain_mlp)
    sizes = [p.shape[0] for p in pieces]
    small = jnp.stack([jnp.pad(p.astype(F32), (0, 128 - p.shape[0])) for p in pieces])
    small = jnp.pad(small, ((0, 8 - len(pieces)), (0, 0)))
    main = (hidden_units // 128 // group_count) * 128
    spare = hidden_units // group_count - main
    ff = (w_gate, w_up, w_down)
    sel, fold = folding(group_count, model_width)
    selk, foldk = folding(group_count, kv_width)
    rows_in = hidden_in.reshape(tokens, model_width)
    grad_final = (cotangent.reshape(tokens, model_width).astype(F32) * valid_rows).astype(BF)
    (
        q_rows, normed, attended, mid, normed_two, vec, columns, qkv_w, pair_all, grad_all, out_w
    ) = front(
        lengths,
        rows_in,
        cos_rows,
        sin_rows,
        sel,
        fold,
        selk,
        foldk,
        small,
        w_query,
        w_key,
        w_value,
        *ff,
        spare_blocks(ff, main, spare),
        grad_final,
        w_out,
        block_len,
        1,
    )
    grad_normed_two, mlp_out, half_sum = mlp(normed_two, grad_all, columns, spare, 3)
    layer_out, grad_input, query_sum, pair_sum, out_sum, vector_sum, main_sum, spare_sum = backward(
        lengths,
        grad_normed_two,
        mlp_out,
        mid,
        grad_final,
        rows_in,
        attended,
        q_rows,
        normed,
        vec,
        cos_rows,
        sin_rows,
        jnp.broadcast_to(valid_rows, (tokens, model_width)),
        sel,
        fold,
        selk,
        foldk,
        pair_all,
        out_w,
        qkv_w,
        half_sum,
        block_len,
        4,
    )
    ff_sums = [
        jnp.concatenate(
            (
                main_sum[i],
                jnp.transpose(spare_sum[:, :, at : at + spare], (1, 0, 2)).reshape(own_rows, -1),
            ),
            axis=1,
        ).astype(F32)
        for i, at in ((0, 0), (1, spare), (2, 128))
    ]
    gain_one_sum, query_bias_sum, key_bias_sum, value_bias_sum, gain_two_sum = [
        vector_sum[i, : sizes[i]] for i in range(len(sizes))
    ]
    return (
        layer_out.reshape(hidden_in.shape),
        grad_input.reshape(hidden_in.shape),
        gain_one_sum,
        query_sum,
        query_bias_sum,
        pair_sum[:, :kv_width],
        key_bias_sum,
        pair_sum[:, kv_width:],
        value_bias_sum,
        out_sum,
        gain_two_sum,
        *ff_sums,
    )


def solution(mesh):
    act = P("replica", "group", None)
    vec = P("group")
    mat = P("group", None)
    return jax.shard_map(
        shards_fast if mesh.shape["group"] == 16 else shards_plain,
        mesh=mesh,
        in_specs=(act, P("replica"), vec, mat, vec, mat, vec, mat, vec, mat, vec, mat, mat, mat, act),
        out_specs=(act, act, vec, mat, vec, mat, vec, mat, vec, mat, vec, mat, mat, mat),
        check_vma=False,
    )
```

```python
import functools

import jax
import jax.numpy as jnp
import numpy as np
from jax import lax
from jax.experimental import pallas as pl
from jax.experimental.pallas import tpu as pltpu
from jax.sharding import PartitionSpec as P

MESH = pl.DeviceIdType.MESH
NZ = 4
MAIN = 512
D = 1536
COLS = 3 * MAIN + 384
HEADS = 12
KV_HEADS = 2
HEAD_DIM = 128
EPSILON = 1e-06
THETA = 1000000.0
BF = jnp.bfloat16
F32 = jnp.float32


def rope_tables(positions, head_dim):
    freqs = THETA ** (-jnp.arange(0, head_dim, 2).astype(F32) / head_dim)
    angles = positions.astype(F32)[:, None] * freqs[None, :]
    angles = jnp.concatenate((angles, angles), axis=-1)
    return (jnp.cos(angles), jnp.sin(angles))


def rotate(tensor, cos_table, sin_table):
    halfway = tensor.shape[-1] // 2
    turned = jnp.concatenate((-tensor[..., halfway:], tensor[..., :halfway]), axis=-1)
    return tensor * cos_table + turned * sin_table


def rotate_back(gradient, cos_table, sin_table):
    halfway = gradient.shape[-1] // 2
    scaled = gradient * sin_table
    turned = jnp.concatenate((scaled[..., halfway:], -scaled[..., :halfway]), axis=-1)
    return gradient * cos_table + turned


def normalize(row_values, gain_vec):
    factor = lax.rsqrt(jnp.mean(row_values * row_values, axis=-1, keepdims=True) + EPSILON)
    return (row_values * factor * gain_vec, factor)


def norm_back(row_values, factor, gain_vec, upstream):
    weighted = upstream * gain_vec
    inner_mean = jnp.mean(weighted * row_values, axis=-1, keepdims=True)
    grad_rows = factor * weighted - row_values * (factor * factor * factor) * inner_mean
    grad_gain = jnp.sum(upstream * row_values * factor, axis=0)
    return (grad_rows, grad_gain)


def matmul(a, b):
    return jnp.dot(a, b, preferred_element_type=F32)


def matmul_nt(a, b):
    return lax.dot_general(a, b, (((1,), (1,)), ((), ())), preferred_element_type=F32)


def matmul_tn(a, b):
    return lax.dot_general(a, b, (((0,), (0,)), ((), ())), preferred_element_type=F32)


def arrange(per_token, kv_heads):
    block_len, head_count, head_dim = per_token.shape
    repeat = head_count // kv_heads
    grouped = per_token.reshape(block_len, kv_heads, repeat, head_dim)
    return jnp.transpose(grouped, (1, 2, 0, 3)).reshape(kv_heads, repeat * block_len, head_dim)


def restore(per_group, block_len):
    kv_heads, row_count, head_dim = per_group.shape
    repeat = row_count // block_len
    grouped = per_group.reshape(kv_heads, repeat, block_len, head_dim)
    return jnp.transpose(grouped, (2, 0, 1, 3)).reshape(block_len, kv_heads * repeat * head_dim)


def masked_exp(query_rows, key_block, row_pos, first_key, length, score_scale):
    key_step = key_block.shape[0]
    raw_scores = jnp.einsum("grd,kgd->grk", query_rows, key_block, preferred_element_type=F32)
    key_pos = first_key + jnp.arange(key_step, dtype=jnp.int32)
    allowed = (key_pos[None, :] <= row_pos[:, None]) & (key_pos[None, :] < length)
    return jnp.where(allowed[None], jnp.exp(raw_scores * score_scale), 0.0)


def block_total(length, rank_end, key_step):
    key_limit = jnp.minimum(length, rank_end)
    return (key_limit + key_step - 1) // key_step


def attend_forward(query_rows, key_all, value_all, row_pos, length, rank_end, key_step, scale):
    kv_heads, row_count, head_dim = query_rows.shape

    def visit(block_index, state_tuple):
        totals, numerator = state_tuple
        first_key = block_index * key_step
        key_block = lax.dynamic_slice_in_dim(key_all, first_key, key_step, 0)
        value_block = lax.dynamic_slice_in_dim(value_all, first_key, key_step, 0)
        weights = masked_exp(query_rows, key_block, row_pos, first_key, length, scale)
        totals = totals + jnp.sum(weights, axis=-1)
        numerator = numerator + jnp.einsum(
            "grk,kgd->grd", weights.astype(BF), value_block, preferred_element_type=F32
        )
        return (totals, numerator)

    initial = (
        jnp.zeros((kv_heads, row_count), F32),
        jnp.zeros((kv_heads, row_count, head_dim), F32),
    )
    return lax.fori_loop(0, block_total(length, rank_end, key_step), visit, initial)


def attend_backward(
    query_rows, key_all, value_all, row_pos, length, rank_end, key_step, scale, grad_numer, grad_total
):
    kv_heads, row_count, head_dim = query_rows.shape

    def visit(block_index, state_tuple):
        grad_query, grad_key, grad_value = state_tuple
        first_key = block_index * key_step
        key_block = lax.dynamic_slice_in_dim(key_all, first_key, key_step, 0)
        value_block = lax.dynamic_slice_in_dim(value_all, first_key, key_step, 0)
        weights = masked_exp(query_rows, key_block, row_pos, first_key, length, scale)
        grad_prob = jnp.einsum("grd,kgd->grk", grad_numer, value_block, preferred_element_type=F32)
        grad_score = (weights * (grad_prob + grad_total[..., None])).astype(BF)
        grad_query = grad_query + jnp.einsum(
            "grk,kgd->grd", grad_score, key_block, preferred_element_type=F32
        )
        key_part = jnp.einsum("grk,grd->kgd", grad_score, query_rows, preferred_element_type=F32)
        value_part = jnp.einsum(
            "grk,grd->kgd", weights.astype(BF), grad_numer, preferred_element_type=F32
        )
        key_old = lax.dynamic_slice_in_dim(grad_key, first_key, key_step, 0)
        value_old = lax.dynamic_slice_in_dim(grad_value, first_key, key_step, 0)
        grad_key = lax.dynamic_update_slice_in_dim(grad_key, key_old + key_part, first_key, 0)
        grad_value = lax.dynamic_update_slice_in_dim(
            grad_value, value_old + value_part, first_key, 0
        )
        return (grad_query, grad_key, grad_value)

    initial = (
        jnp.zeros((kv_heads, row_count, head_dim), F32),
        jnp.zeros(key_all.shape, F32),
        jnp.zeros(value_all.shape, F32),
    )
    return lax.fori_loop(0, block_total(length, rank_end, key_step), visit, initial)


def gather_plain(x):
    return lax.all_gather(x, "group", axis=0, tiled=True)


def scatter_sum(x):
    return lax.psum_scatter(x, "group", scatter_dimension=0, tiled=True)


def shards_plain(
    hidden_in,
    lengths,
    gain_attn,
    w_query,
    b_query,
    w_key,
    b_key,
    w_value,
    b_value,
    w_out,
    gain_mlp,
    w_gate,
    w_up,
    w_down,
    cotangent,
):
    group_count = lax.axis_size("group")
    group_rank = lax.axis_index("group")
    slot_count, block_len, model_width = hidden_in.shape
    kv_heads = KV_HEADS
    head_dim = HEAD_DIM
    kv_width = kv_heads * head_dim
    repeat = HEADS // kv_heads
    slot_span = block_len * group_count
    key_step = min(512, slot_span)
    score_scale = head_dim ** (-0.5)
    tokens = slot_count * block_len
    hidden_units = w_gate.shape[1]
    own_rows = w_gate.shape[0]
    share = hidden_units // group_count
    positions = group_rank * block_len + jnp.arange(block_len, dtype=jnp.int32)
    valid_rows = (positions[None, :] < lengths[:, None]).astype(F32).reshape(tokens, 1)
    cos_table, sin_table = rope_tables(positions, head_dim)
    cos_heads = cos_table[:, None, :]
    sin_heads = sin_table[:, None, :]
    rank_end = (group_rank + 1) * block_len
    row_pos = jnp.tile(positions, repeat)

    pieces = (gain_attn, b_query, b_key, b_value, gain_mlp)
    sizes = [p.shape[0] for p in pieces]
    small = gather_plain(jnp.concatenate(pieces)[None])
    offsets = [sum(sizes[:i]) for i in range(len(sizes) + 1)]
    gain_one, query_b, key_b, value_b, gain_two = [
        small[:, offsets[i] : offsets[i + 1]].reshape(-1).astype(F32) for i in range(len(sizes))
    ]
    qkv_w = gather_plain(jnp.concatenate((w_query, w_key, w_value), axis=1))
    out_w = gather_plain(w_out)
    qkv_b = jnp.concatenate((query_b, key_b, value_b))

    stacked = jnp.stack((w_gate, w_up, w_down)).reshape(3, own_rows, group_count, share)
    stacked = jnp.transpose(stacked, (2, 1, 0, 3)).reshape(group_count, own_rows, 3 * share)
    columns = lax.all_to_all(stacked, "group", 0, 0, tiled=True).reshape(model_width, 3 * share)
    gate_up_w = columns[:, : 2 * share]
    down_w = columns[:, 2 * share :]

    grad_final = cotangent.reshape(tokens, model_width).astype(F32) * valid_rows
    grad_all = gather_plain(grad_final.astype(BF))

    inputs = hidden_in.reshape(tokens, model_width).astype(F32)
    normed_full, factor_one = normalize(inputs, gain_one)
    normed = normed_full.astype(BF)
    qkv = matmul(normed, qkv_w) + qkv_b
    query_rot = rotate(
        qkv[:, :model_width].reshape(slot_count, block_len, HEADS, head_dim), cos_heads, sin_heads
    ).astype(BF)
    key_rot = rotate(
        qkv[:, model_width : model_width + kv_width].reshape(
            slot_count, block_len, kv_heads, head_dim
        ),
        cos_heads,
        sin_heads,
    ).astype(BF)
    value_low = qkv[:, model_width + kv_width :].astype(BF)
    pair = jnp.concatenate(
        (key_rot.reshape(tokens, kv_width), value_low), axis=1
    ).reshape(1, slot_count, block_len, 2 * kv_width)
    pair_all = jnp.transpose(gather_plain(pair), (1, 0, 2, 3)).reshape(
        slot_count, slot_span, 2, kv_heads, head_dim
    )
    key_all = pair_all[:, :, 0]
    value_all = pair_all[:, :, 1]
    query_groups = []
    slot_totals = []
    slot_attended = []
    attended_rows = []
    for s in range(slot_count):
        query_rows = arrange(query_rot[s], kv_heads)
        totals, numerator = attend_forward(
            query_rows, key_all[s], value_all[s], row_pos, lengths[s], rank_end, key_step, score_scale
        )
        attended = numerator / totals[..., None]
        query_groups.append(query_rows)
        slot_totals.append(totals)
        slot_attended.append(attended)
        attended_rows.append(restore(attended, block_len))
    attended_low = jnp.concatenate(attended_rows, axis=0).astype(BF)
    residual_mid = inputs + matmul(attended_low, out_w)
    normed_two_full, factor_two = normalize(residual_mid, gain_two)
    normed_all = gather_plain(normed_two_full.astype(BF))

    pre = matmul(normed_all, gate_up_w)
    gate_pre = pre[:, :share]
    up_pre = pre[:, share:]
    sigmoid_gate = jax.nn.sigmoid(gate_pre)
    silu_gate = gate_pre * sigmoid_gate
    hidden = (silu_gate * up_pre).astype(BF)
    grad_hidden = matmul(grad_all, down_w)
    grad_gate = (
        grad_hidden * up_pre * (sigmoid_gate * (1.0 + gate_pre * (1.0 - sigmoid_gate)))
    ).astype(BF)
    grad_up = (grad_hidden * silu_gate).astype(BF)
    gate_up_grad = jnp.concatenate((grad_gate, grad_up), axis=1)
    grad_normed_two = scatter_sum(matmul_nt(gate_up_grad, gate_up_w).astype(BF)).astype(F32)
    mlp_out = scatter_sum(matmul_nt(hidden, down_w).astype(BF)).astype(F32)
    down_term = matmul_tn(grad_all, hidden)
    gate_up_term = matmul_tn(normed_all, gate_up_grad)
    terms = jnp.concatenate((gate_up_term, down_term), axis=1).astype(BF)
    back = lax.all_to_all(
        terms.reshape(group_count, own_rows, 3 * share), "group", 0, 0, tiled=True
    )
    summed = back.astype(F32) + lax.ppermute(back, "replica", [(0, 1), (1, 0)]).astype(F32)
    summed = jnp.transpose(summed.reshape(group_count, own_rows, 3, share), (2, 1, 0, 3))
    gate_sum, up_sum, down_sum = summed.reshape(3, own_rows, hidden_units)

    final_rows = residual_mid + mlp_out
    layer_out = (final_rows * valid_rows).reshape(slot_count, block_len, model_width).astype(BF)
    grad_mid_norm, grad_gain_two = norm_back(residual_mid, factor_two, gain_two, grad_normed_two)
    grad_mid = grad_final + grad_mid_norm
    grad_branch = grad_mid.astype(BF)
    out_term = matmul_tn(attended_low, grad_branch)
    grad_attended = matmul_nt(grad_branch, out_w)
    grad_query_rows = []
    grad_pairs = []
    for s in range(slot_count):
        slot_grad = grad_attended[s * block_len : (s + 1) * block_len].reshape(
            block_len, HEADS, head_dim
        )
        grad_out = arrange(slot_grad, kv_heads)
        totals = slot_totals[s]
        grad_total = -jnp.sum(grad_out * slot_attended[s], axis=-1) / totals
        grad_numer = (grad_out / totals[..., None]).astype(BF)
        grad_query, grad_key, grad_value = attend_backward(
            query_groups[s],
            key_all[s],
            value_all[s],
            row_pos,
            lengths[s],
            rank_end,
            key_step,
            score_scale,
            grad_numer,
            grad_total,
        )
        query_back_rows = restore(grad_query * score_scale, block_len).reshape(
            block_len, HEADS, head_dim
        )
        grad_query_rows.append(
            rotate_back(query_back_rows, cos_heads, sin_heads).reshape(block_len, HEADS * head_dim)
        )
        grad_pairs.append(
            jnp.concatenate(
                (grad_key.reshape(slot_span, kv_width), grad_value.reshape(slot_span, kv_width)),
                axis=1,
            )
        )
    pair_grads = jnp.stack(grad_pairs).reshape(slot_count, group_count, block_len, 2 * kv_width)
    pair_grads = jnp.transpose(pair_grads, (1, 0, 2, 3)).astype(BF)
    pair_sum = scatter_sum(pair_grads).reshape(slot_count, block_len, 2 * kv_width).astype(F32)
    grad_query_pre = jnp.concatenate(grad_query_rows, axis=0).astype(BF)
    key_sum = pair_sum[..., :kv_width].reshape(slot_count, block_len, kv_heads, head_dim)
    grad_key_pre = (
        rotate_back(key_sum * score_scale, cos_heads, sin_heads).astype(BF).reshape(tokens, kv_width)
    )
    grad_value_pre = pair_sum[..., kv_width:].astype(BF).reshape(tokens, kv_width)
    grad_qkv = jnp.concatenate((grad_query_pre, grad_key_pre, grad_value_pre), axis=1)
    grad_normed = matmul_nt(grad_qkv, qkv_w)
    grad_in_norm, grad_gain_one = norm_back(inputs, factor_one, gain_one, grad_normed)
    grad_input = (grad_mid + grad_in_norm).reshape(slot_count, block_len, model_width)
    qkv_term = matmul_tn(normed, grad_qkv)
    qkv_bias = jnp.sum(grad_qkv.astype(F32), axis=0)

    weight_share = scatter_sum(
        jnp.concatenate((qkv_term, out_term), axis=1).astype(BF)
    )
    weight_sum = weight_share.astype(F32) + lax.ppermute(
        weight_share, "replica", [(0, 1), (1, 0)]
    ).astype(F32)
    vectors = jnp.concatenate(
        [
            grad_gain_one.reshape(group_count, -1),
            qkv_bias[:model_width].reshape(group_count, -1),
            qkv_bias[model_width : model_width + kv_width].reshape(group_count, -1),
            qkv_bias[model_width + kv_width :].reshape(group_count, -1),
            grad_gain_two.reshape(group_count, -1),
        ],
        axis=1,
    )
    vector_sum = lax.psum(scatter_sum(vectors), "replica").reshape(-1)
    gain_one_sum, query_bias_sum, key_bias_sum, value_bias_sum, gain_two_sum = [
        vector_sum[offsets[i] : offsets[i + 1]] for i in range(len(sizes))
    ]
    ends = (0, model_width, model_width + kv_width, model_width + 2 * kv_width)
    query_sum, key_sum_w, value_sum_w = [weight_sum[:, ends[i] : ends[i + 1]] for i in range(3)]
    out_sum = weight_sum[:, ends[3] :]
    return (
        layer_out,
        grad_input,
        gain_one_sum,
        query_sum,
        query_bias_sum,
        key_sum_w,
        key_bias_sum,
        value_sum_w,
        value_bias_sum,
        out_sum,
        gain_two_sum,
        gate_sum,
        up_sum,
        down_sum,
    )


def place():
    g = lax.axis_index("group")
    r = lax.axis_index("replica")
    return r, g // 4, lax.rem(g // 2, 2), lax.rem(g, 2)

def idx(z, x, c):
    return (z * 2 + x) * 2 + c

def greet(r, z, x, c, with_y=False):
    bar = pltpu.get_barrier_semaphore()
    def hail(dev):
        pl.semaphore_signal(bar, inc=1, device_id=dev, device_id_type=MESH)
    hail((r, idx(z, 1 - x, c)))
    hail((r, idx(z, x, 1 - c)))
    if with_y:
        hail((1 - r, idx(z, x, c)))
    @pl.when(z > 0)
    def _():
        hail((r, idx(z - 1, x, c)))
    @pl.when(z < NZ - 1)
    def _():
        hail((r, idx(z + 1, x, c)))
    ends = jnp.where((z > 0) & (z < NZ - 1), 1, 0)
    pl.semaphore_wait(bar, (4 if with_y else 3) + ends)

def planes(z):
    return (
        z,
        jnp.where(z == 0, 1, jnp.where(z == 1, 0, jnp.where(z == 2, 3, 2))),
        jnp.where(z == 0, 2, jnp.where(z == 1, 2, 1)),
        jnp.where(z < 2, 3, 0),
    )

def when(cond, fn):
    pl.when(cond)(fn)

class Gather:
    def __init__(self, at, src, out, send, recv, local):
        self.r, self.z, self.x, self.c = at
        self.src, self.out, self.send, self.recv, self.local = src, out, send, recv, local
        self.mid = (self.z > 0) & (self.z < NZ - 1)
        self.p = planes(self.z)
    def put(self, src, b, k, dev):
        pltpu.make_async_remote_copy(src, self.out.at[b], self.send.at[k], self.recv.at[b], device_id=dev, device_id_type=MESH).start()
    def sent(self, k):
        b = 0
        pltpu.make_async_remote_copy(self.out.at[b], self.out.at[b], self.send.at[k], self.recv.at[b], device_id=(self.r, 0), device_id_type=MESH).wait_send()
    def got(self, b):
        pltpu.make_async_remote_copy(self.out.at[b], self.out.at[b], self.send.at[0], self.recv.at[b], device_id=(self.r, 0), device_id_type=MESH).wait_recv()
    def zdev(self, s): return (self.r, idx(self.z + s, self.x, self.c))
    def xdev(self): return (self.r, idx(self.z, 1 - self.x, self.c))
    def cdev(self): return (self.r, idx(self.z, self.x, 1 - self.c))
    def begin(self):
        z, x, c = self.z, self.x, self.c
        me = idx(z, x, c)
        for s in (1, -1):
            when(self.inside(z + s), lambda s=s: self.put(self.src, me, 0 if s == 1 else 3, self.zdev(s)))
        self.put(self.src, me, 6 + z, self.xdev())
        self.put(self.src, me, 10 + 2 * z + x, self.cdev())
        pltpu.make_async_copy(self.src, self.out.at[me], self.local).start()
    def inside(self, z): return (z >= 0) & (z < NZ)
    def from_z(self, zz):
        z, x, c = self.z, self.x, self.c
        b = idx(zz, x, c)
        self.got(b)
        s = jnp.where(zz < z, 1, -1)
        d = jnp.abs(zz - z)
        slot = jnp.where(zz < z, 0, 3) + d
        when(self.inside(z + s), lambda: self.put(self.out.at[b], b, slot, (self.r, idx(z + s, x, c))))
        self.put(self.out.at[b], b, 6 + zz, self.xdev())
        self.put(self.out.at[b], b, 10 + 2 * zz + x, self.cdev())
    def first(self):
        self.from_z(self.p[1])
        when(self.mid, lambda: self.from_z(self.p[2]))
        self.from_x(self.p[0])
    def second(self):
        self.from_z(jnp.where(self.mid, self.p[3], self.p[2]))
        self.from_x(self.p[1])
    def third(self):
        when(~self.mid, lambda: self.from_z(self.p[3]))
        self.from_x(self.p[2])
    def fourth(self):
        self.from_x(self.p[3])
    def from_x(self, zz):
        b = idx(zz, 1 - self.x, self.c)
        self.got(b)
        self.put(self.out.at[b], b, 10 + 2 * zz + 1 - self.x, self.cdev())
    def from_c(self, zz):
        self.got(idx(zz, self.x, 1 - self.c))
        self.got(idx(zz, 1 - self.x, 1 - self.c))
    def end(self, local=True):
        z = self.z
        for d in range(NZ - 1):
            when((z - d >= 0) & (z < NZ - 1), lambda d=d: self.sent(d))
            when((z + d < NZ) & (z > 0), lambda d=d: self.sent(3 + d))
        for k in range(6, 18):
            self.sent(k)
        if local:
            pltpu.make_async_copy(self.src, self.out.at[0], self.local).wait()

class Scatter:
    def __init__(self, at, part, rc, rx, rz, send, rcs, rxs, rzs):
        self.r, self.z, self.x, self.c = at
        self.part, self.rc, self.rx, self.rz = part, rc, rx, rz
        self.send, self.rcs, self.rxs, self.rzs = send, rcs, rxs, rzs
    def inside(self, z): return (z >= 0) & (z < NZ)
    def copy(self, src, dst, k, rs, dev):
        return pltpu.make_async_remote_copy(src, dst, self.send.at[k], rs, device_id=dev, device_id_type=MESH)
    def over(self, d):
        return [(s, self.z + s * d) for s in ((-1, 1) if d else (1,))]
    def begin(self, far_first=True):
        z, x, c = self.z, self.x, self.c
        dev = (self.r, idx(z, x, 1 - c))
        for xx in (1 - x, x):
            for d in range(NZ - 1, -1, -1):
                for s, zz in self.over(d):
                    k = 2 * zz + xx
                    when(self.inside(zz), lambda zz=zz, k=k, xx=xx: self.copy(self.part.at[idx(zz, xx, 1 - c)], self.rc.at[k], k, self.rcs.at[k], dev).start())
    def send_c(self, zz):
        z, x, c = self.z, self.x, self.c
        dev = (self.r, idx(z, x, 1 - c))
        for xx in (1 - x, x):
            k = 2 * zz + xx
            self.copy(self.part.at[idx(zz, xx, 1 - c)], self.rc.at[k], k, self.rcs.at[k], dev).start()
    def step_x(self, d):
        z, x, c = self.z, self.x, self.c
        dev = (self.r, idx(z, 1 - x, c))
        for s, zz in self.over(d):
            def go(zz=zz):
                k = 2 * zz + 1 - x
                b = idx(zz, 1 - x, c)
                self.copy(self.rc.at[k], self.rc.at[k], 0, self.rcs.at[k], dev).wait_recv()
                self.part[b] = (self.part[b].astype(F32) + self.rc[k].astype(F32)).astype(BF)
                self.copy(self.part.at[b], self.rx.at[zz], 8 + zz, self.rxs.at[zz], dev).start()
            when(self.inside(zz), go)
    def step_z(self, d):
        z, x, c = self.z, self.x, self.c
        for s, zz in self.over(d):
            def go(zz=zz, s=s):
                k = 2 * zz + x
                b = idx(zz, x, c)
                self.copy(self.rc.at[k], self.rc.at[k], 0, self.rcs.at[k], (self.r, 0)).wait_recv()
                self.copy(self.rx.at[zz], self.rx.at[zz], 0, self.rxs.at[zz], (self.r, 0)).wait_recv()
                both = self.part[b].astype(F32) + self.rc[k].astype(F32) + self.rx[zz].astype(F32)
                dev = (self.r, idx(z + s, x, c))
                slot = jnp.where(zz == z + s, NZ, zz) if s == -1 else zz
                self.part[b] = both.astype(BF)
                def more():
                    self.copy(self.rz.at[zz], self.rz.at[zz], 0, self.rzs.at[zz], dev).wait_recv()
                    self.part[b] = (self.part[b].astype(F32) + self.rz[zz].astype(F32)).astype(BF)
                when(self.inside(z - s), more)
                self.copy(self.part.at[b], self.rz.at[slot], 12 + zz, self.rzs.at[slot], dev).start()
            when(self.inside(zz), go)
    def finish(self, out):
        z, x, c = self.z, self.x, self.c
        k = 2 * z + x
        b = idx(z, x, c)
        self.copy(self.rc.at[k], self.rc.at[k], 0, self.rcs.at[k], (self.r, 0)).wait_recv()
        self.copy(self.rx.at[z], self.rx.at[z], 0, self.rxs.at[z], (self.r, 0)).wait_recv()
        out[...] = self.part[b].astype(F32) + self.rc[k].astype(F32) + self.rx[z].astype(F32)
        def lo():
            self.copy(self.rz.at[z], self.rz.at[z], 0, self.rzs.at[z], (self.r, 0)).wait_recv()
            out[...] += self.rz[z].astype(F32)
        when(z > 0, lo)
        def hi():
            self.copy(self.rz.at[NZ], self.rz.at[NZ], 0, self.rzs.at[NZ], (self.r, 0)).wait_recv()
            out[...] += self.rz[NZ].astype(F32)
        when(z < NZ - 1, hi)
        for k in range(8):
            self.copy(self.part.at[0], self.part.at[0], k, self.rcs.at[0], (self.r, 0)).wait_send()
        for k in range(8, 12):
            self.copy(self.part.at[0], self.part.at[0], k, self.rcs.at[0], (self.r, 0)).wait_send()
        for zz in range(NZ):
            when(z != zz, lambda zz=zz: self.copy(self.part.at[0], self.part.at[0], 12 + zz, self.rcs.at[0], (self.r, 0)).wait_send())


KS = (8, 1, 9, 2, 10, 3, 11, 4, 12, 5, 13, 6, 14, 7, 15)
WINDOW = 4

def has(j):
    return lax.rem(j, 3) == 0

def spare_at(j):
    return pl.ds(pl.multiple_of(16 * MAIN + 128 * (j // 3), 128), 128)

class Deal:
    def __init__(self, at, ws, buf, sems, local):
        self.r, self.z, self.x, self.c = at
        self.me = idx(self.z, self.x, self.c)
        self.ws, self.buf, self.sems, self.local = ws, buf, sems, local
        self.n = ws[0].shape[0] // 2
    def rows(self, j, h):
        return pl.ds(pl.multiple_of((2 * j + h) * self.n, self.n), self.n)
    def block(self, j, h, spare):
        return self.buf.at[self.rows(j, h), pl.ds(3 * MAIN, 384) if spare else pl.ds(0, 3 * MAIN)]
    def copy(self, a, b, kind, k, dev):
        send, recv = self.sems[2 * kind : 2 * kind + 2]
        return pltpu.make_async_remote_copy(a, b, send.at[k], recv.at[k], device_id=dev, device_id_type=MESH)
    def launch(self, k):
        r, me, n = self.r, self.me, self.n
        row = pl.ds(pl.multiple_of(r * n, n), n)
        j = jnp.bitwise_xor(me, k)
        dst = self.rows(me, r)
        for i in range(3):
            self.copy(self.ws[i].at[row, pl.ds(pl.multiple_of(j * MAIN, MAIN), MAIN)], self.buf.at[dst, pl.ds(i * MAIN, MAIN)], 0, k, (r, j)).start()
        def spare():
            for i in range(3):
                self.copy(self.ws[i].at[row, spare_at(j)], self.buf.at[dst, pl.ds(3 * MAIN + 128 * i, 128)], 1, k, (r, j)).start()
        when(has(j), spare)
    def locals(self, spare):
        me, n = self.me, self.n
        row = pl.ds(pl.multiple_of(2 * me * n, 2 * n), 2 * n)
        col = spare_at(me) if spare else pl.ds(pl.multiple_of(me * MAIN, MAIN), MAIN)
        for i in range(3):
            to = pl.ds(3 * MAIN + 128 * i, 128) if spare else pl.ds(i * MAIN, MAIN)
            yield pltpu.make_async_copy(self.ws[i].at[:, col], self.buf.at[row, to], self.local.at[1 if spare else 0])
    def begin(self):
        for k in KS[:WINDOW]:
            self.launch(k)
        for l in self.locals(False):
            l.start()
        def spare():
            for l in self.locals(True):
                l.start()
        when(has(self.me), spare)
    def step(self, i):
        k = KS[i]
        r, me = self.r, self.me
        j = jnp.bitwise_xor(me, k)
        dev = (1 - r, me)
        def pass_on(spare):
            blk = self.block(j, r, spare)
            self.copy(blk, blk, spare, k, dev).wait_recv()
            self.copy(blk, blk, 2 + spare, k, dev).start()
        pass_on(0)
        when(has(me), lambda: pass_on(1))
        if i + WINDOW < 15:
            self.launch(KS[i + WINDOW])
    def end(self):
        r, me, n = self.r, self.me, self.n
        dev = (1 - r, me)
        for k in KS:
            j = jnp.bitwise_xor(me, k)
            def done(spare):
                blk = self.block(j, 1 - r, spare)
                self.copy(blk, blk, 2 + spare, k, dev).wait()
            def sent(spare):
                blk = self.block(j, r, spare)
                self.copy(blk, blk, spare, k, dev).wait_send()
            done(0)
            sent(0)
            when(has(me), lambda: done(1))
            when(has(j), lambda: sent(1))
        row = pl.ds(pl.multiple_of(2 * me * n, 2 * n), 2 * n)
        def own(spare):
            blk = self.buf.at[row, pl.ds(3 * MAIN, 384) if spare else pl.ds(0, 3 * MAIN)]
            pltpu.make_async_copy(blk, blk, self.local.at[spare]).wait()
        own(0)
        when(has(me), lambda: own(1))

def hail_all(r, z, x, c):
    bar = pltpu.get_barrier_semaphore()
    me = idx(z, x, c)
    for k in range(1, 16):
        pl.semaphore_signal(bar, inc=1, device_id=(r, lax.rem(me + k, 16)), device_id_type=MESH)
    pl.semaphore_signal(bar, inc=1, device_id=(1 - r, me), device_id_type=MESH)
    pl.semaphore_wait(bar, 16)


def dot(a, b):
    return lax.dot_general(a, b, (((1,), (0,)), ((), ())), preferred_element_type=F32)
def dot_nt(a, b):
    return lax.dot_general(a, b, (((1,), (1,)), ((), ())), preferred_element_type=F32)
def dot_tn(a, b):
    return lax.dot_general(a, b, (((0,), (0,)), ((), ())), preferred_element_type=F32)

def gated(g, u, gh):
    sig = jax.nn.sigmoid(g)
    silu = g * sig
    return (gh * u * (sig * (1.0 + g * (1.0 - sig)))).astype(BF), (gh * silu).astype(BF), (silu * u).astype(BF)

def mlp_kernel(n2_ref, cot_ref, w_ref, gsum, osum, half_ref,
               n2, cot, w, act, pg, po, rcg, rxg, rzg, rco, rxo, rzo, yb,
               gsend, grecv, glocal, lsem, ssend, srcs, srxs, srzs, ysend, yrecv, xsend, xrecv):
    at = place()
    r, z, x, c = at
    me = idx(z, x, c)
    extra = has(me)
    MM, SP = pl.ds(0, 3 * MAIN), pl.ds(3 * MAIN, 384)
    loads = [pltpu.make_async_copy(w_ref.at[:, MM], w.at[:, MM], lsem.at[0]), pltpu.make_async_copy(cot_ref, cot, lsem.at[1])]
    for l in loads: l.start()
    load_spare = pltpu.make_async_copy(w_ref.at[:, SP], w.at[:, SP], lsem.at[3])
    when(extra, load_spare.start)
    greet(*at, with_y=True)
    g = Gather(at, n2_ref, n2, gsend, grecv, glocal)
    rg = Scatter(at, pg, rcg, rxg, rzg, ssend.at[0], srcs.at[0], srxs.at[0], srzs.at[0])
    ro = Scatter(at, po, rco, rxo, rzo, ssend.at[1], srcs.at[1], srxs.at[1], srzs.at[1])
    g.begin()
    for l in loads: l.wait()
    when(extra, load_spare.wait)
    mid = (z > 0) & (z < NZ - 1)
    p = [z,
         jnp.where(z == 0, 1, jnp.where(z == 1, 0, jnp.where(z == 2, 3, 2))),
         jnp.where(z == 0, 2, jnp.where(z == 1, 2, 1)),
         jnp.where(z < 2, 3, 0)]

    def tiles(zz):
        rows = pl.ds(pl.multiple_of(4 * zz, 4), 4)
        tok = pl.ds(pl.multiple_of(512 * zz, 512), 512)
        @pl.loop(0, 2)
        def _(t):
            a = n2[rows].reshape(512, D)
            k = cot[rows].reshape(512, D)
            def col(base):
                return pl.ds(pl.multiple_of(base + 256 * t, 256), 256)
            dg, du, h = gated(dot(a, w[:, col(0)]), dot(a, w[:, col(MAIN)]), dot(k, w[:, col(2 * MAIN)]))
            act[tok, col(0)] = dg
            act[tok, col(MAIN)] = du
            act[tok, col(2 * MAIN)] = h
        def spare():
            pre = dot(n2[rows].reshape(512, D), w[:, 3 * MAIN : 3 * MAIN + 256])
            dg, du, h = gated(pre[:, :128], pre[:, 128:], dot(cot[rows].reshape(512, D), w[:, 3 * MAIN + 256 :]))
            act[tok, 3 * MAIN : 3 * MAIN + 128] = dg
            act[tok, 3 * MAIN + 128 : 3 * MAIN + 256] = du
            act[tok, 3 * MAIN + 256 :] = h
        when(extra, spare)
        def out_tiles(more):
            @pl.loop(0, D // 256)
            def _(t):
                dr = pl.ds(pl.multiple_of(256 * t, 256), 256)
                v = dot_nt(act[tok, : 2 * MAIN], w[dr, : 2 * MAIN])
                u = dot_nt(act[tok, 2 * MAIN : 3 * MAIN], w[dr, 2 * MAIN : 3 * MAIN])
                if more:
                    v += dot_nt(act[tok, 3 * MAIN : 3 * MAIN + 256], w[dr, 3 * MAIN : 3 * MAIN + 256])
                    u += dot_nt(act[tok, 3 * MAIN + 256 :], w[dr, 3 * MAIN + 256 :])
                pg[rows, :, dr] = v.astype(BF).reshape(4, 128, 256)
                po[rows, :, dr] = u.astype(BF).reshape(4, 128, 256)
        when(extra, lambda: out_tiles(True))
        when(~extra, lambda: out_tiles(False))
        rg.send_c(zz)
        ro.send_c(zz)

    g.from_z(p[1])
    when(mid, lambda: g.from_z(p[2]))
    g.from_x(p[0])
    g.from_c(p[0])
    pltpu.make_async_copy(n2_ref, n2.at[0], glocal).wait()
    tiles(p[0])
    g.from_z(jnp.where(mid, p[3], p[2]))
    g.from_x(p[1])
    g.from_c(p[1])
    tiles(p[1])
    when(~mid, lambda: g.from_z(p[3]))
    g.from_x(p[2])
    g.from_c(p[2])
    tiles(p[2])
    g.from_x(p[3])
    g.from_c(p[3])
    tiles(p[3])

    ydev = (1 - r, idx(z, x, c))
    own = D // 16
    half = own // 2
    def ycopy(j, spare):
        cols = SP if spare else MM
        src = w.at[pl.ds(pl.multiple_of(own * j + half * (1 - r), half), half), cols]
        a, b = (xsend, xrecv) if spare else (ysend, yrecv)
        return pltpu.make_async_remote_copy(src, yb.at[j, :, cols], a.at[j], b.at[j], device_id=ydev, device_id_type=MESH)
    def grads(q):
        dr = slice(384 * q, 384 * (q + 1))
        row = slice(384 * q, 384 * (q + 1))
        @pl.loop(0, 4)
        def _(t):
            col = pl.ds(pl.multiple_of(256 * t, 256), 256)
            w[row, col] = dot_tn(n2[:, :, dr].reshape(2048, 384), act[:, col]).astype(BF)
        @pl.loop(0, 2)
        def _(t):
            col = pl.ds(pl.multiple_of(2 * MAIN + 256 * t, 256), 256)
            w[row, col] = dot_tn(cot[:, :, dr].reshape(2048, 384), act[:, col]).astype(BF)
        for j in range(4 * q, 4 * q + 4):
            ycopy(j, 0).start()
        def spare():
            w[row, 3 * MAIN : 3 * MAIN + 256] = dot_tn(n2[:, :, dr].reshape(2048, 384), act[:, 3 * MAIN : 3 * MAIN + 256]).astype(BF)
            w[row, 3 * MAIN + 256 :] = dot_tn(cot[:, :, dr].reshape(2048, 384), act[:, 3 * MAIN + 256 :]).astype(BF)
            for j in range(4 * q, 4 * q + 4):
                ycopy(j, 1).start()
        when(extra, spare)
    def yadd(j):
        def add(spare):
            cols = SP if spare else MM
            ycopy(j, spare).wait()
            mine = w[pl.ds(pl.multiple_of(own * j + half * r, half), half), cols]
            yb[j, :, cols] = (mine.astype(F32) + yb[j, :, cols].astype(F32)).astype(BF)
            pltpu.make_async_copy(yb.at[j, :, cols], half_ref.at[j, :, cols], lsem.at[4 if spare else 2]).start()
        add(0)
        when(extra, lambda: add(1))

    rg.step_x(3)
    rg.step_x(2)
    grads(0)
    rg.step_z(3)
    rg.step_x(1)
    grads(1)
    rg.step_z(2)
    rg.step_x(0)
    grads(2)
    rg.step_z(1)
    ro.step_x(3)
    ro.step_x(2)
    grads(3)
    rg.finish(gsum)
    ro.step_z(3)
    ro.step_x(1)
    for j in range(0, 4): yadd(j)
    ro.step_z(2)
    ro.step_x(0)
    for j in range(4, 8): yadd(j)
    ro.step_z(1)
    for j in range(8, 12): yadd(j)
    ro.finish(osum)
    for j in range(12, 16): yadd(j)
    pltpu.make_async_copy(yb.at[:, :, MM], half_ref.at[:, :, MM], lsem.at[2]).wait()
    when(extra, lambda: pltpu.make_async_copy(yb.at[:, :, SP], half_ref.at[:, :, SP], lsem.at[4]).wait())
    g.end(local=False)

def mlp(n2, cot, w, cid):
    blk = n2.shape
    dma = pltpu.SemaphoreType.DMA
    full = (16,) + blk
    return pl.pallas_call(
        mlp_kernel,
        out_shape=[jax.ShapeDtypeStruct(blk, F32)] * 2 + [jax.ShapeDtypeStruct((16, D // 32, COLS), BF)],
        in_specs=[pl.BlockSpec(memory_space=pl.ANY)] * 3,
        out_specs=[pl.BlockSpec(memory_space=pltpu.VMEM)] * 2 + [pl.BlockSpec(memory_space=pl.ANY)],
        scratch_shapes=[pltpu.VMEM(full, BF), pltpu.VMEM(full, BF), pltpu.VMEM((D, COLS), BF), pltpu.VMEM((16 * blk[0], COLS), BF),
                        pltpu.VMEM(full, BF), pltpu.VMEM(full, BF)]
        + [pltpu.VMEM((k,) + blk, BF) for k in (8, 4, 5, 8, 4, 5)]
        + [pltpu.VMEM((16, D // 32, COLS), BF)]
        + [dma((18,)), dma((16,)), dma(()), dma((5,)), dma((2, 16)), dma((2, 8)), dma((2, 4)), dma((2, 5))] + [dma((16,))] * 4,
        compiler_params=pltpu.CompilerParams(collective_id=cid, has_side_effects=True, vmem_limit_bytes=60 * 2**20),
    )(n2, cot, w)


def spin(u, cos, sin):
    return u * cos + pltpu.roll(u, HEAD_DIM // 2, 1) * sin

def stack_heads(v):
    n = v.shape[1] // HEAD_DIM
    return jnp.concatenate([v[:, HEAD_DIM * i : HEAD_DIM * (i + 1)] for i in range(n)], axis=0)

def spread_heads(v, rows):
    n = v.shape[0] // rows
    return jnp.concatenate([v[rows * i : rows * (i + 1)] for i in range(n)], axis=1)

def exp_scores(q, k, first_row, block, length):
    sc = dot_nt(q, k) * (HEAD_DIM ** -0.5)
    key = lax.broadcasted_iota(jnp.int32, sc.shape, 1)
    row = jnp.bitwise_and(lax.broadcasted_iota(jnp.int32, sc.shape, 0), block - 1) + first_row
    return jnp.where((key <= row) & (key < length), jnp.exp(sc), 0.0)

def rms(v, gain):
    factor = lax.rsqrt(jnp.mean(v * v, axis=-1, keepdims=True) + EPSILON)
    return v * factor * gain


class GatherY(Gather):
    def __init__(self, at, src, out, send, recv, local):
        Gather.__init__(self, at, src, out, send, recv, local)
        self.n = src.shape[0] // 2
        self.ydev = (1 - self.r, idx(self.z, self.x, self.c))
    def rows(self, h):
        return pl.ds(pl.multiple_of(h * self.n, self.n), self.n)
    def half(self, b, h):
        return self.out.at[b, self.rows(h)]
    def move(self, src, dst, k, q, dev):
        return pltpu.make_async_remote_copy(src, dst, self.send.at[k], self.recv.at[q], device_id=dev, device_id_type=MESH)
    def arrived(self, b, h):
        self.move(self.half(b, h), self.half(b, h), 0, 2 * b + h, self.ydev).wait_recv()
    def begin(self):
        z, x, c, r = self.z, self.x, self.c, self.r
        me = idx(z, x, c)
        mine, dst = self.src.at[self.rows(r)], self.half(me, r)
        for s in (1, -1):
            when(self.inside(z + s), lambda s=s: self.move(mine, dst, 0 if s == 1 else 3, 2 * me + r, self.zdev(s)).start())
        self.move(mine, dst, 6 + z, 2 * me + r, self.xdev()).start()
        self.move(self.src, self.out.at[me], 18 + 2 * z + x, 2 * me, self.cdev()).start()
        pltpu.make_async_copy(self.src, self.out.at[me], self.local).start()
    def from_z(self, zz):
        z, x, c, r = self.z, self.x, self.c, self.r
        b = idx(zz, x, c)
        q = 2 * b + r
        self.arrived(b, r)
        s = jnp.where(zz < z, 1, -1)
        slot = jnp.where(zz < z, 0, 3) + jnp.abs(zz - z)
        a = self.half(b, r)
        when(self.inside(z + s), lambda: self.move(a, a, slot, q, (r, idx(z + s, x, c))).start())
        self.move(a, a, 6 + zz, q, self.xdev()).start()
        self.move(a, a, 18 + 2 * zz + x, q, self.cdev()).start()
        self.move(a, a, 10 + 2 * zz + x, q, self.ydev).start()
    def from_x(self, zz):
        x, c, r = self.x, self.c, self.r
        b = idx(zz, 1 - x, c)
        q = 2 * b + r
        self.arrived(b, r)
        a = self.half(b, r)
        self.move(a, a, 18 + 2 * zz + 1 - x, q, self.cdev()).start()
        self.move(a, a, 10 + 2 * zz + 1 - x, q, self.ydev).start()
    def from_y(self, zz):
        x, c, r = self.x, self.c, self.r
        def take(xx):
            b = idx(zz, xx, c)
            self.arrived(b, 1 - r)
            a = self.half(b, 1 - r)
            self.move(a, a, 26 + 2 * zz + xx, 2 * b + 1 - r, self.cdev()).start()
        when(zz != self.z, lambda: take(x))
        take(1 - x)
    def from_c(self, zz):
        x, c, r = self.x, self.c, self.r
        b = idx(zz, x, 1 - c)
        whole = self.out.at[b]
        when(zz == self.z, lambda: self.move(whole, whole, 0, 2 * b, self.ydev).wait_recv())
        def both(b):
            self.arrived(b, r)
            self.arrived(b, 1 - r)
        when(zz != self.z, lambda: both(b))
        both(idx(zz, 1 - x, 1 - c))
    def end(self):
        z, x = self.z, self.x
        own = 2 * z + x
        a = self.half(0, 0)
        def sent(k, a=a):
            self.move(a, a, k, 0, self.ydev).wait_send()
        for d in range(NZ - 1):
            when((z - d >= 0) & (z < NZ - 1), lambda d=d: sent(d))
            when((z + d < NZ) & (z > 0), lambda d=d: sent(3 + d))
        for k in range(6, 10):
            sent(k)
        for k in range(8):
            def other(k=k):
                sent(10 + k)
                sent(18 + k)
                sent(26 + k)
            when(own != k, other)
        sent(18 + own, self.out.at[0])
        pltpu.make_async_copy(self.src, self.out.at[0], self.local).wait()

def front_kernel(block, lens, x_ref, cot_ref, v0, v1, v2, v3, v4, sel, fold, selk, foldk, rope_ref, wq, wk, wv, wg, wu, wd, wo_ref,
                 q_out, normed_out, att_out, mid_out, n2_out, vec, buf, qkv_out, kv_out, cot_out, wo_out,
                 rope, cot_own, small, qkv_own, wqkv, small_all, own, kv, wo,
                 qs, qr, ql, vs, vr, vl, ks, kr, kl, cs, cr, cl, ws, wr, wl, d0, d1, d2, d3, d4, d5, d6, d7, dl, lsem):
    at = place()
    width = HEADS * HEAD_DIM
    kw = KV_HEADS * HEAD_DIM
    loads = [pltpu.make_async_copy(w, qkv_own.at[:, pl.ds(o, n)], lsem.at[i]) for i, (w, o, n) in enumerate(((wq, 0, width), (wk, width, kw), (wv, width + kw, kw)))]
    first_row = lax.axis_index("group") * block
    loads.append(pltpu.make_async_copy(rope_ref.at[:, pl.ds(pl.multiple_of(first_row, block), block)], rope, lsem.at[6]))
    for l in loads: l.start()
    small[...] = jnp.zeros_like(small)
    for i, v in enumerate((v0, v1, v2, v3, v4)):
        small[i : i + 1, : v.shape[1]] = v[...].astype(F32)
    cot_own[...] = (cot_ref[...].astype(F32) * row_mask(lens, first_row, block, (cot_ref.shape[0], 1))).astype(BF)
    hail_all(*at)
    for l in loads: l.wait()
    gq = GatherY(at, qkv_own, wqkv, qs, qr, ql)
    gv = Gather(at, small, small_all, vs, vr, vl)
    gk = Gather(at, own, kv, ks, kr, kl)
    gc = Gather(at, cot_own, cot_out, cs, cr, cl)
    gw = GatherY(at, wo_ref, wo, ws, wr, wl)
    d = Deal(at, (wg, wu, wd), buf, (d0, d1, d2, d3, d4, d5, d6, d7), dl)
    steps = iter(range(15))
    def some(n):
        for _ in range(n):
            i = next(steps, None)
            if i is not None:
                d.step(i)
    gq.begin()
    gv.begin()
    d.begin()
    x = x_ref[...].astype(F32)
    gq.first()
    gv.first()
    gq.second()
    gv.second()
    gq.from_y(gq.p[0])
    some(EARLY[0])
    gq.third()
    gv.third()
    gq.from_y(gq.p[1])
    gq.fourth()
    gv.fourth()
    gc.begin()
    gq.from_y(gq.p[2])
    gq.from_y(gq.p[3])
    for zz in range(NZ):
        gv.from_c(zz)
        gq.from_c(zz)
    gv.end()
    gq.end()
    keep = [pltpu.make_async_copy(wqkv, qkv_out, lsem.at[3]), pltpu.make_async_copy(kv, kv_out, lsem.at[4]), pltpu.make_async_copy(wo, wo_out, lsem.at[5])]
    keep[0].start()
    vec[...] = jnp.zeros_like(vec)
    for i, row, first, a, b in ((0, 0, 0, sel, fold), (1, 1, 0, sel, fold), (2, 1, width, selk, foldk), (3, 1, width + kw, selk, foldk), (4, 2, 0, sel, fold)):
        t = dot_nt(small_all[:, i, :].astype(BF), b[...])
        vec[row : row + 1, first : first + a.shape[1]] = jnp.sum(t * a[...], axis=0, keepdims=True)
    normed_out[...] = rms(x, vec[0:1, :width]).astype(BF)
    cos, sin = [jnp.concatenate((rope[i], rope[i]), axis=0) for i in range(2)]
    def product(base):
        return dot(normed_out[...], wqkv[:, :, pl.ds(pl.multiple_of(base, 256), 256)].reshape(width, 256)) + vec[1:2, pl.ds(pl.multiple_of(base, 256), 256)]
    pre = product(width)
    own[:, :HEAD_DIM] = spin(pre[:, :HEAD_DIM], cos, sin).astype(BF)
    own[:, HEAD_DIM : 2 * HEAD_DIM] = spin(pre[:, HEAD_DIM:], cos, sin).astype(BF)
    own[:, kw:] = product(width + kw).astype(BF)
    gk.begin()
    gw.begin()
    @pl.loop(0, width // 256)
    def _(t):
        pre = product(t * 256)
        for i in range(2):
            col = pl.ds(pl.multiple_of(256 * t + HEAD_DIM * i, HEAD_DIM), HEAD_DIM)
            q_out[:, col] = spin(pre[:, HEAD_DIM * i : HEAD_DIM * (i + 1)], cos, sin).astype(BF)
    some(EARLY[1])
    gc.first()
    gk.first()
    gw.first()
    some(EARLY[2])
    gk.second()
    gc.second()
    gw.second()
    gw.from_y(gw.p[0])
    gk.third()
    some(EARLY[3])
    gk.fourth()
    gc.third()
    gw.third()
    gw.from_y(gw.p[1])
    for zz in range(NZ):
        gk.from_c(zz)
    gk.end()
    keep[1].start()
    span = 16 * block
    @pl.loop(0, 4)
    def _(u):
        s, h = u // 2, lax.rem(u, 2)
        rows = pl.ds(pl.multiple_of(block * s, block), block)
        cols = pl.ds(pl.multiple_of(width // 2 * h, width // 2), width // 2)
        q = stack_heads(q_out[rows, cols])
        k = kv[:, rows, pl.ds(pl.multiple_of(HEAD_DIM * h, HEAD_DIM), HEAD_DIM)].reshape(span, HEAD_DIM)
        v = kv[:, rows, pl.ds(pl.multiple_of(kw + HEAD_DIM * h, HEAD_DIM), HEAD_DIM)].reshape(span, HEAD_DIM)
        e = exp_scores(q, k, first_row, block, lens[s])
        total = jnp.sum(e, axis=-1, keepdims=True)
        att_out[rows, cols] = spread_heads(dot(e.astype(BF), v) / total, block)
    some(EARLY[4])
    gw.fourth()
    gc.fourth()
    gw.from_y(gw.p[2])
    gw.from_y(gw.p[3])
    for zz in range(NZ):
        gw.from_c(zz)
    gw.end()
    keep[2].start()
    @pl.loop(0, width // 256)
    def _(t):
        col = pl.ds(pl.multiple_of(256 * t, 256), 256)
        mid_out[:, col] = x_ref[:, col].astype(F32) + dot(att_out[...].astype(BF), wo[:, :, col].reshape(width, 256))
    n2_out[...] = rms(mid_out[...], vec[2:3, :width]).astype(BF)
    some(15)
    for zz in range(NZ):
        gc.from_c(zz)
    gc.end()
    for k in keep:
        k.wait()
    d.end()

EARLY = (2, 1, 1, 2, 3)

def front(lens, x, cot, vectors, sel, fold, selk, foldk, rope, wq, wk, wv, wg, wu, wd, wo, block, cid):
    rows, width = x.shape
    any_ = pl.BlockSpec(memory_space=pl.ANY)
    vm = pl.BlockSpec(memory_space=pltpu.VMEM)
    dma = pltpu.SemaphoreType.DMA
    act = (rows, width)
    own = wq.shape[0]
    kvw = 2 * KV_HEADS * HEAD_DIM
    wide = width + kvw
    sds = jax.ShapeDtypeStruct
    VM = pltpu.VMEM
    return pl.pallas_call(
        functools.partial(front_kernel, block),
        out_shape=[sds(act, BF), sds(act, BF), sds(act, F32), sds(act, F32), sds(act, BF), sds((8, wide), F32),
                   sds((16 * own, 3 * MAIN + 384), BF), sds((16, own, wide), BF), sds((16, rows, kvw), BF), sds((16,) + act, BF), sds((16,) + wo.shape, BF)],
        in_specs=[pl.BlockSpec(memory_space=pltpu.SMEM)] + [vm] * 11 + [any_] * 8,
        out_specs=[vm] * 6 + [any_] * 5,
        scratch_shapes=[VM((2, block, HEAD_DIM), F32), VM(act, BF), VM((8, 128), F32), VM((own, wide), BF), VM((16, own, wide), BF), VM((16, 8, 128), F32), VM((rows, kvw), BF), VM((16, rows, kvw), BF), VM((16,) + wo.shape, BF)]
        + [dma((34,)), dma((32,)), dma(())] + [dma((18,)), dma((16,)), dma(())] * 3 + [dma((34,)), dma((32,)), dma(())]
        + [dma((16,))] * 8 + [dma((2,)), dma((7,))],
        compiler_params=pltpu.CompilerParams(collective_id=cid, has_side_effects=True, vmem_limit_bytes=60 * 2**20),
    )(lens, x, cot, *vectors, sel, fold, selk, foldk, rope, wq, wk, wv, wg, wu, wd, wo)


class Return:
    def __init__(self, at, half_ref, out, sems, local):
        self.r, self.z, self.x, self.c = at
        self.me = idx(self.z, self.x, self.c)
        self.src, self.out, self.sems, self.local = half_ref, out, sems, local
        self.n = half_ref.shape[1]
    def places(self, j, spare):
        row = pl.ds(pl.multiple_of(self.r * self.n, self.n), self.n)
        col = spare_at(j) if spare else pl.ds(pl.multiple_of(j * MAIN, MAIN), MAIN)
        return [self.out.at[i, row, col] for i in range(3)]
    def parts(self, j, spare):
        if spare:
            return [self.src.at[j, :, pl.ds(3 * MAIN + 128 * i, 128)] for i in range(3)]
        return [self.src.at[j, :, pl.ds(i * MAIN, MAIN)] for i in range(3)]
    def copy(self, a, b, kind, k, dev):
        send, recv = self.sems[2 * kind : 2 * kind + 2]
        return pltpu.make_async_remote_copy(a, b, send.at[k], recv.at[k], device_id=dev, device_id_type=MESH)
    def launch(self, k):
        j = jnp.bitwise_xor(self.me, k)
        def go(spare):
            for a, b in zip(self.parts(j, spare), self.places(self.me, spare)):
                self.copy(a, b, spare, k, (self.r, j)).start()
        go(0)
        when(has(self.me), lambda: go(1))
    def forward(self, j, k, spare):
        for a in self.places(j, spare):
            self.copy(a, a, 2 + spare, k, (1 - self.r, self.me)).start()
    def begin(self, window):
        self.window = window
        def go(spare):
            for a, b in zip(self.parts(self.me, spare), self.places(self.me, spare)):
                pltpu.make_async_copy(a, b, self.local.at[spare]).start()
        go(0)
        when(has(self.me), lambda: go(1))
        for k in KS[:window]:
            self.launch(k)
    def sized(self, spare):
        return self.src.at[0, :, pl.ds(3 * MAIN, 384) if spare else pl.ds(0, 3 * MAIN)]
    def whole(self, kind, k):
        blk = self.sized(kind % 2)
        return self.copy(blk, blk, kind, k, (1 - self.r, self.me))
    def own(self):
        def go(spare):
            blk = self.sized(spare)
            pltpu.make_async_copy(blk, blk, self.local.at[spare]).wait()
            self.forward(self.me, 0, spare)
        go(0)
        when(has(self.me), lambda: go(1))
    def step(self, i):
        k = KS[i]
        j = jnp.bitwise_xor(self.me, k)
        def go(spare):
            self.whole(spare, k).wait_recv()
            self.forward(j, k, spare)
        go(0)
        when(has(j), lambda: go(1))
        if i + self.window < 15:
            self.launch(KS[i + self.window])
    def end(self):
        for k in (0,) + KS:
            j = jnp.bitwise_xor(self.me, k)
            self.whole(2, k).wait()
            when(has(j), lambda: self.whole(3, k).wait())
            if k:
                self.whole(0, k).wait_send()
                when(has(self.me), lambda: self.whole(1, k).wait_send())

def row_mask(lens, first_row, block, shape):
    row = lax.broadcasted_iota(jnp.int32, shape, 0)
    place = jnp.bitwise_and(row, block - 1) + first_row
    return jnp.where(place < jnp.where(row < block, lens[0], lens[1]), 1.0, 0.0)

def norm_gradient(v, gain, upstream):
    factor = lax.rsqrt(jnp.mean(v * v, axis=-1, keepdims=True) + EPSILON)
    weighted = upstream * gain
    inner = jnp.mean(weighted * v, axis=-1, keepdims=True)
    return factor * weighted - v * (factor * factor * factor) * inner, jnp.sum(upstream * v * factor, axis=0, keepdims=True)

def backward_kernel(block, window, lens, gn2, mlp_out, mid, cot, x_ref, att, q_ref, normed, vec, sel, fold, selk, foldk, rope_ref, kv_ref, wo_ref, wqkv_ref, half_ref,
                    layer_out, grad_input, q_out, pair_out, wo_out, vec_out, g_out,
                    rope, kv, wo, wqkv, gmid, branch, gatt, gqkv, pv,
                    p_kv, c_kv, x_kv, z_kv, p_wo, c_wo, x_wo, z_wo, p_qk, c_qk, x_qk, z_qk, p_pw, c_pw, x_pw, z_pw, p_ve, c_ve, x_ve, z_ve,
                    kvsum, y0, y1, y2, y3, y4, y5, y6, y7,
                    ss, sc, sx, sz, r0, r1, r2, r3, r4, r5, r6, r7, rl, ysem, lsem):
    at = place()
    r, z, x, c = at
    width = HEADS * HEAD_DIM
    kw = KV_HEADS * HEAD_DIM
    loads = [pltpu.make_async_copy(a, b, lsem.at[i]) for i, (a, b) in enumerate(((wo_ref, wo), (kv_ref, kv), (wqkv_ref, wqkv)))]
    first_row = lax.axis_index("group") * block
    loads.append(pltpu.make_async_copy(rope_ref.at[:, pl.ds(pl.multiple_of(first_row, block), block)], rope, lsem.at[3]))
    for l in loads: l.start()
    hail_all(*at)
    back = Return(at, half_ref, g_out, (r0, r1, r2, r3, r4, r5, r6, r7), rl)
    back.begin(window)
    sets = ((p_kv, c_kv, x_kv, z_kv), (p_wo, c_wo, x_wo, z_wo), (p_qk, c_qk, x_qk, z_qk), (p_pw, c_pw, x_pw, z_pw), (p_ve, c_ve, x_ve, z_ve))
    ek, eo, eq, ep, ev = [Scatter(at, *b, ss.at[i], sc.at[i], sx.at[i], sz.at[i]) for i, b in enumerate(sets)]
    steps = iter(range(15))
    def some(n):
        for _ in range(n):
            i = next(steps, None)
            if i is not None:
                back.step(i)
    ydev = (1 - r, idx(z, x, c))
    def trade(i, out, a, b):
        a[...] = out[...].astype(BF)
        pltpu.make_async_remote_copy(a, b, ysem.at[2 * i], ysem.at[2 * i + 1], device_id=ydev, device_id_type=MESH).start()
    def traded(i, out, a, b):
        pltpu.make_async_remote_copy(a, b, ysem.at[2 * i], ysem.at[2 * i + 1], device_id=ydev, device_id_type=MESH).wait()
        out[...] = a[...].astype(F32) + b[...].astype(F32)

    grad_norm, gain_two = norm_gradient(mid[...], vec[2:3, :width], gn2[...])
    valid = row_mask(lens, first_row, block, (cot.shape[0], 1))
    gmid[...] = cot[...].astype(F32) * valid + grad_norm
    branch[...] = gmid[...].astype(BF)
    loads[0].wait()
    @pl.loop(0, 4)
    def _(t):
        blocks = pl.ds(pl.multiple_of(4 * t, 4), 4)
        col = pl.ds(pl.multiple_of(384 * t, 384), 384)
        low = att[:, col].astype(BF)
        p_wo[blocks] = dot_tn(low, branch[...]).astype(BF).reshape(4, 96, width)
        gatt[:, col] = dot_nt(branch[...], wo[blocks].reshape(384, width))
    eo.begin()
    eo.step_x(3)
    eo.step_x(2)
    back.own()
    layer_out[...] = ((mid[...] + mlp_out[...]) * valid).astype(BF)
    loads[1].wait()
    loads[3].wait()
    span = 16 * block
    def unit(u):
        s, h = u // 2, lax.rem(u, 2)
        rows = pl.ds(pl.multiple_of(block * s, block), block)
        cols = pl.ds(pl.multiple_of(width // 2 * h, width // 2), width // 2)
        kcol = pl.ds(pl.multiple_of(HEAD_DIM * h, HEAD_DIM), HEAD_DIM)
        vcol = pl.ds(pl.multiple_of(kw + HEAD_DIM * h, HEAD_DIM), HEAD_DIM)
        q = stack_heads(q_ref[rows, cols])
        k = kv[:, rows, kcol].reshape(span, HEAD_DIM)
        v = kv[:, rows, vcol].reshape(span, HEAD_DIM)
        e = exp_scores(q, k, first_row, block, lens[s])
        total = jnp.sum(e, axis=-1, keepdims=True)
        ga = stack_heads(gatt[rows, cols])
        gt = -jnp.sum(ga * stack_heads(att[rows, cols]), axis=-1, keepdims=True) / total
        gn = (ga / total).astype(BF)
        gs = (e * (dot_nt(gn, v) + gt)).astype(BF)
        p_kv[:, rows, kcol] = dot_tn(gs, q).astype(BF).reshape(16, block, HEAD_DIM)
        p_kv[:, rows, vcol] = dot_tn(e.astype(BF), gn).astype(BF).reshape(16, block, HEAD_DIM)
        gq = dot(gs, k) * (HEAD_DIM ** -0.5)
        cos, sin = rope[0], rope[1]
        gqkv[rows, cols] = jnp.concatenate([spin(gq[block * i : block * (i + 1)], cos, -sin) for i in range(HEADS // KV_HEADS)], axis=1).astype(BF)
    unit(0)
    some(1)
    eo.step_z(3)
    eo.step_x(1)
    unit(1)
    some(1)
    eo.step_z(2)
    eo.step_x(0)
    unit(2)
    some(1)
    eo.step_z(1)
    unit(3)
    ek.begin()
    ek.step_x(3)
    ek.step_x(2)
    some(1)
    loads[2].wait()
    @pl.loop(0, 4)
    def _(t):
        blocks = pl.ds(pl.multiple_of(4 * t, 4), 4)
        col = pl.ds(pl.multiple_of(384 * t, 384), 384)
        p_qk[blocks] = dot_tn(normed[:, col], gqkv[:, :width]).astype(BF).reshape(4, 96, width)
    ek.step_z(3)
    ek.step_x(1)
    eq.begin()
    eo.finish(wo_out)
    trade(0, wo_out, y0, y1)
    ek.step_z(2)
    ek.step_x(0)
    eq.step_x(3)
    eq.step_x(2)
    some(1)
    @pl.loop(0, 4)
    def _(t):
        blocks = pl.ds(pl.multiple_of(4 * t, 4), 4)
        col = pl.ds(pl.multiple_of(384 * t, 384), 384)
        gatt[:, col] = dot_nt(gqkv[:, :width], wqkv[blocks, :, :width].reshape(384, width))
    ek.step_z(1)
    some(1)
    ek.finish(kvsum)
    cos, sin = [jnp.concatenate((rope[i], rope[i]), axis=0) for i in range(2)]
    for h in range(KV_HEADS):
        kcol = slice(HEAD_DIM * h, HEAD_DIM * (h + 1))
        gqkv[:, width + HEAD_DIM * h : width + HEAD_DIM * (h + 1)] = spin(kvsum[:, kcol] * (HEAD_DIM ** -0.5), cos, -sin).astype(BF)
    gqkv[:, width + kw :] = kvsum[:, kw:].astype(BF)
    @pl.loop(0, 4)
    def _(t):
        blocks = pl.ds(pl.multiple_of(4 * t, 4), 4)
        col = pl.ds(pl.multiple_of(384 * t, 384), 384)
        p_pw[blocks] = dot_tn(normed[:, col], gqkv[:, width:]).astype(BF).reshape(4, 96, 2 * kw)
        gatt[:, col] += dot_nt(gqkv[:, width:], wqkv[blocks, :, width:].reshape(384, 2 * kw))
    ep.begin()
    ep.step_x(3)
    ep.step_x(2)
    eq.step_z(3)
    eq.step_x(1)
    some(1)
    grad_norm, gain_one = norm_gradient(x_ref[...].astype(F32), vec[0:1, :width], gatt[...])
    grad_input[...] = gmid[...] + grad_norm
    bias = jnp.sum(gqkv[...].astype(F32), axis=0, keepdims=True)
    pv[...] = jnp.zeros_like(pv)
    for i, (v, a, b) in enumerate(((gain_one, sel, fold), (bias[:, :width], sel, fold), (bias[:, width : width + kw], selk, foldk), (bias[:, width + kw :], selk, foldk), (gain_two, sel, fold))):
        pv[:, i, :] = dot((a[...] * v).astype(BF), b[...])
    p_ve[...] = pv[...].astype(BF)
    ev.begin()
    ev.step_x(3)
    ev.step_x(2)
    some(1)
    late = (ep, ev)
    for kind, d in (("z", 3), ("x", 1), ("z", 2), ("x", 0), ("z", 1)):
        for e in late:
            (e.step_x if kind == "x" else e.step_z)(d)
        if (kind, d) not in (("z", 3), ("x", 1)):
            (eq.step_x if kind == "x" else eq.step_z)(d)
        some(1)
    some(15)
    eq.finish(q_out)
    trade(1, q_out, y2, y3)
    ep.finish(pair_out)
    trade(2, pair_out, y4, y5)
    ev.finish(vec_out)
    trade(3, vec_out, y6, y7)
    traded(0, wo_out, y0, y1)
    traded(1, q_out, y2, y3)
    traded(2, pair_out, y4, y5)
    traded(3, vec_out, y6, y7)
    back.end()

def backward(lens, gn2, mlp_out, mid, cot, x, att, q, normed, vec, sel, fold, selk, foldk, rope, kv, wo, wqkv, half, ff, block, cid, window=4):
    any_ = pl.BlockSpec(memory_space=pl.ANY)
    vm = pl.BlockSpec(memory_space=pltpu.VMEM)
    dma = pltpu.SemaphoreType.DMA
    sds = jax.ShapeDtypeStruct
    rows, width = x.shape
    wide = wqkv.shape[-1]
    own = wo.shape[1]
    kvw = kv.shape[-1]
    VM = pltpu.VMEM
    def four(blk):
        return [VM((k,) + blk, BF) for k in (16, 8, 4, 5)]
    return pl.pallas_call(
        functools.partial(backward_kernel, block, window),
        out_shape=[sds((rows, width), BF), sds((rows, width), F32), sds((own, width), F32), sds((own, wide - width), F32), sds((own, width), F32), sds((16, 128), F32), sds((3, own, ff), BF)],
        in_specs=[pl.BlockSpec(memory_space=pltpu.SMEM)] + [vm] * 13 + [any_] * 5,
        out_specs=[vm] * 6 + [any_],
        scratch_shapes=[VM((2, block, HEAD_DIM), F32), VM(kv.shape, BF), VM(wo.shape, BF), VM(wqkv.shape, BF), VM((rows, width), F32), VM((rows, width), BF), VM((rows, width), F32), VM((rows, wide), BF), VM((16, 16, 128), F32)]
        + four((rows, kvw)) + four((own, width)) + four((own, width)) + four((own, wide - width)) + four((16, 128))
        + [VM((rows, kvw), F32)] + [VM((own, width), BF)] * 4 + [VM((own, wide - width), BF)] * 2 + [VM((16, 128), BF)] * 2
        + [dma((5, 16)), dma((5, 8)), dma((5, 4)), dma((5, 5))] + [dma((16,))] * 8 + [dma((2,)), dma((8,)), dma((4,))],
        compiler_params=pltpu.CompilerParams(collective_id=cid, has_side_effects=True, vmem_limit_bytes=60 * 2**20),
    )(lens, gn2, mlp_out, mid, cot, x, att, q, normed, vec, sel, fold, selk, foldk, rope, kv, wo, wqkv, half)


def folding(group_count, width):
    share = width // group_count
    at = np.arange(width)
    sel = (at[None, :] // share == np.arange(group_count)[:, None]).astype(np.float32)
    fold = (at[:, None] % share == np.arange(128)[None, :]).astype(BF)
    return sel, fold


def rope_constants(span):
    freqs = np.float32(THETA) ** (-np.arange(0, HEAD_DIM, 2, dtype=np.float32) / HEAD_DIM)
    angles = np.arange(span, dtype=np.float32)[:, None] * freqs[None, :].astype(np.float32)
    sin = np.sin(angles)
    return np.stack(
        (np.concatenate((np.cos(angles),) * 2, axis=1), np.concatenate((-sin, sin), axis=1))
    ).astype(np.float32)


def shards_fast(
    hidden_in,
    lengths,
    gain_attn,
    w_query,
    b_query,
    w_key,
    b_key,
    w_value,
    b_value,
    w_out,
    gain_mlp,
    w_gate,
    w_up,
    w_down,
    cotangent,
):
    group_count = lax.axis_size("group")
    slot_count, block_len, model_width = hidden_in.shape
    kv_width = KV_HEADS * HEAD_DIM
    tokens = slot_count * block_len
    hidden_units = w_gate.shape[1]
    pieces = (gain_attn, b_query, b_key, b_value, gain_mlp)
    sel, fold = folding(group_count, model_width)
    selk, foldk = folding(group_count, kv_width)
    rope = rope_constants(group_count * block_len)
    rows_in = hidden_in.reshape(tokens, model_width)
    grad_rows = cotangent.reshape(tokens, model_width)
    (
        q_rows, normed, attended, mid, normed_two, vec, columns, qkv_w, pair_all, grad_all, out_w
    ) = front(
        lengths,
        rows_in,
        grad_rows,
        [p[None] for p in pieces],
        sel,
        fold,
        selk,
        foldk,
        rope,
        w_query,
        w_key,
        w_value,
        w_gate,
        w_up,
        w_down,
        w_out,
        block_len,
        1,
    )
    grad_normed_two, mlp_out, half_sum = mlp(normed_two, grad_all, columns, 3)
    layer_out, grad_input, query_sum, pair_sum, out_sum, vector_sum, ff_sum = backward(
        lengths,
        grad_normed_two,
        mlp_out,
        mid,
        grad_rows,
        rows_in,
        attended,
        q_rows,
        normed,
        vec,
        sel,
        fold,
        selk,
        foldk,
        rope,
        pair_all,
        out_w,
        qkv_w,
        half_sum,
        hidden_units,
        block_len,
        4,
    )
    ff_sums = [ff_sum[i].astype(F32) for i in range(3)]
    gain_one_sum, query_bias_sum, key_bias_sum, value_bias_sum, gain_two_sum = [
        vector_sum[i, : p.shape[0]] for i, p in enumerate(pieces)
    ]
    return (
        layer_out.reshape(hidden_in.shape),
        grad_input.reshape(hidden_in.shape),
        gain_one_sum,
        query_sum,
        query_bias_sum,
        pair_sum[:, :kv_width],
        key_bias_sum,
        pair_sum[:, kv_width:],
        value_bias_sum,
        out_sum,
        gain_two_sum,
        *ff_sums,
    )


def solution(mesh):
    act = P("replica", "group", None)
    vec = P("group")
    mat = P("group", None)
    return jax.shard_map(
        shards_fast if mesh.shape["group"] == 16 else shards_plain,
        mesh=mesh,
        in_specs=(act, P("replica"), vec, mat, vec, mat, vec, mat, vec, mat, vec, mat, mat, mat, act),
        out_specs=(act, act, vec, mat, vec, mat, vec, mat, vec, mat, vec, mat, mat, mat),
        check_vma=False,
    )
```

```python
import functools

import jax
import jax.numpy as jnp
import numpy as np
from jax import lax
from jax.experimental import pallas as pl
from jax.experimental.pallas import tpu as pltpu
from jax.sharding import PartitionSpec as P

MESH = pl.DeviceIdType.MESH
NZ = 4
MAIN = 512
D = 1536
COLS = 3 * MAIN + 384
HEADS = 12
KV_HEADS = 2
HEAD_DIM = 128
EPSILON = 1e-06
THETA = 1000000.0
BF = jnp.bfloat16
F32 = jnp.float32


def rope_tables(positions, head_dim):
    freqs = THETA ** (-jnp.arange(0, head_dim, 2).astype(F32) / head_dim)
    angles = positions.astype(F32)[:, None] * freqs[None, :]
    angles = jnp.concatenate((angles, angles), axis=-1)
    return (jnp.cos(angles), jnp.sin(angles))


def rotate(tensor, cos_table, sin_table):
    halfway = tensor.shape[-1] // 2
    turned = jnp.concatenate((-tensor[..., halfway:], tensor[..., :halfway]), axis=-1)
    return tensor * cos_table + turned * sin_table


def rotate_back(gradient, cos_table, sin_table):
    halfway = gradient.shape[-1] // 2
    scaled = gradient * sin_table
    turned = jnp.concatenate((scaled[..., halfway:], -scaled[..., :halfway]), axis=-1)
    return gradient * cos_table + turned


def normalize(row_values, gain_vec):
    factor = lax.rsqrt(jnp.mean(row_values * row_values, axis=-1, keepdims=True) + EPSILON)
    return (row_values * factor * gain_vec, factor)


def norm_back(row_values, factor, gain_vec, upstream):
    weighted = upstream * gain_vec
    inner_mean = jnp.mean(weighted * row_values, axis=-1, keepdims=True)
    grad_rows = factor * weighted - row_values * (factor * factor * factor) * inner_mean
    grad_gain = jnp.sum(upstream * row_values * factor, axis=0)
    return (grad_rows, grad_gain)


def matmul(a, b):
    return jnp.dot(a, b, preferred_element_type=F32)


def matmul_nt(a, b):
    return lax.dot_general(a, b, (((1,), (1,)), ((), ())), preferred_element_type=F32)


def matmul_tn(a, b):
    return lax.dot_general(a, b, (((0,), (0,)), ((), ())), preferred_element_type=F32)


def arrange(per_token, kv_heads):
    block_len, head_count, head_dim = per_token.shape
    repeat = head_count // kv_heads
    grouped = per_token.reshape(block_len, kv_heads, repeat, head_dim)
    return jnp.transpose(grouped, (1, 2, 0, 3)).reshape(kv_heads, repeat * block_len, head_dim)


def restore(per_group, block_len):
    kv_heads, row_count, head_dim = per_group.shape
    repeat = row_count // block_len
    grouped = per_group.reshape(kv_heads, repeat, block_len, head_dim)
    return jnp.transpose(grouped, (2, 0, 1, 3)).reshape(block_len, kv_heads * repeat * head_dim)


def masked_exp(query_rows, key_block, row_pos, first_key, length, score_scale):
    key_step = key_block.shape[0]
    raw_scores = jnp.einsum("grd,kgd->grk", query_rows, key_block, preferred_element_type=F32)
    key_pos = first_key + jnp.arange(key_step, dtype=jnp.int32)
    allowed = (key_pos[None, :] <= row_pos[:, None]) & (key_pos[None, :] < length)
    return jnp.where(allowed[None], jnp.exp(raw_scores * score_scale), 0.0)


def block_total(length, rank_end, key_step):
    key_limit = jnp.minimum(length, rank_end)
    return (key_limit + key_step - 1) // key_step


def attend_forward(query_rows, key_all, value_all, row_pos, length, rank_end, key_step, scale):
    kv_heads, row_count, head_dim = query_rows.shape

    def visit(block_index, state_tuple):
        totals, numerator = state_tuple
        first_key = block_index * key_step
        key_block = lax.dynamic_slice_in_dim(key_all, first_key, key_step, 0)
        value_block = lax.dynamic_slice_in_dim(value_all, first_key, key_step, 0)
        weights = masked_exp(query_rows, key_block, row_pos, first_key, length, scale)
        totals = totals + jnp.sum(weights, axis=-1)
        numerator = numerator + jnp.einsum(
            "grk,kgd->grd", weights.astype(BF), value_block, preferred_element_type=F32
        )
        return (totals, numerator)

    initial = (
        jnp.zeros((kv_heads, row_count), F32),
        jnp.zeros((kv_heads, row_count, head_dim), F32),
    )
    return lax.fori_loop(0, block_total(length, rank_end, key_step), visit, initial)


def attend_backward(
    query_rows, key_all, value_all, row_pos, length, rank_end, key_step, scale, grad_numer, grad_total
):
    kv_heads, row_count, head_dim = query_rows.shape

    def visit(block_index, state_tuple):
        grad_query, grad_key, grad_value = state_tuple
        first_key = block_index * key_step
        key_block = lax.dynamic_slice_in_dim(key_all, first_key, key_step, 0)
        value_block = lax.dynamic_slice_in_dim(value_all, first_key, key_step, 0)
        weights = masked_exp(query_rows, key_block, row_pos, first_key, length, scale)
        grad_prob = jnp.einsum("grd,kgd->grk", grad_numer, value_block, preferred_element_type=F32)
        grad_score = (weights * (grad_prob + grad_total[..., None])).astype(BF)
        grad_query = grad_query + jnp.einsum(
            "grk,kgd->grd", grad_score, key_block, preferred_element_type=F32
        )
        key_part = jnp.einsum("grk,grd->kgd", grad_score, query_rows, preferred_element_type=F32)
        value_part = jnp.einsum(
            "grk,grd->kgd", weights.astype(BF), grad_numer, preferred_element_type=F32
        )
        key_old = lax.dynamic_slice_in_dim(grad_key, first_key, key_step, 0)
        value_old = lax.dynamic_slice_in_dim(grad_value, first_key, key_step, 0)
        grad_key = lax.dynamic_update_slice_in_dim(grad_key, key_old + key_part, first_key, 0)
        grad_value = lax.dynamic_update_slice_in_dim(
            grad_value, value_old + value_part, first_key, 0
        )
        return (grad_query, grad_key, grad_value)

    initial = (
        jnp.zeros((kv_heads, row_count, head_dim), F32),
        jnp.zeros(key_all.shape, F32),
        jnp.zeros(value_all.shape, F32),
    )
    return lax.fori_loop(0, block_total(length, rank_end, key_step), visit, initial)


def gather_plain(x):
    return lax.all_gather(x, "group", axis=0, tiled=True)


def scatter_sum(x):
    return lax.psum_scatter(x, "group", scatter_dimension=0, tiled=True)


def shards_plain(
    hidden_in,
    lengths,
    gain_attn,
    w_query,
    b_query,
    w_key,
    b_key,
    w_value,
    b_value,
    w_out,
    gain_mlp,
    w_gate,
    w_up,
    w_down,
    cotangent,
):
    group_count = lax.axis_size("group")
    group_rank = lax.axis_index("group")
    slot_count, block_len, model_width = hidden_in.shape
    kv_heads = KV_HEADS
    head_dim = HEAD_DIM
    kv_width = kv_heads * head_dim
    repeat = HEADS // kv_heads
    slot_span = block_len * group_count
    key_step = min(512, slot_span)
    score_scale = head_dim ** (-0.5)
    tokens = slot_count * block_len
    hidden_units = w_gate.shape[1]
    own_rows = w_gate.shape[0]
    share = hidden_units // group_count
    positions = group_rank * block_len + jnp.arange(block_len, dtype=jnp.int32)
    valid_rows = (positions[None, :] < lengths[:, None]).astype(F32).reshape(tokens, 1)
    cos_table, sin_table = rope_tables(positions, head_dim)
    cos_heads = cos_table[:, None, :]
    sin_heads = sin_table[:, None, :]
    rank_end = (group_rank + 1) * block_len
    row_pos = jnp.tile(positions, repeat)

    pieces = (gain_attn, b_query, b_key, b_value, gain_mlp)
    sizes = [p.shape[0] for p in pieces]
    small = gather_plain(jnp.concatenate(pieces)[None])
    offsets = [sum(sizes[:i]) for i in range(len(sizes) + 1)]
    gain_one, query_b, key_b, value_b, gain_two = [
        small[:, offsets[i] : offsets[i + 1]].reshape(-1).astype(F32) for i in range(len(sizes))
    ]
    qkv_w = gather_plain(jnp.concatenate((w_query, w_key, w_value), axis=1))
    out_w = gather_plain(w_out)
    qkv_b = jnp.concatenate((query_b, key_b, value_b))

    stacked = jnp.stack((w_gate, w_up, w_down)).reshape(3, own_rows, group_count, share)
    stacked = jnp.transpose(stacked, (2, 1, 0, 3)).reshape(group_count, own_rows, 3 * share)
    columns = lax.all_to_all(stacked, "group", 0, 0, tiled=True).reshape(model_width, 3 * share)
    gate_up_w = columns[:, : 2 * share]
    down_w = columns[:, 2 * share :]

    grad_final = cotangent.reshape(tokens, model_width).astype(F32) * valid_rows
    grad_all = gather_plain(grad_final.astype(BF))

    inputs = hidden_in.reshape(tokens, model_width).astype(F32)
    normed_full, factor_one = normalize(inputs, gain_one)
    normed = normed_full.astype(BF)
    qkv = matmul(normed, qkv_w) + qkv_b
    query_rot = rotate(
        qkv[:, :model_width].reshape(slot_count, block_len, HEADS, head_dim), cos_heads, sin_heads
    ).astype(BF)
    key_rot = rotate(
        qkv[:, model_width : model_width + kv_width].reshape(
            slot_count, block_len, kv_heads, head_dim
        ),
        cos_heads,
        sin_heads,
    ).astype(BF)
    value_low = qkv[:, model_width + kv_width :].astype(BF)
    pair = jnp.concatenate(
        (key_rot.reshape(tokens, kv_width), value_low), axis=1
    ).reshape(1, slot_count, block_len, 2 * kv_width)
    pair_all = jnp.transpose(gather_plain(pair), (1, 0, 2, 3)).reshape(
        slot_count, slot_span, 2, kv_heads, head_dim
    )
    key_all = pair_all[:, :, 0]
    value_all = pair_all[:, :, 1]
    query_groups = []
    slot_totals = []
    slot_attended = []
    attended_rows = []
    for s in range(slot_count):
        query_rows = arrange(query_rot[s], kv_heads)
        totals, numerator = attend_forward(
            query_rows, key_all[s], value_all[s], row_pos, lengths[s], rank_end, key_step, score_scale
        )
        attended = numerator / totals[..., None]
        query_groups.append(query_rows)
        slot_totals.append(totals)
        slot_attended.append(attended)
        attended_rows.append(restore(attended, block_len))
    attended_low = jnp.concatenate(attended_rows, axis=0).astype(BF)
    residual_mid = inputs + matmul(attended_low, out_w)
    normed_two_full, factor_two = normalize(residual_mid, gain_two)
    normed_all = gather_plain(normed_two_full.astype(BF))

    pre = matmul(normed_all, gate_up_w)
    gate_pre = pre[:, :share]
    up_pre = pre[:, share:]
    sigmoid_gate = jax.nn.sigmoid(gate_pre)
    silu_gate = gate_pre * sigmoid_gate
    hidden = (silu_gate * up_pre).astype(BF)
    grad_hidden = matmul(grad_all, down_w)
    grad_gate = (
        grad_hidden * up_pre * (sigmoid_gate * (1.0 + gate_pre * (1.0 - sigmoid_gate)))
    ).astype(BF)
    grad_up = (grad_hidden * silu_gate).astype(BF)
    gate_up_grad = jnp.concatenate((grad_gate, grad_up), axis=1)
    grad_normed_two = scatter_sum(matmul_nt(gate_up_grad, gate_up_w).astype(BF)).astype(F32)
    mlp_out = scatter_sum(matmul_nt(hidden, down_w).astype(BF)).astype(F32)
    down_term = matmul_tn(grad_all, hidden)
    gate_up_term = matmul_tn(normed_all, gate_up_grad)
    terms = jnp.concatenate((gate_up_term, down_term), axis=1).astype(BF)
    back = lax.all_to_all(
        terms.reshape(group_count, own_rows, 3 * share), "group", 0, 0, tiled=True
    )
    summed = back.astype(F32) + lax.ppermute(back, "replica", [(0, 1), (1, 0)]).astype(F32)
    summed = jnp.transpose(summed.reshape(group_count, own_rows, 3, share), (2, 1, 0, 3))
    gate_sum, up_sum, down_sum = summed.reshape(3, own_rows, hidden_units)

    final_rows = residual_mid + mlp_out
    layer_out = (final_rows * valid_rows).reshape(slot_count, block_len, model_width).astype(BF)
    grad_mid_norm, grad_gain_two = norm_back(residual_mid, factor_two, gain_two, grad_normed_two)
    grad_mid = grad_final + grad_mid_norm
    grad_branch = grad_mid.astype(BF)
    out_term = matmul_tn(attended_low, grad_branch)
    grad_attended = matmul_nt(grad_branch, out_w)
    grad_query_rows = []
    grad_pairs = []
    for s in range(slot_count):
        slot_grad = grad_attended[s * block_len : (s + 1) * block_len].reshape(
            block_len, HEADS, head_dim
        )
        grad_out = arrange(slot_grad, kv_heads)
        totals = slot_totals[s]
        grad_total = -jnp.sum(grad_out * slot_attended[s], axis=-1) / totals
        grad_numer = (grad_out / totals[..., None]).astype(BF)
        grad_query, grad_key, grad_value = attend_backward(
            query_groups[s],
            key_all[s],
            value_all[s],
            row_pos,
            lengths[s],
            rank_end,
            key_step,
            score_scale,
            grad_numer,
            grad_total,
        )
        query_back_rows = restore(grad_query * score_scale, block_len).reshape(
            block_len, HEADS, head_dim
        )
        grad_query_rows.append(
            rotate_back(query_back_rows, cos_heads, sin_heads).reshape(block_len, HEADS * head_dim)
        )
        grad_pairs.append(
            jnp.concatenate(
                (grad_key.reshape(slot_span, kv_width), grad_value.reshape(slot_span, kv_width)),
                axis=1,
            )
        )
    pair_grads = jnp.stack(grad_pairs).reshape(slot_count, group_count, block_len, 2 * kv_width)
    pair_grads = jnp.transpose(pair_grads, (1, 0, 2, 3)).astype(BF)
    pair_sum = scatter_sum(pair_grads).reshape(slot_count, block_len, 2 * kv_width).astype(F32)
    grad_query_pre = jnp.concatenate(grad_query_rows, axis=0).astype(BF)
    key_sum = pair_sum[..., :kv_width].reshape(slot_count, block_len, kv_heads, head_dim)
    grad_key_pre = (
        rotate_back(key_sum * score_scale, cos_heads, sin_heads).astype(BF).reshape(tokens, kv_width)
    )
    grad_value_pre = pair_sum[..., kv_width:].astype(BF).reshape(tokens, kv_width)
    grad_qkv = jnp.concatenate((grad_query_pre, grad_key_pre, grad_value_pre), axis=1)
    grad_normed = matmul_nt(grad_qkv, qkv_w)
    grad_in_norm, grad_gain_one = norm_back(inputs, factor_one, gain_one, grad_normed)
    grad_input = (grad_mid + grad_in_norm).reshape(slot_count, block_len, model_width)
    qkv_term = matmul_tn(normed, grad_qkv)
    qkv_bias = jnp.sum(grad_qkv.astype(F32), axis=0)

    weight_share = scatter_sum(
        jnp.concatenate((qkv_term, out_term), axis=1).astype(BF)
    )
    weight_sum = weight_share.astype(F32) + lax.ppermute(
        weight_share, "replica", [(0, 1), (1, 0)]
    ).astype(F32)
    vectors = jnp.concatenate(
        [
            grad_gain_one.reshape(group_count, -1),
            qkv_bias[:model_width].reshape(group_count, -1),
            qkv_bias[model_width : model_width + kv_width].reshape(group_count, -1),
            qkv_bias[model_width + kv_width :].reshape(group_count, -1),
            grad_gain_two.reshape(group_count, -1),
        ],
        axis=1,
    )
    vector_sum = lax.psum(scatter_sum(vectors), "replica").reshape(-1)
    gain_one_sum, query_bias_sum, key_bias_sum, value_bias_sum, gain_two_sum = [
        vector_sum[offsets[i] : offsets[i + 1]] for i in range(len(sizes))
    ]
    ends = (0, model_width, model_width + kv_width, model_width + 2 * kv_width)
    query_sum, key_sum_w, value_sum_w = [weight_sum[:, ends[i] : ends[i + 1]] for i in range(3)]
    out_sum = weight_sum[:, ends[3] :]
    return (
        layer_out,
        grad_input,
        gain_one_sum,
        query_sum,
        query_bias_sum,
        key_sum_w,
        key_bias_sum,
        value_sum_w,
        value_bias_sum,
        out_sum,
        gain_two_sum,
        gate_sum,
        up_sum,
        down_sum,
    )


def place():
    g = lax.axis_index("group")
    r = lax.axis_index("replica")
    return r, g // 4, lax.rem(g // 2, 2), lax.rem(g, 2)

def idx(z, x, c):
    return (z * 2 + x) * 2 + c

def greet(r, z, x, c, with_y=False):
    bar = pltpu.get_barrier_semaphore()
    def hail(dev):
        pl.semaphore_signal(bar, inc=1, device_id=dev, device_id_type=MESH)
    hail((r, idx(z, 1 - x, c)))
    hail((r, idx(z, x, 1 - c)))
    if with_y:
        hail((1 - r, idx(z, x, c)))
    @pl.when(z > 0)
    def _():
        hail((r, idx(z - 1, x, c)))
    @pl.when(z < NZ - 1)
    def _():
        hail((r, idx(z + 1, x, c)))
    ends = jnp.where((z > 0) & (z < NZ - 1), 1, 0)
    pl.semaphore_wait(bar, (4 if with_y else 3) + ends)

def planes(z):
    return (
        z,
        jnp.where(z == 0, 1, jnp.where(z == 1, 0, jnp.where(z == 2, 3, 2))),
        jnp.where(z == 0, 2, jnp.where(z == 1, 2, 1)),
        jnp.where(z < 2, 3, 0),
    )

def when(cond, fn):
    pl.when(cond)(fn)

class Gather:
    def __init__(self, at, src, out, send, recv, local, part=None):
        self.r, self.z, self.x, self.c = at
        self.src, self.out, self.send, self.recv, self.local = src, out, send, recv, local
        self.part = part
        self.mid = (self.z > 0) & (self.z < NZ - 1)
        self.p = planes(self.z)
    def blk(self, b):
        return self.out.at[b] if self.part is None else self.out.at[b, self.part]
    def put(self, src, b, k, dev):
        pltpu.make_async_remote_copy(src, self.blk(b), self.send.at[k], self.recv.at[b], device_id=dev, device_id_type=MESH).start()
    def sent(self, k):
        b = 0
        pltpu.make_async_remote_copy(self.blk(b), self.blk(b), self.send.at[k], self.recv.at[b], device_id=(self.r, 0), device_id_type=MESH).wait_send()
    def got(self, b):
        pltpu.make_async_remote_copy(self.blk(b), self.blk(b), self.send.at[0], self.recv.at[b], device_id=(self.r, 0), device_id_type=MESH).wait_recv()
    def zdev(self, s): return (self.r, idx(self.z + s, self.x, self.c))
    def xdev(self): return (self.r, idx(self.z, 1 - self.x, self.c))
    def cdev(self): return (self.r, idx(self.z, self.x, 1 - self.c))
    def begin(self):
        z, x, c = self.z, self.x, self.c
        me = idx(z, x, c)
        for s in (1, -1):
            when(self.inside(z + s), lambda s=s: self.put(self.src, me, 0 if s == 1 else 3, self.zdev(s)))
        self.put(self.src, me, 6 + z, self.xdev())
        self.put(self.src, me, 10 + 2 * z + x, self.cdev())
        pltpu.make_async_copy(self.src, self.blk(me), self.local).start()
    def inside(self, z): return (z >= 0) & (z < NZ)
    def from_z(self, zz):
        z, x, c = self.z, self.x, self.c
        b = idx(zz, x, c)
        self.got(b)
        s = jnp.where(zz < z, 1, -1)
        d = jnp.abs(zz - z)
        slot = jnp.where(zz < z, 0, 3) + d
        when(self.inside(z + s), lambda: self.put(self.blk(b), b, slot, (self.r, idx(z + s, x, c))))
        self.put(self.blk(b), b, 6 + zz, self.xdev())
        self.put(self.blk(b), b, 10 + 2 * zz + x, self.cdev())
    def first(self):
        self.from_z(self.p[1])
        when(self.mid, lambda: self.from_z(self.p[2]))
        self.from_x(self.p[0])
    def second(self):
        self.from_z(jnp.where(self.mid, self.p[3], self.p[2]))
        self.from_x(self.p[1])
    def third(self):
        when(~self.mid, lambda: self.from_z(self.p[3]))
        self.from_x(self.p[2])
    def fourth(self):
        self.from_x(self.p[3])
    def from_x(self, zz):
        b = idx(zz, 1 - self.x, self.c)
        self.got(b)
        self.put(self.blk(b), b, 10 + 2 * zz + 1 - self.x, self.cdev())
    def from_c(self, zz):
        self.got(idx(zz, self.x, 1 - self.c))
        self.got(idx(zz, 1 - self.x, 1 - self.c))
    def end(self, local=True):
        z = self.z
        for d in range(NZ - 1):
            when((z - d >= 0) & (z < NZ - 1), lambda d=d: self.sent(d))
            when((z + d < NZ) & (z > 0), lambda d=d: self.sent(3 + d))
        for k in range(6, 18):
            self.sent(k)
        if local:
            pltpu.make_async_copy(self.src, self.blk(0), self.local).wait()

class Scatter:
    def __init__(self, at, part, rc, rx, rz, send, rcs, rxs, rzs):
        self.r, self.z, self.x, self.c = at
        self.part, self.rc, self.rx, self.rz = part, rc, rx, rz
        self.send, self.rcs, self.rxs, self.rzs = send, rcs, rxs, rzs
    def inside(self, z): return (z >= 0) & (z < NZ)
    def copy(self, src, dst, k, rs, dev):
        return pltpu.make_async_remote_copy(src, dst, self.send.at[k], rs, device_id=dev, device_id_type=MESH)
    def over(self, d):
        return [(s, self.z + s * d) for s in ((-1, 1) if d else (1,))]
    def begin(self, far_first=True):
        z, x, c = self.z, self.x, self.c
        dev = (self.r, idx(z, x, 1 - c))
        for xx in (1 - x, x):
            for d in range(NZ - 1, -1, -1):
                for s, zz in self.over(d):
                    k = 2 * zz + xx
                    when(self.inside(zz), lambda zz=zz, k=k, xx=xx: self.copy(self.part.at[idx(zz, xx, 1 - c)], self.rc.at[k], k, self.rcs.at[k], dev).start())
    def send_c(self, zz):
        z, x, c = self.z, self.x, self.c
        dev = (self.r, idx(z, x, 1 - c))
        for xx in (1 - x, x):
            k = 2 * zz + xx
            self.copy(self.part.at[idx(zz, xx, 1 - c)], self.rc.at[k], k, self.rcs.at[k], dev).start()
    def x_plane(self, zz):
        z, x, c = self.z, self.x, self.c
        dev = (self.r, idx(z, 1 - x, c))
        k = 2 * zz + 1 - x
        b = idx(zz, 1 - x, c)
        self.copy(self.rc.at[k], self.rc.at[k], 0, self.rcs.at[k], dev).wait_recv()
        self.part[b] = (self.part[b].astype(F32) + self.rc[k].astype(F32)).astype(BF)
        self.copy(self.part.at[b], self.rx.at[zz], 8 + zz, self.rxs.at[zz], dev).start()
    def step_x(self, d):
        for s, zz in self.over(d):
            when(self.inside(zz), lambda zz=zz: self.x_plane(zz))
    def step_z(self, d):
        z, x, c = self.z, self.x, self.c
        for s, zz in self.over(d):
            def go(zz=zz, s=s):
                k = 2 * zz + x
                b = idx(zz, x, c)
                self.copy(self.rc.at[k], self.rc.at[k], 0, self.rcs.at[k], (self.r, 0)).wait_recv()
                self.copy(self.rx.at[zz], self.rx.at[zz], 0, self.rxs.at[zz], (self.r, 0)).wait_recv()
                both = self.part[b].astype(F32) + self.rc[k].astype(F32) + self.rx[zz].astype(F32)
                dev = (self.r, idx(z + s, x, c))
                slot = jnp.where(zz == z + s, NZ, zz) if s == -1 else zz
                self.part[b] = both.astype(BF)
                def more():
                    self.copy(self.rz.at[zz], self.rz.at[zz], 0, self.rzs.at[zz], dev).wait_recv()
                    self.part[b] = (self.part[b].astype(F32) + self.rz[zz].astype(F32)).astype(BF)
                when(self.inside(z - s), more)
                self.copy(self.part.at[b], self.rz.at[slot], 12 + zz, self.rzs.at[slot], dev).start()
            when(self.inside(zz), go)
    def finish(self, out):
        z, x, c = self.z, self.x, self.c
        k = 2 * z + x
        b = idx(z, x, c)
        self.copy(self.rc.at[k], self.rc.at[k], 0, self.rcs.at[k], (self.r, 0)).wait_recv()
        self.copy(self.rx.at[z], self.rx.at[z], 0, self.rxs.at[z], (self.r, 0)).wait_recv()
        out[...] = self.part[b].astype(F32) + self.rc[k].astype(F32) + self.rx[z].astype(F32)
        def lo():
            self.copy(self.rz.at[z], self.rz.at[z], 0, self.rzs.at[z], (self.r, 0)).wait_recv()
            out[...] += self.rz[z].astype(F32)
        when(z > 0, lo)
        def hi():
            self.copy(self.rz.at[NZ], self.rz.at[NZ], 0, self.rzs.at[NZ], (self.r, 0)).wait_recv()
            out[...] += self.rz[NZ].astype(F32)
        when(z < NZ - 1, hi)
        for k in range(8):
            self.copy(self.part.at[0], self.part.at[0], k, self.rcs.at[0], (self.r, 0)).wait_send()
        for k in range(8, 12):
            self.copy(self.part.at[0], self.part.at[0], k, self.rcs.at[0], (self.r, 0)).wait_send()
        for zz in range(NZ):
            when(z != zz, lambda zz=zz: self.copy(self.part.at[0], self.part.at[0], 12 + zz, self.rcs.at[0], (self.r, 0)).wait_send())

class ScatterY(Scatter):
    def __init__(self, at, part, rc, ry, rx, rz, send, rcs, rys, rxs, rzs, ysem):
        Scatter.__init__(self, at, part, rc, rx, rz, send, rcs, rxs, rzs)
        self.ry, self.rys, self.ysem = ry, rys, ysem
        self.n = part.shape[1] // 2
        self.ydev = (1 - self.r, idx(self.z, self.x, self.c))
        self.mine = self.rows(self.r)
    def rows(self, h):
        return pl.ds(pl.multiple_of(h * self.n, self.n), self.n)
    def step_y(self, d):
        x, c, r = self.x, self.c, self.r
        for xx in (1 - x, x):
            for s, zz in self.over(d):
                def go(zz=zz, xx=xx):
                    k = 2 * zz + xx
                    b = idx(zz, xx, c)
                    self.copy(self.rc.at[k], self.rc.at[k], 0, self.rcs.at[k], self.ydev).wait_recv()
                    self.part[b] = (self.part[b].astype(F32) + self.rc[k].astype(F32)).astype(BF)
                    self.copy(self.part.at[b, self.rows(1 - r)], self.ry.at[k], 16 + k, self.rys.at[k], self.ydev).start()
                when(self.inside(zz), go)
    def both(self, zz, xx):
        k = 2 * zz + xx
        self.copy(self.ry.at[k], self.ry.at[k], 0, self.rys.at[k], self.ydev).wait_recv()
        return self.part[idx(zz, xx, self.c), self.mine].astype(F32) + self.ry[k].astype(F32)
    def step_x(self, d):
        z, x, c = self.z, self.x, self.c
        dev = (self.r, idx(z, 1 - x, c))
        for s, zz in self.over(d):
            def go(zz=zz):
                b = idx(zz, 1 - x, c)
                self.part[b, self.mine] = self.both(zz, 1 - x).astype(BF)
                self.copy(self.part.at[b, self.mine], self.rx.at[zz], 8 + zz, self.rxs.at[zz], dev).start()
            when(self.inside(zz), go)
    def arrived(self, ref, sem):
        self.copy(ref, ref, 0, sem, self.ydev).wait_recv()
    def step_z(self, d):
        z, x, c = self.z, self.x, self.c
        for s, zz in self.over(d):
            def go(zz=zz, s=s):
                b = idx(zz, x, c)
                v = self.both(zz, x)
                self.arrived(self.rx.at[zz], self.rxs.at[zz])
                self.part[b, self.mine] = (v + self.rx[zz].astype(F32)).astype(BF)
                def more():
                    self.arrived(self.rz.at[zz], self.rzs.at[zz])
                    self.part[b, self.mine] = (self.part[b, self.mine].astype(F32) + self.rz[zz].astype(F32)).astype(BF)
                when(self.inside(z - s), more)
                slot = jnp.where(zz == z + s, NZ, zz) if s == -1 else zz
                self.copy(self.part.at[b, self.mine], self.rz.at[slot], 12 + zz, self.rzs.at[slot], (self.r, idx(z + s, x, c))).start()
            when(self.inside(zz), go)
    def finish(self, out, low):
        z, x, r = self.z, self.x, self.r
        v = self.both(z, x)
        self.arrived(self.rx.at[z], self.rxs.at[z])
        out[self.mine] = v + self.rx[z].astype(F32)
        def lo():
            self.arrived(self.rz.at[z], self.rzs.at[z])
            out[self.mine] += self.rz[z].astype(F32)
        when(z > 0, lo)
        def hi():
            self.arrived(self.rz.at[NZ], self.rzs.at[NZ])
            out[self.mine] += self.rz[NZ].astype(F32)
        when(z < NZ - 1, hi)
        low[self.mine] = out[self.mine].astype(BF)
        a = low.at[self.mine]
        pltpu.make_async_remote_copy(a, a, self.ysem.at[0], self.ysem.at[1], device_id=self.ydev, device_id_type=MESH).start()
    def traded(self, out, low):
        a = low.at[self.rows(1 - self.r)]
        pltpu.make_async_remote_copy(a, a, self.ysem.at[0], self.ysem.at[1], device_id=self.ydev, device_id_type=MESH).wait()
        out[...] = low[...].astype(F32)
        half = self.part.at[0, self.mine]
        for k in range(8):
            self.copy(self.part.at[0], self.part.at[0], k, self.rcs.at[0], self.ydev).wait_send()
        for k in list(range(16, 24)) + list(range(8, 12)):
            self.copy(half, half, k, self.rcs.at[0], self.ydev).wait_send()
        for zz in range(NZ):
            when(self.z != zz, lambda zz=zz: self.copy(half, half, 12 + zz, self.rcs.at[0], self.ydev).wait_send())


KS = (8, 1, 9, 2, 10, 3, 11, 4, 12, 5, 13, 6, 14, 7, 15)
WINDOW = 4

def has(j):
    return lax.rem(j, 3) == 0

def spare_at(j):
    return pl.ds(pl.multiple_of(16 * MAIN + 128 * (j // 3), 128), 128)

class Deal:
    def __init__(self, at, ws, buf, sems, local):
        self.r, self.z, self.x, self.c = at
        self.me = idx(self.z, self.x, self.c)
        self.ws, self.buf, self.sems, self.local = ws, buf, sems, local
        self.n = ws[0].shape[0] // 2
    def rows(self, j, h):
        return pl.ds(pl.multiple_of((2 * j + h) * self.n, self.n), self.n)
    def block(self, j, h, spare):
        return self.buf.at[self.rows(j, h), pl.ds(3 * MAIN, 384) if spare else pl.ds(0, 3 * MAIN)]
    def copy(self, a, b, kind, k, dev):
        send, recv = self.sems[2 * kind : 2 * kind + 2]
        return pltpu.make_async_remote_copy(a, b, send.at[k], recv.at[k], device_id=dev, device_id_type=MESH)
    def launch(self, k):
        r, me, n = self.r, self.me, self.n
        row = pl.ds(pl.multiple_of(r * n, n), n)
        j = jnp.bitwise_xor(me, k)
        dst = self.rows(me, r)
        for i in range(3):
            self.copy(self.ws[i].at[row, pl.ds(pl.multiple_of(j * MAIN, MAIN), MAIN)], self.buf.at[dst, pl.ds(i * MAIN, MAIN)], 0, k, (r, j)).start()
        def spare():
            for i in range(3):
                self.copy(self.ws[i].at[row, spare_at(j)], self.buf.at[dst, pl.ds(3 * MAIN + 128 * i, 128)], 1, k, (r, j)).start()
        when(has(j), spare)
    def locals(self, spare):
        me, n = self.me, self.n
        row = pl.ds(pl.multiple_of(2 * me * n, 2 * n), 2 * n)
        col = spare_at(me) if spare else pl.ds(pl.multiple_of(me * MAIN, MAIN), MAIN)
        for i in range(3):
            to = pl.ds(3 * MAIN + 128 * i, 128) if spare else pl.ds(i * MAIN, MAIN)
            yield pltpu.make_async_copy(self.ws[i].at[:, col], self.buf.at[row, to], self.local.at[1 if spare else 0])
    def begin(self):
        for k in KS[:WINDOW]:
            self.launch(k)
        for l in self.locals(False):
            l.start()
        def spare():
            for l in self.locals(True):
                l.start()
        when(has(self.me), spare)
    def step(self, i):
        k = KS[i]
        r, me = self.r, self.me
        j = jnp.bitwise_xor(me, k)
        dev = (1 - r, me)
        def pass_on(spare):
            blk = self.block(j, r, spare)
            self.copy(blk, blk, spare, k, dev).wait_recv()
            self.copy(blk, blk, 2 + spare, k, dev).start()
        pass_on(0)
        when(has(me), lambda: pass_on(1))
        if i + WINDOW < 15:
            self.launch(KS[i + WINDOW])
    def end(self):
        r, me, n = self.r, self.me, self.n
        dev = (1 - r, me)
        for k in KS:
            j = jnp.bitwise_xor(me, k)
            def done(spare):
                blk = self.block(j, 1 - r, spare)
                self.copy(blk, blk, 2 + spare, k, dev).wait()
            def sent(spare):
                blk = self.block(j, r, spare)
                self.copy(blk, blk, spare, k, dev).wait_send()
            done(0)
            sent(0)
            when(has(me), lambda: done(1))
            when(has(j), lambda: sent(1))
        row = pl.ds(pl.multiple_of(2 * me * n, 2 * n), 2 * n)
        def own(spare):
            blk = self.buf.at[row, pl.ds(3 * MAIN, 384) if spare else pl.ds(0, 3 * MAIN)]
            pltpu.make_async_copy(blk, blk, self.local.at[spare]).wait()
        own(0)
        when(has(me), lambda: own(1))

def hail_all(r, z, x, c):
    bar = pltpu.get_barrier_semaphore()
    me = idx(z, x, c)
    for k in range(1, 16):
        pl.semaphore_signal(bar, inc=1, device_id=(r, lax.rem(me + k, 16)), device_id_type=MESH)
    pl.semaphore_signal(bar, inc=1, device_id=(1 - r, me), device_id_type=MESH)
    pl.semaphore_wait(bar, 16)


def dot(a, b):
    return lax.dot_general(a, b, (((1,), (0,)), ((), ())), preferred_element_type=F32)
def dot_nt(a, b):
    return lax.dot_general(a, b, (((1,), (1,)), ((), ())), preferred_element_type=F32)
def dot_tn(a, b):
    return lax.dot_general(a, b, (((0,), (0,)), ((), ())), preferred_element_type=F32)

def gated(g, u, gh):
    sig = jax.nn.sigmoid(g)
    silu = g * sig
    return (gh * u * (sig * (1.0 + g * (1.0 - sig)))).astype(BF), (gh * silu).astype(BF), (silu * u).astype(BF)

def mlp_kernel(n2_ref, cot_ref, w_ref, gsum, osum, half_ref,
               n2, cot, w, act, pg, po, rcg, rxg, rzg, rco, rxo, rzo, yb,
               gsend, grecv, glocal, lsem, ssend, srcs, srxs, srzs, ysend, yrecv, xsend, xrecv):
    at = place()
    r, z, x, c = at
    me = idx(z, x, c)
    extra = has(me)
    MM, SP = pl.ds(0, 3 * MAIN), pl.ds(3 * MAIN, 384)
    loads = [pltpu.make_async_copy(w_ref.at[:, MM], w.at[:, MM], lsem.at[0]), pltpu.make_async_copy(cot_ref, cot, lsem.at[1])]
    for l in loads: l.start()
    load_spare = pltpu.make_async_copy(w_ref.at[:, SP], w.at[:, SP], lsem.at[3])
    when(extra, load_spare.start)
    greet(*at, with_y=True)
    g = Gather(at, n2_ref, n2, gsend, grecv, glocal)
    rg = Scatter(at, pg, rcg, rxg, rzg, ssend.at[0], srcs.at[0], srxs.at[0], srzs.at[0])
    ro = Scatter(at, po, rco, rxo, rzo, ssend.at[1], srcs.at[1], srxs.at[1], srzs.at[1])
    g.begin()
    for l in loads: l.wait()
    when(extra, load_spare.wait)
    mid = (z > 0) & (z < NZ - 1)
    p = [z,
         jnp.where(z == 0, 1, jnp.where(z == 1, 0, jnp.where(z == 2, 3, 2))),
         jnp.where(z == 0, 2, jnp.where(z == 1, 2, 1)),
         jnp.where(z < 2, 3, 0)]

    def tiles(zz):
        rows = pl.ds(pl.multiple_of(4 * zz, 4), 4)
        tok = pl.ds(pl.multiple_of(512 * zz, 512), 512)
        @pl.loop(0, 2)
        def _(t):
            a = n2[rows].reshape(512, D)
            k = cot[rows].reshape(512, D)
            def col(base):
                return pl.ds(pl.multiple_of(base + 256 * t, 256), 256)
            dg, du, h = gated(dot(a, w[:, col(0)]), dot(a, w[:, col(MAIN)]), dot(k, w[:, col(2 * MAIN)]))
            act[tok, col(0)] = dg
            act[tok, col(MAIN)] = du
            act[tok, col(2 * MAIN)] = h
        def spare():
            pre = dot(n2[rows].reshape(512, D), w[:, 3 * MAIN : 3 * MAIN + 256])
            dg, du, h = gated(pre[:, :128], pre[:, 128:], dot(cot[rows].reshape(512, D), w[:, 3 * MAIN + 256 :]))
            act[tok, 3 * MAIN : 3 * MAIN + 128] = dg
            act[tok, 3 * MAIN + 128 : 3 * MAIN + 256] = du
            act[tok, 3 * MAIN + 256 :] = h
        when(extra, spare)
        def out_tiles(more):
            @pl.loop(0, D // 256)
            def _(t):
                dr = pl.ds(pl.multiple_of(256 * t, 256), 256)
                v = dot_nt(act[tok, : 2 * MAIN], w[dr, : 2 * MAIN])
                u = dot_nt(act[tok, 2 * MAIN : 3 * MAIN], w[dr, 2 * MAIN : 3 * MAIN])
                if more:
                    v += dot_nt(act[tok, 3 * MAIN : 3 * MAIN + 256], w[dr, 3 * MAIN : 3 * MAIN + 256])
                    u += dot_nt(act[tok, 3 * MAIN + 256 :], w[dr, 3 * MAIN + 256 :])
                pg[rows, :, dr] = v.astype(BF).reshape(4, 128, 256)
                po[rows, :, dr] = u.astype(BF).reshape(4, 128, 256)
        when(extra, lambda: out_tiles(True))
        when(~extra, lambda: out_tiles(False))
        rg.send_c(zz)
        ro.send_c(zz)

    g.from_z(p[1])
    when(mid, lambda: g.from_z(p[2]))
    g.from_x(p[0])
    g.from_c(p[0])
    pltpu.make_async_copy(n2_ref, n2.at[0], glocal).wait()
    tiles(p[0])
    g.from_z(jnp.where(mid, p[3], p[2]))
    g.from_x(p[1])
    g.from_c(p[1])
    tiles(p[1])
    when(~mid, lambda: g.from_z(p[3]))
    g.from_x(p[2])
    g.from_c(p[2])
    tiles(p[2])
    rg.x_plane(p[2])
    g.from_x(p[3])
    g.from_c(p[3])
    tiles(p[3])

    ydev = (1 - r, idx(z, x, c))
    own = D // 16
    half = own // 2
    def ycopy(j, spare):
        cols = SP if spare else MM
        src = w.at[pl.ds(pl.multiple_of(own * j + half * (1 - r), half), half), cols]
        a, b = (xsend, xrecv) if spare else (ysend, yrecv)
        return pltpu.make_async_remote_copy(src, yb.at[j, :, cols], a.at[j], b.at[j], device_id=ydev, device_id_type=MESH)
    def grads(q):
        dr = slice(384 * q, 384 * (q + 1))
        row = slice(384 * q, 384 * (q + 1))
        @pl.loop(0, 4)
        def _(t):
            col = pl.ds(pl.multiple_of(256 * t, 256), 256)
            w[row, col] = dot_tn(n2[:, :, dr].reshape(2048, 384), act[:, col]).astype(BF)
        @pl.loop(0, 2)
        def _(t):
            col = pl.ds(pl.multiple_of(2 * MAIN + 256 * t, 256), 256)
            w[row, col] = dot_tn(cot[:, :, dr].reshape(2048, 384), act[:, col]).astype(BF)
        for j in range(4 * q, 4 * q + 4):
            ycopy(j, 0).start()
        def spare():
            w[row, 3 * MAIN : 3 * MAIN + 256] = dot_tn(n2[:, :, dr].reshape(2048, 384), act[:, 3 * MAIN : 3 * MAIN + 256]).astype(BF)
            w[row, 3 * MAIN + 256 :] = dot_tn(cot[:, :, dr].reshape(2048, 384), act[:, 3 * MAIN + 256 :]).astype(BF)
            for j in range(4 * q, 4 * q + 4):
                ycopy(j, 1).start()
        when(extra, spare)
    def yadd(j):
        def add(spare):
            cols = SP if spare else MM
            ycopy(j, spare).wait()
            mine = w[pl.ds(pl.multiple_of(own * j + half * r, half), half), cols]
            yb[j, :, cols] = (mine.astype(F32) + yb[j, :, cols].astype(F32)).astype(BF)
            pltpu.make_async_copy(yb.at[j, :, cols], half_ref.at[j, :, cols], lsem.at[4 if spare else 2]).start()
        add(0)
        when(extra, lambda: add(1))

    rg.x_plane(p[3])
    rg.x_plane(p[1])
    grads(0)
    rg.step_z(3)
    rg.step_z(2)
    rg.x_plane(p[0])
    ro.x_plane(p[3])
    grads(1)
    rg.step_z(1)
    ro.x_plane(p[2])
    grads(2)
    ro.x_plane(p[1])
    ro.step_z(3)
    rg.finish(gsum)
    grads(3)
    ro.x_plane(p[0])
    ro.step_z(2)
    for j in range(0, 8): yadd(j)
    ro.step_z(1)
    for j in range(8, 12): yadd(j)
    ro.finish(osum)
    for j in range(12, 16): yadd(j)
    pltpu.make_async_copy(yb.at[:, :, MM], half_ref.at[:, :, MM], lsem.at[2]).wait()
    when(extra, lambda: pltpu.make_async_copy(yb.at[:, :, SP], half_ref.at[:, :, SP], lsem.at[4]).wait())
    g.end(local=False)

def mlp(n2, cot, w, cid):
    blk = n2.shape
    dma = pltpu.SemaphoreType.DMA
    full = (16,) + blk
    return pl.pallas_call(
        mlp_kernel,
        out_shape=[jax.ShapeDtypeStruct(blk, F32)] * 2 + [jax.ShapeDtypeStruct((16, D // 32, COLS), BF)],
        in_specs=[pl.BlockSpec(memory_space=pl.ANY)] * 3,
        out_specs=[pl.BlockSpec(memory_space=pltpu.VMEM)] * 2 + [pl.BlockSpec(memory_space=pl.ANY)],
        scratch_shapes=[pltpu.VMEM(full, BF), pltpu.VMEM(full, BF), pltpu.VMEM((D, COLS), BF), pltpu.VMEM((16 * blk[0], COLS), BF),
                        pltpu.VMEM(full, BF), pltpu.VMEM(full, BF)]
        + [pltpu.VMEM((k,) + blk, BF) for k in (8, 4, 5, 8, 4, 5)]
        + [pltpu.VMEM((16, D // 32, COLS), BF)]
        + [dma((18,)), dma((16,)), dma(()), dma((5,)), dma((2, 16)), dma((2, 8)), dma((2, 4)), dma((2, 5))] + [dma((16,))] * 4,
        compiler_params=pltpu.CompilerParams(collective_id=cid, has_side_effects=True, vmem_limit_bytes=60 * 2**20),
    )(n2, cot, w)


def spin(u, cos, sin):
    return u * cos + pltpu.roll(u, HEAD_DIM // 2, 1) * sin

def stack_heads(v):
    n = v.shape[1] // HEAD_DIM
    return jnp.concatenate([v[:, HEAD_DIM * i : HEAD_DIM * (i + 1)] for i in range(n)], axis=0)

def spread_heads(v, rows):
    n = v.shape[0] // rows
    return jnp.concatenate([v[rows * i : rows * (i + 1)] for i in range(n)], axis=1)

def exp_scores(q, k, first_row, block, length):
    sc = dot_nt(q, k) * (HEAD_DIM ** -0.5)
    key = lax.broadcasted_iota(jnp.int32, sc.shape, 1)
    row = jnp.bitwise_and(lax.broadcasted_iota(jnp.int32, sc.shape, 0), block - 1) + first_row
    return jnp.where((key <= row) & (key < length), jnp.exp(sc), 0.0)

def rms(v, gain):
    factor = lax.rsqrt(jnp.mean(v * v, axis=-1, keepdims=True) + EPSILON)
    return v * factor * gain


class GatherY(Gather):
    def __init__(self, at, src, out, send, recv, local):
        Gather.__init__(self, at, src, out, send, recv, local)
        self.n = src.shape[0] // 2
        self.ydev = (1 - self.r, idx(self.z, self.x, self.c))
    def rows(self, h):
        return pl.ds(pl.multiple_of(h * self.n, self.n), self.n)
    def half(self, b, h):
        return self.out.at[b, self.rows(h)]
    def move(self, src, dst, k, q, dev):
        return pltpu.make_async_remote_copy(src, dst, self.send.at[k], self.recv.at[q], device_id=dev, device_id_type=MESH)
    def arrived(self, b, h):
        self.move(self.half(b, h), self.half(b, h), 0, 2 * b + h, self.ydev).wait_recv()
    def begin(self):
        z, x, c, r = self.z, self.x, self.c, self.r
        me = idx(z, x, c)
        mine, dst = self.src.at[self.rows(r)], self.half(me, r)
        for s in (1, -1):
            when(self.inside(z + s), lambda s=s: self.move(mine, dst, 0 if s == 1 else 3, 2 * me + r, self.zdev(s)).start())
        self.move(mine, dst, 6 + z, 2 * me + r, self.xdev()).start()
        self.move(self.src, self.out.at[me], 18 + 2 * z + x, 2 * me, self.cdev()).start()
        pltpu.make_async_copy(self.src, self.out.at[me], self.local).start()
    def from_z(self, zz):
        z, x, c, r = self.z, self.x, self.c, self.r
        b = idx(zz, x, c)
        q = 2 * b + r
        self.arrived(b, r)
        s = jnp.where(zz < z, 1, -1)
        slot = jnp.where(zz < z, 0, 3) + jnp.abs(zz - z)
        a = self.half(b, r)
        when(self.inside(z + s), lambda: self.move(a, a, slot, q, (r, idx(z + s, x, c))).start())
        self.move(a, a, 6 + zz, q, self.xdev()).start()
        self.move(a, a, 18 + 2 * zz + x, q, self.cdev()).start()
        self.move(a, a, 10 + 2 * zz + x, q, self.ydev).start()
    def from_x(self, zz):
        x, c, r = self.x, self.c, self.r
        b = idx(zz, 1 - x, c)
        q = 2 * b + r
        self.arrived(b, r)
        a = self.half(b, r)
        self.move(a, a, 18 + 2 * zz + 1 - x, q, self.cdev()).start()
        self.move(a, a, 10 + 2 * zz + 1 - x, q, self.ydev).start()
    def from_y(self, zz):
        x, c, r = self.x, self.c, self.r
        def take(xx):
            b = idx(zz, xx, c)
            self.arrived(b, 1 - r)
            a = self.half(b, 1 - r)
            self.move(a, a, 26 + 2 * zz + xx, 2 * b + 1 - r, self.cdev()).start()
        when(zz != self.z, lambda: take(x))
        take(1 - x)
    def from_c(self, zz):
        x, c, r = self.x, self.c, self.r
        b = idx(zz, x, 1 - c)
        whole = self.out.at[b]
        when(zz == self.z, lambda: self.move(whole, whole, 0, 2 * b, self.ydev).wait_recv())
        def both(b):
            self.arrived(b, r)
            self.arrived(b, 1 - r)
        when(zz != self.z, lambda: both(b))
        both(idx(zz, 1 - x, 1 - c))
    def end(self):
        z, x = self.z, self.x
        own = 2 * z + x
        a = self.half(0, 0)
        def sent(k, a=a):
            self.move(a, a, k, 0, self.ydev).wait_send()
        for d in range(NZ - 1):
            when((z - d >= 0) & (z < NZ - 1), lambda d=d: sent(d))
            when((z + d < NZ) & (z > 0), lambda d=d: sent(3 + d))
        for k in range(6, 10):
            sent(k)
        for k in range(8):
            def other(k=k):
                sent(10 + k)
                sent(18 + k)
                sent(26 + k)
            when(own != k, other)
        sent(18 + own, self.out.at[0])
        pltpu.make_async_copy(self.src, self.out.at[0], self.local).wait()

def front_kernel(block, lens, x_ref, cot_ref, v0, v1, v2, v3, v4, sel, fold, selk, foldk, rope_ref, wq, wk, wv, wg, wu, wd, wo_ref,
                 q_out, normed_out, att_out, mid_out, n2_out, vec, buf, qkv_out, kv_out, cot_out, wo_out,
                 rope, cot_own, small, qkv_own, wqkv, small_all, own, kv, wo,
                 qs, qr, ql, vs, vr, vl, ks, kr, kl, cs, cr, cl, ws, wr, wl, d0, d1, d2, d3, d4, d5, d6, d7, dl, lsem):
    at = place()
    width = HEADS * HEAD_DIM
    kw = KV_HEADS * HEAD_DIM
    loads = [pltpu.make_async_copy(w, qkv_own.at[:, pl.ds(o, n)], lsem.at[i]) for i, (w, o, n) in enumerate(((wq, 0, width), (wk, width, kw), (wv, width + kw, kw)))]
    first_row = lax.axis_index("group") * block
    loads.append(pltpu.make_async_copy(rope_ref.at[:, pl.ds(pl.multiple_of(first_row, block), block)], rope, lsem.at[6]))
    for l in loads: l.start()
    small[...] = jnp.zeros_like(small)
    for i, v in enumerate((v0, v1, v2, v3, v4)):
        small[i : i + 1, : v.shape[1]] = v[...].astype(F32)
    cot_own[...] = (cot_ref[...].astype(F32) * row_mask(lens, first_row, block, (cot_ref.shape[0], 1))).astype(BF)
    hail_all(*at)
    for l in loads: l.wait()
    gq = GatherY(at, qkv_own, wqkv, qs, qr, ql)
    gv = Gather(at, small, small_all, vs, vr, vl)
    gk = Gather(at, own, kv, ks, kr, kl)
    gc = Gather(at, cot_own, cot_out, cs, cr, cl)
    gw = GatherY(at, wo_ref, wo, ws, wr, wl)
    d = Deal(at, (wg, wu, wd), buf, (d0, d1, d2, d3, d4, d5, d6, d7), dl)
    steps = iter(range(15))
    def some(n):
        for _ in range(n):
            i = next(steps, None)
            if i is not None:
                d.step(i)
    gq.begin()
    gv.begin()
    d.begin()
    x = x_ref[...].astype(F32)
    gq.first()
    gv.first()
    gq.second()
    gv.second()
    gq.from_y(gq.p[0])
    some(EARLY[0])
    gq.third()
    gv.third()
    gq.from_y(gq.p[1])
    gq.fourth()
    gv.fourth()
    gc.begin()
    gq.from_y(gq.p[2])
    gq.from_y(gq.p[3])
    for zz in range(NZ):
        gv.from_c(zz)
        gq.from_c(zz)
    gv.end()
    gq.end()
    keep = [pltpu.make_async_copy(wqkv, qkv_out, lsem.at[3]), pltpu.make_async_copy(kv, kv_out, lsem.at[4]), pltpu.make_async_copy(wo, wo_out, lsem.at[5])]
    keep[0].start()
    vec[...] = jnp.zeros_like(vec)
    for i, row, first, a, b in ((0, 0, 0, sel, fold), (1, 1, 0, sel, fold), (2, 1, width, selk, foldk), (3, 1, width + kw, selk, foldk), (4, 2, 0, sel, fold)):
        t = dot_nt(small_all[:, i, :].astype(BF), b[...])
        vec[row : row + 1, first : first + a.shape[1]] = jnp.sum(t * a[...], axis=0, keepdims=True)
    normed_out[...] = rms(x, vec[0:1, :width]).astype(BF)
    cos, sin = [jnp.concatenate((rope[i], rope[i]), axis=0) for i in range(2)]
    def product(base):
        return dot(normed_out[...], wqkv[:, :, pl.ds(pl.multiple_of(base, 256), 256)].reshape(width, 256)) + vec[1:2, pl.ds(pl.multiple_of(base, 256), 256)]
    pre = product(width)
    own[:, :HEAD_DIM] = spin(pre[:, :HEAD_DIM], cos, sin).astype(BF)
    own[:, HEAD_DIM : 2 * HEAD_DIM] = spin(pre[:, HEAD_DIM:], cos, sin).astype(BF)
    own[:, kw:] = product(width + kw).astype(BF)
    gk.begin()
    gw.begin()
    @pl.loop(0, width // 256)
    def _(t):
        pre = product(t * 256)
        for i in range(2):
            col = pl.ds(pl.multiple_of(256 * t + HEAD_DIM * i, HEAD_DIM), HEAD_DIM)
            q_out[:, col] = spin(pre[:, HEAD_DIM * i : HEAD_DIM * (i + 1)], cos, sin).astype(BF)
    some(EARLY[1])
    gc.first()
    gk.first()
    gw.first()
    some(EARLY[2])
    gk.second()
    gc.second()
    gw.second()
    gw.from_y(gw.p[0])
    gk.third()
    some(EARLY[3])
    gk.fourth()
    gc.third()
    gw.third()
    gw.from_y(gw.p[1])
    for zz in range(NZ):
        gk.from_c(zz)
    gk.end()
    keep[1].start()
    span = 16 * block
    @pl.loop(0, 4)
    def _(u):
        s, h = u // 2, lax.rem(u, 2)
        rows = pl.ds(pl.multiple_of(block * s, block), block)
        cols = pl.ds(pl.multiple_of(width // 2 * h, width // 2), width // 2)
        q = stack_heads(q_out[rows, cols])
        k = kv[:, rows, pl.ds(pl.multiple_of(HEAD_DIM * h, HEAD_DIM), HEAD_DIM)].reshape(span, HEAD_DIM)
        v = kv[:, rows, pl.ds(pl.multiple_of(kw + HEAD_DIM * h, HEAD_DIM), HEAD_DIM)].reshape(span, HEAD_DIM)
        e = exp_scores(q, k, first_row, block, lens[s])
        total = jnp.sum(e, axis=-1, keepdims=True)
        att_out[rows, cols] = spread_heads(dot(e.astype(BF), v) / total, block)
    some(EARLY[4])
    gw.fourth()
    gc.fourth()
    gw.from_y(gw.p[2])
    gw.from_y(gw.p[3])
    for zz in range(NZ):
        gw.from_c(zz)
    gw.end()
    keep[2].start()
    @pl.loop(0, width // 256)
    def _(t):
        col = pl.ds(pl.multiple_of(256 * t, 256), 256)
        mid_out[:, col] = x_ref[:, col].astype(F32) + dot(att_out[...].astype(BF), wo[:, :, col].reshape(width, 256))
    n2_out[...] = rms(mid_out[...], vec[2:3, :width]).astype(BF)
    some(15)
    for zz in range(NZ):
        gc.from_c(zz)
    gc.end()
    for k in keep:
        k.wait()
    d.end()

EARLY = (2, 1, 1, 2, 3)

def front(lens, x, cot, vectors, sel, fold, selk, foldk, rope, wq, wk, wv, wg, wu, wd, wo, block, cid):
    rows, width = x.shape
    any_ = pl.BlockSpec(memory_space=pl.ANY)
    vm = pl.BlockSpec(memory_space=pltpu.VMEM)
    dma = pltpu.SemaphoreType.DMA
    act = (rows, width)
    own = wq.shape[0]
    kvw = 2 * KV_HEADS * HEAD_DIM
    wide = width + kvw
    sds = jax.ShapeDtypeStruct
    VM = pltpu.VMEM
    return pl.pallas_call(
        functools.partial(front_kernel, block),
        out_shape=[sds(act, BF), sds(act, BF), sds(act, F32), sds(act, F32), sds(act, BF), sds((8, wide), F32),
                   sds((16 * own, 3 * MAIN + 384), BF), sds((16, own, wide), BF), sds((16, rows, kvw), BF), sds((16,) + act, BF), sds((16,) + wo.shape, BF)],
        in_specs=[pl.BlockSpec(memory_space=pltpu.SMEM)] + [vm] * 11 + [any_] * 8,
        out_specs=[vm] * 6 + [any_] * 5,
        scratch_shapes=[VM((2, block, HEAD_DIM), F32), VM(act, BF), VM((8, 128), F32), VM((own, wide), BF), VM((16, own, wide), BF), VM((16, 8, 128), F32), VM((rows, kvw), BF), VM((16, rows, kvw), BF), VM((16,) + wo.shape, BF)]
        + [dma((34,)), dma((32,)), dma(())] + [dma((18,)), dma((16,)), dma(())] * 3 + [dma((34,)), dma((32,)), dma(())]
        + [dma((16,))] * 8 + [dma((2,)), dma((7,))],
        compiler_params=pltpu.CompilerParams(collective_id=cid, has_side_effects=True, vmem_limit_bytes=60 * 2**20),
    )(lens, x, cot, *vectors, sel, fold, selk, foldk, rope, wq, wk, wv, wg, wu, wd, wo)


class Return:
    def __init__(self, at, half_ref, out, sems, local):
        self.r, self.z, self.x, self.c = at
        self.me = idx(self.z, self.x, self.c)
        self.src, self.out, self.sems, self.local = half_ref, out, sems, local
        self.n = half_ref.shape[1]
    def places(self, j, spare):
        row = pl.ds(pl.multiple_of(self.r * self.n, self.n), self.n)
        col = spare_at(j) if spare else pl.ds(pl.multiple_of(j * MAIN, MAIN), MAIN)
        return [self.out.at[i, row, col] for i in range(3)]
    def parts(self, j, spare):
        if spare:
            return [self.src.at[j, :, pl.ds(3 * MAIN + 128 * i, 128)] for i in range(3)]
        return [self.src.at[j, :, pl.ds(i * MAIN, MAIN)] for i in range(3)]
    def copy(self, a, b, kind, k, dev):
        send, recv = self.sems[2 * kind : 2 * kind + 2]
        return pltpu.make_async_remote_copy(a, b, send.at[k], recv.at[k], device_id=dev, device_id_type=MESH)
    def launch(self, k):
        j = jnp.bitwise_xor(self.me, k)
        def go(spare):
            for a, b in zip(self.parts(j, spare), self.places(self.me, spare)):
                self.copy(a, b, spare, k, (self.r, j)).start()
        go(0)
        when(has(self.me), lambda: go(1))
    def forward(self, j, k, spare):
        for a in self.places(j, spare):
            self.copy(a, a, 2 + spare, k, (1 - self.r, self.me)).start()
    def begin(self, window):
        self.window = window
        def go(spare):
            for a, b in zip(self.parts(self.me, spare), self.places(self.me, spare)):
                pltpu.make_async_copy(a, b, self.local.at[spare]).start()
        go(0)
        when(has(self.me), lambda: go(1))
        for k in KS[:window]:
            self.launch(k)
    def sized(self, spare):
        return self.src.at[0, :, pl.ds(3 * MAIN, 384) if spare else pl.ds(0, 3 * MAIN)]
    def whole(self, kind, k):
        blk = self.sized(kind % 2)
        return self.copy(blk, blk, kind, k, (1 - self.r, self.me))
    def own(self):
        def go(spare):
            blk = self.sized(spare)
            pltpu.make_async_copy(blk, blk, self.local.at[spare]).wait()
            self.forward(self.me, 0, spare)
        go(0)
        when(has(self.me), lambda: go(1))
    def step(self, i):
        k = KS[i]
        j = jnp.bitwise_xor(self.me, k)
        def go(spare):
            self.whole(spare, k).wait_recv()
            self.forward(j, k, spare)
        go(0)
        when(has(j), lambda: go(1))
        if i + self.window < 15:
            self.launch(KS[i + self.window])
    def end(self):
        for k in (0,) + KS:
            j = jnp.bitwise_xor(self.me, k)
            self.whole(2, k).wait()
            when(has(j), lambda: self.whole(3, k).wait())
            if k:
                self.whole(0, k).wait_send()
                when(has(self.me), lambda: self.whole(1, k).wait_send())

def row_mask(lens, first_row, block, shape):
    row = lax.broadcasted_iota(jnp.int32, shape, 0)
    place = jnp.bitwise_and(row, block - 1) + first_row
    return jnp.where(place < jnp.where(row < block, lens[0], lens[1]), 1.0, 0.0)

def norm_gradient(v, gain, upstream):
    factor = lax.rsqrt(jnp.mean(v * v, axis=-1, keepdims=True) + EPSILON)
    weighted = upstream * gain
    inner = jnp.mean(weighted * v, axis=-1, keepdims=True)
    return factor * weighted - v * (factor * factor * factor) * inner, jnp.sum(upstream * v * factor, axis=0, keepdims=True)

def backward_kernel(block, window, lens, gn2, mlp_out, mid, cot, x_ref, att, q_ref, normed, vec, sel, fold, selk, foldk, rope_ref, kv_ref, wo_ref, wqkv_ref, half_ref,
                    layer_out, grad_input, q_out, pair_out, wo_out, vec_out, g_out,
                    rope, kv, wo, wqkv, gmid, branch, gatt, gqkv, pv,
                    p_kv, c_kv, x_kv, z_kv, p_wo, c_wo, w_wo, x_wo, z_wo, p_qk, c_qk, w_qk, x_qk, z_qk, p_pw, c_pw, x_pw, z_pw, p_ve, c_ve, x_ve, z_ve,
                    kvsum, low_o, low_q, y4, y5, y6, y7,
                    ss, sc, sx, sz, r0, r1, r2, r3, r4, r5, r6, r7, rl, ysem, fs, fc, fy, fx, fz, ft, lsem):
    at = place()
    r, z, x, c = at
    width = HEADS * HEAD_DIM
    kw = KV_HEADS * HEAD_DIM
    loads = [pltpu.make_async_copy(a, b, lsem.at[i]) for i, (a, b) in enumerate(((wo_ref, wo), (kv_ref, kv), (wqkv_ref, wqkv)))]
    first_row = lax.axis_index("group") * block
    loads.append(pltpu.make_async_copy(rope_ref.at[:, pl.ds(pl.multiple_of(first_row, block), block)], rope, lsem.at[3]))
    for l in loads: l.start()
    hail_all(*at)
    back = Return(at, half_ref, g_out, (r0, r1, r2, r3, r4, r5, r6, r7), rl)
    back.begin(window)
    sets = ((p_kv, c_kv, x_kv, z_kv), (p_pw, c_pw, x_pw, z_pw), (p_ve, c_ve, x_ve, z_ve))
    ek, ep, ev = [Scatter(at, *b, ss.at[i], sc.at[i], sx.at[i], sz.at[i]) for i, b in enumerate(sets)]
    sets = ((p_wo, c_wo, w_wo, x_wo, z_wo), (p_qk, c_qk, w_qk, x_qk, z_qk))
    eo, eq = [ScatterY(at, *b, fs.at[i], fc.at[i], fy.at[i], fx.at[i], fz.at[i], ft.at[i]) for i, b in enumerate(sets)]
    steps = iter(range(15))
    def some(n):
        for _ in range(n):
            i = next(steps, None)
            if i is not None:
                back.step(i)
    ydev = (1 - r, idx(z, x, c))
    def trade(i, out, a, b):
        a[...] = out[...].astype(BF)
        pltpu.make_async_remote_copy(a, b, ysem.at[2 * i], ysem.at[2 * i + 1], device_id=ydev, device_id_type=MESH).start()
    def traded(i, out, a, b):
        pltpu.make_async_remote_copy(a, b, ysem.at[2 * i], ysem.at[2 * i + 1], device_id=ydev, device_id_type=MESH).wait()
        out[...] = a[...].astype(F32) + b[...].astype(F32)

    grad_norm, gain_two = norm_gradient(mid[...], vec[2:3, :width], gn2[...])
    valid = row_mask(lens, first_row, block, (cot.shape[0], 1))
    gmid[...] = cot[...].astype(F32) * valid + grad_norm
    branch[...] = gmid[...].astype(BF)
    loads[0].wait()
    @pl.loop(0, 4)
    def _(t):
        blocks = pl.ds(pl.multiple_of(4 * t, 4), 4)
        col = pl.ds(pl.multiple_of(384 * t, 384), 384)
        low = att[:, col].astype(BF)
        p_wo[blocks] = dot_tn(low, branch[...]).astype(BF).reshape(4, 96, width)
        gatt[:, col] = dot_nt(branch[...], wo[blocks].reshape(384, width))
    eo.begin()
    for d in (3, 2, 1, 0):
        eo.step_y(d)
    back.own()
    layer_out[...] = ((mid[...] + mlp_out[...]) * valid).astype(BF)
    loads[1].wait()
    loads[3].wait()
    span = 16 * block
    def unit(u):
        s, h = u // 2, lax.rem(u, 2)
        rows = pl.ds(pl.multiple_of(block * s, block), block)
        cols = pl.ds(pl.multiple_of(width // 2 * h, width // 2), width // 2)
        kcol = pl.ds(pl.multiple_of(HEAD_DIM * h, HEAD_DIM), HEAD_DIM)
        vcol = pl.ds(pl.multiple_of(kw + HEAD_DIM * h, HEAD_DIM), HEAD_DIM)
        q = stack_heads(q_ref[rows, cols])
        k = kv[:, rows, kcol].reshape(span, HEAD_DIM)
        v = kv[:, rows, vcol].reshape(span, HEAD_DIM)
        e = exp_scores(q, k, first_row, block, lens[s])
        total = jnp.sum(e, axis=-1, keepdims=True)
        ga = stack_heads(gatt[rows, cols])
        gt = -jnp.sum(ga * stack_heads(att[rows, cols]), axis=-1, keepdims=True) / total
        gn = (ga / total).astype(BF)
        gs = (e * (dot_nt(gn, v) + gt)).astype(BF)
        p_kv[:, rows, kcol] = dot_tn(gs, q).astype(BF).reshape(16, block, HEAD_DIM)
        p_kv[:, rows, vcol] = dot_tn(e.astype(BF), gn).astype(BF).reshape(16, block, HEAD_DIM)
        gq = dot(gs, k) * (HEAD_DIM ** -0.5)
        cos, sin = rope[0], rope[1]
        gqkv[rows, cols] = jnp.concatenate([spin(gq[block * i : block * (i + 1)], cos, -sin) for i in range(HEADS // KV_HEADS)], axis=1).astype(BF)
    unit(0)
    some(1)
    eo.step_x(3)
    eo.step_x(2)
    unit(1)
    eo.step_z(3)
    eo.step_x(1)
    some(1)
    eo.step_z(2)
    eo.step_x(0)
    unit(2)
    some(1)
    eo.step_z(1)
    unit(3)
    ek.begin()
    ek.step_x(3)
    ek.step_x(2)
    some(1)
    loads[2].wait()
    @pl.loop(0, 4)
    def _(t):
        blocks = pl.ds(pl.multiple_of(4 * t, 4), 4)
        col = pl.ds(pl.multiple_of(384 * t, 384), 384)
        p_qk[blocks] = dot_tn(normed[:, col], gqkv[:, :width]).astype(BF).reshape(4, 96, width)
    ek.step_z(3)
    ek.step_x(1)
    eq.begin()
    eo.finish(wo_out, low_o)
    for d in (3, 2, 1, 0):
        eq.step_y(d)
    ek.step_z(2)
    ek.step_x(0)
    some(1)
    @pl.loop(0, 4)
    def _(t):
        blocks = pl.ds(pl.multiple_of(4 * t, 4), 4)
        col = pl.ds(pl.multiple_of(384 * t, 384), 384)
        gatt[:, col] = dot_nt(gqkv[:, :width], wqkv[blocks, :, :width].reshape(384, width))
    ek.step_z(1)
    eq.step_x(3)
    eq.step_x(2)
    some(1)
    ek.finish(kvsum)
    cos, sin = [jnp.concatenate((rope[i], rope[i]), axis=0) for i in range(2)]
    for h in range(KV_HEADS):
        kcol = slice(HEAD_DIM * h, HEAD_DIM * (h + 1))
        gqkv[:, width + HEAD_DIM * h : width + HEAD_DIM * (h + 1)] = spin(kvsum[:, kcol] * (HEAD_DIM ** -0.5), cos, -sin).astype(BF)
    gqkv[:, width + kw :] = kvsum[:, kw:].astype(BF)
    @pl.loop(0, 4)
    def _(t):
        blocks = pl.ds(pl.multiple_of(4 * t, 4), 4)
        col = pl.ds(pl.multiple_of(384 * t, 384), 384)
        p_pw[blocks] = dot_tn(normed[:, col], gqkv[:, width:]).astype(BF).reshape(4, 96, 2 * kw)
        gatt[:, col] += dot_nt(gqkv[:, width:], wqkv[blocks, :, width:].reshape(384, 2 * kw))
    ep.begin()
    ep.step_x(3)
    ep.step_x(2)
    eq.step_z(3)
    eq.step_x(1)
    some(1)
    grad_norm, gain_one = norm_gradient(x_ref[...].astype(F32), vec[0:1, :width], gatt[...])
    grad_input[...] = gmid[...] + grad_norm
    bias = jnp.sum(gqkv[...].astype(F32), axis=0, keepdims=True)
    pv[...] = jnp.zeros_like(pv)
    for i, (v, a, b) in enumerate(((gain_one, sel, fold), (bias[:, :width], sel, fold), (bias[:, width : width + kw], selk, foldk), (bias[:, width + kw :], selk, foldk), (gain_two, sel, fold))):
        pv[:, i, :] = dot((a[...] * v).astype(BF), b[...])
    p_ve[...] = pv[...].astype(BF)
    ev.begin()
    ev.step_x(3)
    ev.step_x(2)
    some(1)
    late = (ep, ev)
    for kind, d in (("z", 3), ("x", 1), ("z", 2), ("x", 0), ("z", 1)):
        for e in late:
            (e.step_x if kind == "x" else e.step_z)(d)
        if (kind, d) not in (("z", 3), ("x", 1)):
            (eq.step_x if kind == "x" else eq.step_z)(d)
        some(1)
    some(15)
    eq.finish(q_out, low_q)
    ep.finish(pair_out)
    trade(0, pair_out, y4, y5)
    ev.finish(vec_out)
    trade(1, vec_out, y6, y7)
    eo.traded(wo_out, low_o)
    eq.traded(q_out, low_q)
    traded(0, pair_out, y4, y5)
    traded(1, vec_out, y6, y7)
    back.end()

def backward(lens, gn2, mlp_out, mid, cot, x, att, q, normed, vec, sel, fold, selk, foldk, rope, kv, wo, wqkv, half, ff, block, cid, window=4):
    any_ = pl.BlockSpec(memory_space=pl.ANY)
    vm = pl.BlockSpec(memory_space=pltpu.VMEM)
    dma = pltpu.SemaphoreType.DMA
    sds = jax.ShapeDtypeStruct
    rows, width = x.shape
    wide = wqkv.shape[-1]
    own = wo.shape[1]
    kvw = kv.shape[-1]
    VM = pltpu.VMEM
    def four(blk):
        return [VM((k,) + blk, BF) for k in (16, 8, 4, 5)]
    def five(blk):
        part = (blk[0] // 2, blk[1])
        return [VM((k,) + blk, BF) for k in (16, 8)] + [VM((k,) + part, BF) for k in (8, 4, 5)]
    return pl.pallas_call(
        functools.partial(backward_kernel, block, window),
        out_shape=[sds((rows, width), BF), sds((rows, width), F32), sds((own, width), F32), sds((own, wide - width), F32), sds((own, width), F32), sds((16, 128), F32), sds((3, own, ff), BF)],
        in_specs=[pl.BlockSpec(memory_space=pltpu.SMEM)] + [vm] * 13 + [any_] * 5,
        out_specs=[vm] * 6 + [any_],
        scratch_shapes=[VM((2, block, HEAD_DIM), F32), VM(kv.shape, BF), VM(wo.shape, BF), VM(wqkv.shape, BF), VM((rows, width), F32), VM((rows, width), BF), VM((rows, width), F32), VM((rows, wide), BF), VM((16, 16, 128), F32)]
        + four((rows, kvw)) + five((own, width)) + five((own, width)) + four((own, wide - width)) + four((16, 128))
        + [VM((rows, kvw), F32)] + [VM((own, width), BF)] * 2 + [VM((own, wide - width), BF)] * 2 + [VM((16, 128), BF)] * 2
        + [dma((3, 16)), dma((3, 8)), dma((3, 4)), dma((3, 5))] + [dma((16,))] * 8 + [dma((2,)), dma((4,)), dma((2, 24)), dma((2, 8)), dma((2, 8)), dma((2, 4)), dma((2, 5)), dma((2, 2)), dma((4,))],
        compiler_params=pltpu.CompilerParams(collective_id=cid, has_side_effects=True, vmem_limit_bytes=60 * 2**20),
    )(lens, gn2, mlp_out, mid, cot, x, att, q, normed, vec, sel, fold, selk, foldk, rope, kv, wo, wqkv, half)


def folding(group_count, width):
    share = width // group_count
    at = np.arange(width)
    sel = (at[None, :] // share == np.arange(group_count)[:, None]).astype(np.float32)
    fold = (at[:, None] % share == np.arange(128)[None, :]).astype(BF)
    return sel, fold


def rope_constants(span):
    freqs = np.float32(THETA) ** (-np.arange(0, HEAD_DIM, 2, dtype=np.float32) / HEAD_DIM)
    angles = np.arange(span, dtype=np.float32)[:, None] * freqs[None, :].astype(np.float32)
    sin = np.sin(angles)
    return np.stack(
        (np.concatenate((np.cos(angles),) * 2, axis=1), np.concatenate((-sin, sin), axis=1))
    ).astype(np.float32)


def shards_fast(
    hidden_in,
    lengths,
    gain_attn,
    w_query,
    b_query,
    w_key,
    b_key,
    w_value,
    b_value,
    w_out,
    gain_mlp,
    w_gate,
    w_up,
    w_down,
    cotangent,
):
    group_count = lax.axis_size("group")
    slot_count, block_len, model_width = hidden_in.shape
    kv_width = KV_HEADS * HEAD_DIM
    tokens = slot_count * block_len
    hidden_units = w_gate.shape[1]
    pieces = (gain_attn, b_query, b_key, b_value, gain_mlp)
    sel, fold = folding(group_count, model_width)
    selk, foldk = folding(group_count, kv_width)
    rope = rope_constants(group_count * block_len)
    rows_in = hidden_in.reshape(tokens, model_width)
    grad_rows = cotangent.reshape(tokens, model_width)
    (
        q_rows, normed, attended, mid, normed_two, vec, columns, qkv_w, pair_all, grad_all, out_w
    ) = front(
        lengths,
        rows_in,
        grad_rows,
        [p[None] for p in pieces],
        sel,
        fold,
        selk,
        foldk,
        rope,
        w_query,
        w_key,
        w_value,
        w_gate,
        w_up,
        w_down,
        w_out,
        block_len,
        1,
    )
    grad_normed_two, mlp_out, half_sum = mlp(normed_two, grad_all, columns, 3)
    layer_out, grad_input, query_sum, pair_sum, out_sum, vector_sum, ff_sum = backward(
        lengths,
        grad_normed_two,
        mlp_out,
        mid,
        grad_rows,
        rows_in,
        attended,
        q_rows,
        normed,
        vec,
        sel,
        fold,
        selk,
        foldk,
        rope,
        pair_all,
        out_w,
        qkv_w,
        half_sum,
        hidden_units,
        block_len,
        4,
    )
    ff_sums = [ff_sum[i].astype(F32) for i in range(3)]
    gain_one_sum, query_bias_sum, key_bias_sum, value_bias_sum, gain_two_sum = [
        vector_sum[i, : p.shape[0]] for i, p in enumerate(pieces)
    ]
    return (
        layer_out.reshape(hidden_in.shape),
        grad_input.reshape(hidden_in.shape),
        gain_one_sum,
        query_sum,
        query_bias_sum,
        pair_sum[:, :kv_width],
        key_bias_sum,
        pair_sum[:, kv_width:],
        value_bias_sum,
        out_sum,
        gain_two_sum,
        *ff_sums,
    )


def solution(mesh):
    act = P("replica", "group", None)
    vec = P("group")
    mat = P("group", None)
    return jax.shard_map(
        shards_fast if mesh.shape["group"] == 16 else shards_plain,
        mesh=mesh,
        in_specs=(act, P("replica"), vec, mat, vec, mat, vec, mat, vec, mat, vec, mat, mat, mat, act),
        out_specs=(act, act, vec, mat, vec, mat, vec, mat, vec, mat, vec, mat, mat, mat),
        check_vma=False,
    )
```

```python
import functools

import jax
import jax.numpy as jnp
import numpy as np
from jax import lax
from jax.experimental import pallas as pl
from jax.experimental.pallas import tpu as pltpu
from jax.sharding import PartitionSpec as P

MESH = pl.DeviceIdType.MESH
NZ = 4
MAIN = 512
D = 1536
COLS = 3 * MAIN + 384
HEADS = 12
KV_HEADS = 2
HEAD_DIM = 128
EPSILON = 1e-06
THETA = 1000000.0
BF = jnp.bfloat16
F32 = jnp.float32


def rope_tables(positions, head_dim):
    freqs = THETA ** (-jnp.arange(0, head_dim, 2).astype(F32) / head_dim)
    angles = positions.astype(F32)[:, None] * freqs[None, :]
    angles = jnp.concatenate((angles, angles), axis=-1)
    return (jnp.cos(angles), jnp.sin(angles))


def rotate(tensor, cos_table, sin_table):
    halfway = tensor.shape[-1] // 2
    turned = jnp.concatenate((-tensor[..., halfway:], tensor[..., :halfway]), axis=-1)
    return tensor * cos_table + turned * sin_table


def rotate_back(gradient, cos_table, sin_table):
    halfway = gradient.shape[-1] // 2
    scaled = gradient * sin_table
    turned = jnp.concatenate((scaled[..., halfway:], -scaled[..., :halfway]), axis=-1)
    return gradient * cos_table + turned


def normalize(row_values, gain_vec):
    factor = lax.rsqrt(jnp.mean(row_values * row_values, axis=-1, keepdims=True) + EPSILON)
    return (row_values * factor * gain_vec, factor)


def norm_back(row_values, factor, gain_vec, upstream):
    weighted = upstream * gain_vec
    inner_mean = jnp.mean(weighted * row_values, axis=-1, keepdims=True)
    grad_rows = factor * weighted - row_values * (factor * factor * factor) * inner_mean
    grad_gain = jnp.sum(upstream * row_values * factor, axis=0)
    return (grad_rows, grad_gain)


def matmul(a, b):
    return jnp.dot(a, b, preferred_element_type=F32)


def matmul_nt(a, b):
    return lax.dot_general(a, b, (((1,), (1,)), ((), ())), preferred_element_type=F32)


def matmul_tn(a, b):
    return lax.dot_general(a, b, (((0,), (0,)), ((), ())), preferred_element_type=F32)


def arrange(per_token, kv_heads):
    block_len, head_count, head_dim = per_token.shape
    repeat = head_count // kv_heads
    grouped = per_token.reshape(block_len, kv_heads, repeat, head_dim)
    return jnp.transpose(grouped, (1, 2, 0, 3)).reshape(kv_heads, repeat * block_len, head_dim)


def restore(per_group, block_len):
    kv_heads, row_count, head_dim = per_group.shape
    repeat = row_count // block_len
    grouped = per_group.reshape(kv_heads, repeat, block_len, head_dim)
    return jnp.transpose(grouped, (2, 0, 1, 3)).reshape(block_len, kv_heads * repeat * head_dim)


def masked_exp(query_rows, key_block, row_pos, first_key, length, score_scale):
    key_step = key_block.shape[0]
    raw_scores = jnp.einsum("grd,kgd->grk", query_rows, key_block, preferred_element_type=F32)
    key_pos = first_key + jnp.arange(key_step, dtype=jnp.int32)
    allowed = (key_pos[None, :] <= row_pos[:, None]) & (key_pos[None, :] < length)
    return jnp.where(allowed[None], jnp.exp(raw_scores * score_scale), 0.0)


def block_total(length, rank_end, key_step):
    key_limit = jnp.minimum(length, rank_end)
    return (key_limit + key_step - 1) // key_step


def attend_forward(query_rows, key_all, value_all, row_pos, length, rank_end, key_step, scale):
    kv_heads, row_count, head_dim = query_rows.shape

    def visit(block_index, state_tuple):
        totals, numerator = state_tuple
        first_key = block_index * key_step
        key_block = lax.dynamic_slice_in_dim(key_all, first_key, key_step, 0)
        value_block = lax.dynamic_slice_in_dim(value_all, first_key, key_step, 0)
        weights = masked_exp(query_rows, key_block, row_pos, first_key, length, scale)
        totals = totals + jnp.sum(weights, axis=-1)
        numerator = numerator + jnp.einsum(
            "grk,kgd->grd", weights.astype(BF), value_block, preferred_element_type=F32
        )
        return (totals, numerator)

    initial = (
        jnp.zeros((kv_heads, row_count), F32),
        jnp.zeros((kv_heads, row_count, head_dim), F32),
    )
    return lax.fori_loop(0, block_total(length, rank_end, key_step), visit, initial)


def attend_backward(
    query_rows, key_all, value_all, row_pos, length, rank_end, key_step, scale, grad_numer, grad_total
):
    kv_heads, row_count, head_dim = query_rows.shape

    def visit(block_index, state_tuple):
        grad_query, grad_key, grad_value = state_tuple
        first_key = block_index * key_step
        key_block = lax.dynamic_slice_in_dim(key_all, first_key, key_step, 0)
        value_block = lax.dynamic_slice_in_dim(value_all, first_key, key_step, 0)
        weights = masked_exp(query_rows, key_block, row_pos, first_key, length, scale)
        grad_prob = jnp.einsum("grd,kgd->grk", grad_numer, value_block, preferred_element_type=F32)
        grad_score = (weights * (grad_prob + grad_total[..., None])).astype(BF)
        grad_query = grad_query + jnp.einsum(
            "grk,kgd->grd", grad_score, key_block, preferred_element_type=F32
        )
        key_part = jnp.einsum("grk,grd->kgd", grad_score, query_rows, preferred_element_type=F32)
        value_part = jnp.einsum(
            "grk,grd->kgd", weights.astype(BF), grad_numer, preferred_element_type=F32
        )
        key_old = lax.dynamic_slice_in_dim(grad_key, first_key, key_step, 0)
        value_old = lax.dynamic_slice_in_dim(grad_value, first_key, key_step, 0)
        grad_key = lax.dynamic_update_slice_in_dim(grad_key, key_old + key_part, first_key, 0)
        grad_value = lax.dynamic_update_slice_in_dim(
            grad_value, value_old + value_part, first_key, 0
        )
        return (grad_query, grad_key, grad_value)

    initial = (
        jnp.zeros((kv_heads, row_count, head_dim), F32),
        jnp.zeros(key_all.shape, F32),
        jnp.zeros(value_all.shape, F32),
    )
    return lax.fori_loop(0, block_total(length, rank_end, key_step), visit, initial)


def gather_plain(x):
    return lax.all_gather(x, "group", axis=0, tiled=True)


def scatter_sum(x):
    return lax.psum_scatter(x, "group", scatter_dimension=0, tiled=True)


def shards_plain(
    hidden_in,
    lengths,
    gain_attn,
    w_query,
    b_query,
    w_key,
    b_key,
    w_value,
    b_value,
    w_out,
    gain_mlp,
    w_gate,
    w_up,
    w_down,
    cotangent,
):
    group_count = lax.axis_size("group")
    group_rank = lax.axis_index("group")
    slot_count, block_len, model_width = hidden_in.shape
    kv_heads = KV_HEADS
    head_dim = HEAD_DIM
    kv_width = kv_heads * head_dim
    repeat = HEADS // kv_heads
    slot_span = block_len * group_count
    key_step = min(512, slot_span)
    score_scale = head_dim ** (-0.5)
    tokens = slot_count * block_len
    hidden_units = w_gate.shape[1]
    own_rows = w_gate.shape[0]
    share = hidden_units // group_count
    positions = group_rank * block_len + jnp.arange(block_len, dtype=jnp.int32)
    valid_rows = (positions[None, :] < lengths[:, None]).astype(F32).reshape(tokens, 1)
    cos_table, sin_table = rope_tables(positions, head_dim)
    cos_heads = cos_table[:, None, :]
    sin_heads = sin_table[:, None, :]
    rank_end = (group_rank + 1) * block_len
    row_pos = jnp.tile(positions, repeat)

    pieces = (gain_attn, b_query, b_key, b_value, gain_mlp)
    sizes = [p.shape[0] for p in pieces]
    small = gather_plain(jnp.concatenate(pieces)[None])
    offsets = [sum(sizes[:i]) for i in range(len(sizes) + 1)]
    gain_one, query_b, key_b, value_b, gain_two = [
        small[:, offsets[i] : offsets[i + 1]].reshape(-1).astype(F32) for i in range(len(sizes))
    ]
    qkv_w = gather_plain(jnp.concatenate((w_query, w_key, w_value), axis=1))
    out_w = gather_plain(w_out)
    qkv_b = jnp.concatenate((query_b, key_b, value_b))

    stacked = jnp.stack((w_gate, w_up, w_down)).reshape(3, own_rows, group_count, share)
    stacked = jnp.transpose(stacked, (2, 1, 0, 3)).reshape(group_count, own_rows, 3 * share)
    columns = lax.all_to_all(stacked, "group", 0, 0, tiled=True).reshape(model_width, 3 * share)
    gate_up_w = columns[:, : 2 * share]
    down_w = columns[:, 2 * share :]

    grad_final = cotangent.reshape(tokens, model_width).astype(F32) * valid_rows
    grad_all = gather_plain(grad_final.astype(BF))

    inputs = hidden_in.reshape(tokens, model_width).astype(F32)
    normed_full, factor_one = normalize(inputs, gain_one)
    normed = normed_full.astype(BF)
    qkv = matmul(normed, qkv_w) + qkv_b
    query_rot = rotate(
        qkv[:, :model_width].reshape(slot_count, block_len, HEADS, head_dim), cos_heads, sin_heads
    ).astype(BF)
    key_rot = rotate(
        qkv[:, model_width : model_width + kv_width].reshape(
            slot_count, block_len, kv_heads, head_dim
        ),
        cos_heads,
        sin_heads,
    ).astype(BF)
    value_low = qkv[:, model_width + kv_width :].astype(BF)
    pair = jnp.concatenate(
        (key_rot.reshape(tokens, kv_width), value_low), axis=1
    ).reshape(1, slot_count, block_len, 2 * kv_width)
    pair_all = jnp.transpose(gather_plain(pair), (1, 0, 2, 3)).reshape(
        slot_count, slot_span, 2, kv_heads, head_dim
    )
    key_all = pair_all[:, :, 0]
    value_all = pair_all[:, :, 1]
    query_groups = []
    slot_totals = []
    slot_attended = []
    attended_rows = []
    for s in range(slot_count):
        query_rows = arrange(query_rot[s], kv_heads)
        totals, numerator = attend_forward(
            query_rows, key_all[s], value_all[s], row_pos, lengths[s], rank_end, key_step, score_scale
        )
        attended = numerator / totals[..., None]
        query_groups.append(query_rows)
        slot_totals.append(totals)
        slot_attended.append(attended)
        attended_rows.append(restore(attended, block_len))
    attended_low = jnp.concatenate(attended_rows, axis=0).astype(BF)
    residual_mid = inputs + matmul(attended_low, out_w)
    normed_two_full, factor_two = normalize(residual_mid, gain_two)
    normed_all = gather_plain(normed_two_full.astype(BF))

    pre = matmul(normed_all, gate_up_w)
    gate_pre = pre[:, :share]
    up_pre = pre[:, share:]
    sigmoid_gate = jax.nn.sigmoid(gate_pre)
    silu_gate = gate_pre * sigmoid_gate
    hidden = (silu_gate * up_pre).astype(BF)
    grad_hidden = matmul(grad_all, down_w)
    grad_gate = (
        grad_hidden * up_pre * (sigmoid_gate * (1.0 + gate_pre * (1.0 - sigmoid_gate)))
    ).astype(BF)
    grad_up = (grad_hidden * silu_gate).astype(BF)
    gate_up_grad = jnp.concatenate((grad_gate, grad_up), axis=1)
    grad_normed_two = scatter_sum(matmul_nt(gate_up_grad, gate_up_w).astype(BF)).astype(F32)
    mlp_out = scatter_sum(matmul_nt(hidden, down_w).astype(BF)).astype(F32)
    down_term = matmul_tn(grad_all, hidden)
    gate_up_term = matmul_tn(normed_all, gate_up_grad)
    terms = jnp.concatenate((gate_up_term, down_term), axis=1).astype(BF)
    back = lax.all_to_all(
        terms.reshape(group_count, own_rows, 3 * share), "group", 0, 0, tiled=True
    )
    summed = back.astype(F32) + lax.ppermute(back, "replica", [(0, 1), (1, 0)]).astype(F32)
    summed = jnp.transpose(summed.reshape(group_count, own_rows, 3, share), (2, 1, 0, 3))
    gate_sum, up_sum, down_sum = summed.reshape(3, own_rows, hidden_units)

    final_rows = residual_mid + mlp_out
    layer_out = (final_rows * valid_rows).reshape(slot_count, block_len, model_width).astype(BF)
    grad_mid_norm, grad_gain_two = norm_back(residual_mid, factor_two, gain_two, grad_normed_two)
    grad_mid = grad_final + grad_mid_norm
    grad_branch = grad_mid.astype(BF)
    out_term = matmul_tn(attended_low, grad_branch)
    grad_attended = matmul_nt(grad_branch, out_w)
    grad_query_rows = []
    grad_pairs = []
    for s in range(slot_count):
        slot_grad = grad_attended[s * block_len : (s + 1) * block_len].reshape(
            block_len, HEADS, head_dim
        )
        grad_out = arrange(slot_grad, kv_heads)
        totals = slot_totals[s]
        grad_total = -jnp.sum(grad_out * slot_attended[s], axis=-1) / totals
        grad_numer = (grad_out / totals[..., None]).astype(BF)
        grad_query, grad_key, grad_value = attend_backward(
            query_groups[s],
            key_all[s],
            value_all[s],
            row_pos,
            lengths[s],
            rank_end,
            key_step,
            score_scale,
            grad_numer,
            grad_total,
        )
        query_back_rows = restore(grad_query * score_scale, block_len).reshape(
            block_len, HEADS, head_dim
        )
        grad_query_rows.append(
            rotate_back(query_back_rows, cos_heads, sin_heads).reshape(block_len, HEADS * head_dim)
        )
        grad_pairs.append(
            jnp.concatenate(
                (grad_key.reshape(slot_span, kv_width), grad_value.reshape(slot_span, kv_width)),
                axis=1,
            )
        )
    pair_grads = jnp.stack(grad_pairs).reshape(slot_count, group_count, block_len, 2 * kv_width)
    pair_grads = jnp.transpose(pair_grads, (1, 0, 2, 3)).astype(BF)
    pair_sum = scatter_sum(pair_grads).reshape(slot_count, block_len, 2 * kv_width).astype(F32)
    grad_query_pre = jnp.concatenate(grad_query_rows, axis=0).astype(BF)
    key_sum = pair_sum[..., :kv_width].reshape(slot_count, block_len, kv_heads, head_dim)
    grad_key_pre = (
        rotate_back(key_sum * score_scale, cos_heads, sin_heads).astype(BF).reshape(tokens, kv_width)
    )
    grad_value_pre = pair_sum[..., kv_width:].astype(BF).reshape(tokens, kv_width)
    grad_qkv = jnp.concatenate((grad_query_pre, grad_key_pre, grad_value_pre), axis=1)
    grad_normed = matmul_nt(grad_qkv, qkv_w)
    grad_in_norm, grad_gain_one = norm_back(inputs, factor_one, gain_one, grad_normed)
    grad_input = (grad_mid + grad_in_norm).reshape(slot_count, block_len, model_width)
    qkv_term = matmul_tn(normed, grad_qkv)
    qkv_bias = jnp.sum(grad_qkv.astype(F32), axis=0)

    weight_share = scatter_sum(
        jnp.concatenate((qkv_term, out_term), axis=1).astype(BF)
    )
    weight_sum = weight_share.astype(F32) + lax.ppermute(
        weight_share, "replica", [(0, 1), (1, 0)]
    ).astype(F32)
    vectors = jnp.concatenate(
        [
            grad_gain_one.reshape(group_count, -1),
            qkv_bias[:model_width].reshape(group_count, -1),
            qkv_bias[model_width : model_width + kv_width].reshape(group_count, -1),
            qkv_bias[model_width + kv_width :].reshape(group_count, -1),
            grad_gain_two.reshape(group_count, -1),
        ],
        axis=1,
    )
    vector_sum = lax.psum(scatter_sum(vectors), "replica").reshape(-1)
    gain_one_sum, query_bias_sum, key_bias_sum, value_bias_sum, gain_two_sum = [
        vector_sum[offsets[i] : offsets[i + 1]] for i in range(len(sizes))
    ]
    ends = (0, model_width, model_width + kv_width, model_width + 2 * kv_width)
    query_sum, key_sum_w, value_sum_w = [weight_sum[:, ends[i] : ends[i + 1]] for i in range(3)]
    out_sum = weight_sum[:, ends[3] :]
    return (
        layer_out,
        grad_input,
        gain_one_sum,
        query_sum,
        query_bias_sum,
        key_sum_w,
        key_bias_sum,
        value_sum_w,
        value_bias_sum,
        out_sum,
        gain_two_sum,
        gate_sum,
        up_sum,
        down_sum,
    )


def place():
    g = lax.axis_index("group")
    r = lax.axis_index("replica")
    return r, g // 4, lax.rem(g // 2, 2), lax.rem(g, 2)

def idx(z, x, c):
    return (z * 2 + x) * 2 + c

def greet(r, z, x, c, with_y=False):
    bar = pltpu.get_barrier_semaphore()
    def hail(dev):
        pl.semaphore_signal(bar, inc=1, device_id=dev, device_id_type=MESH)
    hail((r, idx(z, 1 - x, c)))
    hail((r, idx(z, x, 1 - c)))
    if with_y:
        hail((1 - r, idx(z, x, c)))
    @pl.when(z > 0)
    def _():
        hail((r, idx(z - 1, x, c)))
    @pl.when(z < NZ - 1)
    def _():
        hail((r, idx(z + 1, x, c)))
    ends = jnp.where((z > 0) & (z < NZ - 1), 1, 0)
    pl.semaphore_wait(bar, (4 if with_y else 3) + ends)

def planes(z):
    return (
        z,
        jnp.where(z == 0, 1, jnp.where(z == 1, 0, jnp.where(z == 2, 3, 2))),
        jnp.where(z == 0, 2, jnp.where(z == 1, 2, 1)),
        jnp.where(z < 2, 3, 0),
    )

def when(cond, fn):
    pl.when(cond)(fn)

class Gather:
    def __init__(self, at, src, out, send, recv, local, part=None):
        self.r, self.z, self.x, self.c = at
        self.src, self.out, self.send, self.recv, self.local = src, out, send, recv, local
        self.part = part
        self.mid = (self.z > 0) & (self.z < NZ - 1)
        self.p = planes(self.z)
    def blk(self, b):
        return self.out.at[b] if self.part is None else self.out.at[b, self.part]
    def put(self, src, b, k, dev):
        pltpu.make_async_remote_copy(src, self.blk(b), self.send.at[k], self.recv.at[b], device_id=dev, device_id_type=MESH).start()
    def sent(self, k):
        b = 0
        pltpu.make_async_remote_copy(self.blk(b), self.blk(b), self.send.at[k], self.recv.at[b], device_id=(self.r, 0), device_id_type=MESH).wait_send()
    def got(self, b):
        pltpu.make_async_remote_copy(self.blk(b), self.blk(b), self.send.at[0], self.recv.at[b], device_id=(self.r, 0), device_id_type=MESH).wait_recv()
    def zdev(self, s): return (self.r, idx(self.z + s, self.x, self.c))
    def xdev(self): return (self.r, idx(self.z, 1 - self.x, self.c))
    def cdev(self): return (self.r, idx(self.z, self.x, 1 - self.c))
    def begin(self):
        z, x, c = self.z, self.x, self.c
        me = idx(z, x, c)
        for s in (1, -1):
            when(self.inside(z + s), lambda s=s: self.put(self.src, me, 0 if s == 1 else 3, self.zdev(s)))
        self.put(self.src, me, 6 + z, self.xdev())
        self.put(self.src, me, 10 + 2 * z + x, self.cdev())
        pltpu.make_async_copy(self.src, self.blk(me), self.local).start()
    def inside(self, z): return (z >= 0) & (z < NZ)
    def from_z(self, zz):
        z, x, c = self.z, self.x, self.c
        b = idx(zz, x, c)
        self.got(b)
        s = jnp.where(zz < z, 1, -1)
        d = jnp.abs(zz - z)
        slot = jnp.where(zz < z, 0, 3) + d
        when(self.inside(z + s), lambda: self.put(self.blk(b), b, slot, (self.r, idx(z + s, x, c))))
        self.put(self.blk(b), b, 6 + zz, self.xdev())
        self.put(self.blk(b), b, 10 + 2 * zz + x, self.cdev())
    def first(self):
        self.from_z(self.p[1])
        when(self.mid, lambda: self.from_z(self.p[2]))
        self.from_x(self.p[0])
    def second(self):
        self.from_z(jnp.where(self.mid, self.p[3], self.p[2]))
        self.from_x(self.p[1])
    def third(self):
        when(~self.mid, lambda: self.from_z(self.p[3]))
        self.from_x(self.p[2])
    def fourth(self):
        self.from_x(self.p[3])
    def from_x(self, zz):
        b = idx(zz, 1 - self.x, self.c)
        self.got(b)
        self.put(self.blk(b), b, 10 + 2 * zz + 1 - self.x, self.cdev())
    def from_c(self, zz):
        self.got(idx(zz, self.x, 1 - self.c))
        self.got(idx(zz, 1 - self.x, 1 - self.c))
    def end(self, local=True):
        z = self.z
        for d in range(NZ - 1):
            when((z - d >= 0) & (z < NZ - 1), lambda d=d: self.sent(d))
            when((z + d < NZ) & (z > 0), lambda d=d: self.sent(3 + d))
        for k in range(6, 18):
            self.sent(k)
        if local:
            pltpu.make_async_copy(self.src, self.blk(0), self.local).wait()

class Scatter:
    def __init__(self, at, part, rc, rx, rz, send, rcs, rxs, rzs):
        self.r, self.z, self.x, self.c = at
        self.part, self.rc, self.rx, self.rz = part, rc, rx, rz
        self.send, self.rcs, self.rxs, self.rzs = send, rcs, rxs, rzs
    def inside(self, z): return (z >= 0) & (z < NZ)
    def copy(self, src, dst, k, rs, dev):
        return pltpu.make_async_remote_copy(src, dst, self.send.at[k], rs, device_id=dev, device_id_type=MESH)
    def over(self, d):
        return [(s, self.z + s * d) for s in ((-1, 1) if d else (1,))]
    def begin(self, far_first=True):
        z, x, c = self.z, self.x, self.c
        dev = (self.r, idx(z, x, 1 - c))
        for xx in (1 - x, x):
            for d in range(NZ - 1, -1, -1):
                for s, zz in self.over(d):
                    k = 2 * zz + xx
                    when(self.inside(zz), lambda zz=zz, k=k, xx=xx: self.copy(self.part.at[idx(zz, xx, 1 - c)], self.rc.at[k], k, self.rcs.at[k], dev).start())
    def send_c(self, zz):
        z, x, c = self.z, self.x, self.c
        dev = (self.r, idx(z, x, 1 - c))
        for xx in (1 - x, x):
            k = 2 * zz + xx
            self.copy(self.part.at[idx(zz, xx, 1 - c)], self.rc.at[k], k, self.rcs.at[k], dev).start()
    def x_plane(self, zz):
        z, x, c = self.z, self.x, self.c
        dev = (self.r, idx(z, 1 - x, c))
        k = 2 * zz + 1 - x
        b = idx(zz, 1 - x, c)
        self.copy(self.rc.at[k], self.rc.at[k], 0, self.rcs.at[k], dev).wait_recv()
        self.part[b] = (self.part[b].astype(F32) + self.rc[k].astype(F32)).astype(BF)
        self.copy(self.part.at[b], self.rx.at[zz], 8 + zz, self.rxs.at[zz], dev).start()
    def step_x(self, d):
        for s, zz in self.over(d):
            when(self.inside(zz), lambda zz=zz: self.x_plane(zz))
    def step_z(self, d):
        z, x, c = self.z, self.x, self.c
        for s, zz in self.over(d):
            def go(zz=zz, s=s):
                k = 2 * zz + x
                b = idx(zz, x, c)
                self.copy(self.rc.at[k], self.rc.at[k], 0, self.rcs.at[k], (self.r, 0)).wait_recv()
                self.copy(self.rx.at[zz], self.rx.at[zz], 0, self.rxs.at[zz], (self.r, 0)).wait_recv()
                both = self.part[b].astype(F32) + self.rc[k].astype(F32) + self.rx[zz].astype(F32)
                dev = (self.r, idx(z + s, x, c))
                slot = jnp.where(zz == z + s, NZ, zz) if s == -1 else zz
                self.part[b] = both.astype(BF)
                def more():
                    self.copy(self.rz.at[zz], self.rz.at[zz], 0, self.rzs.at[zz], dev).wait_recv()
                    self.part[b] = (self.part[b].astype(F32) + self.rz[zz].astype(F32)).astype(BF)
                when(self.inside(z - s), more)
                self.copy(self.part.at[b], self.rz.at[slot], 12 + zz, self.rzs.at[slot], dev).start()
            when(self.inside(zz), go)
    def finish(self, out):
        z, x, c = self.z, self.x, self.c
        k = 2 * z + x
        b = idx(z, x, c)
        self.copy(self.rc.at[k], self.rc.at[k], 0, self.rcs.at[k], (self.r, 0)).wait_recv()
        self.copy(self.rx.at[z], self.rx.at[z], 0, self.rxs.at[z], (self.r, 0)).wait_recv()
        out[...] = self.part[b].astype(F32) + self.rc[k].astype(F32) + self.rx[z].astype(F32)
        def lo():
            self.copy(self.rz.at[z], self.rz.at[z], 0, self.rzs.at[z], (self.r, 0)).wait_recv()
            out[...] += self.rz[z].astype(F32)
        when(z > 0, lo)
        def hi():
            self.copy(self.rz.at[NZ], self.rz.at[NZ], 0, self.rzs.at[NZ], (self.r, 0)).wait_recv()
            out[...] += self.rz[NZ].astype(F32)
        when(z < NZ - 1, hi)
        for k in range(8):
            self.copy(self.part.at[0], self.part.at[0], k, self.rcs.at[0], (self.r, 0)).wait_send()
        for k in range(8, 12):
            self.copy(self.part.at[0], self.part.at[0], k, self.rcs.at[0], (self.r, 0)).wait_send()
        for zz in range(NZ):
            when(z != zz, lambda zz=zz: self.copy(self.part.at[0], self.part.at[0], 12 + zz, self.rcs.at[0], (self.r, 0)).wait_send())

class ScatterY(Scatter):
    def __init__(self, at, part, rc, ry, rx, rz, send, rcs, rys, rxs, rzs, ysem):
        Scatter.__init__(self, at, part, rc, rx, rz, send, rcs, rxs, rzs)
        self.ry, self.rys, self.ysem = ry, rys, ysem
        self.n = part.shape[1] // 2
        self.ydev = (1 - self.r, idx(self.z, self.x, self.c))
        self.mine = self.rows(self.r)
    def rows(self, h):
        return pl.ds(pl.multiple_of(h * self.n, self.n), self.n)
    def step_y(self, d):
        x, c, r = self.x, self.c, self.r
        for xx in (1 - x, x):
            for s, zz in self.over(d):
                def go(zz=zz, xx=xx):
                    k = 2 * zz + xx
                    b = idx(zz, xx, c)
                    self.copy(self.rc.at[k], self.rc.at[k], 0, self.rcs.at[k], self.ydev).wait_recv()
                    self.part[b] = (self.part[b].astype(F32) + self.rc[k].astype(F32)).astype(BF)
                    self.copy(self.part.at[b, self.rows(1 - r)], self.ry.at[k], 16 + k, self.rys.at[k], self.ydev).start()
                when(self.inside(zz), go)
    def both(self, zz, xx):
        k = 2 * zz + xx
        self.copy(self.ry.at[k], self.ry.at[k], 0, self.rys.at[k], self.ydev).wait_recv()
        return self.part[idx(zz, xx, self.c), self.mine].astype(F32) + self.ry[k].astype(F32)
    def step_x(self, d):
        z, x, c = self.z, self.x, self.c
        dev = (self.r, idx(z, 1 - x, c))
        for s, zz in self.over(d):
            def go(zz=zz):
                b = idx(zz, 1 - x, c)
                self.part[b, self.mine] = self.both(zz, 1 - x).astype(BF)
                self.copy(self.part.at[b, self.mine], self.rx.at[zz], 8 + zz, self.rxs.at[zz], dev).start()
            when(self.inside(zz), go)
    def arrived(self, ref, sem):
        self.copy(ref, ref, 0, sem, self.ydev).wait_recv()
    def step_z(self, d):
        z, x, c = self.z, self.x, self.c
        for s, zz in self.over(d):
            def go(zz=zz, s=s):
                b = idx(zz, x, c)
                v = self.both(zz, x)
                self.arrived(self.rx.at[zz], self.rxs.at[zz])
                self.part[b, self.mine] = (v + self.rx[zz].astype(F32)).astype(BF)
                def more():
                    self.arrived(self.rz.at[zz], self.rzs.at[zz])
                    self.part[b, self.mine] = (self.part[b, self.mine].astype(F32) + self.rz[zz].astype(F32)).astype(BF)
                when(self.inside(z - s), more)
                slot = jnp.where(zz == z + s, NZ, zz) if s == -1 else zz
                self.copy(self.part.at[b, self.mine], self.rz.at[slot], 12 + zz, self.rzs.at[slot], (self.r, idx(z + s, x, c))).start()
            when(self.inside(zz), go)
    def finish(self, out, low):
        z, x, r = self.z, self.x, self.r
        v = self.both(z, x)
        self.arrived(self.rx.at[z], self.rxs.at[z])
        out[self.mine] = v + self.rx[z].astype(F32)
        def lo():
            self.arrived(self.rz.at[z], self.rzs.at[z])
            out[self.mine] += self.rz[z].astype(F32)
        when(z > 0, lo)
        def hi():
            self.arrived(self.rz.at[NZ], self.rzs.at[NZ])
            out[self.mine] += self.rz[NZ].astype(F32)
        when(z < NZ - 1, hi)
        low[self.mine] = out[self.mine].astype(BF)
        a = low.at[self.mine]
        pltpu.make_async_remote_copy(a, a, self.ysem.at[0], self.ysem.at[1], device_id=self.ydev, device_id_type=MESH).start()
    def traded(self, out, low):
        a = low.at[self.rows(1 - self.r)]
        pltpu.make_async_remote_copy(a, a, self.ysem.at[0], self.ysem.at[1], device_id=self.ydev, device_id_type=MESH).wait()
        out[...] = low[...].astype(F32)
        half = self.part.at[0, self.mine]
        for k in range(8):
            self.copy(self.part.at[0], self.part.at[0], k, self.rcs.at[0], self.ydev).wait_send()
        for k in list(range(16, 24)) + list(range(8, 12)):
            self.copy(half, half, k, self.rcs.at[0], self.ydev).wait_send()
        for zz in range(NZ):
            when(self.z != zz, lambda zz=zz: self.copy(half, half, 12 + zz, self.rcs.at[0], self.ydev).wait_send())


KS = (8, 1, 9, 2, 10, 3, 11, 4, 12, 5, 13, 6, 14, 7, 15)
WINDOW = 2

def has(j):
    return lax.rem(j, 3) == 0

def spare_at(j):
    return pl.ds(pl.multiple_of(16 * MAIN + 128 * (j // 3), 128), 128)

class Deal:
    def __init__(self, at, ws, buf, sems, local):
        self.r, self.z, self.x, self.c = at
        self.me = idx(self.z, self.x, self.c)
        self.ws, self.buf, self.sems, self.local = ws, buf, sems, local
        self.n = ws[0].shape[0] // 2
    def rows(self, j, h):
        return pl.ds(pl.multiple_of((2 * j + h) * self.n, self.n), self.n)
    def block(self, j, h, spare):
        return self.buf.at[self.rows(j, h), pl.ds(3 * MAIN, 384) if spare else pl.ds(0, 3 * MAIN)]
    def copy(self, a, b, kind, k, dev):
        send, recv = self.sems[2 * kind : 2 * kind + 2]
        return pltpu.make_async_remote_copy(a, b, send.at[k], recv.at[k], device_id=dev, device_id_type=MESH)
    def launch(self, k):
        r, me, n = self.r, self.me, self.n
        row = pl.ds(pl.multiple_of(r * n, n), n)
        j = jnp.bitwise_xor(me, k)
        dst = self.rows(me, r)
        for i in range(3):
            self.copy(self.ws[i].at[row, pl.ds(pl.multiple_of(j * MAIN, MAIN), MAIN)], self.buf.at[dst, pl.ds(i * MAIN, MAIN)], 0, k, (r, j)).start()
        def spare():
            for i in range(3):
                self.copy(self.ws[i].at[row, spare_at(j)], self.buf.at[dst, pl.ds(3 * MAIN + 128 * i, 128)], 1, k, (r, j)).start()
        when(has(j), spare)
    def locals(self, spare):
        me, n = self.me, self.n
        row = pl.ds(pl.multiple_of(2 * me * n, 2 * n), 2 * n)
        col = spare_at(me) if spare else pl.ds(pl.multiple_of(me * MAIN, MAIN), MAIN)
        for i in range(3):
            to = pl.ds(3 * MAIN + 128 * i, 128) if spare else pl.ds(i * MAIN, MAIN)
            yield pltpu.make_async_copy(self.ws[i].at[:, col], self.buf.at[row, to], self.local.at[1 if spare else 0])
    def begin(self):
        for k in KS[:WINDOW]:
            self.launch(k)
        for l in self.locals(False):
            l.start()
        def spare():
            for l in self.locals(True):
                l.start()
        when(has(self.me), spare)
    def step(self, i):
        k = KS[i]
        r, me = self.r, self.me
        j = jnp.bitwise_xor(me, k)
        dev = (1 - r, me)
        def pass_on(spare):
            blk = self.block(j, r, spare)
            self.copy(blk, blk, spare, k, dev).wait_recv()
            self.copy(blk, blk, 2 + spare, k, dev).start()
        pass_on(0)
        when(has(me), lambda: pass_on(1))
        if i + WINDOW < 15:
            self.launch(KS[i + WINDOW])
    def end(self):
        r, me, n = self.r, self.me, self.n
        dev = (1 - r, me)
        for k in KS:
            j = jnp.bitwise_xor(me, k)
            def done(spare):
                blk = self.block(j, 1 - r, spare)
                self.copy(blk, blk, 2 + spare, k, dev).wait()
            def sent(spare):
                blk = self.block(j, r, spare)
                self.copy(blk, blk, spare, k, dev).wait_send()
            done(0)
            sent(0)
            when(has(me), lambda: done(1))
            when(has(j), lambda: sent(1))
        row = pl.ds(pl.multiple_of(2 * me * n, 2 * n), 2 * n)
        def own(spare):
            blk = self.buf.at[row, pl.ds(3 * MAIN, 384) if spare else pl.ds(0, 3 * MAIN)]
            pltpu.make_async_copy(blk, blk, self.local.at[spare]).wait()
        own(0)
        when(has(me), lambda: own(1))

def hail_all(r, z, x, c):
    bar = pltpu.get_barrier_semaphore()
    me = idx(z, x, c)
    for k in range(1, 16):
        pl.semaphore_signal(bar, inc=1, device_id=(r, lax.rem(me + k, 16)), device_id_type=MESH)
    pl.semaphore_signal(bar, inc=1, device_id=(1 - r, me), device_id_type=MESH)
    pl.semaphore_wait(bar, 16)


def dot(a, b):
    return lax.dot_general(a, b, (((1,), (0,)), ((), ())), preferred_element_type=F32)
def dot_nt(a, b):
    return lax.dot_general(a, b, (((1,), (1,)), ((), ())), preferred_element_type=F32)
def dot_tn(a, b):
    return lax.dot_general(a, b, (((0,), (0,)), ((), ())), preferred_element_type=F32)

def gated(g, u, gh):
    sig = jax.nn.sigmoid(g)
    silu = g * sig
    return (gh * u * (sig * (1.0 + g * (1.0 - sig)))).astype(BF), (gh * silu).astype(BF), (silu * u).astype(BF)

def mlp_kernel(n2_ref, cot_ref, w_ref, gsum, osum, half_ref,
               n2, cot, w, act, pg, po, rcg, rxg, rzg, rco, rxo, rzo, yb,
               gsend, grecv, glocal, lsem, ssend, srcs, srxs, srzs, ysend, yrecv, xsend, xrecv):
    at = place()
    r, z, x, c = at
    me = idx(z, x, c)
    extra = has(me)
    MM, SP = pl.ds(0, 3 * MAIN), pl.ds(3 * MAIN, 384)
    loads = [pltpu.make_async_copy(w_ref.at[:, MM], w.at[:, MM], lsem.at[0]), pltpu.make_async_copy(cot_ref, cot, lsem.at[1])]
    for l in loads: l.start()
    load_spare = pltpu.make_async_copy(w_ref.at[:, SP], w.at[:, SP], lsem.at[3])
    when(extra, load_spare.start)
    greet(*at, with_y=True)
    g = Gather(at, n2_ref, n2, gsend, grecv, glocal)
    rg = Scatter(at, pg, rcg, rxg, rzg, ssend.at[0], srcs.at[0], srxs.at[0], srzs.at[0])
    ro = Scatter(at, po, rco, rxo, rzo, ssend.at[1], srcs.at[1], srxs.at[1], srzs.at[1])
    g.begin()
    for l in loads: l.wait()
    when(extra, load_spare.wait)
    mid = (z > 0) & (z < NZ - 1)
    p = [z,
         jnp.where(z == 0, 1, jnp.where(z == 1, 0, jnp.where(z == 2, 3, 2))),
         jnp.where(z == 0, 2, jnp.where(z == 1, 2, 1)),
         jnp.where(z < 2, 3, 0)]

    def tiles(zz):
        rows = pl.ds(pl.multiple_of(4 * zz, 4), 4)
        tok = pl.ds(pl.multiple_of(512 * zz, 512), 512)
        @pl.loop(0, 2)
        def _(t):
            a = n2[rows].reshape(512, D)
            k = cot[rows].reshape(512, D)
            def col(base):
                return pl.ds(pl.multiple_of(base + 256 * t, 256), 256)
            dg, du, h = gated(dot(a, w[:, col(0)]), dot(a, w[:, col(MAIN)]), dot(k, w[:, col(2 * MAIN)]))
            act[tok, col(0)] = dg
            act[tok, col(MAIN)] = du
            act[tok, col(2 * MAIN)] = h
        def spare():
            pre = dot(n2[rows].reshape(512, D), w[:, 3 * MAIN : 3 * MAIN + 256])
            dg, du, h = gated(pre[:, :128], pre[:, 128:], dot(cot[rows].reshape(512, D), w[:, 3 * MAIN + 256 :]))
            act[tok, 3 * MAIN : 3 * MAIN + 128] = dg
            act[tok, 3 * MAIN + 128 : 3 * MAIN + 256] = du
            act[tok, 3 * MAIN + 256 :] = h
        when(extra, spare)
        def out_tiles(more):
            @pl.loop(0, D // 256)
            def _(t):
                dr = pl.ds(pl.multiple_of(256 * t, 256), 256)
                v = dot_nt(act[tok, : 2 * MAIN], w[dr, : 2 * MAIN])
                u = dot_nt(act[tok, 2 * MAIN : 3 * MAIN], w[dr, 2 * MAIN : 3 * MAIN])
                if more:
                    v += dot_nt(act[tok, 3 * MAIN : 3 * MAIN + 256], w[dr, 3 * MAIN : 3 * MAIN + 256])
                    u += dot_nt(act[tok, 3 * MAIN + 256 :], w[dr, 3 * MAIN + 256 :])
                pg[rows, :, dr] = v.astype(BF).reshape(4, 128, 256)
                po[rows, :, dr] = u.astype(BF).reshape(4, 128, 256)
        when(extra, lambda: out_tiles(True))
        when(~extra, lambda: out_tiles(False))
        rg.send_c(zz)
        ro.send_c(zz)

    g.from_z(p[1])
    when(mid, lambda: g.from_z(p[2]))
    g.from_x(p[0])
    g.from_c(p[0])
    pltpu.make_async_copy(n2_ref, n2.at[0], glocal).wait()
    tiles(p[0])
    g.from_z(jnp.where(mid, p[3], p[2]))
    g.from_x(p[1])
    g.from_c(p[1])
    tiles(p[1])
    when(~mid, lambda: g.from_z(p[3]))
    g.from_x(p[2])
    g.from_c(p[2])
    tiles(p[2])
    rg.x_plane(p[2])
    g.from_x(p[3])
    g.from_c(p[3])
    tiles(p[3])

    ydev = (1 - r, idx(z, x, c))
    own = D // 16
    half = own // 2
    def ycopy(j, spare):
        cols = SP if spare else MM
        src = w.at[pl.ds(pl.multiple_of(own * j + half * (1 - r), half), half), cols]
        a, b = (xsend, xrecv) if spare else (ysend, yrecv)
        return pltpu.make_async_remote_copy(src, yb.at[j, :, cols], a.at[j], b.at[j], device_id=ydev, device_id_type=MESH)
    def grads(q):
        dr = slice(384 * q, 384 * (q + 1))
        row = slice(384 * q, 384 * (q + 1))
        @pl.loop(0, 4)
        def _(t):
            col = pl.ds(pl.multiple_of(256 * t, 256), 256)
            w[row, col] = dot_tn(n2[:, :, dr].reshape(2048, 384), act[:, col]).astype(BF)
        @pl.loop(0, 2)
        def _(t):
            col = pl.ds(pl.multiple_of(2 * MAIN + 256 * t, 256), 256)
            w[row, col] = dot_tn(cot[:, :, dr].reshape(2048, 384), act[:, col]).astype(BF)
        for j in range(4 * q, 4 * q + 4):
            ycopy(j, 0).start()
        def spare():
            w[row, 3 * MAIN : 3 * MAIN + 256] = dot_tn(n2[:, :, dr].reshape(2048, 384), act[:, 3 * MAIN : 3 * MAIN + 256]).astype(BF)
            w[row, 3 * MAIN + 256 :] = dot_tn(cot[:, :, dr].reshape(2048, 384), act[:, 3 * MAIN + 256 :]).astype(BF)
            for j in range(4 * q, 4 * q + 4):
                ycopy(j, 1).start()
        when(extra, spare)
    def yadd(j):
        def add(spare):
            cols = SP if spare else MM
            ycopy(j, spare).wait()
            mine = w[pl.ds(pl.multiple_of(own * j + half * r, half), half), cols]
            yb[j, :, cols] = (mine.astype(F32) + yb[j, :, cols].astype(F32)).astype(BF)
            pltpu.make_async_copy(yb.at[j, :, cols], half_ref.at[j, :, cols], lsem.at[4 if spare else 2]).start()
        add(0)
        when(extra, lambda: add(1))

    rg.x_plane(p[3])
    rg.x_plane(p[1])
    grads(0)
    rg.step_z(3)
    rg.step_z(2)
    rg.x_plane(p[0])
    ro.x_plane(p[3])
    grads(1)
    rg.step_z(1)
    ro.x_plane(p[2])
    grads(2)
    ro.x_plane(p[1])
    ro.step_z(3)
    rg.finish(gsum)
    grads(3)
    ro.x_plane(p[0])
    ro.step_z(2)
    for j in range(0, 8): yadd(j)
    ro.step_z(1)
    for j in range(8, 12): yadd(j)
    ro.finish(osum)
    for j in range(12, 16): yadd(j)
    pltpu.make_async_copy(yb.at[:, :, MM], half_ref.at[:, :, MM], lsem.at[2]).wait()
    when(extra, lambda: pltpu.make_async_copy(yb.at[:, :, SP], half_ref.at[:, :, SP], lsem.at[4]).wait())
    g.end(local=False)

def mlp(n2, cot, w, cid):
    blk = n2.shape
    dma = pltpu.SemaphoreType.DMA
    full = (16,) + blk
    return pl.pallas_call(
        mlp_kernel,
        out_shape=[jax.ShapeDtypeStruct(blk, F32)] * 2 + [jax.ShapeDtypeStruct((16, D // 32, COLS), BF)],
        in_specs=[pl.BlockSpec(memory_space=pl.ANY)] * 3,
        out_specs=[pl.BlockSpec(memory_space=pltpu.VMEM)] * 2 + [pl.BlockSpec(memory_space=pl.ANY)],
        scratch_shapes=[pltpu.VMEM(full, BF), pltpu.VMEM(full, BF), pltpu.VMEM((D, COLS), BF), pltpu.VMEM((16 * blk[0], COLS), BF),
                        pltpu.VMEM(full, BF), pltpu.VMEM(full, BF)]
        + [pltpu.VMEM((k,) + blk, BF) for k in (8, 4, 5, 8, 4, 5)]
        + [pltpu.VMEM((16, D // 32, COLS), BF)]
        + [dma((18,)), dma((16,)), dma(()), dma((5,)), dma((2, 16)), dma((2, 8)), dma((2, 4)), dma((2, 5))] + [dma((16,))] * 4,
        compiler_params=pltpu.CompilerParams(collective_id=cid, has_side_effects=True, vmem_limit_bytes=60 * 2**20),
    )(n2, cot, w)


def spin(u, cos, sin):
    return u * cos + pltpu.roll(u, HEAD_DIM // 2, 1) * sin

def stack_heads(v):
    n = v.shape[1] // HEAD_DIM
    return jnp.concatenate([v[:, HEAD_DIM * i : HEAD_DIM * (i + 1)] for i in range(n)], axis=0)

def spread_heads(v, rows):
    n = v.shape[0] // rows
    return jnp.concatenate([v[rows * i : rows * (i + 1)] for i in range(n)], axis=1)

def exp_scores(q, k, first_row, block, length):
    sc = dot_nt(q, k) * (HEAD_DIM ** -0.5)
    key = lax.broadcasted_iota(jnp.int32, sc.shape, 1)
    row = jnp.bitwise_and(lax.broadcasted_iota(jnp.int32, sc.shape, 0), block - 1) + first_row
    return jnp.where((key <= row) & (key < length), jnp.exp(sc), 0.0)

def rms(v, gain):
    factor = lax.rsqrt(jnp.mean(v * v, axis=-1, keepdims=True) + EPSILON)
    return v * factor * gain


class GatherY(Gather):
    def __init__(self, at, src, out, send, recv, local):
        Gather.__init__(self, at, src, out, send, recv, local)
        self.n = src.shape[0] // 2
        self.ydev = (1 - self.r, idx(self.z, self.x, self.c))
    def rows(self, h):
        return pl.ds(pl.multiple_of(h * self.n, self.n), self.n)
    def half(self, b, h):
        return self.out.at[b, self.rows(h)]
    def move(self, src, dst, k, q, dev):
        return pltpu.make_async_remote_copy(src, dst, self.send.at[k], self.recv.at[q], device_id=dev, device_id_type=MESH)
    def arrived(self, b, h):
        self.move(self.half(b, h), self.half(b, h), 0, 2 * b + h, self.ydev).wait_recv()
    def begin(self):
        z, x, c, r = self.z, self.x, self.c, self.r
        me = idx(z, x, c)
        mine, dst = self.src.at[self.rows(r)], self.half(me, r)
        for s in (1, -1):
            when(self.inside(z + s), lambda s=s: self.move(mine, dst, 0 if s == 1 else 3, 2 * me + r, self.zdev(s)).start())
        self.move(mine, dst, 6 + z, 2 * me + r, self.xdev()).start()
        self.move(self.src, self.out.at[me], 18 + 2 * z + x, 2 * me, self.cdev()).start()
        pltpu.make_async_copy(self.src, self.out.at[me], self.local).start()
    def from_z(self, zz):
        z, x, c, r = self.z, self.x, self.c, self.r
        b = idx(zz, x, c)
        q = 2 * b + r
        self.arrived(b, r)
        s = jnp.where(zz < z, 1, -1)
        slot = jnp.where(zz < z, 0, 3) + jnp.abs(zz - z)
        a = self.half(b, r)
        when(self.inside(z + s), lambda: self.move(a, a, slot, q, (r, idx(z + s, x, c))).start())
        self.move(a, a, 6 + zz, q, self.xdev()).start()
        self.move(a, a, 18 + 2 * zz + x, q, self.cdev()).start()
        self.move(a, a, 10 + 2 * zz + x, q, self.ydev).start()
    def from_x(self, zz):
        x, c, r = self.x, self.c, self.r
        b = idx(zz, 1 - x, c)
        q = 2 * b + r
        self.arrived(b, r)
        a = self.half(b, r)
        self.move(a, a, 18 + 2 * zz + 1 - x, q, self.cdev()).start()
        self.move(a, a, 10 + 2 * zz + 1 - x, q, self.ydev).start()
    def from_y(self, zz):
        x, c, r = self.x, self.c, self.r
        def take(xx):
            b = idx(zz, xx, c)
            self.arrived(b, 1 - r)
            a = self.half(b, 1 - r)
            self.move(a, a, 26 + 2 * zz + xx, 2 * b + 1 - r, self.cdev()).start()
        when(zz != self.z, lambda: take(x))
        take(1 - x)
    def from_c(self, zz):
        x, c, r = self.x, self.c, self.r
        b = idx(zz, x, 1 - c)
        whole = self.out.at[b]
        when(zz == self.z, lambda: self.move(whole, whole, 0, 2 * b, self.ydev).wait_recv())
        def both(b):
            self.arrived(b, r)
            self.arrived(b, 1 - r)
        when(zz != self.z, lambda: both(b))
        both(idx(zz, 1 - x, 1 - c))
    def end(self):
        z, x = self.z, self.x
        own = 2 * z + x
        a = self.half(0, 0)
        def sent(k, a=a):
            self.move(a, a, k, 0, self.ydev).wait_send()
        for d in range(NZ - 1):
            when((z - d >= 0) & (z < NZ - 1), lambda d=d: sent(d))
            when((z + d < NZ) & (z > 0), lambda d=d: sent(3 + d))
        for k in range(6, 10):
            sent(k)
        for k in range(8):
            def other(k=k):
                sent(10 + k)
                sent(18 + k)
                sent(26 + k)
            when(own != k, other)
        sent(18 + own, self.out.at[0])
        pltpu.make_async_copy(self.src, self.out.at[0], self.local).wait()

def front_kernel(block, lens, x_ref, cot_ref, v0, v1, v2, v3, v4, sel, fold, selk, foldk, rope_ref, wq, wk, wv, wg, wu, wd, wo_ref,
                 q_out, normed_out, att_out, mid_out, n2_out, vec, buf, qkv_out, kv_out, cot_out, wo_out,
                 rope, cot_own, small, qkv_own, wqkv, small_all, own, kv, wo,
                 qs, qr, ql, vs, vr, vl, ks, kr, kl, cs, cr, cl, ws, wr, wl, d0, d1, d2, d3, d4, d5, d6, d7, dl, lsem):
    at = place()
    width = HEADS * HEAD_DIM
    kw = KV_HEADS * HEAD_DIM
    loads = [pltpu.make_async_copy(w, qkv_own.at[:, pl.ds(o, n)], lsem.at[i]) for i, (w, o, n) in enumerate(((wq, 0, width), (wk, width, kw), (wv, width + kw, kw)))]
    first_row = lax.axis_index("group") * block
    loads.append(pltpu.make_async_copy(rope_ref.at[:, pl.ds(pl.multiple_of(first_row, block), block)], rope, lsem.at[6]))
    for l in loads: l.start()
    small[...] = jnp.zeros_like(small)
    for i, v in enumerate((v0, v1, v2, v3, v4)):
        small[i : i + 1, : v.shape[1]] = v[...].astype(F32)
    cot_own[...] = (cot_ref[...].astype(F32) * row_mask(lens, first_row, block, (cot_ref.shape[0], 1))).astype(BF)
    hail_all(*at)
    for l in loads: l.wait()
    gq = GatherY(at, qkv_own, wqkv, qs, qr, ql)
    gv = Gather(at, small, small_all, vs, vr, vl)
    gk = Gather(at, own, kv, ks, kr, kl)
    gc = Gather(at, cot_own, cot_out, cs, cr, cl)
    gw = GatherY(at, wo_ref, wo, ws, wr, wl)
    d = Deal(at, (wg, wu, wd), buf, (d0, d1, d2, d3, d4, d5, d6, d7), dl)
    steps = iter(range(15))
    def some(n):
        for _ in range(n):
            i = next(steps, None)
            if i is not None:
                d.step(i)
    gq.begin()
    gv.begin()
    d.begin()
    x = x_ref[...].astype(F32)
    gq.first()
    gv.first()
    some(1)
    gq.second()
    gv.second()
    gq.from_y(gq.p[0])
    some(EARLY[0])
    gq.third()
    gv.third()
    gq.from_y(gq.p[1])
    some(1)
    gq.fourth()
    gv.fourth()
    gc.begin()
    gq.from_y(gq.p[2])
    gq.from_y(gq.p[3])
    for zz in range(NZ):
        gv.from_c(zz)
        gq.from_c(zz)
    gv.end()
    gq.end()
    keep = [pltpu.make_async_copy(wqkv, qkv_out, lsem.at[3]), pltpu.make_async_copy(kv, kv_out, lsem.at[4]), pltpu.make_async_copy(wo, wo_out, lsem.at[5])]
    keep[0].start()
    vec[...] = jnp.zeros_like(vec)
    for i, row, first, a, b in ((0, 0, 0, sel, fold), (1, 1, 0, sel, fold), (2, 1, width, selk, foldk), (3, 1, width + kw, selk, foldk), (4, 2, 0, sel, fold)):
        t = dot_nt(small_all[:, i, :].astype(BF), b[...])
        vec[row : row + 1, first : first + a.shape[1]] = jnp.sum(t * a[...], axis=0, keepdims=True)
    normed_out[...] = rms(x, vec[0:1, :width]).astype(BF)
    cos, sin = [jnp.concatenate((rope[i], rope[i]), axis=0) for i in range(2)]
    def product(base):
        return dot(normed_out[...], wqkv[:, :, pl.ds(pl.multiple_of(base, 256), 256)].reshape(width, 256)) + vec[1:2, pl.ds(pl.multiple_of(base, 256), 256)]
    pre = product(width)
    own[:, :HEAD_DIM] = spin(pre[:, :HEAD_DIM], cos, sin).astype(BF)
    own[:, HEAD_DIM : 2 * HEAD_DIM] = spin(pre[:, HEAD_DIM:], cos, sin).astype(BF)
    own[:, kw:] = product(width + kw).astype(BF)
    gk.begin()
    gw.begin()
    @pl.loop(0, width // 256)
    def _(t):
        pre = product(t * 256)
        for i in range(2):
            col = pl.ds(pl.multiple_of(256 * t + HEAD_DIM * i, HEAD_DIM), HEAD_DIM)
            q_out[:, col] = spin(pre[:, HEAD_DIM * i : HEAD_DIM * (i + 1)], cos, sin).astype(BF)
    some(EARLY[1])
    gc.first()
    gk.first()
    some(1)
    gw.first()
    some(EARLY[2])
    gk.second()
    gc.second()
    gw.second()
    some(1)
    gw.from_y(gw.p[0])
    gk.third()
    some(EARLY[3])
    gk.fourth()
    gc.third()
    gw.third()
    some(1)
    gw.from_y(gw.p[1])
    for zz in range(NZ):
        gk.from_c(zz)
    gk.end()
    keep[1].start()
    span = 16 * block
    @pl.loop(0, 4)
    def _(u):
        s, h = u // 2, lax.rem(u, 2)
        rows = pl.ds(pl.multiple_of(block * s, block), block)
        cols = pl.ds(pl.multiple_of(width // 2 * h, width // 2), width // 2)
        q = stack_heads(q_out[rows, cols])
        k = kv[:, rows, pl.ds(pl.multiple_of(HEAD_DIM * h, HEAD_DIM), HEAD_DIM)].reshape(span, HEAD_DIM)
        v = kv[:, rows, pl.ds(pl.multiple_of(kw + HEAD_DIM * h, HEAD_DIM), HEAD_DIM)].reshape(span, HEAD_DIM)
        e = exp_scores(q, k, first_row, block, lens[s])
        total = jnp.sum(e, axis=-1, keepdims=True)
        att_out[rows, cols] = spread_heads(dot(e.astype(BF), v) / total, block)
    some(EARLY[4])
    gw.fourth()
    some(1)
    gc.fourth()
    some(1)
    gw.from_y(gw.p[2])
    gw.from_y(gw.p[3])
    for zz in range(NZ):
        gw.from_c(zz)
    gw.end()
    keep[2].start()
    @pl.loop(0, width // 256)
    def _(t):
        col = pl.ds(pl.multiple_of(256 * t, 256), 256)
        mid_out[:, col] = x_ref[:, col].astype(F32) + dot(att_out[...].astype(BF), wo[:, :, col].reshape(width, 256))
    n2_out[...] = rms(mid_out[...], vec[2:3, :width]).astype(BF)
    some(15)
    for zz in range(NZ):
        gc.from_c(zz)
    gc.end()
    for k in keep:
        k.wait()
    d.end()

EARLY = (1, 1, 1, 1, 2)

def front(lens, x, cot, vectors, sel, fold, selk, foldk, rope, wq, wk, wv, wg, wu, wd, wo, block, cid):
    rows, width = x.shape
    any_ = pl.BlockSpec(memory_space=pl.ANY)
    vm = pl.BlockSpec(memory_space=pltpu.VMEM)
    dma = pltpu.SemaphoreType.DMA
    act = (rows, width)
    own = wq.shape[0]
    kvw = 2 * KV_HEADS * HEAD_DIM
    wide = width + kvw
    sds = jax.ShapeDtypeStruct
    VM = pltpu.VMEM
    return pl.pallas_call(
        functools.partial(front_kernel, block),
        out_shape=[sds(act, BF), sds(act, BF), sds(act, F32), sds(act, F32), sds(act, BF), sds((8, wide), F32),
                   sds((16 * own, 3 * MAIN + 384), BF), sds((16, own, wide), BF), sds((16, rows, kvw), BF), sds((16,) + act, BF), sds((16,) + wo.shape, BF)],
        in_specs=[pl.BlockSpec(memory_space=pltpu.SMEM)] + [vm] * 11 + [any_] * 8,
        out_specs=[vm] * 6 + [any_] * 5,
        scratch_shapes=[VM((2, block, HEAD_DIM), F32), VM(act, BF), VM((8, 128), F32), VM((own, wide), BF), VM((16, own, wide), BF), VM((16, 8, 128), F32), VM((rows, kvw), BF), VM((16, rows, kvw), BF), VM((16,) + wo.shape, BF)]
        + [dma((34,)), dma((32,)), dma(())] + [dma((18,)), dma((16,)), dma(())] * 3 + [dma((34,)), dma((32,)), dma(())]
        + [dma((16,))] * 8 + [dma((2,)), dma((7,))],
        compiler_params=pltpu.CompilerParams(collective_id=cid, has_side_effects=True, vmem_limit_bytes=60 * 2**20),
    )(lens, x, cot, *vectors, sel, fold, selk, foldk, rope, wq, wk, wv, wg, wu, wd, wo)


class Return:
    def __init__(self, at, half_ref, out, sems, local):
        self.r, self.z, self.x, self.c = at
        self.me = idx(self.z, self.x, self.c)
        self.src, self.out, self.sems, self.local = half_ref, out, sems, local
        self.n = half_ref.shape[1]
    def places(self, j, spare):
        row = pl.ds(pl.multiple_of(self.r * self.n, self.n), self.n)
        col = spare_at(j) if spare else pl.ds(pl.multiple_of(j * MAIN, MAIN), MAIN)
        return [o.at[row, col] for o in self.out]
    def parts(self, j, spare):
        if spare:
            return [self.src.at[j, :, pl.ds(3 * MAIN + 128 * i, 128)] for i in range(3)]
        return [self.src.at[j, :, pl.ds(i * MAIN, MAIN)] for i in range(3)]
    def copy(self, a, b, kind, k, dev):
        send, recv = self.sems[2 * kind : 2 * kind + 2]
        return pltpu.make_async_remote_copy(a, b, send.at[k], recv.at[k], device_id=dev, device_id_type=MESH)
    def launch(self, k):
        j = jnp.bitwise_xor(self.me, k)
        def go(spare):
            for a, b in zip(self.parts(j, spare), self.places(self.me, spare)):
                self.copy(a, b, spare, k, (self.r, j)).start()
        go(0)
        when(has(self.me), lambda: go(1))
    def forward(self, j, k, spare):
        for a in self.places(j, spare):
            self.copy(a, a, 2 + spare, k, (1 - self.r, self.me)).start()
    def begin(self, window):
        self.window = window
        def go(spare):
            for a, b in zip(self.parts(self.me, spare), self.places(self.me, spare)):
                pltpu.make_async_copy(a, b, self.local.at[spare]).start()
        go(0)
        when(has(self.me), lambda: go(1))
        for k in KS[:window]:
            self.launch(k)
    def sized(self, spare):
        return self.src.at[0, :, pl.ds(3 * MAIN, 384) if spare else pl.ds(0, 3 * MAIN)]
    def whole(self, kind, k):
        blk = self.sized(kind % 2)
        return self.copy(blk, blk, kind, k, (1 - self.r, self.me))
    def own(self):
        def go(spare):
            blk = self.sized(spare)
            pltpu.make_async_copy(blk, blk, self.local.at[spare]).wait()
            self.forward(self.me, 0, spare)
        go(0)
        when(has(self.me), lambda: go(1))
    def step(self, i):
        k = KS[i]
        j = jnp.bitwise_xor(self.me, k)
        def go(spare):
            self.whole(spare, k).wait_recv()
            self.forward(j, k, spare)
        go(0)
        when(has(j), lambda: go(1))
        if i + self.window < 15:
            self.launch(KS[i + self.window])
    def end(self):
        for k in (0,) + KS:
            j = jnp.bitwise_xor(self.me, k)
            self.whole(2, k).wait()
            when(has(j), lambda: self.whole(3, k).wait())
            if k:
                self.whole(0, k).wait_send()
                when(has(self.me), lambda: self.whole(1, k).wait_send())

def row_mask(lens, first_row, block, shape):
    row = lax.broadcasted_iota(jnp.int32, shape, 0)
    place = jnp.bitwise_and(row, block - 1) + first_row
    return jnp.where(place < jnp.where(row < block, lens[0], lens[1]), 1.0, 0.0)

def norm_gradient(v, gain, upstream):
    factor = lax.rsqrt(jnp.mean(v * v, axis=-1, keepdims=True) + EPSILON)
    weighted = upstream * gain
    inner = jnp.mean(weighted * v, axis=-1, keepdims=True)
    return factor * weighted - v * (factor * factor * factor) * inner, jnp.sum(upstream * v * factor, axis=0, keepdims=True)

def backward_kernel(block, window, lens, gn2, mlp_out, mid, cot, x_ref, att, q_ref, normed, vec, sel, fold, selk, foldk, rope_ref, kv_ref, wo_ref, wqkv_ref, half_ref,
                    layer_out, grad_input, q_out, k_out, v_out, wo_out, vec_out, g0, g1, g2,
                    rope, kv, wo, wqkv, gmid, branch, gatt, gqkv, pv,
                    p_kv, c_kv, x_kv, z_kv, p_wo, c_wo, x_wo, z_wo, p_qk, c_qk, w_qk, x_qk, z_qk, p_pw, c_pw, x_pw, z_pw, p_ve, c_ve, x_ve, z_ve,
                    kvsum, pair_out, low_q, y2, y3, y4, y5, y6, y7,
                    ss, sc, sx, sz, r0, r1, r2, r3, r4, r5, r6, r7, rl, ysem, fs, fc, fy, fx, fz, ft, lsem):
    at = place()
    r, z, x, c = at
    width = HEADS * HEAD_DIM
    kw = KV_HEADS * HEAD_DIM
    loads = [pltpu.make_async_copy(a, b, lsem.at[i]) for i, (a, b) in enumerate(((wo_ref, wo), (kv_ref, kv), (wqkv_ref, wqkv)))]
    first_row = lax.axis_index("group") * block
    loads.append(pltpu.make_async_copy(rope_ref.at[:, pl.ds(pl.multiple_of(first_row, block), block)], rope, lsem.at[3]))
    for l in loads: l.start()
    hail_all(*at)
    back = Return(at, half_ref, (g0, g1, g2), (r0, r1, r2, r3, r4, r5, r6, r7), rl)
    back.begin(window)
    sets = ((p_kv, c_kv, x_kv, z_kv), (p_wo, c_wo, x_wo, z_wo), (p_pw, c_pw, x_pw, z_pw), (p_ve, c_ve, x_ve, z_ve))
    ek, eo, ep, ev = [Scatter(at, *b, ss.at[i], sc.at[i], sx.at[i], sz.at[i]) for i, b in enumerate(sets)]
    eq = ScatterY(at, p_qk, c_qk, w_qk, x_qk, z_qk, fs, fc, fy, fx, fz, ft)
    steps = iter(range(15))
    def some(n):
        for _ in range(n):
            i = next(steps, None)
            if i is not None:
                back.step(i)
    ydev = (1 - r, idx(z, x, c))
    def trade(i, out, a, b):
        a[...] = out[...].astype(BF)
        pltpu.make_async_remote_copy(a, b, ysem.at[2 * i], ysem.at[2 * i + 1], device_id=ydev, device_id_type=MESH).start()
    def traded(i, out, a, b):
        pltpu.make_async_remote_copy(a, b, ysem.at[2 * i], ysem.at[2 * i + 1], device_id=ydev, device_id_type=MESH).wait()
        out[...] = a[...].astype(F32) + b[...].astype(F32)

    grad_norm, gain_two = norm_gradient(mid[...], vec[2:3, :width], gn2[...])
    valid = row_mask(lens, first_row, block, (cot.shape[0], 1))
    gmid[...] = cot[...].astype(F32) * valid + grad_norm
    branch[...] = gmid[...].astype(BF)
    loads[0].wait()
    @pl.loop(0, 4)
    def _(t):
        blocks = pl.ds(pl.multiple_of(4 * t, 4), 4)
        col = pl.ds(pl.multiple_of(384 * t, 384), 384)
        low = att[:, col].astype(BF)
        p_wo[blocks] = dot_tn(low, branch[...]).astype(BF).reshape(4, 96, width)
        gatt[:, col] = dot_nt(branch[...], wo[blocks].reshape(384, width))
    eo.begin()
    eo.step_x(3)
    eo.step_x(2)
    back.own()
    layer_out[...] = ((mid[...] + mlp_out[...]) * valid).astype(BF)
    loads[1].wait()
    loads[3].wait()
    span = 16 * block
    def unit(u):
        s, h = u // 2, lax.rem(u, 2)
        rows = pl.ds(pl.multiple_of(block * s, block), block)
        cols = pl.ds(pl.multiple_of(width // 2 * h, width // 2), width // 2)
        kcol = pl.ds(pl.multiple_of(HEAD_DIM * h, HEAD_DIM), HEAD_DIM)
        vcol = pl.ds(pl.multiple_of(kw + HEAD_DIM * h, HEAD_DIM), HEAD_DIM)
        q = stack_heads(q_ref[rows, cols])
        k = kv[:, rows, kcol].reshape(span, HEAD_DIM)
        v = kv[:, rows, vcol].reshape(span, HEAD_DIM)
        e = exp_scores(q, k, first_row, block, lens[s])
        total = jnp.sum(e, axis=-1, keepdims=True)
        ga = stack_heads(gatt[rows, cols])
        gt = -jnp.sum(ga * stack_heads(att[rows, cols]), axis=-1, keepdims=True) / total
        gn = (ga / total).astype(BF)
        gs = (e * (dot_nt(gn, v) + gt)).astype(BF)
        p_kv[:, rows, kcol] = dot_tn(gs, q).astype(BF).reshape(16, block, HEAD_DIM)
        p_kv[:, rows, vcol] = dot_tn(e.astype(BF), gn).astype(BF).reshape(16, block, HEAD_DIM)
        gq = dot(gs, k) * (HEAD_DIM ** -0.5)
        cos, sin = rope[0], rope[1]
        gqkv[rows, cols] = jnp.concatenate([spin(gq[block * i : block * (i + 1)], cos, -sin) for i in range(HEADS // KV_HEADS)], axis=1).astype(BF)
    unit(0)
    some(1)
    eo.step_z(3)
    eo.step_x(1)
    unit(1)
    some(1)
    eo.step_z(2)
    eo.step_x(0)
    unit(2)
    some(1)
    eo.step_z(1)
    unit(3)
    ek.begin()
    ek.step_x(3)
    ek.step_x(2)
    some(1)
    loads[2].wait()
    @pl.loop(0, 4)
    def _(t):
        blocks = pl.ds(pl.multiple_of(4 * t, 4), 4)
        col = pl.ds(pl.multiple_of(384 * t, 384), 384)
        p_qk[blocks] = dot_tn(normed[:, col], gqkv[:, :width]).astype(BF).reshape(4, 96, width)
    ek.step_z(3)
    ek.step_x(1)
    eq.begin()
    eo.finish(wo_out)
    trade(2, wo_out, y2, y3)
    for d in (3, 2, 1, 0):
        eq.step_y(d)
    ek.step_z(2)
    ek.step_x(0)
    some(1)
    @pl.loop(0, 4)
    def _(t):
        blocks = pl.ds(pl.multiple_of(4 * t, 4), 4)
        col = pl.ds(pl.multiple_of(384 * t, 384), 384)
        gatt[:, col] = dot_nt(gqkv[:, :width], wqkv[blocks, :, :width].reshape(384, width))
    ek.step_z(1)
    eq.step_x(3)
    eq.step_x(2)
    some(1)
    ek.finish(kvsum)
    cos, sin = [jnp.concatenate((rope[i], rope[i]), axis=0) for i in range(2)]
    for h in range(KV_HEADS):
        kcol = slice(HEAD_DIM * h, HEAD_DIM * (h + 1))
        gqkv[:, width + HEAD_DIM * h : width + HEAD_DIM * (h + 1)] = spin(kvsum[:, kcol] * (HEAD_DIM ** -0.5), cos, -sin).astype(BF)
    gqkv[:, width + kw :] = kvsum[:, kw:].astype(BF)
    @pl.loop(0, 4)
    def _(t):
        blocks = pl.ds(pl.multiple_of(4 * t, 4), 4)
        col = pl.ds(pl.multiple_of(384 * t, 384), 384)
        p_pw[blocks] = dot_tn(normed[:, col], gqkv[:, width:]).astype(BF).reshape(4, 96, 2 * kw)
        gatt[:, col] += dot_nt(gqkv[:, width:], wqkv[blocks, :, width:].reshape(384, 2 * kw))
    ep.begin()
    ep.step_x(3)
    ep.step_x(2)
    eq.step_z(3)
    eq.step_x(1)
    some(1)
    grad_norm, gain_one = norm_gradient(x_ref[...].astype(F32), vec[0:1, :width], gatt[...])
    grad_input[...] = gmid[...] + grad_norm
    bias = jnp.sum(gqkv[...].astype(F32), axis=0, keepdims=True)
    pv[...] = jnp.zeros_like(pv)
    for i, (v, a, b) in enumerate(((gain_one, sel, fold), (bias[:, :width], sel, fold), (bias[:, width : width + kw], selk, foldk), (bias[:, width + kw :], selk, foldk), (gain_two, sel, fold))):
        pv[:, i, :] = dot((a[...] * v).astype(BF), b[...])
    p_ve[...] = pv[...].astype(BF)
    ev.begin()
    ev.step_x(3)
    ev.step_x(2)
    some(1)
    late = (ep, ev)
    for kind, d in (("z", 3), ("x", 1), ("z", 2), ("x", 0), ("z", 1)):
        for e in late:
            (e.step_x if kind == "x" else e.step_z)(d)
        if (kind, d) not in (("z", 3), ("x", 1)):
            (eq.step_x if kind == "x" else eq.step_z)(d)
        some(1)
    some(15)
    eq.finish(q_out, low_q)
    ep.finish(pair_out)
    trade(0, pair_out, y4, y5)
    ev.finish(vec_out)
    trade(1, vec_out, y6, y7)
    traded(2, wo_out, y2, y3)
    eq.traded(q_out, low_q)
    traded(0, pair_out, y4, y5)
    k_out[...] = pair_out[:, :kw]
    v_out[...] = pair_out[:, kw:]
    traded(1, vec_out, y6, y7)
    back.end()

def backward(lens, gn2, mlp_out, mid, cot, x, att, q, normed, vec, sel, fold, selk, foldk, rope, kv, wo, wqkv, half, ff, block, cid, window=4):
    any_ = pl.BlockSpec(memory_space=pl.ANY)
    vm = pl.BlockSpec(memory_space=pltpu.VMEM)
    dma = pltpu.SemaphoreType.DMA
    sds = jax.ShapeDtypeStruct
    rows, width = x.shape
    wide = wqkv.shape[-1]
    own = wo.shape[1]
    kvw = kv.shape[-1]
    VM = pltpu.VMEM
    def four(blk):
        return [VM((k,) + blk, BF) for k in (16, 8, 4, 5)]
    def five(blk):
        part = (blk[0] // 2, blk[1])
        return [VM((k,) + blk, BF) for k in (16, 8)] + [VM((k,) + part, BF) for k in (8, 4, 5)]
    return pl.pallas_call(
        functools.partial(backward_kernel, block, window),
        out_shape=[sds((rows, width), BF), sds((rows, width), F32), sds((own, width), F32), sds((own, (wide - width) // 2), F32), sds((own, (wide - width) // 2), F32), sds((own, width), F32), sds((16, 128), F32), sds((own, ff), BF)] + [sds((own, ff), BF)] * 2,
        in_specs=[pl.BlockSpec(memory_space=pltpu.SMEM)] + [vm] * 13 + [any_] * 5,
        out_specs=[vm] * 7 + [any_] * 3,
        scratch_shapes=[VM((2, block, HEAD_DIM), F32), VM(kv.shape, BF), VM(wo.shape, BF), VM(wqkv.shape, BF), VM((rows, width), F32), VM((rows, width), BF), VM((rows, width), F32), VM((rows, wide), BF), VM((16, 16, 128), F32)]
        + four((rows, kvw)) + four((own, width)) + five((own, width)) + four((own, wide - width)) + four((16, 128))
        + [VM((rows, kvw), F32), VM((own, wide - width), F32)] + [VM((own, width), BF)] * 3 + [VM((own, wide - width), BF)] * 2 + [VM((16, 128), BF)] * 2
        + [dma((4, 16)), dma((4, 8)), dma((4, 4)), dma((4, 5))] + [dma((16,))] * 8 + [dma((2,)), dma((6,)), dma((24,)), dma((8,)), dma((8,)), dma((4,)), dma((5,)), dma((2,)), dma((4,))],
        compiler_params=pltpu.CompilerParams(collective_id=cid, has_side_effects=True, vmem_limit_bytes=60 * 2**20),
    )(lens, gn2, mlp_out, mid, cot, x, att, q, normed, vec, sel, fold, selk, foldk, rope, kv, wo, wqkv, half)


def folding(group_count, width):
    share = width // group_count
    at = np.arange(width)
    sel = (at[None, :] // share == np.arange(group_count)[:, None]).astype(np.float32)
    fold = (at[:, None] % share == np.arange(128)[None, :]).astype(BF)
    return sel, fold


def rope_constants(span):
    freqs = np.float32(THETA) ** (-np.arange(0, HEAD_DIM, 2, dtype=np.float32) / HEAD_DIM)
    angles = np.arange(span, dtype=np.float32)[:, None] * freqs[None, :].astype(np.float32)
    sin = np.sin(angles)
    return np.stack(
        (np.concatenate((np.cos(angles),) * 2, axis=1), np.concatenate((-sin, sin), axis=1))
    ).astype(np.float32)


def shards_fast(
    hidden_in,
    lengths,
    gain_attn,
    w_query,
    b_query,
    w_key,
    b_key,
    w_value,
    b_value,
    w_out,
    gain_mlp,
    w_gate,
    w_up,
    w_down,
    cotangent,
):
    group_count = lax.axis_size("group")
    slot_count, block_len, model_width = hidden_in.shape
    kv_width = KV_HEADS * HEAD_DIM
    tokens = slot_count * block_len
    hidden_units = w_gate.shape[1]
    pieces = (gain_attn, b_query, b_key, b_value, gain_mlp)
    sel, fold = folding(group_count, model_width)
    selk, foldk = folding(group_count, kv_width)
    rope = rope_constants(group_count * block_len)
    rows_in = hidden_in.reshape(tokens, model_width)
    grad_rows = cotangent.reshape(tokens, model_width)
    (
        q_rows, normed, attended, mid, normed_two, vec, columns, qkv_w, pair_all, grad_all, out_w
    ) = front(
        lengths,
        rows_in,
        grad_rows,
        [p[None] for p in pieces],
        sel,
        fold,
        selk,
        foldk,
        rope,
        w_query,
        w_key,
        w_value,
        w_gate,
        w_up,
        w_down,
        w_out,
        block_len,
        1,
    )
    grad_normed_two, mlp_out, half_sum = mlp(normed_two, grad_all, columns, 3)
    layer_out, grad_input, query_sum, key_sum, value_sum, out_sum, vector_sum, *ff_sums = backward(
        lengths,
        grad_normed_two,
        mlp_out,
        mid,
        grad_rows,
        rows_in,
        attended,
        q_rows,
        normed,
        vec,
        sel,
        fold,
        selk,
        foldk,
        rope,
        pair_all,
        out_w,
        qkv_w,
        half_sum,
        hidden_units,
        block_len,
        4,
        2,
    )
    ff_sums = [p.astype(F32) for p in ff_sums]
    gain_one_sum, query_bias_sum, key_bias_sum, value_bias_sum, gain_two_sum = [
        vector_sum[i, : p.shape[0]] for i, p in enumerate(pieces)
    ]
    return (
        layer_out.reshape(hidden_in.shape),
        grad_input.reshape(hidden_in.shape),
        gain_one_sum,
        query_sum,
        query_bias_sum,
        key_sum,
        key_bias_sum,
        value_sum,
        value_bias_sum,
        out_sum,
        gain_two_sum,
        *ff_sums,
    )


def solution(mesh):
    act = P("replica", "group", None)
    vec = P("group")
    mat = P("group", None)
    return jax.shard_map(
        shards_fast if mesh.shape["group"] == 16 else shards_plain,
        mesh=mesh,
        in_specs=(act, P("replica"), vec, mat, vec, mat, vec, mat, vec, mat, vec, mat, mat, mat, act),
        out_specs=(act, act, vec, mat, vec, mat, vec, mat, vec, mat, vec, mat, mat, mat),
        check_vma=False,
    )
```

```python
import functools

import jax
import jax.numpy as jnp
import numpy as np
from jax import lax
from jax.experimental import pallas as pl
from jax.experimental.pallas import tpu as pltpu
from jax.sharding import PartitionSpec as P

MESH = pl.DeviceIdType.MESH
NZ = 4
MAIN = 512
D = 1536
COLS = 3 * MAIN + 384
HEADS = 12
KV_HEADS = 2
HEAD_DIM = 128
EPSILON = 1e-06
THETA = 1000000.0
BF = jnp.bfloat16
F32 = jnp.float32


def rope_tables(positions, head_dim):
    freqs = THETA ** (-jnp.arange(0, head_dim, 2).astype(F32) / head_dim)
    angles = positions.astype(F32)[:, None] * freqs[None, :]
    angles = jnp.concatenate((angles, angles), axis=-1)
    return (jnp.cos(angles), jnp.sin(angles))


def rotate(tensor, cos_table, sin_table):
    halfway = tensor.shape[-1] // 2
    turned = jnp.concatenate((-tensor[..., halfway:], tensor[..., :halfway]), axis=-1)
    return tensor * cos_table + turned * sin_table


def rotate_back(gradient, cos_table, sin_table):
    halfway = gradient.shape[-1] // 2
    scaled = gradient * sin_table
    turned = jnp.concatenate((scaled[..., halfway:], -scaled[..., :halfway]), axis=-1)
    return gradient * cos_table + turned


def normalize(row_values, gain_vec):
    factor = lax.rsqrt(jnp.mean(row_values * row_values, axis=-1, keepdims=True) + EPSILON)
    return (row_values * factor * gain_vec, factor)


def norm_back(row_values, factor, gain_vec, upstream):
    weighted = upstream * gain_vec
    inner_mean = jnp.mean(weighted * row_values, axis=-1, keepdims=True)
    grad_rows = factor * weighted - row_values * (factor * factor * factor) * inner_mean
    grad_gain = jnp.sum(upstream * row_values * factor, axis=0)
    return (grad_rows, grad_gain)


def matmul(a, b):
    return jnp.dot(a, b, preferred_element_type=F32)


def matmul_nt(a, b):
    return lax.dot_general(a, b, (((1,), (1,)), ((), ())), preferred_element_type=F32)


def matmul_tn(a, b):
    return lax.dot_general(a, b, (((0,), (0,)), ((), ())), preferred_element_type=F32)


def arrange(per_token, kv_heads):
    block_len, head_count, head_dim = per_token.shape
    repeat = head_count // kv_heads
    grouped = per_token.reshape(block_len, kv_heads, repeat, head_dim)
    return jnp.transpose(grouped, (1, 2, 0, 3)).reshape(kv_heads, repeat * block_len, head_dim)


def restore(per_group, block_len):
    kv_heads, row_count, head_dim = per_group.shape
    repeat = row_count // block_len
    grouped = per_group.reshape(kv_heads, repeat, block_len, head_dim)
    return jnp.transpose(grouped, (2, 0, 1, 3)).reshape(block_len, kv_heads * repeat * head_dim)


def masked_exp(query_rows, key_block, row_pos, first_key, length, score_scale):
    key_step = key_block.shape[0]
    raw_scores = jnp.einsum("grd,kgd->grk", query_rows, key_block, preferred_element_type=F32)
    key_pos = first_key + jnp.arange(key_step, dtype=jnp.int32)
    allowed = (key_pos[None, :] <= row_pos[:, None]) & (key_pos[None, :] < length)
    return jnp.where(allowed[None], jnp.exp(raw_scores * score_scale), 0.0)


def block_total(length, rank_end, key_step):
    key_limit = jnp.minimum(length, rank_end)
    return (key_limit + key_step - 1) // key_step


def attend_forward(query_rows, key_all, value_all, row_pos, length, rank_end, key_step, scale):
    kv_heads, row_count, head_dim = query_rows.shape

    def visit(block_index, state_tuple):
        totals, numerator = state_tuple
        first_key = block_index * key_step
        key_block = lax.dynamic_slice_in_dim(key_all, first_key, key_step, 0)
        value_block = lax.dynamic_slice_in_dim(value_all, first_key, key_step, 0)
        weights = masked_exp(query_rows, key_block, row_pos, first_key, length, scale)
        totals = totals + jnp.sum(weights, axis=-1)
        numerator = numerator + jnp.einsum(
            "grk,kgd->grd", weights.astype(BF), value_block, preferred_element_type=F32
        )
        return (totals, numerator)

    initial = (
        jnp.zeros((kv_heads, row_count), F32),
        jnp.zeros((kv_heads, row_count, head_dim), F32),
    )
    return lax.fori_loop(0, block_total(length, rank_end, key_step), visit, initial)


def attend_backward(
    query_rows, key_all, value_all, row_pos, length, rank_end, key_step, scale, grad_numer, grad_total
):
    kv_heads, row_count, head_dim = query_rows.shape

    def visit(block_index, state_tuple):
        grad_query, grad_key, grad_value = state_tuple
        first_key = block_index * key_step
        key_block = lax.dynamic_slice_in_dim(key_all, first_key, key_step, 0)
        value_block = lax.dynamic_slice_in_dim(value_all, first_key, key_step, 0)
        weights = masked_exp(query_rows, key_block, row_pos, first_key, length, scale)
        grad_prob = jnp.einsum("grd,kgd->grk", grad_numer, value_block, preferred_element_type=F32)
        grad_score = (weights * (grad_prob + grad_total[..., None])).astype(BF)
        grad_query = grad_query + jnp.einsum(
            "grk,kgd->grd", grad_score, key_block, preferred_element_type=F32
        )
        key_part = jnp.einsum("grk,grd->kgd", grad_score, query_rows, preferred_element_type=F32)
        value_part = jnp.einsum(
            "grk,grd->kgd", weights.astype(BF), grad_numer, preferred_element_type=F32
        )
        key_old = lax.dynamic_slice_in_dim(grad_key, first_key, key_step, 0)
        value_old = lax.dynamic_slice_in_dim(grad_value, first_key, key_step, 0)
        grad_key = lax.dynamic_update_slice_in_dim(grad_key, key_old + key_part, first_key, 0)
        grad_value = lax.dynamic_update_slice_in_dim(
            grad_value, value_old + value_part, first_key, 0
        )
        return (grad_query, grad_key, grad_value)

    initial = (
        jnp.zeros((kv_heads, row_count, head_dim), F32),
        jnp.zeros(key_all.shape, F32),
        jnp.zeros(value_all.shape, F32),
    )
    return lax.fori_loop(0, block_total(length, rank_end, key_step), visit, initial)


def gather_plain(x):
    return lax.all_gather(x, "group", axis=0, tiled=True)


def scatter_sum(x):
    return lax.psum_scatter(x, "group", scatter_dimension=0, tiled=True)


def shards_plain(
    hidden_in,
    lengths,
    gain_attn,
    w_query,
    b_query,
    w_key,
    b_key,
    w_value,
    b_value,
    w_out,
    gain_mlp,
    w_gate,
    w_up,
    w_down,
    cotangent,
):
    group_count = lax.axis_size("group")
    group_rank = lax.axis_index("group")
    slot_count, block_len, model_width = hidden_in.shape
    kv_heads = KV_HEADS
    head_dim = HEAD_DIM
    kv_width = kv_heads * head_dim
    repeat = HEADS // kv_heads
    slot_span = block_len * group_count
    key_step = min(512, slot_span)
    score_scale = head_dim ** (-0.5)
    tokens = slot_count * block_len
    hidden_units = w_gate.shape[1]
    own_rows = w_gate.shape[0]
    share = hidden_units // group_count
    positions = group_rank * block_len + jnp.arange(block_len, dtype=jnp.int32)
    valid_rows = (positions[None, :] < lengths[:, None]).astype(F32).reshape(tokens, 1)
    cos_table, sin_table = rope_tables(positions, head_dim)
    cos_heads = cos_table[:, None, :]
    sin_heads = sin_table[:, None, :]
    rank_end = (group_rank + 1) * block_len
    row_pos = jnp.tile(positions, repeat)

    pieces = (gain_attn, b_query, b_key, b_value, gain_mlp)
    sizes = [p.shape[0] for p in pieces]
    small = gather_plain(jnp.concatenate(pieces)[None])
    offsets = [sum(sizes[:i]) for i in range(len(sizes) + 1)]
    gain_one, query_b, key_b, value_b, gain_two = [
        small[:, offsets[i] : offsets[i + 1]].reshape(-1).astype(F32) for i in range(len(sizes))
    ]
    qkv_w = gather_plain(jnp.concatenate((w_query, w_key, w_value), axis=1))
    out_w = gather_plain(w_out)
    qkv_b = jnp.concatenate((query_b, key_b, value_b))

    stacked = jnp.stack((w_gate, w_up, w_down)).reshape(3, own_rows, group_count, share)
    stacked = jnp.transpose(stacked, (2, 1, 0, 3)).reshape(group_count, own_rows, 3 * share)
    columns = lax.all_to_all(stacked, "group", 0, 0, tiled=True).reshape(model_width, 3 * share)
    gate_up_w = columns[:, : 2 * share]
    down_w = columns[:, 2 * share :]

    grad_final = cotangent.reshape(tokens, model_width).astype(F32) * valid_rows
    grad_all = gather_plain(grad_final.astype(BF))

    inputs = hidden_in.reshape(tokens, model_width).astype(F32)
    normed_full, factor_one = normalize(inputs, gain_one)
    normed = normed_full.astype(BF)
    qkv = matmul(normed, qkv_w) + qkv_b
    query_rot = rotate(
        qkv[:, :model_width].reshape(slot_count, block_len, HEADS, head_dim), cos_heads, sin_heads
    ).astype(BF)
    key_rot = rotate(
        qkv[:, model_width : model_width + kv_width].reshape(
            slot_count, block_len, kv_heads, head_dim
        ),
        cos_heads,
        sin_heads,
    ).astype(BF)
    value_low = qkv[:, model_width + kv_width :].astype(BF)
    pair = jnp.concatenate(
        (key_rot.reshape(tokens, kv_width), value_low), axis=1
    ).reshape(1, slot_count, block_len, 2 * kv_width)
    pair_all = jnp.transpose(gather_plain(pair), (1, 0, 2, 3)).reshape(
        slot_count, slot_span, 2, kv_heads, head_dim
    )
    key_all = pair_all[:, :, 0]
    value_all = pair_all[:, :, 1]
    query_groups = []
    slot_totals = []
    slot_attended = []
    attended_rows = []
    for s in range(slot_count):
        query_rows = arrange(query_rot[s], kv_heads)
        totals, numerator = attend_forward(
            query_rows, key_all[s], value_all[s], row_pos, lengths[s], rank_end, key_step, score_scale
        )
        attended = numerator / totals[..., None]
        query_groups.append(query_rows)
        slot_totals.append(totals)
        slot_attended.append(attended)
        attended_rows.append(restore(attended, block_len))
    attended_low = jnp.concatenate(attended_rows, axis=0).astype(BF)
    residual_mid = inputs + matmul(attended_low, out_w)
    normed_two_full, factor_two = normalize(residual_mid, gain_two)
    normed_all = gather_plain(normed_two_full.astype(BF))

    pre = matmul(normed_all, gate_up_w)
    gate_pre = pre[:, :share]
    up_pre = pre[:, share:]
    sigmoid_gate = jax.nn.sigmoid(gate_pre)
    silu_gate = gate_pre * sigmoid_gate
    hidden = (silu_gate * up_pre).astype(BF)
    grad_hidden = matmul(grad_all, down_w)
    grad_gate = (
        grad_hidden * up_pre * (sigmoid_gate * (1.0 + gate_pre * (1.0 - sigmoid_gate)))
    ).astype(BF)
    grad_up = (grad_hidden * silu_gate).astype(BF)
    gate_up_grad = jnp.concatenate((grad_gate, grad_up), axis=1)
    grad_normed_two = scatter_sum(matmul_nt(gate_up_grad, gate_up_w).astype(BF)).astype(F32)
    mlp_out = scatter_sum(matmul_nt(hidden, down_w).astype(BF)).astype(F32)
    down_term = matmul_tn(grad_all, hidden)
    gate_up_term = matmul_tn(normed_all, gate_up_grad)
    terms = jnp.concatenate((gate_up_term, down_term), axis=1).astype(BF)
    back = lax.all_to_all(
        terms.reshape(group_count, own_rows, 3 * share), "group", 0, 0, tiled=True
    )
    summed = back.astype(F32) + lax.ppermute(back, "replica", [(0, 1), (1, 0)]).astype(F32)
    summed = jnp.transpose(summed.reshape(group_count, own_rows, 3, share), (2, 1, 0, 3))
    gate_sum, up_sum, down_sum = summed.reshape(3, own_rows, hidden_units)

    final_rows = residual_mid + mlp_out
    layer_out = (final_rows * valid_rows).reshape(slot_count, block_len, model_width).astype(BF)
    grad_mid_norm, grad_gain_two = norm_back(residual_mid, factor_two, gain_two, grad_normed_two)
    grad_mid = grad_final + grad_mid_norm
    grad_branch = grad_mid.astype(BF)
    out_term = matmul_tn(attended_low, grad_branch)
    grad_attended = matmul_nt(grad_branch, out_w)
    grad_query_rows = []
    grad_pairs = []
    for s in range(slot_count):
        slot_grad = grad_attended[s * block_len : (s + 1) * block_len].reshape(
            block_len, HEADS, head_dim
        )
        grad_out = arrange(slot_grad, kv_heads)
        totals = slot_totals[s]
        grad_total = -jnp.sum(grad_out * slot_attended[s], axis=-1) / totals
        grad_numer = (grad_out / totals[..., None]).astype(BF)
        grad_query, grad_key, grad_value = attend_backward(
            query_groups[s],
            key_all[s],
            value_all[s],
            row_pos,
            lengths[s],
            rank_end,
            key_step,
            score_scale,
            grad_numer,
            grad_total,
        )
        query_back_rows = restore(grad_query * score_scale, block_len).reshape(
            block_len, HEADS, head_dim
        )
        grad_query_rows.append(
            rotate_back(query_back_rows, cos_heads, sin_heads).reshape(block_len, HEADS * head_dim)
        )
        grad_pairs.append(
            jnp.concatenate(
                (grad_key.reshape(slot_span, kv_width), grad_value.reshape(slot_span, kv_width)),
                axis=1,
            )
        )
    pair_grads = jnp.stack(grad_pairs).reshape(slot_count, group_count, block_len, 2 * kv_width)
    pair_grads = jnp.transpose(pair_grads, (1, 0, 2, 3)).astype(BF)
    pair_sum = scatter_sum(pair_grads).reshape(slot_count, block_len, 2 * kv_width).astype(F32)
    grad_query_pre = jnp.concatenate(grad_query_rows, axis=0).astype(BF)
    key_sum = pair_sum[..., :kv_width].reshape(slot_count, block_len, kv_heads, head_dim)
    grad_key_pre = (
        rotate_back(key_sum * score_scale, cos_heads, sin_heads).astype(BF).reshape(tokens, kv_width)
    )
    grad_value_pre = pair_sum[..., kv_width:].astype(BF).reshape(tokens, kv_width)
    grad_qkv = jnp.concatenate((grad_query_pre, grad_key_pre, grad_value_pre), axis=1)
    grad_normed = matmul_nt(grad_qkv, qkv_w)
    grad_in_norm, grad_gain_one = norm_back(inputs, factor_one, gain_one, grad_normed)
    grad_input = (grad_mid + grad_in_norm).reshape(slot_count, block_len, model_width)
    qkv_term = matmul_tn(normed, grad_qkv)
    qkv_bias = jnp.sum(grad_qkv.astype(F32), axis=0)

    weight_share = scatter_sum(
        jnp.concatenate((qkv_term, out_term), axis=1).astype(BF)
    )
    weight_sum = weight_share.astype(F32) + lax.ppermute(
        weight_share, "replica", [(0, 1), (1, 0)]
    ).astype(F32)
    vectors = jnp.concatenate(
        [
            grad_gain_one.reshape(group_count, -1),
            qkv_bias[:model_width].reshape(group_count, -1),
            qkv_bias[model_width : model_width + kv_width].reshape(group_count, -1),
            qkv_bias[model_width + kv_width :].reshape(group_count, -1),
            grad_gain_two.reshape(group_count, -1),
        ],
        axis=1,
    )
    vector_sum = lax.psum(scatter_sum(vectors), "replica").reshape(-1)
    gain_one_sum, query_bias_sum, key_bias_sum, value_bias_sum, gain_two_sum = [
        vector_sum[offsets[i] : offsets[i + 1]] for i in range(len(sizes))
    ]
    ends = (0, model_width, model_width + kv_width, model_width + 2 * kv_width)
    query_sum, key_sum_w, value_sum_w = [weight_sum[:, ends[i] : ends[i + 1]] for i in range(3)]
    out_sum = weight_sum[:, ends[3] :]
    return (
        layer_out,
        grad_input,
        gain_one_sum,
        query_sum,
        query_bias_sum,
        key_sum_w,
        key_bias_sum,
        value_sum_w,
        value_bias_sum,
        out_sum,
        gain_two_sum,
        gate_sum,
        up_sum,
        down_sum,
    )


def place():
    g = lax.axis_index("group")
    r = lax.axis_index("replica")
    return r, g // 4, lax.rem(g // 2, 2), lax.rem(g, 2)

def idx(z, x, c):
    return (z * 2 + x) * 2 + c

def greet(r, z, x, c, with_y=False):
    bar = pltpu.get_barrier_semaphore()
    def hail(dev):
        pl.semaphore_signal(bar, inc=1, device_id=dev, device_id_type=MESH)
    hail((r, idx(z, 1 - x, c)))
    hail((r, idx(z, x, 1 - c)))
    if with_y:
        hail((1 - r, idx(z, x, c)))
    @pl.when(z > 0)
    def _():
        hail((r, idx(z - 1, x, c)))
    @pl.when(z < NZ - 1)
    def _():
        hail((r, idx(z + 1, x, c)))
    ends = jnp.where((z > 0) & (z < NZ - 1), 1, 0)
    pl.semaphore_wait(bar, (4 if with_y else 3) + ends)

def planes(z):
    return (
        z,
        jnp.where(z == 0, 1, jnp.where(z == 1, 0, jnp.where(z == 2, 3, 2))),
        jnp.where(z == 0, 2, jnp.where(z == 1, 2, 1)),
        jnp.where(z < 2, 3, 0),
    )

def when(cond, fn):
    pl.when(cond)(fn)

class Gather:
    def __init__(self, at, src, out, send, recv, local, part=None):
        self.r, self.z, self.x, self.c = at
        self.src, self.out, self.send, self.recv, self.local = src, out, send, recv, local
        self.part = part
        self.mid = (self.z > 0) & (self.z < NZ - 1)
        self.p = planes(self.z)
    def blk(self, b):
        return self.out.at[b] if self.part is None else self.out.at[b, self.part]
    def put(self, src, b, k, dev):
        pltpu.make_async_remote_copy(src, self.blk(b), self.send.at[k], self.recv.at[b], device_id=dev, device_id_type=MESH).start()
    def sent(self, k):
        b = 0
        pltpu.make_async_remote_copy(self.blk(b), self.blk(b), self.send.at[k], self.recv.at[b], device_id=(self.r, 0), device_id_type=MESH).wait_send()
    def got(self, b):
        pltpu.make_async_remote_copy(self.blk(b), self.blk(b), self.send.at[0], self.recv.at[b], device_id=(self.r, 0), device_id_type=MESH).wait_recv()
    def zdev(self, s): return (self.r, idx(self.z + s, self.x, self.c))
    def xdev(self): return (self.r, idx(self.z, 1 - self.x, self.c))
    def cdev(self): return (self.r, idx(self.z, self.x, 1 - self.c))
    def begin(self):
        z, x, c = self.z, self.x, self.c
        me = idx(z, x, c)
        for s in (1, -1):
            when(self.inside(z + s), lambda s=s: self.put(self.src, me, 0 if s == 1 else 3, self.zdev(s)))
        self.put(self.src, me, 6 + z, self.xdev())
        self.put(self.src, me, 10 + 2 * z + x, self.cdev())
        pltpu.make_async_copy(self.src, self.blk(me), self.local).start()
    def inside(self, z): return (z >= 0) & (z < NZ)
    def from_z(self, zz):
        z, x, c = self.z, self.x, self.c
        b = idx(zz, x, c)
        self.got(b)
        s = jnp.where(zz < z, 1, -1)
        d = jnp.abs(zz - z)
        slot = jnp.where(zz < z, 0, 3) + d
        when(self.inside(z + s), lambda: self.put(self.blk(b), b, slot, (self.r, idx(z + s, x, c))))
        self.put(self.blk(b), b, 6 + zz, self.xdev())
        self.put(self.blk(b), b, 10 + 2 * zz + x, self.cdev())
    def first(self):
        self.from_z(self.p[1])
        when(self.mid, lambda: self.from_z(self.p[2]))
        self.from_x(self.p[0])
    def second(self):
        self.from_z(jnp.where(self.mid, self.p[3], self.p[2]))
        self.from_x(self.p[1])
    def third(self):
        when(~self.mid, lambda: self.from_z(self.p[3]))
        self.from_x(self.p[2])
    def fourth(self):
        self.from_x(self.p[3])
    def from_x(self, zz):
        b = idx(zz, 1 - self.x, self.c)
        self.got(b)
        self.put(self.blk(b), b, 10 + 2 * zz + 1 - self.x, self.cdev())
    def from_c(self, zz):
        self.got(idx(zz, self.x, 1 - self.c))
        self.got(idx(zz, 1 - self.x, 1 - self.c))
    def end(self, local=True):
        z = self.z
        for d in range(NZ - 1):
            when((z - d >= 0) & (z < NZ - 1), lambda d=d: self.sent(d))
            when((z + d < NZ) & (z > 0), lambda d=d: self.sent(3 + d))
        for k in range(6, 18):
            self.sent(k)
        if local:
            pltpu.make_async_copy(self.src, self.blk(0), self.local).wait()

class Scatter:
    def __init__(self, at, part, rc, rx, rz, send, rcs, rxs, rzs):
        self.r, self.z, self.x, self.c = at
        self.part, self.rc, self.rx, self.rz = part, rc, rx, rz
        self.send, self.rcs, self.rxs, self.rzs = send, rcs, rxs, rzs
    def inside(self, z): return (z >= 0) & (z < NZ)
    def copy(self, src, dst, k, rs, dev):
        return pltpu.make_async_remote_copy(src, dst, self.send.at[k], rs, device_id=dev, device_id_type=MESH)
    def over(self, d):
        return [(s, self.z + s * d) for s in ((-1, 1) if d else (1,))]
    def begin(self, far_first=True):
        z, x, c = self.z, self.x, self.c
        dev = (self.r, idx(z, x, 1 - c))
        for xx in (1 - x, x):
            for d in range(NZ - 1, -1, -1):
                for s, zz in self.over(d):
                    k = 2 * zz + xx
                    when(self.inside(zz), lambda zz=zz, k=k, xx=xx: self.copy(self.part.at[idx(zz, xx, 1 - c)], self.rc.at[k], k, self.rcs.at[k], dev).start())
    def send_c(self, zz):
        z, x, c = self.z, self.x, self.c
        dev = (self.r, idx(z, x, 1 - c))
        for xx in (1 - x, x):
            k = 2 * zz + xx
            self.copy(self.part.at[idx(zz, xx, 1 - c)], self.rc.at[k], k, self.rcs.at[k], dev).start()
    def x_plane(self, zz):
        z, x, c = self.z, self.x, self.c
        dev = (self.r, idx(z, 1 - x, c))
        k = 2 * zz + 1 - x
        b = idx(zz, 1 - x, c)
        self.copy(self.rc.at[k], self.rc.at[k], 0, self.rcs.at[k], dev).wait_recv()
        self.part[b] = (self.part[b].astype(F32) + self.rc[k].astype(F32)).astype(BF)
        self.copy(self.part.at[b], self.rx.at[zz], 8 + zz, self.rxs.at[zz], dev).start()
    def step_x(self, d):
        for s, zz in self.over(d):
            when(self.inside(zz), lambda zz=zz: self.x_plane(zz))
    def step_z(self, d):
        z, x, c = self.z, self.x, self.c
        for s, zz in self.over(d):
            def go(zz=zz, s=s):
                k = 2 * zz + x
                b = idx(zz, x, c)
                self.copy(self.rc.at[k], self.rc.at[k], 0, self.rcs.at[k], (self.r, 0)).wait_recv()
                self.copy(self.rx.at[zz], self.rx.at[zz], 0, self.rxs.at[zz], (self.r, 0)).wait_recv()
                both = self.part[b].astype(F32) + self.rc[k].astype(F32) + self.rx[zz].astype(F32)
                dev = (self.r, idx(z + s, x, c))
                slot = jnp.where(zz == z + s, NZ, zz) if s == -1 else zz
                self.part[b] = both.astype(BF)
                def more():
                    self.copy(self.rz.at[zz], self.rz.at[zz], 0, self.rzs.at[zz], dev).wait_recv()
                    self.part[b] = (self.part[b].astype(F32) + self.rz[zz].astype(F32)).astype(BF)
                when(self.inside(z - s), more)
                self.copy(self.part.at[b], self.rz.at[slot], 12 + zz, self.rzs.at[slot], dev).start()
            when(self.inside(zz), go)
    def finish(self, out):
        z, x, c = self.z, self.x, self.c
        k = 2 * z + x
        b = idx(z, x, c)
        self.copy(self.rc.at[k], self.rc.at[k], 0, self.rcs.at[k], (self.r, 0)).wait_recv()
        self.copy(self.rx.at[z], self.rx.at[z], 0, self.rxs.at[z], (self.r, 0)).wait_recv()
        out[...] = self.part[b].astype(F32) + self.rc[k].astype(F32) + self.rx[z].astype(F32)
        def lo():
            self.copy(self.rz.at[z], self.rz.at[z], 0, self.rzs.at[z], (self.r, 0)).wait_recv()
            out[...] += self.rz[z].astype(F32)
        when(z > 0, lo)
        def hi():
            self.copy(self.rz.at[NZ], self.rz.at[NZ], 0, self.rzs.at[NZ], (self.r, 0)).wait_recv()
            out[...] += self.rz[NZ].astype(F32)
        when(z < NZ - 1, hi)
        for k in range(8):
            self.copy(self.part.at[0], self.part.at[0], k, self.rcs.at[0], (self.r, 0)).wait_send()
        for k in range(8, 12):
            self.copy(self.part.at[0], self.part.at[0], k, self.rcs.at[0], (self.r, 0)).wait_send()
        for zz in range(NZ):
            when(z != zz, lambda zz=zz: self.copy(self.part.at[0], self.part.at[0], 12 + zz, self.rcs.at[0], (self.r, 0)).wait_send())

class ScatterY(Scatter):
    def __init__(self, at, part, rc, ry, rx, rz, send, rcs, rys, rxs, rzs, ysem):
        Scatter.__init__(self, at, part, rc, rx, rz, send, rcs, rxs, rzs)
        self.ry, self.rys, self.ysem = ry, rys, ysem
        self.n = part.shape[1] // 2
        self.ydev = (1 - self.r, idx(self.z, self.x, self.c))
        self.mine = self.rows(self.r)
    def rows(self, h):
        return pl.ds(pl.multiple_of(h * self.n, self.n), self.n)
    def step_y(self, d):
        x, c, r = self.x, self.c, self.r
        for xx in (1 - x, x):
            for s, zz in self.over(d):
                def go(zz=zz, xx=xx):
                    k = 2 * zz + xx
                    b = idx(zz, xx, c)
                    self.copy(self.rc.at[k], self.rc.at[k], 0, self.rcs.at[k], self.ydev).wait_recv()
                    self.part[b] = (self.part[b].astype(F32) + self.rc[k].astype(F32)).astype(BF)
                    self.copy(self.part.at[b, self.rows(1 - r)], self.ry.at[k], 16 + k, self.rys.at[k], self.ydev).start()
                when(self.inside(zz), go)
    def both(self, zz, xx):
        k = 2 * zz + xx
        self.copy(self.ry.at[k], self.ry.at[k], 0, self.rys.at[k], self.ydev).wait_recv()
        return self.part[idx(zz, xx, self.c), self.mine].astype(F32) + self.ry[k].astype(F32)
    def step_x(self, d):
        z, x, c = self.z, self.x, self.c
        dev = (self.r, idx(z, 1 - x, c))
        for s, zz in self.over(d):
            def go(zz=zz):
                b = idx(zz, 1 - x, c)
                self.part[b, self.mine] = self.both(zz, 1 - x).astype(BF)
                self.copy(self.part.at[b, self.mine], self.rx.at[zz], 8 + zz, self.rxs.at[zz], dev).start()
            when(self.inside(zz), go)
    def arrived(self, ref, sem):
        self.copy(ref, ref, 0, sem, self.ydev).wait_recv()
    def step_z(self, d):
        z, x, c = self.z, self.x, self.c
        for s, zz in self.over(d):
            def go(zz=zz, s=s):
                b = idx(zz, x, c)
                v = self.both(zz, x)
                self.arrived(self.rx.at[zz], self.rxs.at[zz])
                self.part[b, self.mine] = (v + self.rx[zz].astype(F32)).astype(BF)
                def more():
                    self.arrived(self.rz.at[zz], self.rzs.at[zz])
                    self.part[b, self.mine] = (self.part[b, self.mine].astype(F32) + self.rz[zz].astype(F32)).astype(BF)
                when(self.inside(z - s), more)
                slot = jnp.where(zz == z + s, NZ, zz) if s == -1 else zz
                self.copy(self.part.at[b, self.mine], self.rz.at[slot], 12 + zz, self.rzs.at[slot], (self.r, idx(z + s, x, c))).start()
            when(self.inside(zz), go)
    def finish(self, out, low):
        z, x, r = self.z, self.x, self.r
        v = self.both(z, x)
        self.arrived(self.rx.at[z], self.rxs.at[z])
        out[self.mine] = v + self.rx[z].astype(F32)
        def lo():
            self.arrived(self.rz.at[z], self.rzs.at[z])
            out[self.mine] += self.rz[z].astype(F32)
        when(z > 0, lo)
        def hi():
            self.arrived(self.rz.at[NZ], self.rzs.at[NZ])
            out[self.mine] += self.rz[NZ].astype(F32)
        when(z < NZ - 1, hi)
        low[self.mine] = out[self.mine].astype(BF)
        a = low.at[self.mine]
        pltpu.make_async_remote_copy(a, a, self.ysem.at[0], self.ysem.at[1], device_id=self.ydev, device_id_type=MESH).start()
    def traded(self, out, low):
        a = low.at[self.rows(1 - self.r)]
        pltpu.make_async_remote_copy(a, a, self.ysem.at[0], self.ysem.at[1], device_id=self.ydev, device_id_type=MESH).wait()
        out[...] = low[...].astype(F32)
        half = self.part.at[0, self.mine]
        for k in range(8):
            self.copy(self.part.at[0], self.part.at[0], k, self.rcs.at[0], self.ydev).wait_send()
        for k in list(range(16, 24)) + list(range(8, 12)):
            self.copy(half, half, k, self.rcs.at[0], self.ydev).wait_send()
        for zz in range(NZ):
            when(self.z != zz, lambda zz=zz: self.copy(half, half, 12 + zz, self.rcs.at[0], self.ydev).wait_send())


KS = (8, 4, 9, 5, 10, 6, 11, 7, 12, 1, 13, 2, 14, 3, 15)
WINDOW = 2

def has(j):
    return lax.rem(j, 3) == 0

def spare_at(j):
    return pl.ds(pl.multiple_of(16 * MAIN + 128 * (j // 3), 128), 128)

class Deal:
    def __init__(self, at, ws, buf, sems, local):
        self.r, self.z, self.x, self.c = at
        self.me = idx(self.z, self.x, self.c)
        self.ws, self.buf, self.sems, self.local = ws, buf, sems, local
        self.n = ws[0].shape[0] // 2
    def rows(self, j, h):
        return pl.ds(pl.multiple_of((2 * j + h) * self.n, self.n), self.n)
    def block(self, j, h, spare):
        return self.buf.at[self.rows(j, h), pl.ds(3 * MAIN, 384) if spare else pl.ds(0, 3 * MAIN)]
    def copy(self, a, b, kind, k, dev):
        send, recv = self.sems[2 * kind : 2 * kind + 2]
        return pltpu.make_async_remote_copy(a, b, send.at[k], recv.at[k], device_id=dev, device_id_type=MESH)
    def launch(self, k):
        r, me, n = self.r, self.me, self.n
        row = pl.ds(pl.multiple_of(r * n, n), n)
        j = jnp.bitwise_xor(me, k)
        dst = self.rows(me, r)
        for i in range(3):
            self.copy(self.ws[i].at[row, pl.ds(pl.multiple_of(j * MAIN, MAIN), MAIN)], self.buf.at[dst, pl.ds(i * MAIN, MAIN)], 0, k, (r, j)).start()
        def spare():
            for i in range(3):
                self.copy(self.ws[i].at[row, spare_at(j)], self.buf.at[dst, pl.ds(3 * MAIN + 128 * i, 128)], 1, k, (r, j)).start()
        when(has(j), spare)
    def locals(self, spare):
        me, n = self.me, self.n
        row = pl.ds(pl.multiple_of(2 * me * n, 2 * n), 2 * n)
        col = spare_at(me) if spare else pl.ds(pl.multiple_of(me * MAIN, MAIN), MAIN)
        for i in range(3):
            to = pl.ds(3 * MAIN + 128 * i, 128) if spare else pl.ds(i * MAIN, MAIN)
            yield pltpu.make_async_copy(self.ws[i].at[:, col], self.buf.at[row, to], self.local.at[1 if spare else 0])
    def begin(self):
        for k in KS[:WINDOW]:
            self.launch(k)
        for l in self.locals(False):
            l.start()
        def spare():
            for l in self.locals(True):
                l.start()
        when(has(self.me), spare)
    def step(self, i):
        k = KS[i]
        r, me = self.r, self.me
        j = jnp.bitwise_xor(me, k)
        dev = (1 - r, me)
        def pass_on(spare):
            blk = self.block(j, r, spare)
            self.copy(blk, blk, spare, k, dev).wait_recv()
            self.copy(blk, blk, 2 + spare, k, dev).start()
        pass_on(0)
        when(has(me), lambda: pass_on(1))
        if i + WINDOW < 15:
            self.launch(KS[i + WINDOW])
    def end(self):
        r, me, n = self.r, self.me, self.n
        dev = (1 - r, me)
        for k in KS:
            j = jnp.bitwise_xor(me, k)
            def done(spare):
                blk = self.block(j, 1 - r, spare)
                self.copy(blk, blk, 2 + spare, k, dev).wait()
            def sent(spare):
                blk = self.block(j, r, spare)
                self.copy(blk, blk, spare, k, dev).wait_send()
            done(0)
            sent(0)
            when(has(me), lambda: done(1))
            when(has(j), lambda: sent(1))
        row = pl.ds(pl.multiple_of(2 * me * n, 2 * n), 2 * n)
        def own(spare):
            blk = self.buf.at[row, pl.ds(3 * MAIN, 384) if spare else pl.ds(0, 3 * MAIN)]
            pltpu.make_async_copy(blk, blk, self.local.at[spare]).wait()
        own(0)
        when(has(me), lambda: own(1))

def hail_all(r, z, x, c):
    bar = pltpu.get_barrier_semaphore()
    me = idx(z, x, c)
    for k in range(1, 16):
        pl.semaphore_signal(bar, inc=1, device_id=(r, lax.rem(me + k, 16)), device_id_type=MESH)
    pl.semaphore_signal(bar, inc=1, device_id=(1 - r, me), device_id_type=MESH)
    pl.semaphore_wait(bar, 16)


def dot(a, b):
    return lax.dot_general(a, b, (((1,), (0,)), ((), ())), preferred_element_type=F32)
def dot_nt(a, b):
    return lax.dot_general(a, b, (((1,), (1,)), ((), ())), preferred_element_type=F32)
def dot_tn(a, b):
    return lax.dot_general(a, b, (((0,), (0,)), ((), ())), preferred_element_type=F32)

def gated(g, u, gh):
    sig = jax.nn.sigmoid(g)
    silu = g * sig
    return (gh * u * (sig * (1.0 + g * (1.0 - sig)))).astype(BF), (gh * silu).astype(BF), (silu * u).astype(BF)

def mlp_kernel(n2_ref, cot_ref, w_ref, gsum, osum, half_ref,
               n2, cot, w, act, pg, po, rcg, rxg, rzg, rco, rxo, rzo, yb,
               gsend, grecv, glocal, lsem, ssend, srcs, srxs, srzs, ysend, yrecv, xsend, xrecv):
    at = place()
    r, z, x, c = at
    me = idx(z, x, c)
    extra = has(me)
    MM, SP = pl.ds(0, 3 * MAIN), pl.ds(3 * MAIN, 384)
    loads = [pltpu.make_async_copy(w_ref.at[:, MM], w.at[:, MM], lsem.at[0]), pltpu.make_async_copy(cot_ref, cot, lsem.at[1])]
    for l in loads: l.start()
    load_spare = pltpu.make_async_copy(w_ref.at[:, SP], w.at[:, SP], lsem.at[3])
    when(extra, load_spare.start)
    greet(*at, with_y=True)
    g = Gather(at, n2_ref, n2, gsend, grecv, glocal)
    rg = Scatter(at, pg, rcg, rxg, rzg, ssend.at[0], srcs.at[0], srxs.at[0], srzs.at[0])
    ro = Scatter(at, po, rco, rxo, rzo, ssend.at[1], srcs.at[1], srxs.at[1], srzs.at[1])
    g.begin()
    for l in loads: l.wait()
    when(extra, load_spare.wait)
    mid = (z > 0) & (z < NZ - 1)
    p = [z,
         jnp.where(z == 0, 1, jnp.where(z == 1, 0, jnp.where(z == 2, 3, 2))),
         jnp.where(z == 0, 2, jnp.where(z == 1, 2, 1)),
         jnp.where(z < 2, 3, 0)]

    def tiles(zz):
        rows = pl.ds(pl.multiple_of(4 * zz, 4), 4)
        tok = pl.ds(pl.multiple_of(512 * zz, 512), 512)
        @pl.loop(0, 2)
        def _(t):
            a = n2[rows].reshape(512, D)
            k = cot[rows].reshape(512, D)
            def col(base):
                return pl.ds(pl.multiple_of(base + 256 * t, 256), 256)
            dg, du, h = gated(dot(a, w[:, col(0)]), dot(a, w[:, col(MAIN)]), dot(k, w[:, col(2 * MAIN)]))
            act[tok, col(0)] = dg
            act[tok, col(MAIN)] = du
            act[tok, col(2 * MAIN)] = h
        def spare():
            pre = dot(n2[rows].reshape(512, D), w[:, 3 * MAIN : 3 * MAIN + 256])
            dg, du, h = gated(pre[:, :128], pre[:, 128:], dot(cot[rows].reshape(512, D), w[:, 3 * MAIN + 256 :]))
            act[tok, 3 * MAIN : 3 * MAIN + 128] = dg
            act[tok, 3 * MAIN + 128 : 3 * MAIN + 256] = du
            act[tok, 3 * MAIN + 256 :] = h
        when(extra, spare)
        def out_tiles(more):
            @pl.loop(0, D // 256)
            def _(t):
                dr = pl.ds(pl.multiple_of(256 * t, 256), 256)
                v = dot_nt(act[tok, : 2 * MAIN], w[dr, : 2 * MAIN])
                u = dot_nt(act[tok, 2 * MAIN : 3 * MAIN], w[dr, 2 * MAIN : 3 * MAIN])
                if more:
                    v += dot_nt(act[tok, 3 * MAIN : 3 * MAIN + 256], w[dr, 3 * MAIN : 3 * MAIN + 256])
                    u += dot_nt(act[tok, 3 * MAIN + 256 :], w[dr, 3 * MAIN + 256 :])
                pg[rows, :, dr] = v.astype(BF).reshape(4, 128, 256)
                po[rows, :, dr] = u.astype(BF).reshape(4, 128, 256)
        when(extra, lambda: out_tiles(True))
        when(~extra, lambda: out_tiles(False))
        rg.send_c(zz)
        ro.send_c(zz)

    g.from_z(p[1])
    when(mid, lambda: g.from_z(p[2]))
    g.from_x(p[0])
    g.from_c(p[0])
    pltpu.make_async_copy(n2_ref, n2.at[0], glocal).wait()
    tiles(p[0])
    g.from_z(jnp.where(mid, p[3], p[2]))
    g.from_x(p[1])
    g.from_c(p[1])
    tiles(p[1])
    when(~mid, lambda: g.from_z(p[3]))
    g.from_x(p[2])
    g.from_c(p[2])
    tiles(p[2])
    rg.x_plane(p[2])
    g.from_x(p[3])
    g.from_c(p[3])
    tiles(p[3])

    ydev = (1 - r, idx(z, x, c))
    own = D // 16
    half = own // 2
    def ycopy(j, spare):
        cols = SP if spare else MM
        src = w.at[pl.ds(pl.multiple_of(own * j + half * (1 - r), half), half), cols]
        a, b = (xsend, xrecv) if spare else (ysend, yrecv)
        return pltpu.make_async_remote_copy(src, yb.at[j, :, cols], a.at[j], b.at[j], device_id=ydev, device_id_type=MESH)
    def grads(q):
        dr = slice(384 * q, 384 * (q + 1))
        row = slice(384 * q, 384 * (q + 1))
        @pl.loop(0, 4)
        def _(t):
            col = pl.ds(pl.multiple_of(256 * t, 256), 256)
            w[row, col] = dot_tn(n2[:, :, dr].reshape(2048, 384), act[:, col]).astype(BF)
        @pl.loop(0, 2)
        def _(t):
            col = pl.ds(pl.multiple_of(2 * MAIN + 256 * t, 256), 256)
            w[row, col] = dot_tn(cot[:, :, dr].reshape(2048, 384), act[:, col]).astype(BF)
        for j in range(4 * q, 4 * q + 4):
            ycopy(j, 0).start()
        def spare():
            w[row, 3 * MAIN : 3 * MAIN + 256] = dot_tn(n2[:, :, dr].reshape(2048, 384), act[:, 3 * MAIN : 3 * MAIN + 256]).astype(BF)
            w[row, 3 * MAIN + 256 :] = dot_tn(cot[:, :, dr].reshape(2048, 384), act[:, 3 * MAIN + 256 :]).astype(BF)
            for j in range(4 * q, 4 * q + 4):
                ycopy(j, 1).start()
        when(extra, spare)
    def yadd(j):
        def add(spare):
            cols = SP if spare else MM
            ycopy(j, spare).wait()
            mine = w[pl.ds(pl.multiple_of(own * j + half * r, half), half), cols]
            yb[j, :, cols] = (mine.astype(F32) + yb[j, :, cols].astype(F32)).astype(BF)
            pltpu.make_async_copy(yb.at[j, :, cols], half_ref.at[j, :, cols], lsem.at[4 if spare else 2]).start()
        add(0)
        when(extra, lambda: add(1))

    rg.x_plane(p[3])
    rg.x_plane(p[1])
    grads(0)
    rg.step_z(3)
    rg.step_z(2)
    rg.x_plane(p[0])
    ro.x_plane(p[3])
    grads(1)
    rg.step_z(1)
    ro.x_plane(p[2])
    grads(2)
    ro.x_plane(p[1])
    ro.step_z(3)
    rg.finish(gsum)
    grads(3)
    ro.x_plane(p[0])
    ro.step_z(2)
    for j in range(0, 8): yadd(j)
    ro.step_z(1)
    for j in range(8, 12): yadd(j)
    ro.finish(osum)
    for j in range(12, 16): yadd(j)
    pltpu.make_async_copy(yb.at[:, :, MM], half_ref.at[:, :, MM], lsem.at[2]).wait()
    when(extra, lambda: pltpu.make_async_copy(yb.at[:, :, SP], half_ref.at[:, :, SP], lsem.at[4]).wait())
    g.end(local=False)

def mlp(n2, cot, w, cid):
    blk = n2.shape
    dma = pltpu.SemaphoreType.DMA
    full = (16,) + blk
    return pl.pallas_call(
        mlp_kernel,
        out_shape=[jax.ShapeDtypeStruct(blk, F32)] * 2 + [jax.ShapeDtypeStruct((16, D // 32, COLS), BF)],
        in_specs=[pl.BlockSpec(memory_space=pl.ANY)] * 3,
        out_specs=[pl.BlockSpec(memory_space=pltpu.VMEM)] * 2 + [pl.BlockSpec(memory_space=pl.ANY)],
        scratch_shapes=[pltpu.VMEM(full, BF), pltpu.VMEM(full, BF), pltpu.VMEM((D, COLS), BF), pltpu.VMEM((16 * blk[0], COLS), BF),
                        pltpu.VMEM(full, BF), pltpu.VMEM(full, BF)]
        + [pltpu.VMEM((k,) + blk, BF) for k in (8, 4, 5, 8, 4, 5)]
        + [pltpu.VMEM((16, D // 32, COLS), BF)]
        + [dma((18,)), dma((16,)), dma(()), dma((5,)), dma((2, 16)), dma((2, 8)), dma((2, 4)), dma((2, 5))] + [dma((16,))] * 4,
        compiler_params=pltpu.CompilerParams(collective_id=cid, has_side_effects=True, vmem_limit_bytes=60 * 2**20),
    )(n2, cot, w)


def spin(u, cos, sin):
    return u * cos + pltpu.roll(u, HEAD_DIM // 2, 1) * sin

def stack_heads(v):
    n = v.shape[1] // HEAD_DIM
    return jnp.concatenate([v[:, HEAD_DIM * i : HEAD_DIM * (i + 1)] for i in range(n)], axis=0)

def spread_heads(v, rows):
    n = v.shape[0] // rows
    return jnp.concatenate([v[rows * i : rows * (i + 1)] for i in range(n)], axis=1)

def exp_scores(q, k, first_row, block, length):
    sc = dot_nt(q, k) * (HEAD_DIM ** -0.5)
    key = lax.broadcasted_iota(jnp.int32, sc.shape, 1)
    row = jnp.bitwise_and(lax.broadcasted_iota(jnp.int32, sc.shape, 0), block - 1) + first_row
    return jnp.where((key <= row) & (key < length), jnp.exp(sc), 0.0)

def rms(v, gain):
    factor = lax.rsqrt(jnp.mean(v * v, axis=-1, keepdims=True) + EPSILON)
    return v * factor * gain


class GatherY(Gather):
    def __init__(self, at, src, out, send, recv, local):
        Gather.__init__(self, at, src, out, send, recv, local)
        self.n = src.shape[0] // 2
        self.ydev = (1 - self.r, idx(self.z, self.x, self.c))
    def rows(self, h):
        return pl.ds(pl.multiple_of(h * self.n, self.n), self.n)
    def half(self, b, h):
        return self.out.at[b, self.rows(h)]
    def move(self, src, dst, k, q, dev):
        return pltpu.make_async_remote_copy(src, dst, self.send.at[k], self.recv.at[q], device_id=dev, device_id_type=MESH)
    def arrived(self, b, h):
        self.move(self.half(b, h), self.half(b, h), 0, 2 * b + h, self.ydev).wait_recv()
    def begin(self):
        z, x, c, r = self.z, self.x, self.c, self.r
        me = idx(z, x, c)
        mine, dst = self.src.at[self.rows(r)], self.half(me, r)
        for s in (1, -1):
            when(self.inside(z + s), lambda s=s: self.move(mine, dst, 0 if s == 1 else 3, 2 * me + r, self.zdev(s)).start())
        self.move(mine, dst, 6 + z, 2 * me + r, self.xdev()).start()
        self.move(self.src, self.out.at[me], 18 + 2 * z + x, 2 * me, self.cdev()).start()
        pltpu.make_async_copy(self.src, self.out.at[me], self.local).start()
    def from_z(self, zz):
        z, x, c, r = self.z, self.x, self.c, self.r
        b = idx(zz, x, c)
        q = 2 * b + r
        self.arrived(b, r)
        s = jnp.where(zz < z, 1, -1)
        slot = jnp.where(zz < z, 0, 3) + jnp.abs(zz - z)
        a = self.half(b, r)
        when(self.inside(z + s), lambda: self.move(a, a, slot, q, (r, idx(z + s, x, c))).start())
        self.move(a, a, 6 + zz, q, self.xdev()).start()
        self.move(a, a, 18 + 2 * zz + x, q, self.cdev()).start()
        self.move(a, a, 10 + 2 * zz + x, q, self.ydev).start()
    def from_x(self, zz):
        x, c, r = self.x, self.c, self.r
        b = idx(zz, 1 - x, c)
        q = 2 * b + r
        self.arrived(b, r)
        a = self.half(b, r)
        self.move(a, a, 18 + 2 * zz + 1 - x, q, self.cdev()).start()
        self.move(a, a, 10 + 2 * zz + 1 - x, q, self.ydev).start()
    def from_y(self, zz):
        x, c, r = self.x, self.c, self.r
        def take(xx):
            b = idx(zz, xx, c)
            self.arrived(b, 1 - r)
            a = self.half(b, 1 - r)
            self.move(a, a, 26 + 2 * zz + xx, 2 * b + 1 - r, self.cdev()).start()
        when(zz != self.z, lambda: take(x))
        take(1 - x)
    def from_c(self, zz):
        x, c, r = self.x, self.c, self.r
        b = idx(zz, x, 1 - c)
        whole = self.out.at[b]
        when(zz == self.z, lambda: self.move(whole, whole, 0, 2 * b, self.ydev).wait_recv())
        def both(b):
            self.arrived(b, r)
            self.arrived(b, 1 - r)
        when(zz != self.z, lambda: both(b))
        both(idx(zz, 1 - x, 1 - c))
    def end(self):
        z, x = self.z, self.x
        own = 2 * z + x
        a = self.half(0, 0)
        def sent(k, a=a):
            self.move(a, a, k, 0, self.ydev).wait_send()
        for d in range(NZ - 1):
            when((z - d >= 0) & (z < NZ - 1), lambda d=d: sent(d))
            when((z + d < NZ) & (z > 0), lambda d=d: sent(3 + d))
        for k in range(6, 10):
            sent(k)
        for k in range(8):
            def other(k=k):
                sent(10 + k)
                sent(18 + k)
                sent(26 + k)
            when(own != k, other)
        sent(18 + own, self.out.at[0])
        pltpu.make_async_copy(self.src, self.out.at[0], self.local).wait()

def front_kernel(block, lens, x_ref, cot_ref, v0, v1, v2, v3, v4, sel, fold, selk, foldk, rope_ref, wq, wk, wv, wg, wu, wd, wo_ref,
                 q_out, normed_out, att_out, mid_out, n2_out, vec, buf, qkv_out, kv_out, cot_out, wo_out,
                 rope, cot_own, small, qkv_own, wqkv, small_all, own, kv, wo,
                 qs, qr, ql, vs, vr, vl, ks, kr, kl, cs, cr, cl, ws, wr, wl, d0, d1, d2, d3, d4, d5, d6, d7, dl, lsem):
    at = place()
    width = HEADS * HEAD_DIM
    kw = KV_HEADS * HEAD_DIM
    loads = [pltpu.make_async_copy(w, qkv_own.at[:, pl.ds(o, n)], lsem.at[i]) for i, (w, o, n) in enumerate(((wq, 0, width), (wk, width, kw), (wv, width + kw, kw)))]
    first_row = lax.axis_index("group") * block
    loads.append(pltpu.make_async_copy(rope_ref.at[:, pl.ds(pl.multiple_of(first_row, block), block)], rope, lsem.at[6]))
    for l in loads: l.start()
    small[...] = jnp.zeros_like(small)
    for i, v in enumerate((v0, v1, v2, v3, v4)):
        small[i : i + 1, : v.shape[1]] = v[...].astype(F32)
    cot_own[...] = (cot_ref[...].astype(F32) * row_mask(lens, first_row, block, (cot_ref.shape[0], 1))).astype(BF)
    hail_all(*at)
    for l in loads: l.wait()
    gq = GatherY(at, qkv_own, wqkv, qs, qr, ql)
    gv = Gather(at, small, small_all, vs, vr, vl)
    gk = Gather(at, own, kv, ks, kr, kl)
    gc = Gather(at, cot_own, cot_out, cs, cr, cl)
    gw = GatherY(at, wo_ref, wo, ws, wr, wl)
    d = Deal(at, (wg, wu, wd), buf, (d0, d1, d2, d3, d4, d5, d6, d7), dl)
    steps = iter(range(15))
    def some(n):
        for _ in range(n):
            i = next(steps, None)
            if i is not None:
                d.step(i)
    gq.begin()
    gv.begin()
    d.begin()
    x = x_ref[...].astype(F32)
    gq.first()
    gv.first()
    some(1)
    gq.second()
    gv.second()
    gq.from_y(gq.p[0])
    some(EARLY[0])
    gq.third()
    gv.third()
    gq.from_y(gq.p[1])
    some(1)
    gq.fourth()
    gv.fourth()
    gc.begin()
    gq.from_y(gq.p[2])
    gq.from_y(gq.p[3])
    for zz in range(NZ):
        gv.from_c(zz)
        gq.from_c(zz)
    gv.end()
    gq.end()
    keep = [pltpu.make_async_copy(wqkv, qkv_out, lsem.at[3]), pltpu.make_async_copy(kv, kv_out, lsem.at[4]), pltpu.make_async_copy(wo, wo_out, lsem.at[5])]
    keep[0].start()
    vec[...] = jnp.zeros_like(vec)
    for i, row, first, a, b in ((0, 0, 0, sel, fold), (1, 1, 0, sel, fold), (2, 1, width, selk, foldk), (3, 1, width + kw, selk, foldk), (4, 2, 0, sel, fold)):
        t = dot_nt(small_all[:, i, :].astype(BF), b[...])
        vec[row : row + 1, first : first + a.shape[1]] = jnp.sum(t * a[...], axis=0, keepdims=True)
    normed_out[...] = rms(x, vec[0:1, :width]).astype(BF)
    cos, sin = [jnp.concatenate((rope[i], rope[i]), axis=0) for i in range(2)]
    def product(base):
        return dot(normed_out[...], wqkv[:, :, pl.ds(pl.multiple_of(base, 256), 256)].reshape(width, 256)) + vec[1:2, pl.ds(pl.multiple_of(base, 256), 256)]
    pre = product(width)
    own[:, :HEAD_DIM] = spin(pre[:, :HEAD_DIM], cos, sin).astype(BF)
    own[:, HEAD_DIM : 2 * HEAD_DIM] = spin(pre[:, HEAD_DIM:], cos, sin).astype(BF)
    own[:, kw:] = product(width + kw).astype(BF)
    gk.begin()
    gw.begin()
    @pl.loop(0, width // 256)
    def _(t):
        pre = product(t * 256)
        for i in range(2):
            col = pl.ds(pl.multiple_of(256 * t + HEAD_DIM * i, HEAD_DIM), HEAD_DIM)
            q_out[:, col] = spin(pre[:, HEAD_DIM * i : HEAD_DIM * (i + 1)], cos, sin).astype(BF)
    some(EARLY[1])
    gc.first()
    gk.first()
    some(1)
    gw.first()
    some(EARLY[2])
    gk.second()
    gc.second()
    gw.second()
    some(1)
    gw.from_y(gw.p[0])
    gk.third()
    some(EARLY[3])
    gk.fourth()
    gc.third()
    gw.third()
    some(1)
    gw.from_y(gw.p[1])
    for zz in range(NZ):
        gk.from_c(zz)
    gk.end()
    keep[1].start()
    span = 16 * block
    @pl.loop(0, 4)
    def _(u):
        s, h = u // 2, lax.rem(u, 2)
        rows = pl.ds(pl.multiple_of(block * s, block), block)
        cols = pl.ds(pl.multiple_of(width // 2 * h, width // 2), width // 2)
        q = stack_heads(q_out[rows, cols])
        k = kv[:, rows, pl.ds(pl.multiple_of(HEAD_DIM * h, HEAD_DIM), HEAD_DIM)].reshape(span, HEAD_DIM)
        v = kv[:, rows, pl.ds(pl.multiple_of(kw + HEAD_DIM * h, HEAD_DIM), HEAD_DIM)].reshape(span, HEAD_DIM)
        e = exp_scores(q, k, first_row, block, lens[s])
        total = jnp.sum(e, axis=-1, keepdims=True)
        att_out[rows, cols] = spread_heads(dot(e.astype(BF), v) / total, block)
    some(EARLY[4])
    gw.fourth()
    some(1)
    gc.fourth()
    some(1)
    gw.from_y(gw.p[2])
    gw.from_y(gw.p[3])
    for zz in range(NZ):
        gw.from_c(zz)
    gw.end()
    keep[2].start()
    @pl.loop(0, width // 256)
    def _(t):
        col = pl.ds(pl.multiple_of(256 * t, 256), 256)
        mid_out[:, col] = x_ref[:, col].astype(F32) + dot(att_out[...].astype(BF), wo[:, :, col].reshape(width, 256))
    n2_out[...] = rms(mid_out[...], vec[2:3, :width]).astype(BF)
    some(15)
    for zz in range(NZ):
        gc.from_c(zz)
    gc.end()
    for k in keep:
        k.wait()
    d.end()

EARLY = (1, 1, 1, 1, 2)

def front(lens, x, cot, vectors, sel, fold, selk, foldk, rope, wq, wk, wv, wg, wu, wd, wo, block, cid):
    rows, width = x.shape
    any_ = pl.BlockSpec(memory_space=pl.ANY)
    vm = pl.BlockSpec(memory_space=pltpu.VMEM)
    dma = pltpu.SemaphoreType.DMA
    act = (rows, width)
    own = wq.shape[0]
    kvw = 2 * KV_HEADS * HEAD_DIM
    wide = width + kvw
    sds = jax.ShapeDtypeStruct
    VM = pltpu.VMEM
    return pl.pallas_call(
        functools.partial(front_kernel, block),
        out_shape=[sds(act, BF), sds(act, BF), sds(act, F32), sds(act, F32), sds(act, BF), sds((8, wide), F32),
                   sds((16 * own, 3 * MAIN + 384), BF), sds((16, own, wide), BF), sds((16, rows, kvw), BF), sds((16,) + act, BF), sds((16,) + wo.shape, BF)],
        in_specs=[pl.BlockSpec(memory_space=pltpu.SMEM)] + [vm] * 11 + [any_] * 8,
        out_specs=[vm] * 6 + [any_] * 5,
        scratch_shapes=[VM((2, block, HEAD_DIM), F32), VM(act, BF), VM((8, 128), F32), VM((own, wide), BF), VM((16, own, wide), BF), VM((16, 8, 128), F32), VM((rows, kvw), BF), VM((16, rows, kvw), BF), VM((16,) + wo.shape, BF)]
        + [dma((34,)), dma((32,)), dma(())] + [dma((18,)), dma((16,)), dma(())] * 3 + [dma((34,)), dma((32,)), dma(())]
        + [dma((16,))] * 8 + [dma((2,)), dma((7,))],
        compiler_params=pltpu.CompilerParams(collective_id=cid, has_side_effects=True, vmem_limit_bytes=60 * 2**20),
    )(lens, x, cot, *vectors, sel, fold, selk, foldk, rope, wq, wk, wv, wg, wu, wd, wo)


class Return:
    def __init__(self, at, half_ref, out, sems, local):
        self.r, self.z, self.x, self.c = at
        self.me = idx(self.z, self.x, self.c)
        self.src, self.out, self.sems, self.local = half_ref, out, sems, local
        self.n = half_ref.shape[1]
    def places(self, j, spare):
        row = pl.ds(pl.multiple_of(self.r * self.n, self.n), self.n)
        col = spare_at(j) if spare else pl.ds(pl.multiple_of(j * MAIN, MAIN), MAIN)
        return [o.at[row, col] for o in self.out]
    def parts(self, j, spare):
        if spare:
            return [self.src.at[j, :, pl.ds(3 * MAIN + 128 * i, 128)] for i in range(3)]
        return [self.src.at[j, :, pl.ds(i * MAIN, MAIN)] for i in range(3)]
    def copy(self, a, b, kind, k, dev):
        send, recv = self.sems[2 * kind : 2 * kind + 2]
        return pltpu.make_async_remote_copy(a, b, send.at[k], recv.at[k], device_id=dev, device_id_type=MESH)
    def launch(self, k):
        j = jnp.bitwise_xor(self.me, k)
        def go(spare):
            for a, b in zip(self.parts(j, spare), self.places(self.me, spare)):
                self.copy(a, b, spare, k, (self.r, j)).start()
        go(0)
        when(has(self.me), lambda: go(1))
    def forward(self, j, k, spare):
        for a in self.places(j, spare):
            self.copy(a, a, 2 + spare, k, (1 - self.r, self.me)).start()
    def begin(self, window):
        self.window = window
        def go(spare):
            for a, b in zip(self.parts(self.me, spare), self.places(self.me, spare)):
                pltpu.make_async_copy(a, b, self.local.at[spare]).start()
        go(0)
        when(has(self.me), lambda: go(1))
        for k in KS[:window]:
            self.launch(k)
    def sized(self, spare):
        return self.src.at[0, :, pl.ds(3 * MAIN, 384) if spare else pl.ds(0, 3 * MAIN)]
    def whole(self, kind, k):
        blk = self.sized(kind % 2)
        return self.copy(blk, blk, kind, k, (1 - self.r, self.me))
    def own(self):
        def go(spare):
            blk = self.sized(spare)
            pltpu.make_async_copy(blk, blk, self.local.at[spare]).wait()
            self.forward(self.me, 0, spare)
        go(0)
        when(has(self.me), lambda: go(1))
    def step(self, i):
        k = KS[i]
        j = jnp.bitwise_xor(self.me, k)
        def go(spare):
            self.whole(spare, k).wait_recv()
            self.forward(j, k, spare)
        go(0)
        when(has(j), lambda: go(1))
        if i + self.window < 15:
            self.launch(KS[i + self.window])
    def end(self):
        for k in (0,) + KS:
            j = jnp.bitwise_xor(self.me, k)
            self.whole(2, k).wait()
            when(has(j), lambda: self.whole(3, k).wait())
            if k:
                self.whole(0, k).wait_send()
                when(has(self.me), lambda: self.whole(1, k).wait_send())

def row_mask(lens, first_row, block, shape):
    row = lax.broadcasted_iota(jnp.int32, shape, 0)
    place = jnp.bitwise_and(row, block - 1) + first_row
    return jnp.where(place < jnp.where(row < block, lens[0], lens[1]), 1.0, 0.0)

def norm_gradient(v, gain, upstream):
    factor = lax.rsqrt(jnp.mean(v * v, axis=-1, keepdims=True) + EPSILON)
    weighted = upstream * gain
    inner = jnp.mean(weighted * v, axis=-1, keepdims=True)
    return factor * weighted - v * (factor * factor * factor) * inner, jnp.sum(upstream * v * factor, axis=0, keepdims=True)

def backward_kernel(block, window, lens, gn2, mlp_out, mid, cot, x_ref, att, q_ref, normed, vec, sel, fold, selk, foldk, rope_ref, kv_ref, wo_ref, wqkv_ref, half_ref,
                    layer_out, grad_input, q_out, k_out, v_out, wo_out, vec_out, g0, g1, g2,
                    rope, kv, wo, wqkv, gmid, branch, gatt, gqkv, pv,
                    p_kv, c_kv, x_kv, z_kv, p_wo, c_wo, x_wo, z_wo, p_qk, c_qk, w_qk, x_qk, z_qk, p_pw, c_pw, x_pw, z_pw, p_ve, c_ve, x_ve, z_ve,
                    kvsum, pair_out, low_q, y2, y3, y4, y5, y6, y7,
                    ss, sc, sx, sz, r0, r1, r2, r3, r4, r5, r6, r7, rl, ysem, fs, fc, fy, fx, fz, ft, lsem):
    at = place()
    r, z, x, c = at
    width = HEADS * HEAD_DIM
    kw = KV_HEADS * HEAD_DIM
    loads = [pltpu.make_async_copy(a, b, lsem.at[i]) for i, (a, b) in enumerate(((wo_ref, wo), (kv_ref, kv), (wqkv_ref, wqkv)))]
    first_row = lax.axis_index("group") * block
    loads.append(pltpu.make_async_copy(rope_ref.at[:, pl.ds(pl.multiple_of(first_row, block), block)], rope, lsem.at[3]))
    for l in loads: l.start()
    hail_all(*at)
    back = Return(at, half_ref, (g0, g1, g2), (r0, r1, r2, r3, r4, r5, r6, r7), rl)
    back.begin(window)
    sets = ((p_kv, c_kv, x_kv, z_kv), (p_wo, c_wo, x_wo, z_wo), (p_pw, c_pw, x_pw, z_pw), (p_ve, c_ve, x_ve, z_ve))
    ek, eo, ep, ev = [Scatter(at, *b, ss.at[i], sc.at[i], sx.at[i], sz.at[i]) for i, b in enumerate(sets)]
    eq = ScatterY(at, p_qk, c_qk, w_qk, x_qk, z_qk, fs, fc, fy, fx, fz, ft)
    steps = iter(range(15))
    def some(n):
        for _ in range(n):
            i = next(steps, None)
            if i is not None:
                back.step(i)
    ydev = (1 - r, idx(z, x, c))
    def trade(i, out, a, b):
        a[...] = out[...].astype(BF)
        pltpu.make_async_remote_copy(a, b, ysem.at[2 * i], ysem.at[2 * i + 1], device_id=ydev, device_id_type=MESH).start()
    def traded(i, out, a, b):
        pltpu.make_async_remote_copy(a, b, ysem.at[2 * i], ysem.at[2 * i + 1], device_id=ydev, device_id_type=MESH).wait()
        out[...] = a[...].astype(F32) + b[...].astype(F32)

    grad_norm, gain_two = norm_gradient(mid[...], vec[2:3, :width], gn2[...])
    valid = row_mask(lens, first_row, block, (cot.shape[0], 1))
    gmid[...] = cot[...].astype(F32) * valid + grad_norm
    branch[...] = gmid[...].astype(BF)
    loads[0].wait()
    @pl.loop(0, 4)
    def _(t):
        blocks = pl.ds(pl.multiple_of(4 * t, 4), 4)
        col = pl.ds(pl.multiple_of(384 * t, 384), 384)
        low = att[:, col].astype(BF)
        p_wo[blocks] = dot_tn(low, branch[...]).astype(BF).reshape(4, 96, width)
        gatt[:, col] = dot_nt(branch[...], wo[blocks].reshape(384, width))
    eo.begin()
    eo.step_x(3)
    eo.step_x(2)
    back.own()
    layer_out[...] = ((mid[...] + mlp_out[...]) * valid).astype(BF)
    loads[1].wait()
    loads[3].wait()
    span = 16 * block
    def unit(u):
        s, h = u // 2, lax.rem(u, 2)
        rows = pl.ds(pl.multiple_of(block * s, block), block)
        cols = pl.ds(pl.multiple_of(width // 2 * h, width // 2), width // 2)
        kcol = pl.ds(pl.multiple_of(HEAD_DIM * h, HEAD_DIM), HEAD_DIM)
        vcol = pl.ds(pl.multiple_of(kw + HEAD_DIM * h, HEAD_DIM), HEAD_DIM)
        q = stack_heads(q_ref[rows, cols])
        k = kv[:, rows, kcol].reshape(span, HEAD_DIM)
        v = kv[:, rows, vcol].reshape(span, HEAD_DIM)
        e = exp_scores(q, k, first_row, block, lens[s])
        total = jnp.sum(e, axis=-1, keepdims=True)
        ga = stack_heads(gatt[rows, cols])
        gt = -jnp.sum(ga * stack_heads(att[rows, cols]), axis=-1, keepdims=True) / total
        gn = (ga / total).astype(BF)
        gs = (e * (dot_nt(gn, v) + gt)).astype(BF)
        p_kv[:, rows, kcol] = dot_tn(gs, q).astype(BF).reshape(16, block, HEAD_DIM)
        p_kv[:, rows, vcol] = dot_tn(e.astype(BF), gn).astype(BF).reshape(16, block, HEAD_DIM)
        gq = dot(gs, k) * (HEAD_DIM ** -0.5)
        cos, sin = rope[0], rope[1]
        gqkv[rows, cols] = jnp.concatenate([spin(gq[block * i : block * (i + 1)], cos, -sin) for i in range(HEADS // KV_HEADS)], axis=1).astype(BF)
    unit(0)
    some(1)
    eo.step_z(3)
    eo.step_x(1)
    unit(1)
    some(1)
    eo.step_z(2)
    eo.step_x(0)
    unit(2)
    some(1)
    eo.step_z(1)
    unit(3)
    ek.begin()
    ek.step_x(3)
    ek.step_x(2)
    some(1)
    loads[2].wait()
    @pl.loop(0, 4)
    def _(t):
        blocks = pl.ds(pl.multiple_of(4 * t, 4), 4)
        col = pl.ds(pl.multiple_of(384 * t, 384), 384)
        p_qk[blocks] = dot_tn(normed[:, col], gqkv[:, :width]).astype(BF).reshape(4, 96, width)
    ek.step_z(3)
    ek.step_x(1)
    eq.begin()
    eo.finish(wo_out)
    trade(2, wo_out, y2, y3)
    for d in (3, 2, 1, 0):
        eq.step_y(d)
    ek.step_z(2)
    ek.step_x(0)
    some(1)
    @pl.loop(0, 4)
    def _(t):
        blocks = pl.ds(pl.multiple_of(4 * t, 4), 4)
        col = pl.ds(pl.multiple_of(384 * t, 384), 384)
        gatt[:, col] = dot_nt(gqkv[:, :width], wqkv[blocks, :, :width].reshape(384, width))
    ek.step_z(1)
    eq.step_x(3)
    eq.step_x(2)
    some(1)
    ek.finish(kvsum)
    cos, sin = [jnp.concatenate((rope[i], rope[i]), axis=0) for i in range(2)]
    for h in range(KV_HEADS):
        kcol = slice(HEAD_DIM * h, HEAD_DIM * (h + 1))
        gqkv[:, width + HEAD_DIM * h : width + HEAD_DIM * (h + 1)] = spin(kvsum[:, kcol] * (HEAD_DIM ** -0.5), cos, -sin).astype(BF)
    gqkv[:, width + kw :] = kvsum[:, kw:].astype(BF)
    @pl.loop(0, 4)
    def _(t):
        blocks = pl.ds(pl.multiple_of(4 * t, 4), 4)
        col = pl.ds(pl.multiple_of(384 * t, 384), 384)
        p_pw[blocks] = dot_tn(normed[:, col], gqkv[:, width:]).astype(BF).reshape(4, 96, 2 * kw)
        gatt[:, col] += dot_nt(gqkv[:, width:], wqkv[blocks, :, width:].reshape(384, 2 * kw))
    ep.begin()
    ep.step_x(3)
    ep.step_x(2)
    eq.step_z(3)
    eq.step_x(1)
    some(1)
    grad_norm, gain_one = norm_gradient(x_ref[...].astype(F32), vec[0:1, :width], gatt[...])
    grad_input[...] = gmid[...] + grad_norm
    bias = jnp.sum(gqkv[...].astype(F32), axis=0, keepdims=True)
    pv[...] = jnp.zeros_like(pv)
    for i, (v, a, b) in enumerate(((gain_one, sel, fold), (bias[:, :width], sel, fold), (bias[:, width : width + kw], selk, foldk), (bias[:, width + kw :], selk, foldk), (gain_two, sel, fold))):
        pv[:, i, :] = dot((a[...] * v).astype(BF), b[...])
    p_ve[...] = pv[...].astype(BF)
    ev.begin()
    ev.step_x(3)
    ev.step_x(2)
    some(1)
    late = (ep, ev)
    for kind, d in (("z", 3), ("x", 1), ("z", 2), ("x", 0), ("z", 1)):
        for e in late:
            (e.step_x if kind == "x" else e.step_z)(d)
        if (kind, d) not in (("z", 3), ("x", 1)):
            (eq.step_x if kind == "x" else eq.step_z)(d)
        some(1)
    some(15)
    eq.finish(q_out, low_q)
    ep.finish(pair_out)
    trade(0, pair_out, y4, y5)
    ev.finish(vec_out)
    trade(1, vec_out, y6, y7)
    traded(2, wo_out, y2, y3)
    eq.traded(q_out, low_q)
    traded(0, pair_out, y4, y5)
    k_out[...] = pair_out[:, :kw]
    v_out[...] = pair_out[:, kw:]
    traded(1, vec_out, y6, y7)
    back.end()

def backward(lens, gn2, mlp_out, mid, cot, x, att, q, normed, vec, sel, fold, selk, foldk, rope, kv, wo, wqkv, half, ff, block, cid, window=4):
    any_ = pl.BlockSpec(memory_space=pl.ANY)
    vm = pl.BlockSpec(memory_space=pltpu.VMEM)
    dma = pltpu.SemaphoreType.DMA
    sds = jax.ShapeDtypeStruct
    rows, width = x.shape
    wide = wqkv.shape[-1]
    own = wo.shape[1]
    kvw = kv.shape[-1]
    VM = pltpu.VMEM
    def four(blk):
        return [VM((k,) + blk, BF) for k in (16, 8, 4, 5)]
    def five(blk):
        part = (blk[0] // 2, blk[1])
        return [VM((k,) + blk, BF) for k in (16, 8)] + [VM((k,) + part, BF) for k in (8, 4, 5)]
    return pl.pallas_call(
        functools.partial(backward_kernel, block, window),
        out_shape=[sds((rows, width), BF), sds((rows, width), F32), sds((own, width), F32), sds((own, (wide - width) // 2), F32), sds((own, (wide - width) // 2), F32), sds((own, width), F32), sds((16, 128), F32), sds((own, ff), BF)] + [sds((own, ff), BF)] * 2,
        in_specs=[pl.BlockSpec(memory_space=pltpu.SMEM)] + [vm] * 13 + [any_] * 5,
        out_specs=[vm] * 7 + [any_] * 3,
        scratch_shapes=[VM((2, block, HEAD_DIM), F32), VM(kv.shape, BF), VM(wo.shape, BF), VM(wqkv.shape, BF), VM((rows, width), F32), VM((rows, width), BF), VM((rows, width), F32), VM((rows, wide), BF), VM((16, 16, 128), F32)]
        + four((rows, kvw)) + four((own, width)) + five((own, width)) + four((own, wide - width)) + four((16, 128))
        + [VM((rows, kvw), F32), VM((own, wide - width), F32)] + [VM((own, width), BF)] * 3 + [VM((own, wide - width), BF)] * 2 + [VM((16, 128), BF)] * 2
        + [dma((4, 16)), dma((4, 8)), dma((4, 4)), dma((4, 5))] + [dma((16,))] * 8 + [dma((2,)), dma((6,)), dma((24,)), dma((8,)), dma((8,)), dma((4,)), dma((5,)), dma((2,)), dma((4,))],
        compiler_params=pltpu.CompilerParams(collective_id=cid, has_side_effects=True, vmem_limit_bytes=60 * 2**20),
    )(lens, gn2, mlp_out, mid, cot, x, att, q, normed, vec, sel, fold, selk, foldk, rope, kv, wo, wqkv, half)


def folding(group_count, width):
    share = width // group_count
    at = np.arange(width)
    sel = (at[None, :] // share == np.arange(group_count)[:, None]).astype(np.float32)
    fold = (at[:, None] % share == np.arange(128)[None, :]).astype(BF)
    return sel, fold


def rope_constants(span):
    freqs = np.float32(THETA) ** (-np.arange(0, HEAD_DIM, 2, dtype=np.float32) / HEAD_DIM)
    angles = np.arange(span, dtype=np.float32)[:, None] * freqs[None, :].astype(np.float32)
    sin = np.sin(angles)
    return np.stack(
        (np.concatenate((np.cos(angles),) * 2, axis=1), np.concatenate((-sin, sin), axis=1))
    ).astype(np.float32)


def shards_fast(
    hidden_in,
    lengths,
    gain_attn,
    w_query,
    b_query,
    w_key,
    b_key,
    w_value,
    b_value,
    w_out,
    gain_mlp,
    w_gate,
    w_up,
    w_down,
    cotangent,
):
    group_count = lax.axis_size("group")
    slot_count, block_len, model_width = hidden_in.shape
    kv_width = KV_HEADS * HEAD_DIM
    tokens = slot_count * block_len
    hidden_units = w_gate.shape[1]
    pieces = (gain_attn, b_query, b_key, b_value, gain_mlp)
    sel, fold = folding(group_count, model_width)
    selk, foldk = folding(group_count, kv_width)
    rope = rope_constants(group_count * block_len)
    rows_in = hidden_in.reshape(tokens, model_width)
    grad_rows = cotangent.reshape(tokens, model_width)
    (
        q_rows, normed, attended, mid, normed_two, vec, columns, qkv_w, pair_all, grad_all, out_w
    ) = front(
        lengths,
        rows_in,
        grad_rows,
        [p[None] for p in pieces],
        sel,
        fold,
        selk,
        foldk,
        rope,
        w_query,
        w_key,
        w_value,
        w_gate,
        w_up,
        w_down,
        w_out,
        block_len,
        1,
    )
    grad_normed_two, mlp_out, half_sum = mlp(normed_two, grad_all, columns, 3)
    layer_out, grad_input, query_sum, key_sum, value_sum, out_sum, vector_sum, *ff_sums = backward(
        lengths,
        grad_normed_two,
        mlp_out,
        mid,
        grad_rows,
        rows_in,
        attended,
        q_rows,
        normed,
        vec,
        sel,
        fold,
        selk,
        foldk,
        rope,
        pair_all,
        out_w,
        qkv_w,
        half_sum,
        hidden_units,
        block_len,
        4,
        2,
    )
    ff_sums = [p.astype(F32) for p in ff_sums]
    gain_one_sum, query_bias_sum, key_bias_sum, value_bias_sum, gain_two_sum = [
        vector_sum[i, : p.shape[0]] for i, p in enumerate(pieces)
    ]
    return (
        layer_out.reshape(hidden_in.shape),
        grad_input.reshape(hidden_in.shape),
        gain_one_sum,
        query_sum,
        query_bias_sum,
        key_sum,
        key_bias_sum,
        value_sum,
        value_bias_sum,
        out_sum,
        gain_two_sum,
        *ff_sums,
    )


def solution(mesh):
    act = P("replica", "group", None)
    vec = P("group")
    mat = P("group", None)
    return jax.shard_map(
        shards_fast if mesh.shape["group"] == 16 else shards_plain,
        mesh=mesh,
        in_specs=(act, P("replica"), vec, mat, vec, mat, vec, mat, vec, mat, vec, mat, mat, mat, act),
        out_specs=(act, act, vec, mat, vec, mat, vec, mat, vec, mat, vec, mat, mat, mat),
        check_vma=False,
    )
```

```python
import functools

import jax
import jax.numpy as jnp
import numpy as np
from jax import lax
from jax.experimental import pallas as pl
from jax.experimental.pallas import tpu as pltpu
from jax.sharding import PartitionSpec as P

MESH = pl.DeviceIdType.MESH
NZ = 4
MAIN = 512
D = 1536
COLS = 3 * MAIN + 384
HEADS = 12
KV_HEADS = 2
HEAD_DIM = 128
EPSILON = 1e-06
THETA = 1000000.0
BF = jnp.bfloat16
F32 = jnp.float32


def rope_tables(positions, head_dim):
    freqs = THETA ** (-jnp.arange(0, head_dim, 2).astype(F32) / head_dim)
    angles = positions.astype(F32)[:, None] * freqs[None, :]
    angles = jnp.concatenate((angles, angles), axis=-1)
    return (jnp.cos(angles), jnp.sin(angles))


def rotate(tensor, cos_table, sin_table):
    halfway = tensor.shape[-1] // 2
    turned = jnp.concatenate((-tensor[..., halfway:], tensor[..., :halfway]), axis=-1)
    return tensor * cos_table + turned * sin_table


def rotate_back(gradient, cos_table, sin_table):
    halfway = gradient.shape[-1] // 2
    scaled = gradient * sin_table
    turned = jnp.concatenate((scaled[..., halfway:], -scaled[..., :halfway]), axis=-1)
    return gradient * cos_table + turned


def normalize(row_values, gain_vec):
    factor = lax.rsqrt(jnp.mean(row_values * row_values, axis=-1, keepdims=True) + EPSILON)
    return (row_values * factor * gain_vec, factor)


def norm_back(row_values, factor, gain_vec, upstream):
    weighted = upstream * gain_vec
    inner_mean = jnp.mean(weighted * row_values, axis=-1, keepdims=True)
    grad_rows = factor * weighted - row_values * (factor * factor * factor) * inner_mean
    grad_gain = jnp.sum(upstream * row_values * factor, axis=0)
    return (grad_rows, grad_gain)


def matmul(a, b):
    return jnp.dot(a, b, preferred_element_type=F32)


def matmul_nt(a, b):
    return lax.dot_general(a, b, (((1,), (1,)), ((), ())), preferred_element_type=F32)


def matmul_tn(a, b):
    return lax.dot_general(a, b, (((0,), (0,)), ((), ())), preferred_element_type=F32)


def arrange(per_token, kv_heads):
    block_len, head_count, head_dim = per_token.shape
    repeat = head_count // kv_heads
    grouped = per_token.reshape(block_len, kv_heads, repeat, head_dim)
    return jnp.transpose(grouped, (1, 2, 0, 3)).reshape(kv_heads, repeat * block_len, head_dim)


def restore(per_group, block_len):
    kv_heads, row_count, head_dim = per_group.shape
    repeat = row_count // block_len
    grouped = per_group.reshape(kv_heads, repeat, block_len, head_dim)
    return jnp.transpose(grouped, (2, 0, 1, 3)).reshape(block_len, kv_heads * repeat * head_dim)


def masked_exp(query_rows, key_block, row_pos, first_key, length, score_scale):
    key_step = key_block.shape[0]
    raw_scores = jnp.einsum("grd,kgd->grk", query_rows, key_block, preferred_element_type=F32)
    key_pos = first_key + jnp.arange(key_step, dtype=jnp.int32)
    allowed = (key_pos[None, :] <= row_pos[:, None]) & (key_pos[None, :] < length)
    return jnp.where(allowed[None], jnp.exp(raw_scores * score_scale), 0.0)


def block_total(length, rank_end, key_step):
    key_limit = jnp.minimum(length, rank_end)
    return (key_limit + key_step - 1) // key_step


def attend_forward(query_rows, key_all, value_all, row_pos, length, rank_end, key_step, scale):
    kv_heads, row_count, head_dim = query_rows.shape

    def visit(block_index, state_tuple):
        totals, numerator = state_tuple
        first_key = block_index * key_step
        key_block = lax.dynamic_slice_in_dim(key_all, first_key, key_step, 0)
        value_block = lax.dynamic_slice_in_dim(value_all, first_key, key_step, 0)
        weights = masked_exp(query_rows, key_block, row_pos, first_key, length, scale)
        totals = totals + jnp.sum(weights, axis=-1)
        numerator = numerator + jnp.einsum(
            "grk,kgd->grd", weights.astype(BF), value_block, preferred_element_type=F32
        )
        return (totals, numerator)

    initial = (
        jnp.zeros((kv_heads, row_count), F32),
        jnp.zeros((kv_heads, row_count, head_dim), F32),
    )
    return lax.fori_loop(0, block_total(length, rank_end, key_step), visit, initial)


def attend_backward(
    query_rows, key_all, value_all, row_pos, length, rank_end, key_step, scale, grad_numer, grad_total
):
    kv_heads, row_count, head_dim = query_rows.shape

    def visit(block_index, state_tuple):
        grad_query, grad_key, grad_value = state_tuple
        first_key = block_index * key_step
        key_block = lax.dynamic_slice_in_dim(key_all, first_key, key_step, 0)
        value_block = lax.dynamic_slice_in_dim(value_all, first_key, key_step, 0)
        weights = masked_exp(query_rows, key_block, row_pos, first_key, length, scale)
        grad_prob = jnp.einsum("grd,kgd->grk", grad_numer, value_block, preferred_element_type=F32)
        grad_score = (weights * (grad_prob + grad_total[..., None])).astype(BF)
        grad_query = grad_query + jnp.einsum(
            "grk,kgd->grd", grad_score, key_block, preferred_element_type=F32
        )
        key_part = jnp.einsum("grk,grd->kgd", grad_score, query_rows, preferred_element_type=F32)
        value_part = jnp.einsum(
            "grk,grd->kgd", weights.astype(BF), grad_numer, preferred_element_type=F32
        )
        key_old = lax.dynamic_slice_in_dim(grad_key, first_key, key_step, 0)
        value_old = lax.dynamic_slice_in_dim(grad_value, first_key, key_step, 0)
        grad_key = lax.dynamic_update_slice_in_dim(grad_key, key_old + key_part, first_key, 0)
        grad_value = lax.dynamic_update_slice_in_dim(
            grad_value, value_old + value_part, first_key, 0
        )
        return (grad_query, grad_key, grad_value)

    initial = (
        jnp.zeros((kv_heads, row_count, head_dim), F32),
        jnp.zeros(key_all.shape, F32),
        jnp.zeros(value_all.shape, F32),
    )
    return lax.fori_loop(0, block_total(length, rank_end, key_step), visit, initial)


def gather_plain(x):
    return lax.all_gather(x, "group", axis=0, tiled=True)


def scatter_sum(x):
    return lax.psum_scatter(x, "group", scatter_dimension=0, tiled=True)


def shards_plain(
    hidden_in,
    lengths,
    gain_attn,
    w_query,
    b_query,
    w_key,
    b_key,
    w_value,
    b_value,
    w_out,
    gain_mlp,
    w_gate,
    w_up,
    w_down,
    cotangent,
):
    group_count = lax.axis_size("group")
    group_rank = lax.axis_index("group")
    slot_count, block_len, model_width = hidden_in.shape
    kv_heads = KV_HEADS
    head_dim = HEAD_DIM
    kv_width = kv_heads * head_dim
    repeat = HEADS // kv_heads
    slot_span = block_len * group_count
    key_step = min(512, slot_span)
    score_scale = head_dim ** (-0.5)
    tokens = slot_count * block_len
    hidden_units = w_gate.shape[1]
    own_rows = w_gate.shape[0]
    share = hidden_units // group_count
    positions = group_rank * block_len + jnp.arange(block_len, dtype=jnp.int32)
    valid_rows = (positions[None, :] < lengths[:, None]).astype(F32).reshape(tokens, 1)
    cos_table, sin_table = rope_tables(positions, head_dim)
    cos_heads = cos_table[:, None, :]
    sin_heads = sin_table[:, None, :]
    rank_end = (group_rank + 1) * block_len
    row_pos = jnp.tile(positions, repeat)

    pieces = (gain_attn, b_query, b_key, b_value, gain_mlp)
    sizes = [p.shape[0] for p in pieces]
    small = gather_plain(jnp.concatenate(pieces)[None])
    offsets = [sum(sizes[:i]) for i in range(len(sizes) + 1)]
    gain_one, query_b, key_b, value_b, gain_two = [
        small[:, offsets[i] : offsets[i + 1]].reshape(-1).astype(F32) for i in range(len(sizes))
    ]
    qkv_w = gather_plain(jnp.concatenate((w_query, w_key, w_value), axis=1))
    out_w = gather_plain(w_out)
    qkv_b = jnp.concatenate((query_b, key_b, value_b))

    stacked = jnp.stack((w_gate, w_up, w_down)).reshape(3, own_rows, group_count, share)
    stacked = jnp.transpose(stacked, (2, 1, 0, 3)).reshape(group_count, own_rows, 3 * share)
    columns = lax.all_to_all(stacked, "group", 0, 0, tiled=True).reshape(model_width, 3 * share)
    gate_up_w = columns[:, : 2 * share]
    down_w = columns[:, 2 * share :]

    grad_final = cotangent.reshape(tokens, model_width).astype(F32) * valid_rows
    grad_all = gather_plain(grad_final.astype(BF))

    inputs = hidden_in.reshape(tokens, model_width).astype(F32)
    normed_full, factor_one = normalize(inputs, gain_one)
    normed = normed_full.astype(BF)
    qkv = matmul(normed, qkv_w) + qkv_b
    query_rot = rotate(
        qkv[:, :model_width].reshape(slot_count, block_len, HEADS, head_dim), cos_heads, sin_heads
    ).astype(BF)
    key_rot = rotate(
        qkv[:, model_width : model_width + kv_width].reshape(
            slot_count, block_len, kv_heads, head_dim
        ),
        cos_heads,
        sin_heads,
    ).astype(BF)
    value_low = qkv[:, model_width + kv_width :].astype(BF)
    pair = jnp.concatenate(
        (key_rot.reshape(tokens, kv_width), value_low), axis=1
    ).reshape(1, slot_count, block_len, 2 * kv_width)
    pair_all = jnp.transpose(gather_plain(pair), (1, 0, 2, 3)).reshape(
        slot_count, slot_span, 2, kv_heads, head_dim
    )
    key_all = pair_all[:, :, 0]
    value_all = pair_all[:, :, 1]
    query_groups = []
    slot_totals = []
    slot_attended = []
    attended_rows = []
    for s in range(slot_count):
        query_rows = arrange(query_rot[s], kv_heads)
        totals, numerator = attend_forward(
            query_rows, key_all[s], value_all[s], row_pos, lengths[s], rank_end, key_step, score_scale
        )
        attended = numerator / totals[..., None]
        query_groups.append(query_rows)
        slot_totals.append(totals)
        slot_attended.append(attended)
        attended_rows.append(restore(attended, block_len))
    attended_low = jnp.concatenate(attended_rows, axis=0).astype(BF)
    residual_mid = inputs + matmul(attended_low, out_w)
    normed_two_full, factor_two = normalize(residual_mid, gain_two)
    normed_all = gather_plain(normed_two_full.astype(BF))

    pre = matmul(normed_all, gate_up_w)
    gate_pre = pre[:, :share]
    up_pre = pre[:, share:]
    sigmoid_gate = jax.nn.sigmoid(gate_pre)
    silu_gate = gate_pre * sigmoid_gate
    hidden = (silu_gate * up_pre).astype(BF)
    grad_hidden = matmul(grad_all, down_w)
    grad_gate = (
        grad_hidden * up_pre * (sigmoid_gate * (1.0 + gate_pre * (1.0 - sigmoid_gate)))
    ).astype(BF)
    grad_up = (grad_hidden * silu_gate).astype(BF)
    gate_up_grad = jnp.concatenate((grad_gate, grad_up), axis=1)
    grad_normed_two = scatter_sum(matmul_nt(gate_up_grad, gate_up_w).astype(BF)).astype(F32)
    mlp_out = scatter_sum(matmul_nt(hidden, down_w).astype(BF)).astype(F32)
    down_term = matmul_tn(grad_all, hidden)
    gate_up_term = matmul_tn(normed_all, gate_up_grad)
    terms = jnp.concatenate((gate_up_term, down_term), axis=1).astype(BF)
    back = lax.all_to_all(
        terms.reshape(group_count, own_rows, 3 * share), "group", 0, 0, tiled=True
    )
    summed = back.astype(F32) + lax.ppermute(back, "replica", [(0, 1), (1, 0)]).astype(F32)
    summed = jnp.transpose(summed.reshape(group_count, own_rows, 3, share), (2, 1, 0, 3))
    gate_sum, up_sum, down_sum = summed.reshape(3, own_rows, hidden_units)

    final_rows = residual_mid + mlp_out
    layer_out = (final_rows * valid_rows).reshape(slot_count, block_len, model_width).astype(BF)
    grad_mid_norm, grad_gain_two = norm_back(residual_mid, factor_two, gain_two, grad_normed_two)
    grad_mid = grad_final + grad_mid_norm
    grad_branch = grad_mid.astype(BF)
    out_term = matmul_tn(attended_low, grad_branch)
    grad_attended = matmul_nt(grad_branch, out_w)
    grad_query_rows = []
    grad_pairs = []
    for s in range(slot_count):
        slot_grad = grad_attended[s * block_len : (s + 1) * block_len].reshape(
            block_len, HEADS, head_dim
        )
        grad_out = arrange(slot_grad, kv_heads)
        totals = slot_totals[s]
        grad_total = -jnp.sum(grad_out * slot_attended[s], axis=-1) / totals
        grad_numer = (grad_out / totals[..., None]).astype(BF)
        grad_query, grad_key, grad_value = attend_backward(
            query_groups[s],
            key_all[s],
            value_all[s],
            row_pos,
            lengths[s],
            rank_end,
            key_step,
            score_scale,
            grad_numer,
            grad_total,
        )
        query_back_rows = restore(grad_query * score_scale, block_len).reshape(
            block_len, HEADS, head_dim
        )
        grad_query_rows.append(
            rotate_back(query_back_rows, cos_heads, sin_heads).reshape(block_len, HEADS * head_dim)
        )
        grad_pairs.append(
            jnp.concatenate(
                (grad_key.reshape(slot_span, kv_width), grad_value.reshape(slot_span, kv_width)),
                axis=1,
            )
        )
    pair_grads = jnp.stack(grad_pairs).reshape(slot_count, group_count, block_len, 2 * kv_width)
    pair_grads = jnp.transpose(pair_grads, (1, 0, 2, 3)).astype(BF)
    pair_sum = scatter_sum(pair_grads).reshape(slot_count, block_len, 2 * kv_width).astype(F32)
    grad_query_pre = jnp.concatenate(grad_query_rows, axis=0).astype(BF)
    key_sum = pair_sum[..., :kv_width].reshape(slot_count, block_len, kv_heads, head_dim)
    grad_key_pre = (
        rotate_back(key_sum * score_scale, cos_heads, sin_heads).astype(BF).reshape(tokens, kv_width)
    )
    grad_value_pre = pair_sum[..., kv_width:].astype(BF).reshape(tokens, kv_width)
    grad_qkv = jnp.concatenate((grad_query_pre, grad_key_pre, grad_value_pre), axis=1)
    grad_normed = matmul_nt(grad_qkv, qkv_w)
    grad_in_norm, grad_gain_one = norm_back(inputs, factor_one, gain_one, grad_normed)
    grad_input = (grad_mid + grad_in_norm).reshape(slot_count, block_len, model_width)
    qkv_term = matmul_tn(normed, grad_qkv)
    qkv_bias = jnp.sum(grad_qkv.astype(F32), axis=0)

    weight_share = scatter_sum(
        jnp.concatenate((qkv_term, out_term), axis=1).astype(BF)
    )
    weight_sum = weight_share.astype(F32) + lax.ppermute(
        weight_share, "replica", [(0, 1), (1, 0)]
    ).astype(F32)
    vectors = jnp.concatenate(
        [
            grad_gain_one.reshape(group_count, -1),
            qkv_bias[:model_width].reshape(group_count, -1),
            qkv_bias[model_width : model_width + kv_width].reshape(group_count, -1),
            qkv_bias[model_width + kv_width :].reshape(group_count, -1),
            grad_gain_two.reshape(group_count, -1),
        ],
        axis=1,
    )
    vector_sum = lax.psum(scatter_sum(vectors), "replica").reshape(-1)
    gain_one_sum, query_bias_sum, key_bias_sum, value_bias_sum, gain_two_sum = [
        vector_sum[offsets[i] : offsets[i + 1]] for i in range(len(sizes))
    ]
    ends = (0, model_width, model_width + kv_width, model_width + 2 * kv_width)
    query_sum, key_sum_w, value_sum_w = [weight_sum[:, ends[i] : ends[i + 1]] for i in range(3)]
    out_sum = weight_sum[:, ends[3] :]
    return (
        layer_out,
        grad_input,
        gain_one_sum,
        query_sum,
        query_bias_sum,
        key_sum_w,
        key_bias_sum,
        value_sum_w,
        value_bias_sum,
        out_sum,
        gain_two_sum,
        gate_sum,
        up_sum,
        down_sum,
    )


def place():
    g = lax.axis_index("group")
    r = lax.axis_index("replica")
    return r, g // 4, lax.rem(g // 2, 2), lax.rem(g, 2)

def idx(z, x, c):
    return (z * 2 + x) * 2 + c

def greet(r, z, x, c, with_y=False):
    bar = pltpu.get_barrier_semaphore()
    def hail(dev):
        pl.semaphore_signal(bar, inc=1, device_id=dev, device_id_type=MESH)
    hail((r, idx(z, 1 - x, c)))
    hail((r, idx(z, x, 1 - c)))
    if with_y:
        hail((1 - r, idx(z, x, c)))
    @pl.when(z > 0)
    def _():
        hail((r, idx(z - 1, x, c)))
    @pl.when(z < NZ - 1)
    def _():
        hail((r, idx(z + 1, x, c)))
    ends = jnp.where((z > 0) & (z < NZ - 1), 1, 0)
    pl.semaphore_wait(bar, (4 if with_y else 3) + ends)

def planes(z):
    return (
        z,
        jnp.where(z == 0, 1, jnp.where(z == 1, 0, jnp.where(z == 2, 3, 2))),
        jnp.where(z == 0, 2, jnp.where(z == 1, 2, 1)),
        jnp.where(z < 2, 3, 0),
    )

def when(cond, fn):
    pl.when(cond)(fn)

class Gather:
    def __init__(self, at, src, out, send, recv, local, part=None):
        self.r, self.z, self.x, self.c = at
        self.src, self.out, self.send, self.recv, self.local = src, out, send, recv, local
        self.part = part
        self.mid = (self.z > 0) & (self.z < NZ - 1)
        self.p = planes(self.z)
    def blk(self, b):
        return self.out.at[b] if self.part is None else self.out.at[b, self.part]
    def put(self, src, b, k, dev):
        pltpu.make_async_remote_copy(src, self.blk(b), self.send.at[k], self.recv.at[b], device_id=dev, device_id_type=MESH).start()
    def sent(self, k):
        b = 0
        pltpu.make_async_remote_copy(self.blk(b), self.blk(b), self.send.at[k], self.recv.at[b], device_id=(self.r, 0), device_id_type=MESH).wait_send()
    def got(self, b):
        pltpu.make_async_remote_copy(self.blk(b), self.blk(b), self.send.at[0], self.recv.at[b], device_id=(self.r, 0), device_id_type=MESH).wait_recv()
    def zdev(self, s): return (self.r, idx(self.z + s, self.x, self.c))
    def xdev(self): return (self.r, idx(self.z, 1 - self.x, self.c))
    def cdev(self): return (self.r, idx(self.z, self.x, 1 - self.c))
    def begin(self):
        z, x, c = self.z, self.x, self.c
        me = idx(z, x, c)
        for s in (1, -1):
            when(self.inside(z + s), lambda s=s: self.put(self.src, me, 0 if s == 1 else 3, self.zdev(s)))
        self.put(self.src, me, 6 + z, self.xdev())
        self.put(self.src, me, 10 + 2 * z + x, self.cdev())
        pltpu.make_async_copy(self.src, self.blk(me), self.local).start()
    def inside(self, z): return (z >= 0) & (z < NZ)
    def from_z(self, zz):
        z, x, c = self.z, self.x, self.c
        b = idx(zz, x, c)
        self.got(b)
        s = jnp.where(zz < z, 1, -1)
        d = jnp.abs(zz - z)
        slot = jnp.where(zz < z, 0, 3) + d
        when(self.inside(z + s), lambda: self.put(self.blk(b), b, slot, (self.r, idx(z + s, x, c))))
        self.put(self.blk(b), b, 6 + zz, self.xdev())
        self.put(self.blk(b), b, 10 + 2 * zz + x, self.cdev())
    def first(self):
        self.from_z(self.p[1])
        when(self.mid, lambda: self.from_z(self.p[2]))
        self.from_x(self.p[0])
    def second(self):
        self.from_z(jnp.where(self.mid, self.p[3], self.p[2]))
        self.from_x(self.p[1])
    def third(self):
        when(~self.mid, lambda: self.from_z(self.p[3]))
        self.from_x(self.p[2])
    def fourth(self):
        self.from_x(self.p[3])
    def from_x(self, zz):
        b = idx(zz, 1 - self.x, self.c)
        self.got(b)
        self.put(self.blk(b), b, 10 + 2 * zz + 1 - self.x, self.cdev())
    def from_c(self, zz):
        self.got(idx(zz, self.x, 1 - self.c))
        self.got(idx(zz, 1 - self.x, 1 - self.c))
    def end(self, local=True):
        z = self.z
        for d in range(NZ - 1):
            when((z - d >= 0) & (z < NZ - 1), lambda d=d: self.sent(d))
            when((z + d < NZ) & (z > 0), lambda d=d: self.sent(3 + d))
        for k in range(6, 18):
            self.sent(k)
        if local:
            pltpu.make_async_copy(self.src, self.blk(0), self.local).wait()

class Scatter:
    def __init__(self, at, part, rc, rx, rz, send, rcs, rxs, rzs):
        self.r, self.z, self.x, self.c = at
        self.part, self.rc, self.rx, self.rz = part, rc, rx, rz
        self.send, self.rcs, self.rxs, self.rzs = send, rcs, rxs, rzs
    def inside(self, z): return (z >= 0) & (z < NZ)
    def copy(self, src, dst, k, rs, dev):
        return pltpu.make_async_remote_copy(src, dst, self.send.at[k], rs, device_id=dev, device_id_type=MESH)
    def over(self, d):
        return [(s, self.z + s * d) for s in ((-1, 1) if d else (1,))]
    def begin(self, far_first=True):
        z, x, c = self.z, self.x, self.c
        dev = (self.r, idx(z, x, 1 - c))
        for xx in (1 - x, x):
            for d in range(NZ - 1, -1, -1):
                for s, zz in self.over(d):
                    k = 2 * zz + xx
                    when(self.inside(zz), lambda zz=zz, k=k, xx=xx: self.copy(self.part.at[idx(zz, xx, 1 - c)], self.rc.at[k], k, self.rcs.at[k], dev).start())
    def send_c(self, zz):
        z, x, c = self.z, self.x, self.c
        dev = (self.r, idx(z, x, 1 - c))
        for xx in (1 - x, x):
            k = 2 * zz + xx
            self.copy(self.part.at[idx(zz, xx, 1 - c)], self.rc.at[k], k, self.rcs.at[k], dev).start()
    def x_plane(self, zz):
        z, x, c = self.z, self.x, self.c
        dev = (self.r, idx(z, 1 - x, c))
        k = 2 * zz + 1 - x
        b = idx(zz, 1 - x, c)
        self.copy(self.rc.at[k], self.rc.at[k], 0, self.rcs.at[k], dev).wait_recv()
        self.part[b] = (self.part[b].astype(F32) + self.rc[k].astype(F32)).astype(BF)
        self.copy(self.part.at[b], self.rx.at[zz], 8 + zz, self.rxs.at[zz], dev).start()
    def step_x(self, d):
        for s, zz in self.over(d):
            when(self.inside(zz), lambda zz=zz: self.x_plane(zz))
    def step_z(self, d):
        z, x, c = self.z, self.x, self.c
        for s, zz in self.over(d):
            def go(zz=zz, s=s):
                k = 2 * zz + x
                b = idx(zz, x, c)
                self.copy(self.rc.at[k], self.rc.at[k], 0, self.rcs.at[k], (self.r, 0)).wait_recv()
                self.copy(self.rx.at[zz], self.rx.at[zz], 0, self.rxs.at[zz], (self.r, 0)).wait_recv()
                both = self.part[b].astype(F32) + self.rc[k].astype(F32) + self.rx[zz].astype(F32)
                dev = (self.r, idx(z + s, x, c))
                slot = jnp.where(zz == z + s, NZ, zz) if s == -1 else zz
                self.part[b] = both.astype(BF)
                def more():
                    self.copy(self.rz.at[zz], self.rz.at[zz], 0, self.rzs.at[zz], dev).wait_recv()
                    self.part[b] = (self.part[b].astype(F32) + self.rz[zz].astype(F32)).astype(BF)
                when(self.inside(z - s), more)
                self.copy(self.part.at[b], self.rz.at[slot], 12 + zz, self.rzs.at[slot], dev).start()
            when(self.inside(zz), go)
    def finish(self, out):
        z, x, c = self.z, self.x, self.c
        k = 2 * z + x
        b = idx(z, x, c)
        self.copy(self.rc.at[k], self.rc.at[k], 0, self.rcs.at[k], (self.r, 0)).wait_recv()
        self.copy(self.rx.at[z], self.rx.at[z], 0, self.rxs.at[z], (self.r, 0)).wait_recv()
        out[...] = self.part[b].astype(F32) + self.rc[k].astype(F32) + self.rx[z].astype(F32)
        def lo():
            self.copy(self.rz.at[z], self.rz.at[z], 0, self.rzs.at[z], (self.r, 0)).wait_recv()
            out[...] += self.rz[z].astype(F32)
        when(z > 0, lo)
        def hi():
            self.copy(self.rz.at[NZ], self.rz.at[NZ], 0, self.rzs.at[NZ], (self.r, 0)).wait_recv()
            out[...] += self.rz[NZ].astype(F32)
        when(z < NZ - 1, hi)
        for k in range(8):
            self.copy(self.part.at[0], self.part.at[0], k, self.rcs.at[0], (self.r, 0)).wait_send()
        for k in range(8, 12):
            self.copy(self.part.at[0], self.part.at[0], k, self.rcs.at[0], (self.r, 0)).wait_send()
        for zz in range(NZ):
            when(z != zz, lambda zz=zz: self.copy(self.part.at[0], self.part.at[0], 12 + zz, self.rcs.at[0], (self.r, 0)).wait_send())

class ScatterY(Scatter):
    def __init__(self, at, part, rc, ry, rx, rz, send, rcs, rys, rxs, rzs, ysem):
        Scatter.__init__(self, at, part, rc, rx, rz, send, rcs, rxs, rzs)
        self.ry, self.rys, self.ysem = ry, rys, ysem
        self.n = part.shape[1] // 2
        self.ydev = (1 - self.r, idx(self.z, self.x, self.c))
        self.mine = self.rows(self.r)
    def rows(self, h):
        return pl.ds(pl.multiple_of(h * self.n, self.n), self.n)
    def step_y(self, d):
        x, c, r = self.x, self.c, self.r
        for xx in (1 - x, x):
            for s, zz in self.over(d):
                def go(zz=zz, xx=xx):
                    k = 2 * zz + xx
                    b = idx(zz, xx, c)
                    self.copy(self.rc.at[k], self.rc.at[k], 0, self.rcs.at[k], self.ydev).wait_recv()
                    self.part[b] = (self.part[b].astype(F32) + self.rc[k].astype(F32)).astype(BF)
                    self.copy(self.part.at[b, self.rows(1 - r)], self.ry.at[k], 16 + k, self.rys.at[k], self.ydev).start()
                when(self.inside(zz), go)
    def both(self, zz, xx):
        k = 2 * zz + xx
        self.copy(self.ry.at[k], self.ry.at[k], 0, self.rys.at[k], self.ydev).wait_recv()
        return self.part[idx(zz, xx, self.c), self.mine].astype(F32) + self.ry[k].astype(F32)
    def step_x(self, d):
        z, x, c = self.z, self.x, self.c
        dev = (self.r, idx(z, 1 - x, c))
        for s, zz in self.over(d):
            def go(zz=zz):
                b = idx(zz, 1 - x, c)
                self.part[b, self.mine] = self.both(zz, 1 - x).astype(BF)
                self.copy(self.part.at[b, self.mine], self.rx.at[zz], 8 + zz, self.rxs.at[zz], dev).start()
            when(self.inside(zz), go)
    def arrived(self, ref, sem):
        self.copy(ref, ref, 0, sem, self.ydev).wait_recv()
    def step_z(self, d):
        z, x, c = self.z, self.x, self.c
        for s, zz in self.over(d):
            def go(zz=zz, s=s):
                b = idx(zz, x, c)
                v = self.both(zz, x)
                self.arrived(self.rx.at[zz], self.rxs.at[zz])
                self.part[b, self.mine] = (v + self.rx[zz].astype(F32)).astype(BF)
                def more():
                    self.arrived(self.rz.at[zz], self.rzs.at[zz])
                    self.part[b, self.mine] = (self.part[b, self.mine].astype(F32) + self.rz[zz].astype(F32)).astype(BF)
                when(self.inside(z - s), more)
                slot = jnp.where(zz == z + s, NZ, zz) if s == -1 else zz
                self.copy(self.part.at[b, self.mine], self.rz.at[slot], 12 + zz, self.rzs.at[slot], (self.r, idx(z + s, x, c))).start()
            when(self.inside(zz), go)
    def finish(self, out, low):
        z, x, r = self.z, self.x, self.r
        v = self.both(z, x)
        self.arrived(self.rx.at[z], self.rxs.at[z])
        out[self.mine] = v + self.rx[z].astype(F32)
        def lo():
            self.arrived(self.rz.at[z], self.rzs.at[z])
            out[self.mine] += self.rz[z].astype(F32)
        when(z > 0, lo)
        def hi():
            self.arrived(self.rz.at[NZ], self.rzs.at[NZ])
            out[self.mine] += self.rz[NZ].astype(F32)
        when(z < NZ - 1, hi)
        low[self.mine] = out[self.mine].astype(BF)
        a = low.at[self.mine]
        pltpu.make_async_remote_copy(a, a, self.ysem.at[0], self.ysem.at[1], device_id=self.ydev, device_id_type=MESH).start()
    def traded(self, out, low):
        a = low.at[self.rows(1 - self.r)]
        pltpu.make_async_remote_copy(a, a, self.ysem.at[0], self.ysem.at[1], device_id=self.ydev, device_id_type=MESH).wait()
        out[...] = low[...].astype(F32)
        half = self.part.at[0, self.mine]
        for k in range(8):
            self.copy(self.part.at[0], self.part.at[0], k, self.rcs.at[0], self.ydev).wait_send()
        for k in list(range(16, 24)) + list(range(8, 12)):
            self.copy(half, half, k, self.rcs.at[0], self.ydev).wait_send()
        for zz in range(NZ):
            when(self.z != zz, lambda zz=zz: self.copy(half, half, 12 + zz, self.rcs.at[0], self.ydev).wait_send())


KS = (8, 4, 9, 5, 10, 6, 11, 7, 12, 1, 13, 2, 14, 3, 15)
WINDOW = 2

def has(j):
    return lax.rem(j, 3) == 0

def spare_at(j):
    return pl.ds(pl.multiple_of(16 * MAIN + 128 * (j // 3), 128), 128)

class Deal:
    def __init__(self, at, ws, buf, sems, local):
        self.r, self.z, self.x, self.c = at
        self.me = idx(self.z, self.x, self.c)
        self.ws, self.buf, self.sems, self.local = ws, buf, sems, local
        self.n = ws[0].shape[0] // 2
    def rows(self, j, h):
        return pl.ds(pl.multiple_of((2 * j + h) * self.n, self.n), self.n)
    def block(self, j, h, spare):
        return self.buf.at[self.rows(j, h), pl.ds(3 * MAIN, 384) if spare else pl.ds(0, 3 * MAIN)]
    def copy(self, a, b, kind, k, dev):
        send, recv = self.sems[2 * kind : 2 * kind + 2]
        return pltpu.make_async_remote_copy(a, b, send.at[k], recv.at[k], device_id=dev, device_id_type=MESH)
    def launch(self, k):
        r, me, n = self.r, self.me, self.n
        row = pl.ds(pl.multiple_of(r * n, n), n)
        j = jnp.bitwise_xor(me, k)
        dst = self.rows(me, r)
        for i in range(3):
            self.copy(self.ws[i].at[row, pl.ds(pl.multiple_of(j * MAIN, MAIN), MAIN)], self.buf.at[dst, pl.ds(i * MAIN, MAIN)], 0, k, (r, j)).start()
        def spare():
            for i in range(3):
                self.copy(self.ws[i].at[row, spare_at(j)], self.buf.at[dst, pl.ds(3 * MAIN + 128 * i, 128)], 1, k, (r, j)).start()
        when(has(j), spare)
    def locals(self, spare):
        me, n = self.me, self.n
        row = pl.ds(pl.multiple_of(2 * me * n, 2 * n), 2 * n)
        col = spare_at(me) if spare else pl.ds(pl.multiple_of(me * MAIN, MAIN), MAIN)
        for i in range(3):
            to = pl.ds(3 * MAIN + 128 * i, 128) if spare else pl.ds(i * MAIN, MAIN)
            yield pltpu.make_async_copy(self.ws[i].at[:, col], self.buf.at[row, to], self.local.at[1 if spare else 0])
    def begin(self):
        for k in KS[:WINDOW]:
            self.launch(k)
        for l in self.locals(False):
            l.start()
        def spare():
            for l in self.locals(True):
                l.start()
        when(has(self.me), spare)
    def step(self, i):
        k = KS[i]
        r, me = self.r, self.me
        j = jnp.bitwise_xor(me, k)
        dev = (1 - r, me)
        def pass_on(spare):
            blk = self.block(j, r, spare)
            self.copy(blk, blk, spare, k, dev).wait_recv()
            self.copy(blk, blk, 2 + spare, k, dev).start()
        pass_on(0)
        when(has(me), lambda: pass_on(1))
        if i + WINDOW < 15:
            self.launch(KS[i + WINDOW])
    def end(self):
        r, me, n = self.r, self.me, self.n
        dev = (1 - r, me)
        for k in KS:
            j = jnp.bitwise_xor(me, k)
            def done(spare):
                blk = self.block(j, 1 - r, spare)
                self.copy(blk, blk, 2 + spare, k, dev).wait()
            def sent(spare):
                blk = self.block(j, r, spare)
                self.copy(blk, blk, spare, k, dev).wait_send()
            done(0)
            sent(0)
            when(has(me), lambda: done(1))
            when(has(j), lambda: sent(1))
        row = pl.ds(pl.multiple_of(2 * me * n, 2 * n), 2 * n)
        def own(spare):
            blk = self.buf.at[row, pl.ds(3 * MAIN, 384) if spare else pl.ds(0, 3 * MAIN)]
            pltpu.make_async_copy(blk, blk, self.local.at[spare]).wait()
        own(0)
        when(has(me), lambda: own(1))

def hail_all(r, z, x, c):
    bar = pltpu.get_barrier_semaphore()
    me = idx(z, x, c)
    for k in range(1, 16):
        pl.semaphore_signal(bar, inc=1, device_id=(r, lax.rem(me + k, 16)), device_id_type=MESH)
    pl.semaphore_signal(bar, inc=1, device_id=(1 - r, me), device_id_type=MESH)
    pl.semaphore_wait(bar, 16)


def dot(a, b):
    return lax.dot_general(a, b, (((1,), (0,)), ((), ())), preferred_element_type=F32)
def dot_nt(a, b):
    return lax.dot_general(a, b, (((1,), (1,)), ((), ())), preferred_element_type=F32)
def dot_tn(a, b):
    return lax.dot_general(a, b, (((0,), (0,)), ((), ())), preferred_element_type=F32)

def gated(g, u, gh):
    sig = jax.nn.sigmoid(g)
    silu = g * sig
    return (gh * u * (sig * (1.0 + g * (1.0 - sig)))).astype(BF), (gh * silu).astype(BF), (silu * u).astype(BF)

def mlp_kernel(n2_ref, cot_ref, w_ref, gsum, osum, half_ref,
               n2, cot, w, act, pg, po, rcg, rxg, rzg, rco, rxo, rzo, yb,
               gsend, grecv, glocal, lsem, ssend, srcs, srxs, srzs, ysend, yrecv, xsend, xrecv):
    at = place()
    r, z, x, c = at
    me = idx(z, x, c)
    extra = has(me)
    MM, SP = pl.ds(0, 3 * MAIN), pl.ds(3 * MAIN, 384)
    loads = [pltpu.make_async_copy(w_ref.at[:, MM], w.at[:, MM], lsem.at[0]), pltpu.make_async_copy(cot_ref, cot, lsem.at[1])]
    for l in loads: l.start()
    load_spare = pltpu.make_async_copy(w_ref.at[:, SP], w.at[:, SP], lsem.at[3])
    when(extra, load_spare.start)
    greet(*at, with_y=True)
    g = Gather(at, n2_ref, n2, gsend, grecv, glocal)
    rg = Scatter(at, pg, rcg, rxg, rzg, ssend.at[0], srcs.at[0], srxs.at[0], srzs.at[0])
    ro = Scatter(at, po, rco, rxo, rzo, ssend.at[1], srcs.at[1], srxs.at[1], srzs.at[1])
    g.begin()
    for l in loads: l.wait()
    when(extra, load_spare.wait)
    mid = (z > 0) & (z < NZ - 1)
    p = [z,
         jnp.where(z == 0, 1, jnp.where(z == 1, 0, jnp.where(z == 2, 3, 2))),
         jnp.where(z == 0, 2, jnp.where(z == 1, 2, 1)),
         jnp.where(z < 2, 3, 0)]

    def tiles(zz):
        rows = pl.ds(pl.multiple_of(4 * zz, 4), 4)
        tok = pl.ds(pl.multiple_of(512 * zz, 512), 512)
        @pl.loop(0, 2)
        def _(t):
            a = n2[rows].reshape(512, D)
            k = cot[rows].reshape(512, D)
            def col(base):
                return pl.ds(pl.multiple_of(base + 256 * t, 256), 256)
            dg, du, h = gated(dot(a, w[:, col(0)]), dot(a, w[:, col(MAIN)]), dot(k, w[:, col(2 * MAIN)]))
            act[tok, col(0)] = dg
            act[tok, col(MAIN)] = du
            act[tok, col(2 * MAIN)] = h
        def spare():
            pre = dot(n2[rows].reshape(512, D), w[:, 3 * MAIN : 3 * MAIN + 256])
            dg, du, h = gated(pre[:, :128], pre[:, 128:], dot(cot[rows].reshape(512, D), w[:, 3 * MAIN + 256 :]))
            act[tok, 3 * MAIN : 3 * MAIN + 128] = dg
            act[tok, 3 * MAIN + 128 : 3 * MAIN + 256] = du
            act[tok, 3 * MAIN + 256 :] = h
        when(extra, spare)
        def out_tiles(more):
            @pl.loop(0, D // 256)
            def _(t):
                dr = pl.ds(pl.multiple_of(256 * t, 256), 256)
                v = dot_nt(act[tok, : 2 * MAIN], w[dr, : 2 * MAIN])
                u = dot_nt(act[tok, 2 * MAIN : 3 * MAIN], w[dr, 2 * MAIN : 3 * MAIN])
                if more:
                    v += dot_nt(act[tok, 3 * MAIN : 3 * MAIN + 256], w[dr, 3 * MAIN : 3 * MAIN + 256])
                    u += dot_nt(act[tok, 3 * MAIN + 256 :], w[dr, 3 * MAIN + 256 :])
                pg[rows, :, dr] = v.astype(BF).reshape(4, 128, 256)
                po[rows, :, dr] = u.astype(BF).reshape(4, 128, 256)
        when(extra, lambda: out_tiles(True))
        when(~extra, lambda: out_tiles(False))
        rg.send_c(zz)
        ro.send_c(zz)

    g.from_z(p[1])
    when(mid, lambda: g.from_z(p[2]))
    g.from_x(p[0])
    g.from_c(p[0])
    pltpu.make_async_copy(n2_ref, n2.at[0], glocal).wait()
    tiles(p[0])
    g.from_z(jnp.where(mid, p[3], p[2]))
    g.from_x(p[1])
    g.from_c(p[1])
    tiles(p[1])
    when(~mid, lambda: g.from_z(p[3]))
    g.from_x(p[2])
    g.from_c(p[2])
    tiles(p[2])
    rg.x_plane(p[2])
    g.from_x(p[3])
    g.from_c(p[3])
    tiles(p[3])

    ydev = (1 - r, idx(z, x, c))
    own = D // 16
    half = own // 2
    def ycopy(j, spare):
        cols = SP if spare else MM
        src = w.at[pl.ds(pl.multiple_of(own * j + half * (1 - r), half), half), cols]
        a, b = (xsend, xrecv) if spare else (ysend, yrecv)
        return pltpu.make_async_remote_copy(src, yb.at[j, :, cols], a.at[j], b.at[j], device_id=ydev, device_id_type=MESH)
    def grads(q):
        dr = slice(384 * q, 384 * (q + 1))
        row = slice(384 * q, 384 * (q + 1))
        @pl.loop(0, 4)
        def _(t):
            col = pl.ds(pl.multiple_of(256 * t, 256), 256)
            w[row, col] = dot_tn(n2[:, :, dr].reshape(2048, 384), act[:, col]).astype(BF)
        @pl.loop(0, 2)
        def _(t):
            col = pl.ds(pl.multiple_of(2 * MAIN + 256 * t, 256), 256)
            w[row, col] = dot_tn(cot[:, :, dr].reshape(2048, 384), act[:, col]).astype(BF)
        for j in range(4 * q, 4 * q + 4):
            ycopy(j, 0).start()
        def spare():
            w[row, 3 * MAIN : 3 * MAIN + 256] = dot_tn(n2[:, :, dr].reshape(2048, 384), act[:, 3 * MAIN : 3 * MAIN + 256]).astype(BF)
            w[row, 3 * MAIN + 256 :] = dot_tn(cot[:, :, dr].reshape(2048, 384), act[:, 3 * MAIN + 256 :]).astype(BF)
            for j in range(4 * q, 4 * q + 4):
                ycopy(j, 1).start()
        when(extra, spare)
    def yadd(j):
        def add(spare):
            cols = SP if spare else MM
            ycopy(j, spare).wait()
            mine = w[pl.ds(pl.multiple_of(own * j + half * r, half), half), cols]
            yb[j, :, cols] = (mine.astype(F32) + yb[j, :, cols].astype(F32)).astype(BF)
            pltpu.make_async_copy(yb.at[j, :, cols], half_ref.at[j, :, cols], lsem.at[4 if spare else 2]).start()
        add(0)
        when(extra, lambda: add(1))

    rg.x_plane(p[3])
    rg.x_plane(p[1])
    rg.x_plane(p[0])
    grads(0)
    rg.step_z(3)
    rg.step_z(2)
    ro.x_plane(p[3])
    grads(1)
    rg.step_z(1)
    ro.x_plane(p[2])
    grads(2)
    ro.x_plane(p[1])
    ro.step_z(3)
    rg.finish(gsum)
    grads(3)
    ro.x_plane(p[0])
    ro.step_z(2)
    for j in range(0, 8): yadd(j)
    ro.step_z(1)
    for j in range(8, 12): yadd(j)
    ro.finish(osum)
    for j in range(12, 16): yadd(j)
    pltpu.make_async_copy(yb.at[:, :, MM], half_ref.at[:, :, MM], lsem.at[2]).wait()
    when(extra, lambda: pltpu.make_async_copy(yb.at[:, :, SP], half_ref.at[:, :, SP], lsem.at[4]).wait())
    g.end(local=False)

def mlp(n2, cot, w, cid):
    blk = n2.shape
    dma = pltpu.SemaphoreType.DMA
    full = (16,) + blk
    return pl.pallas_call(
        mlp_kernel,
        out_shape=[jax.ShapeDtypeStruct(blk, F32)] * 2 + [jax.ShapeDtypeStruct((16, D // 32, COLS), BF)],
        in_specs=[pl.BlockSpec(memory_space=pl.ANY)] * 3,
        out_specs=[pl.BlockSpec(memory_space=pltpu.VMEM)] * 2 + [pl.BlockSpec(memory_space=pl.ANY)],
        scratch_shapes=[pltpu.VMEM(full, BF), pltpu.VMEM(full, BF), pltpu.VMEM((D, COLS), BF), pltpu.VMEM((16 * blk[0], COLS), BF),
                        pltpu.VMEM(full, BF), pltpu.VMEM(full, BF)]
        + [pltpu.VMEM((k,) + blk, BF) for k in (8, 4, 5, 8, 4, 5)]
        + [pltpu.VMEM((16, D // 32, COLS), BF)]
        + [dma((18,)), dma((16,)), dma(()), dma((5,)), dma((2, 16)), dma((2, 8)), dma((2, 4)), dma((2, 5))] + [dma((16,))] * 4,
        compiler_params=pltpu.CompilerParams(collective_id=cid, has_side_effects=True, vmem_limit_bytes=60 * 2**20),
    )(n2, cot, w)


def spin(u, cos, sin):
    return u * cos + pltpu.roll(u, HEAD_DIM // 2, 1) * sin

def stack_heads(v):
    n = v.shape[1] // HEAD_DIM
    return jnp.concatenate([v[:, HEAD_DIM * i : HEAD_DIM * (i + 1)] for i in range(n)], axis=0)

def spread_heads(v, rows):
    n = v.shape[0] // rows
    return jnp.concatenate([v[rows * i : rows * (i + 1)] for i in range(n)], axis=1)

def exp_scores(q, k, first_row, block, length):
    sc = dot_nt(q, k) * (HEAD_DIM ** -0.5)
    key = lax.broadcasted_iota(jnp.int32, sc.shape, 1)
    row = jnp.bitwise_and(lax.broadcasted_iota(jnp.int32, sc.shape, 0), block - 1) + first_row
    return jnp.where((key <= row) & (key < length), jnp.exp(sc), 0.0)

def rms(v, gain):
    factor = lax.rsqrt(jnp.mean(v * v, axis=-1, keepdims=True) + EPSILON)
    return v * factor * gain


class GatherY(Gather):
    def __init__(self, at, src, out, send, recv, local):
        Gather.__init__(self, at, src, out, send, recv, local)
        self.n = src.shape[0] // 2
        self.ydev = (1 - self.r, idx(self.z, self.x, self.c))
    def rows(self, h):
        return pl.ds(pl.multiple_of(h * self.n, self.n), self.n)
    def half(self, b, h):
        return self.out.at[b, self.rows(h)]
    def move(self, src, dst, k, q, dev):
        return pltpu.make_async_remote_copy(src, dst, self.send.at[k], self.recv.at[q], device_id=dev, device_id_type=MESH)
    def arrived(self, b, h):
        self.move(self.half(b, h), self.half(b, h), 0, 2 * b + h, self.ydev).wait_recv()
    def begin(self):
        z, x, c, r = self.z, self.x, self.c, self.r
        me = idx(z, x, c)
        mine, dst = self.src.at[self.rows(r)], self.half(me, r)
        for s in (1, -1):
            when(self.inside(z + s), lambda s=s: self.move(mine, dst, 0 if s == 1 else 3, 2 * me + r, self.zdev(s)).start())
        self.move(mine, dst, 6 + z, 2 * me + r, self.xdev()).start()
        self.move(self.src, self.out.at[me], 18 + 2 * z + x, 2 * me, self.cdev()).start()
        pltpu.make_async_copy(self.src, self.out.at[me], self.local).start()
    def from_z(self, zz):
        z, x, c, r = self.z, self.x, self.c, self.r
        b = idx(zz, x, c)
        q = 2 * b + r
        self.arrived(b, r)
        s = jnp.where(zz < z, 1, -1)
        slot = jnp.where(zz < z, 0, 3) + jnp.abs(zz - z)
        a = self.half(b, r)
        when(self.inside(z + s), lambda: self.move(a, a, slot, q, (r, idx(z + s, x, c))).start())
        self.move(a, a, 6 + zz, q, self.xdev()).start()
        self.move(a, a, 18 + 2 * zz + x, q, self.cdev()).start()
        self.move(a, a, 10 + 2 * zz + x, q, self.ydev).start()
    def from_x(self, zz):
        x, c, r = self.x, self.c, self.r
        b = idx(zz, 1 - x, c)
        q = 2 * b + r
        self.arrived(b, r)
        a = self.half(b, r)
        self.move(a, a, 18 + 2 * zz + 1 - x, q, self.cdev()).start()
        self.move(a, a, 10 + 2 * zz + 1 - x, q, self.ydev).start()
    def from_y(self, zz):
        x, c, r = self.x, self.c, self.r
        def take(xx):
            b = idx(zz, xx, c)
            self.arrived(b, 1 - r)
            a = self.half(b, 1 - r)
            self.move(a, a, 26 + 2 * zz + xx, 2 * b + 1 - r, self.cdev()).start()
        when(zz != self.z, lambda: take(x))
        take(1 - x)
    def from_c(self, zz):
        x, c, r = self.x, self.c, self.r
        b = idx(zz, x, 1 - c)
        whole = self.out.at[b]
        when(zz == self.z, lambda: self.move(whole, whole, 0, 2 * b, self.ydev).wait_recv())
        def both(b):
            self.arrived(b, r)
            self.arrived(b, 1 - r)
        when(zz != self.z, lambda: both(b))
        both(idx(zz, 1 - x, 1 - c))
    def end(self):
        z, x = self.z, self.x
        own = 2 * z + x
        a = self.half(0, 0)
        def sent(k, a=a):
            self.move(a, a, k, 0, self.ydev).wait_send()
        for d in range(NZ - 1):
            when((z - d >= 0) & (z < NZ - 1), lambda d=d: sent(d))
            when((z + d < NZ) & (z > 0), lambda d=d: sent(3 + d))
        for k in range(6, 10):
            sent(k)
        for k in range(8):
            def other(k=k):
                sent(10 + k)
                sent(18 + k)
                sent(26 + k)
            when(own != k, other)
        sent(18 + own, self.out.at[0])
        pltpu.make_async_copy(self.src, self.out.at[0], self.local).wait()

def front_kernel(block, lens, x_ref, cot_ref, v0, v1, v2, v3, v4, sel, fold, selk, foldk, rope_ref, wq, wk, wv, wg, wu, wd, wo_ref,
                 q_out, normed_out, att_out, mid_out, n2_out, vec, buf, qkv_out, kv_out, cot_out, wo_out,
                 rope, cot_own, small, qkv_own, wqkv, small_all, own, kv, wo,
                 qs, qr, ql, vs, vr, vl, ks, kr, kl, cs, cr, cl, ws, wr, wl, d0, d1, d2, d3, d4, d5, d6, d7, dl, lsem):
    at = place()
    width = HEADS * HEAD_DIM
    kw = KV_HEADS * HEAD_DIM
    loads = [pltpu.make_async_copy(w, qkv_own.at[:, pl.ds(o, n)], lsem.at[i]) for i, (w, o, n) in enumerate(((wq, 0, width), (wk, width, kw), (wv, width + kw, kw)))]
    first_row = lax.axis_index("group") * block
    loads.append(pltpu.make_async_copy(rope_ref.at[:, pl.ds(pl.multiple_of(first_row, block), block)], rope, lsem.at[6]))
    for l in loads: l.start()
    small[...] = jnp.zeros_like(small)
    for i, v in enumerate((v0, v1, v2, v3, v4)):
        small[i : i + 1, : v.shape[1]] = v[...].astype(F32)
    cot_own[...] = (cot_ref[...].astype(F32) * row_mask(lens, first_row, block, (cot_ref.shape[0], 1))).astype(BF)
    hail_all(*at)
    for l in loads: l.wait()
    gq = GatherY(at, qkv_own, wqkv, qs, qr, ql)
    gv = Gather(at, small, small_all, vs, vr, vl)
    gk = Gather(at, own, kv, ks, kr, kl)
    gc = Gather(at, cot_own, cot_out, cs, cr, cl)
    gw = GatherY(at, wo_ref, wo, ws, wr, wl)
    d = Deal(at, (wg, wu, wd), buf, (d0, d1, d2, d3, d4, d5, d6, d7), dl)
    steps = iter(range(15))
    def some(n):
        for _ in range(n):
            i = next(steps, None)
            if i is not None:
                d.step(i)
    gq.begin()
    gv.begin()
    d.begin()
    x = x_ref[...].astype(F32)
    gq.first()
    gv.first()
    some(1)
    gq.second()
    gv.second()
    gq.from_y(gq.p[0])
    some(EARLY[0])
    gq.third()
    gv.third()
    gq.from_y(gq.p[1])
    some(1)
    gq.fourth()
    gv.fourth()
    gc.begin()
    gq.from_y(gq.p[2])
    gq.from_y(gq.p[3])
    for zz in range(NZ):
        gv.from_c(zz)
        gq.from_c(zz)
    gv.end()
    gq.end()
    keep = [pltpu.make_async_copy(wqkv, qkv_out, lsem.at[3]), pltpu.make_async_copy(kv, kv_out, lsem.at[4]), pltpu.make_async_copy(wo, wo_out, lsem.at[5])]
    keep[0].start()
    vec[...] = jnp.zeros_like(vec)
    for i, row, first, a, b in ((0, 0, 0, sel, fold), (1, 1, 0, sel, fold), (2, 1, width, selk, foldk), (3, 1, width + kw, selk, foldk), (4, 2, 0, sel, fold)):
        t = dot_nt(small_all[:, i, :].astype(BF), b[...])
        vec[row : row + 1, first : first + a.shape[1]] = jnp.sum(t * a[...], axis=0, keepdims=True)
    normed_out[...] = rms(x, vec[0:1, :width]).astype(BF)
    cos, sin = [jnp.concatenate((rope[i], rope[i]), axis=0) for i in range(2)]
    def product(base):
        return dot(normed_out[...], wqkv[:, :, pl.ds(pl.multiple_of(base, 256), 256)].reshape(width, 256)) + vec[1:2, pl.ds(pl.multiple_of(base, 256), 256)]
    pre = product(width)
    own[:, :HEAD_DIM] = spin(pre[:, :HEAD_DIM], cos, sin).astype(BF)
    own[:, HEAD_DIM : 2 * HEAD_DIM] = spin(pre[:, HEAD_DIM:], cos, sin).astype(BF)
    own[:, kw:] = product(width + kw).astype(BF)
    gk.begin()
    gw.begin()
    @pl.loop(0, width // 256)
    def _(t):
        pre = product(t * 256)
        for i in range(2):
            col = pl.ds(pl.multiple_of(256 * t + HEAD_DIM * i, HEAD_DIM), HEAD_DIM)
            q_out[:, col] = spin(pre[:, HEAD_DIM * i : HEAD_DIM * (i + 1)], cos, sin).astype(BF)
    some(EARLY[1])
    gc.first()
    gk.first()
    some(1)
    gw.first()
    some(EARLY[2])
    gk.second()
    gc.second()
    gw.second()
    some(1)
    gw.from_y(gw.p[0])
    gk.third()
    some(EARLY[3])
    gk.fourth()
    gc.third()
    gw.third()
    some(1)
    gw.from_y(gw.p[1])
    for zz in range(NZ):
        gk.from_c(zz)
    gk.end()
    keep[1].start()
    span = 16 * block
    @pl.loop(0, 4)
    def _(u):
        s, h = u // 2, lax.rem(u, 2)
        rows = pl.ds(pl.multiple_of(block * s, block), block)
        cols = pl.ds(pl.multiple_of(width // 2 * h, width // 2), width // 2)
        q = stack_heads(q_out[rows, cols])
        k = kv[:, rows, pl.ds(pl.multiple_of(HEAD_DIM * h, HEAD_DIM), HEAD_DIM)].reshape(span, HEAD_DIM)
        v = kv[:, rows, pl.ds(pl.multiple_of(kw + HEAD_DIM * h, HEAD_DIM), HEAD_DIM)].reshape(span, HEAD_DIM)
        e = exp_scores(q, k, first_row, block, lens[s])
        total = jnp.sum(e, axis=-1, keepdims=True)
        att_out[rows, cols] = spread_heads(dot(e.astype(BF), v) / total, block)
    some(EARLY[4])
    gw.fourth()
    some(1)
    gc.fourth()
    some(1)
    gw.from_y(gw.p[2])
    gw.from_y(gw.p[3])
    for zz in range(NZ):
        gw.from_c(zz)
    gw.end()
    keep[2].start()
    @pl.loop(0, width // 256)
    def _(t):
        col = pl.ds(pl.multiple_of(256 * t, 256), 256)
        mid_out[:, col] = x_ref[:, col].astype(F32) + dot(att_out[...].astype(BF), wo[:, :, col].reshape(width, 256))
    n2_out[...] = rms(mid_out[...], vec[2:3, :width]).astype(BF)
    some(15)
    for zz in range(NZ):
        gc.from_c(zz)
    gc.end()
    for k in keep:
        k.wait()
    d.end()

EARLY = (1, 1, 1, 1, 2)

def front(lens, x, cot, vectors, sel, fold, selk, foldk, rope, wq, wk, wv, wg, wu, wd, wo, block, cid):
    rows, width = x.shape
    any_ = pl.BlockSpec(memory_space=pl.ANY)
    vm = pl.BlockSpec(memory_space=pltpu.VMEM)
    dma = pltpu.SemaphoreType.DMA
    act = (rows, width)
    own = wq.shape[0]
    kvw = 2 * KV_HEADS * HEAD_DIM
    wide = width + kvw
    sds = jax.ShapeDtypeStruct
    VM = pltpu.VMEM
    return pl.pallas_call(
        functools.partial(front_kernel, block),
        out_shape=[sds(act, BF), sds(act, BF), sds(act, F32), sds(act, F32), sds(act, BF), sds((8, wide), F32),
                   sds((16 * own, 3 * MAIN + 384), BF), sds((16, own, wide), BF), sds((16, rows, kvw), BF), sds((16,) + act, BF), sds((16,) + wo.shape, BF)],
        in_specs=[pl.BlockSpec(memory_space=pltpu.SMEM)] + [vm] * 11 + [any_] * 8,
        out_specs=[vm] * 6 + [any_] * 5,
        scratch_shapes=[VM((2, block, HEAD_DIM), F32), VM(act, BF), VM((8, 128), F32), VM((own, wide), BF), VM((16, own, wide), BF), VM((16, 8, 128), F32), VM((rows, kvw), BF), VM((16, rows, kvw), BF), VM((16,) + wo.shape, BF)]
        + [dma((34,)), dma((32,)), dma(())] + [dma((18,)), dma((16,)), dma(())] * 3 + [dma((34,)), dma((32,)), dma(())]
        + [dma((16,))] * 8 + [dma((2,)), dma((7,))],
        compiler_params=pltpu.CompilerParams(collective_id=cid, has_side_effects=True, vmem_limit_bytes=60 * 2**20),
    )(lens, x, cot, *vectors, sel, fold, selk, foldk, rope, wq, wk, wv, wg, wu, wd, wo)


class Return:
    def __init__(self, at, half_ref, out, sems, local):
        self.r, self.z, self.x, self.c = at
        self.me = idx(self.z, self.x, self.c)
        self.src, self.out, self.sems, self.local = half_ref, out, sems, local
        self.n = half_ref.shape[1]
    def places(self, j, spare):
        row = pl.ds(pl.multiple_of(self.r * self.n, self.n), self.n)
        col = spare_at(j) if spare else pl.ds(pl.multiple_of(j * MAIN, MAIN), MAIN)
        return [o.at[row, col] for o in self.out]
    def parts(self, j, spare):
        if spare:
            return [self.src.at[j, :, pl.ds(3 * MAIN + 128 * i, 128)] for i in range(3)]
        return [self.src.at[j, :, pl.ds(i * MAIN, MAIN)] for i in range(3)]
    def copy(self, a, b, kind, k, dev):
        send, recv = self.sems[2 * kind : 2 * kind + 2]
        return pltpu.make_async_remote_copy(a, b, send.at[k], recv.at[k], device_id=dev, device_id_type=MESH)
    def launch(self, k):
        j = jnp.bitwise_xor(self.me, k)
        def go(spare):
            for a, b in zip(self.parts(j, spare), self.places(self.me, spare)):
                self.copy(a, b, spare, k, (self.r, j)).start()
        go(0)
        when(has(self.me), lambda: go(1))
    def forward(self, j, k, spare):
        for a in self.places(j, spare):
            self.copy(a, a, 2 + spare, k, (1 - self.r, self.me)).start()
    def begin(self, window):
        self.window = window
        def go(spare):
            for a, b in zip(self.parts(self.me, spare), self.places(self.me, spare)):
                pltpu.make_async_copy(a, b, self.local.at[spare]).start()
        go(0)
        when(has(self.me), lambda: go(1))
        for k in KS[:window]:
            self.launch(k)
    def sized(self, spare):
        return self.src.at[0, :, pl.ds(3 * MAIN, 384) if spare else pl.ds(0, 3 * MAIN)]
    def whole(self, kind, k):
        blk = self.sized(kind % 2)
        return self.copy(blk, blk, kind, k, (1 - self.r, self.me))
    def own(self):
        def go(spare):
            blk = self.sized(spare)
            pltpu.make_async_copy(blk, blk, self.local.at[spare]).wait()
            self.forward(self.me, 0, spare)
        go(0)
        when(has(self.me), lambda: go(1))
    def step(self, i):
        k = KS[i]
        j = jnp.bitwise_xor(self.me, k)
        def go(spare):
            self.whole(spare, k).wait_recv()
            self.forward(j, k, spare)
        go(0)
        when(has(j), lambda: go(1))
        if i + self.window < 15:
            self.launch(KS[i + self.window])
    def end(self):
        for k in (0,) + KS:
            j = jnp.bitwise_xor(self.me, k)
            self.whole(2, k).wait()
            when(has(j), lambda: self.whole(3, k).wait())
            if k:
                self.whole(0, k).wait_send()
                when(has(self.me), lambda: self.whole(1, k).wait_send())

def row_mask(lens, first_row, block, shape):
    row = lax.broadcasted_iota(jnp.int32, shape, 0)
    place = jnp.bitwise_and(row, block - 1) + first_row
    return jnp.where(place < jnp.where(row < block, lens[0], lens[1]), 1.0, 0.0)

def norm_gradient(v, gain, upstream):
    factor = lax.rsqrt(jnp.mean(v * v, axis=-1, keepdims=True) + EPSILON)
    weighted = upstream * gain
    inner = jnp.mean(weighted * v, axis=-1, keepdims=True)
    return factor * weighted - v * (factor * factor * factor) * inner, jnp.sum(upstream * v * factor, axis=0, keepdims=True)

def backward_kernel(block, window, lens, gn2, mlp_out, mid, cot, x_ref, att, q_ref, normed, vec, sel, fold, selk, foldk, rope_ref, kv_ref, wo_ref, wqkv_ref, half_ref,
                    layer_out, grad_input, q_out, k_out, v_out, wo_out, vec_out, g0, g1, g2,
                    rope, kv, wo, wqkv, gmid, branch, gatt, gqkv, pv,
                    p_kv, c_kv, x_kv, z_kv, p_wo, c_wo, x_wo, z_wo, p_qk, c_qk, w_qk, x_qk, z_qk, p_pw, c_pw, x_pw, z_pw, p_ve, c_ve, x_ve, z_ve,
                    kvsum, pair_out, low_q, y2, y3, y4, y5, y6, y7,
                    ss, sc, sx, sz, r0, r1, r2, r3, r4, r5, r6, r7, rl, ysem, fs, fc, fy, fx, fz, ft, lsem):
    at = place()
    r, z, x, c = at
    width = HEADS * HEAD_DIM
    kw = KV_HEADS * HEAD_DIM
    loads = [pltpu.make_async_copy(a, b, lsem.at[i]) for i, (a, b) in enumerate(((wo_ref, wo), (kv_ref, kv), (wqkv_ref, wqkv)))]
    first_row = lax.axis_index("group") * block
    loads.append(pltpu.make_async_copy(rope_ref.at[:, pl.ds(pl.multiple_of(first_row, block), block)], rope, lsem.at[3]))
    for l in loads: l.start()
    hail_all(*at)
    back = Return(at, half_ref, (g0, g1, g2), (r0, r1, r2, r3, r4, r5, r6, r7), rl)
    back.begin(window)
    sets = ((p_kv, c_kv, x_kv, z_kv), (p_wo, c_wo, x_wo, z_wo), (p_pw, c_pw, x_pw, z_pw), (p_ve, c_ve, x_ve, z_ve))
    ek, eo, ep, ev = [Scatter(at, *b, ss.at[i], sc.at[i], sx.at[i], sz.at[i]) for i, b in enumerate(sets)]
    eq = ScatterY(at, p_qk, c_qk, w_qk, x_qk, z_qk, fs, fc, fy, fx, fz, ft)
    steps = iter(range(15))
    def some(n):
        for _ in range(n):
            i = next(steps, None)
            if i is not None:
                back.step(i)
    ydev = (1 - r, idx(z, x, c))
    def trade(i, out, a, b):
        a[...] = out[...].astype(BF)
        pltpu.make_async_remote_copy(a, b, ysem.at[2 * i], ysem.at[2 * i + 1], device_id=ydev, device_id_type=MESH).start()
    def traded(i, out, a, b):
        pltpu.make_async_remote_copy(a, b, ysem.at[2 * i], ysem.at[2 * i + 1], device_id=ydev, device_id_type=MESH).wait()
        out[...] = a[...].astype(F32) + b[...].astype(F32)

    grad_norm, gain_two = norm_gradient(mid[...], vec[2:3, :width], gn2[...])
    valid = row_mask(lens, first_row, block, (cot.shape[0], 1))
    gmid[...] = cot[...].astype(F32) * valid + grad_norm
    branch[...] = gmid[...].astype(BF)
    loads[0].wait()
    @pl.loop(0, 4)
    def _(t):
        blocks = pl.ds(pl.multiple_of(4 * t, 4), 4)
        col = pl.ds(pl.multiple_of(384 * t, 384), 384)
        low = att[:, col].astype(BF)
        p_wo[blocks] = dot_tn(low, branch[...]).astype(BF).reshape(4, 96, width)
        gatt[:, col] = dot_nt(branch[...], wo[blocks].reshape(384, width))
    eo.begin()
    eo.step_x(3)
    eo.step_x(2)
    back.own()
    layer_out[...] = ((mid[...] + mlp_out[...]) * valid).astype(BF)
    loads[1].wait()
    loads[3].wait()
    span = 16 * block
    def unit(u):
        s, h = u // 2, lax.rem(u, 2)
        rows = pl.ds(pl.multiple_of(block * s, block), block)
        cols = pl.ds(pl.multiple_of(width // 2 * h, width // 2), width // 2)
        kcol = pl.ds(pl.multiple_of(HEAD_DIM * h, HEAD_DIM), HEAD_DIM)
        vcol = pl.ds(pl.multiple_of(kw + HEAD_DIM * h, HEAD_DIM), HEAD_DIM)
        q = stack_heads(q_ref[rows, cols])
        k = kv[:, rows, kcol].reshape(span, HEAD_DIM)
        v = kv[:, rows, vcol].reshape(span, HEAD_DIM)
        e = exp_scores(q, k, first_row, block, lens[s])
        total = jnp.sum(e, axis=-1, keepdims=True)
        ga = stack_heads(gatt[rows, cols])
        gt = -jnp.sum(ga * stack_heads(att[rows, cols]), axis=-1, keepdims=True) / total
        gn = (ga / total).astype(BF)
        gs = (e * (dot_nt(gn, v) + gt)).astype(BF)
        p_kv[:, rows, kcol] = dot_tn(gs, q).astype(BF).reshape(16, block, HEAD_DIM)
        p_kv[:, rows, vcol] = dot_tn(e.astype(BF), gn).astype(BF).reshape(16, block, HEAD_DIM)
        gq = dot(gs, k) * (HEAD_DIM ** -0.5)
        cos, sin = rope[0], rope[1]
        gqkv[rows, cols] = jnp.concatenate([spin(gq[block * i : block * (i + 1)], cos, -sin) for i in range(HEADS // KV_HEADS)], axis=1).astype(BF)
    unit(0)
    some(1)
    eo.step_z(3)
    eo.step_x(1)
    unit(1)
    some(1)
    eo.step_z(2)
    eo.step_x(0)
    unit(2)
    some(1)
    eo.step_z(1)
    unit(3)
    ek.begin()
    ek.step_x(3)
    ek.step_x(2)
    some(1)
    loads[2].wait()
    @pl.loop(0, 4)
    def _(t):
        blocks = pl.ds(pl.multiple_of(4 * t, 4), 4)
        col = pl.ds(pl.multiple_of(384 * t, 384), 384)
        p_qk[blocks] = dot_tn(normed[:, col], gqkv[:, :width]).astype(BF).reshape(4, 96, width)
    ek.step_z(3)
    ek.step_x(1)
    eq.begin()
    eo.finish(wo_out)
    trade(2, wo_out, y2, y3)
    for d in (3, 2, 1, 0):
        eq.step_y(d)
    ek.step_z(2)
    ek.step_x(0)
    some(1)
    @pl.loop(0, 4)
    def _(t):
        blocks = pl.ds(pl.multiple_of(4 * t, 4), 4)
        col = pl.ds(pl.multiple_of(384 * t, 384), 384)
        gatt[:, col] = dot_nt(gqkv[:, :width], wqkv[blocks, :, :width].reshape(384, width))
    ek.step_z(1)
    eq.step_x(3)
    eq.step_x(2)
    some(1)
    ek.finish(kvsum)
    cos, sin = [jnp.concatenate((rope[i], rope[i]), axis=0) for i in range(2)]
    for h in range(KV_HEADS):
        kcol = slice(HEAD_DIM * h, HEAD_DIM * (h + 1))
        gqkv[:, width + HEAD_DIM * h : width + HEAD_DIM * (h + 1)] = spin(kvsum[:, kcol] * (HEAD_DIM ** -0.5), cos, -sin).astype(BF)
    gqkv[:, width + kw :] = kvsum[:, kw:].astype(BF)
    @pl.loop(0, 4)
    def _(t):
        blocks = pl.ds(pl.multiple_of(4 * t, 4), 4)
        col = pl.ds(pl.multiple_of(384 * t, 384), 384)
        p_pw[blocks] = dot_tn(normed[:, col], gqkv[:, width:]).astype(BF).reshape(4, 96, 2 * kw)
        gatt[:, col] += dot_nt(gqkv[:, width:], wqkv[blocks, :, width:].reshape(384, 2 * kw))
    ep.begin()
    ep.step_x(3)
    ep.step_x(2)
    eq.step_z(3)
    eq.step_x(1)
    some(1)
    grad_norm, gain_one = norm_gradient(x_ref[...].astype(F32), vec[0:1, :width], gatt[...])
    grad_input[...] = gmid[...] + grad_norm
    bias = jnp.sum(gqkv[...].astype(F32), axis=0, keepdims=True)
    pv[...] = jnp.zeros_like(pv)
    for i, (v, a, b) in enumerate(((gain_one, sel, fold), (bias[:, :width], sel, fold), (bias[:, width : width + kw], selk, foldk), (bias[:, width + kw :], selk, foldk), (gain_two, sel, fold))):
        pv[:, i, :] = dot((a[...] * v).astype(BF), b[...])
    p_ve[...] = pv[...].astype(BF)
    ev.begin()
    ev.step_x(3)
    ev.step_x(2)
    some(1)
    late = (ep, ev)
    for kind, d in (("z", 3), ("x", 1), ("z", 2), ("x", 0), ("z", 1)):
        for e in late:
            (e.step_x if kind == "x" else e.step_z)(d)
        if (kind, d) not in (("z", 3), ("x", 1)):
            (eq.step_x if kind == "x" else eq.step_z)(d)
        some(1)
    some(15)
    eq.finish(q_out, low_q)
    ep.finish(pair_out)
    trade(0, pair_out, y4, y5)
    ev.finish(vec_out)
    trade(1, vec_out, y6, y7)
    traded(2, wo_out, y2, y3)
    eq.traded(q_out, low_q)
    traded(0, pair_out, y4, y5)
    k_out[...] = pair_out[:, :kw]
    v_out[...] = pair_out[:, kw:]
    traded(1, vec_out, y6, y7)
    back.end()

def backward(lens, gn2, mlp_out, mid, cot, x, att, q, normed, vec, sel, fold, selk, foldk, rope, kv, wo, wqkv, half, ff, block, cid, window=4):
    any_ = pl.BlockSpec(memory_space=pl.ANY)
    vm = pl.BlockSpec(memory_space=pltpu.VMEM)
    dma = pltpu.SemaphoreType.DMA
    sds = jax.ShapeDtypeStruct
    rows, width = x.shape
    wide = wqkv.shape[-1]
    own = wo.shape[1]
    kvw = kv.shape[-1]
    VM = pltpu.VMEM
    def four(blk):
        return [VM((k,) + blk, BF) for k in (16, 8, 4, 5)]
    def five(blk):
        part = (blk[0] // 2, blk[1])
        return [VM((k,) + blk, BF) for k in (16, 8)] + [VM((k,) + part, BF) for k in (8, 4, 5)]
    return pl.pallas_call(
        functools.partial(backward_kernel, block, window),
        out_shape=[sds((rows, width), BF), sds((rows, width), F32), sds((own, width), F32), sds((own, (wide - width) // 2), F32), sds((own, (wide - width) // 2), F32), sds((own, width), F32), sds((16, 128), F32), sds((own, ff), BF)] + [sds((own, ff), BF)] * 2,
        in_specs=[pl.BlockSpec(memory_space=pltpu.SMEM)] + [vm] * 13 + [any_] * 5,
        out_specs=[vm] * 7 + [any_] * 3,
        scratch_shapes=[VM((2, block, HEAD_DIM), F32), VM(kv.shape, BF), VM(wo.shape, BF), VM(wqkv.shape, BF), VM((rows, width), F32), VM((rows, width), BF), VM((rows, width), F32), VM((rows, wide), BF), VM((16, 16, 128), F32)]
        + four((rows, kvw)) + four((own, width)) + five((own, width)) + four((own, wide - width)) + four((16, 128))
        + [VM((rows, kvw), F32), VM((own, wide - width), F32)] + [VM((own, width), BF)] * 3 + [VM((own, wide - width), BF)] * 2 + [VM((16, 128), BF)] * 2
        + [dma((4, 16)), dma((4, 8)), dma((4, 4)), dma((4, 5))] + [dma((16,))] * 8 + [dma((2,)), dma((6,)), dma((24,)), dma((8,)), dma((8,)), dma((4,)), dma((5,)), dma((2,)), dma((4,))],
        compiler_params=pltpu.CompilerParams(collective_id=cid, has_side_effects=True, vmem_limit_bytes=60 * 2**20),
    )(lens, gn2, mlp_out, mid, cot, x, att, q, normed, vec, sel, fold, selk, foldk, rope, kv, wo, wqkv, half)


def folding(group_count, width):
    share = width // group_count
    at = np.arange(width)
    sel = (at[None, :] // share == np.arange(group_count)[:, None]).astype(np.float32)
    fold = (at[:, None] % share == np.arange(128)[None, :]).astype(BF)
    return sel, fold


def rope_constants(span):
    freqs = np.float32(THETA) ** (-np.arange(0, HEAD_DIM, 2, dtype=np.float32) / HEAD_DIM)
    angles = np.arange(span, dtype=np.float32)[:, None] * freqs[None, :].astype(np.float32)
    sin = np.sin(angles)
    return np.stack(
        (np.concatenate((np.cos(angles),) * 2, axis=1), np.concatenate((-sin, sin), axis=1))
    ).astype(np.float32)


def shards_fast(
    hidden_in,
    lengths,
    gain_attn,
    w_query,
    b_query,
    w_key,
    b_key,
    w_value,
    b_value,
    w_out,
    gain_mlp,
    w_gate,
    w_up,
    w_down,
    cotangent,
):
    group_count = lax.axis_size("group")
    slot_count, block_len, model_width = hidden_in.shape
    kv_width = KV_HEADS * HEAD_DIM
    tokens = slot_count * block_len
    hidden_units = w_gate.shape[1]
    pieces = (gain_attn, b_query, b_key, b_value, gain_mlp)
    sel, fold = folding(group_count, model_width)
    selk, foldk = folding(group_count, kv_width)
    rope = rope_constants(group_count * block_len)
    rows_in = hidden_in.reshape(tokens, model_width)
    grad_rows = cotangent.reshape(tokens, model_width)
    (
        q_rows, normed, attended, mid, normed_two, vec, columns, qkv_w, pair_all, grad_all, out_w
    ) = front(
        lengths,
        rows_in,
        grad_rows,
        [p[None] for p in pieces],
        sel,
        fold,
        selk,
        foldk,
        rope,
        w_query,
        w_key,
        w_value,
        w_gate,
        w_up,
        w_down,
        w_out,
        block_len,
        1,
    )
    grad_normed_two, mlp_out, half_sum = mlp(normed_two, grad_all, columns, 3)
    layer_out, grad_input, query_sum, key_sum, value_sum, out_sum, vector_sum, *ff_sums = backward(
        lengths,
        grad_normed_two,
        mlp_out,
        mid,
        grad_rows,
        rows_in,
        attended,
        q_rows,
        normed,
        vec,
        sel,
        fold,
        selk,
        foldk,
        rope,
        pair_all,
        out_w,
        qkv_w,
        half_sum,
        hidden_units,
        block_len,
        4,
        2,
    )
    ff_sums = [p.astype(F32) for p in ff_sums]
    gain_one_sum, query_bias_sum, key_bias_sum, value_bias_sum, gain_two_sum = [
        vector_sum[i, : p.shape[0]] for i, p in enumerate(pieces)
    ]
    return (
        layer_out.reshape(hidden_in.shape),
        grad_input.reshape(hidden_in.shape),
        gain_one_sum,
        query_sum,
        query_bias_sum,
        key_sum,
        key_bias_sum,
        value_sum,
        value_bias_sum,
        out_sum,
        gain_two_sum,
        *ff_sums,
    )


def solution(mesh):
    act = P("replica", "group", None)
    vec = P("group")
    mat = P("group", None)
    return jax.shard_map(
        shards_fast if mesh.shape["group"] == 16 else shards_plain,
        mesh=mesh,
        in_specs=(act, P("replica"), vec, mat, vec, mat, vec, mat, vec, mat, vec, mat, mat, mat, act),
        out_specs=(act, act, vec, mat, vec, mat, vec, mat, vec, mat, vec, mat, mat, mat),
        check_vma=False,
    )
```
